32 devices in a mesh: dp: 4 (over z), mp: 8 (over y, x, core).
Axes of the slice: x: 2, y: 2, z: 4, core: 2. Of those that a mesh axis runs over, the one named last changes fastest.
Arguments:
- tokens: bfloat16 [12288, 1024], P(('dp', 'mp')), may hold values from -6 to 6
- lengths: int32 [96], P('dp'), may hold values from 16 to 128, as said below
- student_qkv: float32 [1024, 3, 1024], P(None, None, 'mp'), may hold values from -0.1875 to 0.1875
- student_qv_bias: bfloat16 [2, 1024], P(None, 'mp'), may hold values from -3 to 3
- student_out: float32 [1024, 1024], P('mp'), may hold values from -0.5 to 0.5
- student_up: float32 [1024, 4096], P(None, 'mp'), may hold values from -0.1875 to 0.1875
- student_up_bias: bfloat16 [4096], P('mp'), may hold values from -3 to 3
- student_down: float32 [4096, 1024], P('mp'), may hold values from -0.09375 to 0.09375
- student_out_bias: bfloat16 [2, 1024], replicated, may hold values from -3 to 3
- student_gain: bfloat16 [2, 1024], replicated, may hold values from 0.25 to 1.75
- student_shift: bfloat16 [2, 1024], replicated, may hold values from -3 to 3
- teacher_qkv: bfloat16 [1024, 3, 1024], P(None, None, 'mp'), may hold values from -0.1875 to 0.1875
- teacher_qv_bias: bfloat16 [2, 1024], P(None, 'mp'), may hold values from -3 to 3
- teacher_out: bfloat16 [1024, 1024], P('mp'), may hold values from -0.5 to 0.5
- teacher_up: bfloat16 [1024, 4096], P(None, 'mp'), may hold values from -0.1875 to 0.1875
- teacher_up_bias: bfloat16 [4096], P('mp'), may hold values from -3 to 3
- teacher_down: bfloat16 [4096, 1024], P('mp'), may hold values from -0.09375 to 0.09375
- teacher_out_bias: bfloat16 [2, 1024], replicated, may hold values from -3 to 3
- teacher_gain: bfloat16 [2, 1024], replicated, may hold values from 0.25 to 1.75
- teacher_shift: bfloat16 [2, 1024], replicated, may hold values from -3 to 3
Outputs:
- student_output: bfloat16 [12288, 1024], P(('dp', 'mp'))
- input_grad: float32 [12288, 1024], P(('dp', 'mp'))
- grad_qkv: float32 [1024, 3, 1024], P(None, None, 'mp')
- grad_qv_bias: float32 [2, 1024], P(None, 'mp')
- grad_out: float32 [1024, 1024], P('mp')
- grad_up: float32 [1024, 4096], P(None, 'mp')
- grad_up_bias: float32 [4096], P('mp')
- grad_down: float32 [4096, 1024], P('mp')
- grad_out_bias: float32 [2, 1024], replicated
- grad_gain: float32 [2, 1024], replicated
- grad_shift: float32 [2, 1024], replicated
The draws below stay inside these ranges and needn't reach their ends.
Inputs may be any that keep to these rules, and one draw needn't show every extreme that they name: `lengths`: the true length of each sentence pair; pairs are in groups of five starting at indices that are multiples of five; in each group the first pair has length 128 and the third 128 // 8.
All inputs are finite; a program needn't handle non-finite values.
Results may differ from the reference program's by a relative error of at most 0.015.
Values may be sent and summed in bfloat16 or wider, within the bound.
A program may use at most 256 MiB of HBM per device.

```python
import math
import jax
import jax.numpy as jnp
from jax import lax

D = 1024
H = 16
DH = 64
FF = 4096
LEN = 128
TOK_DEV = 384
TOKENS = 12288
N_DP = 4
N_MP = 8


def draw_lengths(key, part):
    key = jax.random.fold_in(key, 11)
    number = TOKENS // LEN
    drawn = jax.random.randint(key, (number,), LEN // 8, LEN + 1)
    places = jnp.arange(number, dtype=jnp.int32)
    shaped = jnp.where(places % 5 == 0, LEN, jnp.where(places % 5 == 2, LEN // 8, drawn))
    return shaped.astype(jnp.int32)


def shard_levels(key, shape, split, least, high):
    def one(position, blocks):
        steps = jax.random.uniform(jax.random.fold_in(jax.random.fold_in(key, 6), position), (blocks,), jnp.float32, least / len(split), high / len(split))
        return jnp.repeat(jnp.exp(steps), shape[position] // blocks).reshape((-1,) + (1,) * (len(shape) - position - 1))

    gain = one(*split[0])
    for cut in split[1:]:
        gain = gain * one(*cut)
    return gain


def gaussian(rng, dims, width, reach, shards=(), kind=jnp.bfloat16):
    result = width * jax.random.normal(rng, dims, jnp.float32)
    if shards:
        result = result * shard_levels(rng, dims, shards, -0.22, 0.18)
    return jnp.clip(result, -reach, reach).astype(kind)


def setup_inputs(seed: int = 0) -> dict:
    keys = jax.random.split(jax.random.key(seed), 21)
    return {
        "tokens": gaussian(keys[0], (TOKENS, D), 1.0, 6.0, ((0, 32),)),
        "lengths": draw_lengths(jax.random.fold_in(keys[20], 71), 0),
        "student_qkv": gaussian(keys[2], (D, 3, D), D ** -0.5, 0.1875, ((2, 8),), jnp.float32),
        "student_qv_bias": gaussian(keys[3], (2, D), 0.5, 3.0, ((1, 8),)),
        "student_out": gaussian(keys[4], (D, D), (D // 8) ** -0.5, 0.5, ((0, 8),), jnp.float32),
        "student_up": gaussian(keys[5], (D, FF), D ** -0.5, 0.1875, ((1, 8),), jnp.float32),
        "student_up_bias": gaussian(keys[6], (FF,), 0.5, 3.0, ((0, 8),)),
        "student_down": gaussian(keys[7], (FF, D), FF ** -0.5, 0.09375, ((0, 8),), jnp.float32),
        "student_out_bias": gaussian(keys[8], (2, D), 0.5, 3.0),
        "student_gain": jnp.clip(1.0 + 0.15 * jax.random.normal(keys[9], (2, D), jnp.float32), 0.25, 1.75).astype(jnp.bfloat16),
        "student_shift": gaussian(keys[10], (2, D), 0.5, 3.0),
        "teacher_qkv": gaussian(keys[11], (D, 3, D), D ** -0.5, 0.1875, ((2, 8),)),
        "teacher_qv_bias": gaussian(keys[12], (2, D), 0.5, 3.0, ((1, 8),)),
        "teacher_out": gaussian(keys[13], (D, D), (D // 8) ** -0.5, 0.5, ((0, 8),)),
        "teacher_up": gaussian(keys[14], (D, FF), D ** -0.5, 0.1875, ((1, 8),)),
        "teacher_up_bias": gaussian(keys[15], (FF,), 0.5, 3.0, ((0, 8),)),
        "teacher_down": gaussian(keys[16], (FF, D), FF ** -0.5, 0.09375, ((0, 8),)),
        "teacher_out_bias": gaussian(keys[17], (2, D), 0.5, 3.0),
        "teacher_gain": jnp.clip(1.0 + 0.15 * jax.random.normal(keys[18], (2, D), jnp.float32), 0.25, 1.75).astype(jnp.bfloat16),
        "teacher_shift": gaussian(keys[19], (2, D), 0.5, 3.0),
    }


@jax.custom_vjp
def low(v):
    return lax.optimization_barrier(v.astype(jnp.bfloat16)).astype(jnp.float32)

@jax.custom_vjp
def low_back(v):
    return v

def low_keep(v):
    return (low(v), None)

def low_pass(kept, grad):
    return (grad,)

def back_keep(v):
    return (v, None)

def back_low(kept, grad):
    return (low(grad),)
low.defvjp(low_keep, low_pass)
low_back.defvjp(back_keep, back_low)
highest = lax.Precision.HIGHEST
norm_epsilon = 1e-06
clip_level = 2.5
score_weight = 0.05
masked_fill = -1000000000.0

def round_both(values):
    return low(low_back(values))

def binarize(matrix, axis_index):
    return lax.optimization_barrier(jnp.mean(jnp.abs(matrix), axis=axis_index, keepdims=True)) * jnp.sign(matrix)

def norm_affine(values, gain_row, shift_row):
    centred = values - lax.optimization_barrier(jnp.mean(values, axis=-1, keepdims=True))
    variance = lax.optimization_barrier(jnp.mean(centred * centred, axis=-1, keepdims=True))
    return centred * lax.rsqrt(variance + norm_epsilon) * gain_row + shift_row

def bert_layer(inputs, seq_lengths, params, student):
    qkv_weight, qv_bias, out_weight, up_weight, up_bias, down_weight, out_bias, gain_rows, shift_rows = params
    row_count = inputs.shape[0]
    seq_count = seq_lengths.shape[0]
    places = jnp.arange(LEN, dtype=jnp.int32)
    key_valid = places[None, :] < seq_lengths[:, None]
    head_shape = (seq_count, LEN, H, DH)
    projected = jnp.dot(inputs, low(qkv_weight).reshape(D, 3 * D), precision=highest, preferred_element_type=jnp.float32)
    projected = projected.reshape(row_count, 3, D)
    queries = low(low_back(projected[:, 0]) + qv_bias[0]).reshape(head_shape)
    key_rows = low(low_back(projected[:, 1])).reshape(head_shape)
    value_rows = low(low_back(projected[:, 2]) + qv_bias[1]).reshape(head_shape)
    scores = jnp.einsum('bqhe,bkhe->bhqk', queries, key_rows, precision=highest) * (1.0 / math.sqrt(DH))
    scores = low_back(scores)
    masked = jnp.where(key_valid[:, None, None, :], scores, masked_fill)
    attention = jax.nn.softmax(masked, axis=-1)
    context = jnp.einsum('bhqk,bkhe->bqhe', low(attention), value_rows, precision=highest)
    context = round_both(context.reshape(row_count, D))
    attended = low_back(jnp.dot(context, low(out_weight), precision=highest, preferred_element_type=jnp.float32)) + out_bias[0]
    normed = norm_affine(inputs + attended, gain_rows[0], shift_rows[0])
    hidden = low_back(jnp.dot(low(normed), low(up_weight), precision=highest, preferred_element_type=jnp.float32)) + up_bias
    hidden = jax.nn.gelu(hidden, approximate=False)
    if student:
        hidden = clip_level * jnp.tanh(hidden / clip_level)
    branch = low_back(jnp.dot(low(hidden), low(down_weight), precision=highest, preferred_element_type=jnp.float32)) + out_bias[1]
    return (norm_affine(normed + branch, gain_rows[1], shift_rows[1]), scores)

def distill_loss(inputs, seq_lengths, student_params, teacher_params):
    student_out, student_scores = bert_layer(inputs, seq_lengths, student_params, True)
    teacher_out, teacher_scores = bert_layer(inputs, seq_lengths, teacher_params, False)
    places = jnp.arange(LEN, dtype=jnp.int32)
    valid = places[None, :] < seq_lengths[:, None]
    token_valid = valid.reshape(-1).astype(inputs.dtype)[:, None]
    difference = student_out - teacher_out
    hidden_term = 0.5 * jnp.sum(token_valid * difference * difference)
    pair_valid = valid[:, None, :, None] & valid[:, None, None, :]
    score_gap = student_scores - teacher_scores
    score_term = 0.5 * score_weight * jnp.sum(jnp.where(pair_valid, score_gap * score_gap, 0.0))
    return (hidden_term + score_term, student_out)

def reference(tokens, lengths, student_qkv, student_qv_bias, student_out, student_up, student_up_bias, student_down, student_out_bias, student_gain, student_shift, teacher_qkv, teacher_qv_bias, teacher_out, teacher_up, teacher_up_bias, teacher_down, teacher_out_bias, teacher_gain, teacher_shift):
    student_params = (binarize(student_qkv.astype(jnp.float32), 0), student_qv_bias.astype(jnp.float32), binarize(student_out.astype(jnp.float32), 1), binarize(student_up.astype(jnp.float32), 0), student_up_bias.astype(jnp.float32), binarize(student_down.astype(jnp.float32), 1), student_out_bias.astype(jnp.float32), student_gain.astype(jnp.float32), student_shift.astype(jnp.float32))
    teacher_params = tuple((item.astype(jnp.float32) for item in (teacher_qkv, teacher_qv_bias, teacher_out, teacher_up, teacher_up_bias, teacher_down, teacher_out_bias, teacher_gain, teacher_shift)))
    group_rows = TOK_DEV * N_MP
    input_blocks = tokens.astype(jnp.float32).reshape(N_DP, group_rows, D)
    length_blocks = lengths.reshape(N_DP, group_rows // LEN)

    def block_step(grad_sums, block_item):
        block_inputs, block_lengths = block_item

        def objective(inputs, params):
            return distill_loss(inputs, block_lengths, params, teacher_params)
        loss_value, pullback, student_out_block = jax.vjp(objective, block_inputs, student_params, has_aux=True)
        input_grads, param_grads = pullback(jnp.ones_like(loss_value))
        grad_sums = jax.tree.map(lambda left, right: left + right, grad_sums, param_grads)
        return (grad_sums, (student_out_block.astype(jnp.bfloat16), input_grads))
    initial = jax.tree.map(jnp.zeros_like, student_params)
    grad_sums, (out_blocks, input_blocks_grad) = lax.scan(block_step, initial, (input_blocks, length_blocks))
    return (out_blocks.reshape(TOKENS, D), input_blocks_grad.reshape(TOKENS, D), grad_sums[0], grad_sums[1], grad_sums[2], grad_sums[3], grad_sums[4], grad_sums[5], grad_sums[6], grad_sums[7], grad_sums[8])
```

```python
import math

import jax
import jax.numpy as jnp
from jax import lax
from jax.experimental import pallas as pl
from jax.experimental.pallas import tpu as pltpu
from jax.sharding import PartitionSpec as P

DH = 64
LEN = 128


norm_epsilon = 1e-06
clip_level = 2.5
score_weight = 0.05
masked_fill = -1000000000.0


def to_float(values):
    return values.astype(jnp.float32)


def to_low(values):
    return values.astype(jnp.bfloat16)


def binarize(matrix, axis_index):
    scaling = jnp.mean(jnp.abs(matrix), axis=axis_index, keepdims=True)
    return (scaling * jnp.sign(matrix)).astype(jnp.bfloat16)


def norm_stats(values):
    centred = values - jnp.mean(values, axis=-1, keepdims=True)
    variance = jnp.mean(centred * centred, axis=-1, keepdims=True)
    inverse = lax.rsqrt(variance + norm_epsilon)
    return (centred * inverse, inverse)


def norm_back(grad, unit, inverse, gain_row):
    scaled = grad * gain_row
    first = jnp.mean(scaled, axis=-1, keepdims=True)
    second = jnp.mean(scaled * unit, axis=-1, keepdims=True)
    return inverse * (scaled - first - unit * second)


def dot(left, right):
    return jnp.dot(left, right, preferred_element_type=jnp.float32)


def dot_nt(left, right):
    return lax.dot_general(left, right, (((1,), (1,)), ((), ())), preferred_element_type=jnp.float32)


def dot_tn(left, right):
    return lax.dot_general(left, right, (((0,), (0,)), ((), ())), preferred_element_type=jnp.float32)


class Cube:
    def __init__(self, n_dp):
        self.n_dp = n_dp
        self.axes = ("dp", "mp")

    def flip(self, values, bits):
        pairs = [
            (z * 8 + m, z * 8 + (m ^ bits)) for z in range(self.n_dp) for m in range(8)
        ]
        return lax.ppermute(values, self.axes, pairs)

    def flip_dp(self, values, bits):
        pairs = [
            (z * 8 + m, (z ^ bits) * 8 + m) for z in range(self.n_dp) for m in range(8)
        ]
        return lax.ppermute(values, self.axes, pairs)

    def gather(self, block):
        half = block.shape[0] // 2
        along_x = self.flip(block, 2)
        along_y = self.flip(block, 4)
        across = jnp.concatenate(
            [self.flip(along_y[:half], 2), self.flip(along_x[half:], 4)], axis=0
        )
        same = [block, along_x, along_y, across]
        other = [self.flip(item, 1) for item in same]
        return [item for pair in zip(same, other) for item in pair]

    def scatter(self, blocks):
        half = blocks[0].shape[0] // 2
        own, to_x, to_y, to_far = [
            to_float(blocks[k]) + to_float(self.flip(blocks[k + 1], 1)) for k in (0, 2, 4, 6)
        ]
        far = to_low(to_far)
        via_x = to_float(self.flip(far[:half], 2))
        via_y = to_float(self.flip(far[half:], 4))
        to_y = to_low(jnp.concatenate([to_y[:half] + via_x, to_y[half:]], axis=0))
        to_x = to_low(jnp.concatenate([to_x[:half], to_x[half:] + via_y], axis=0))
        return own + to_float(self.flip(to_x, 2)) + to_float(self.flip(to_y, 4))

    def sum_dp(self, values):
        half = values.shape[0] // 2
        odd = lax.axis_index("dp") % 2
        low = to_low(values)
        sent = lax.dynamic_slice_in_dim(low, (1 - odd) * half, half)
        kept = lax.dynamic_slice_in_dim(values, odd * half, half)
        kept = kept + to_float(self.flip_dp(sent, 1))
        kept_low = to_low(kept)
        kept = to_low(kept + to_float(self.flip_dp(kept_low, 2)))
        other = self.flip_dp(kept, 1)
        return to_float(
            jnp.concatenate(
                [jnp.where(odd == 0, kept, other), jnp.where(odd == 0, other, kept)], axis=0
            )
        )

    def sum_all(self, values):
        for bits in (1, 2, 4):
            values = values + self.flip(values, bits)
        for bits in (1, 2):
            values = values + self.flip_dp(values, bits)
        return values

    def place(self, values):
        me = lax.axis_index("mp")
        for bit in range(3):
            shape = values.shape
            split = values.reshape((8 >> (bit + 1), 2, 1 << bit) + shape[1:])
            flipped = split[:, ::-1]
            values = jnp.where((me >> bit) % 2 == 1, flipped, split).reshape(shape)
        return values


class Plain:
    def __init__(self, n_mp):
        self.n_mp = n_mp

    def gather(self, block):
        every = lax.all_gather(block, "mp", axis=0)
        return [every[k] for k in range(self.n_mp)]

    def scatter(self, blocks):
        return to_float(
            lax.psum_scatter(jnp.stack(blocks), "mp", scatter_dimension=0, tiled=False)
        )

    def sum_dp(self, values):
        return to_float(lax.psum(to_low(values), "dp"))

    def sum_all(self, values):
        return lax.psum(values, ("dp", "mp"))

    def place(self, values):
        return values


def plain_act(pre):
    gate = 0.5 * (1.0 + lax.erf(pre * math.sqrt(0.5)))
    slope = gate + pre * jnp.exp(-0.5 * pre * pre) * (1.0 / math.sqrt(2.0 * math.pi))
    return (pre * gate, slope)


def clipped_act(pre):
    value, slope = plain_act(pre)
    bent = jnp.tanh(value * (1.0 / clip_level))
    return (clip_level * bent, slope * (1.0 - bent * bent))


def gather_layer(net, qkv, qv_bias, out, up, up_bias, down):
    width = qkv.shape[2]
    units = up.shape[1]
    features = qkv.shape[0]
    extra = jnp.zeros((16, features), jnp.bfloat16)
    extra = extra.at[0, :width].set(qv_bias[0]).at[1, :width].set(qv_bias[1])
    extra = extra.at[2, :units].set(up_bias)
    qkv_parts = net.gather(qkv.transpose(1, 0, 2).reshape(3 * features, width))
    out_parts = net.gather(jnp.concatenate([out, extra], axis=0))
    up_parts = net.gather(up)
    down_parts = net.gather(down)
    count = len(qkv_parts)
    qkv_full = jnp.concatenate(
        [part.reshape(3, features, width) for part in qkv_parts], axis=2
    )
    out_full = jnp.concatenate([part[:width] for part in out_parts], axis=0)
    q_bias = jnp.concatenate([part[width, :width] for part in out_parts])
    v_bias = jnp.concatenate([part[width + 1, :width] for part in out_parts])
    up_b = jnp.concatenate([part[width + 2, :units] for part in out_parts])
    up_full = jnp.concatenate(up_parts, axis=1)
    down_full = jnp.concatenate(down_parts, axis=0)
    return (qkv_full, to_float(q_bias), to_float(v_bias), out_full, up_full, to_float(up_b), down_full)


def forward(tokens, weights, out_bias, gain, shift, activation, key_valid):
    qkv, q_bias, v_bias, out, up, up_bias, down = weights
    rows, features = tokens.shape
    pairs = rows // LEN
    shape = (pairs, LEN, features // DH, DH)
    query = to_low(dot(tokens, qkv[0]) + q_bias).reshape(shape)
    key = to_low(dot(tokens, qkv[1])).reshape(shape)
    value = to_low(dot(tokens, qkv[2]) + v_bias).reshape(shape)
    scores = jnp.einsum("bqhe,bkhe->bhqk", query, key, preferred_element_type=jnp.float32) * (
        1.0 / math.sqrt(DH)
    )
    masked = jnp.where(key_valid[:, None, None, :], scores, masked_fill)
    log_norm = jax.nn.logsumexp(masked, axis=-1, keepdims=True)
    attention = jnp.exp(masked - log_norm)
    context = jnp.einsum(
        "bhqk,bkhe->bqhe", to_low(attention), value, preferred_element_type=jnp.float32
    )
    context = to_low(context).reshape(rows, features)
    first = to_float(tokens) + dot(context, out) + out_bias[0]
    unit_one, inverse_one = norm_stats(first)
    normed = unit_one * gain[0] + shift[0]
    normed_low = to_low(normed)
    hidden, slope = activation(dot(normed_low, up) + up_bias)
    hidden = to_low(hidden)
    second = normed + dot(hidden, down) + out_bias[1]
    unit_two, inverse_two = norm_stats(second)
    final = unit_two * gain[1] + shift[1]
    kept = (query, key, value, scores, attention, context, unit_one, inverse_one, normed_low, hidden,
            to_low(slope), unit_two, inverse_two)
    return (final, kept)


def backward_ffn(kept, weights, second_grad, gain):
    qkv, q_bias, v_bias, out, up, up_bias, down = weights
    (query, key, value, scores, attention, context, unit_one, inverse_one, normed_low, hidden,
     slope, unit_two, inverse_two) = kept
    second_low = to_low(second_grad)
    pre_grad = dot_nt(second_low, down) * slope
    pre_low = to_low(pre_grad)
    normed_grad = second_grad + dot_nt(pre_low, up)
    first_grad = norm_back(normed_grad, unit_one, inverse_one, gain[0])
    return (second_grad, second_low, pre_grad, pre_low, normed_grad, first_grad)


def backward_attention(kept, first_low, out, extra):
    query, key, value, scores, attention = kept[:5]
    rows = first_low.shape[0]
    factor = 1.0 / math.sqrt(DH)
    context_grad = to_low(dot_nt(first_low, out)).reshape(query.shape)
    attention_grad = jnp.einsum(
        "bqhe,bkhe->bhqk", context_grad, value, preferred_element_type=jnp.float32
    )
    value_grad = jnp.einsum(
        "bhqk,bqhe->bkhe", to_low(attention), context_grad, preferred_element_type=jnp.float32
    )
    inner = jnp.sum(attention * attention_grad, axis=-1, keepdims=True)
    score_low = to_low(attention * (attention_grad - inner) + extra)
    query_grad = factor * jnp.einsum(
        "bhqk,bkhe->bqhe", score_low, key, preferred_element_type=jnp.float32
    )
    key_grad = factor * jnp.einsum(
        "bhqk,bqhe->bkhe", score_low, query, preferred_element_type=jnp.float32
    )
    return [item.reshape(rows, -1) for item in (query_grad, key_grad, value_grad)]


MESH = pl.DeviceIdType.MESH
SLOTS = 8
PACKS = 6
ATT_ROWS = 528
FFN_ROWS = 512
HALF_UNITS = 256
COLS = 128


def flipped(me, bits):
    return me + bits - 2 * bits * lax.rem(lax.div(me, bits), 2)


def pack_rows(pack):
    return ATT_ROWS if pack < 2 else FFN_ROWS


def pack_half(pack):
    return 272 if pack < 2 else 256


def masked_probs(scores, length):
    rows = scores.shape[0]
    position = lax.broadcasted_iota(jnp.int32, (rows, LEN), 1)
    parts = []
    for head in range(2):
        part = jnp.where(position < length, scores[:, head * LEN : (head + 1) * LEN], masked_fill)
        part = jnp.exp(part - jnp.max(part, axis=1, keepdims=True))
        parts.append(part / jnp.sum(part, axis=1, keepdims=True))
    return jnp.concatenate(parts, axis=1)


def two_heads(rows):
    first = lax.broadcasted_iota(jnp.int32, rows.shape, 1) < DH
    zero = jnp.zeros_like(rows)
    return jnp.concatenate([jnp.where(first, rows, zero), jnp.where(first, zero, rows)], axis=0)


def norm_block(values):
    centred = values - jnp.mean(values, axis=1, keepdims=True)
    inverse = lax.rsqrt(jnp.mean(centred * centred, axis=1, keepdims=True) + norm_epsilon)
    return (centred * inverse, inverse)


def forward_kernel(
    lengths,
    x_ref,
    packs_att,
    packs_ffn,
    t_bias,
    t_gain,
    t_shift,
    s_bias,
    s_gain,
    s_shift,
    gathered,
    qkv_t,
    qkv_s,
    context_s,
    slope_t,
    slope_s,
    hidden_s,
    unit_t,
    inverse_t,
    unit_s,
    inverse_s,
    low_s,
    grad_t,
    grad_s,
    final_low,
    vectors,
    wide,
    total,
    normed,
    low_t,
    context_t,
    bias_rows,
    final_t,
    unit_two,
    inverse_two,
    send,
    recv,
    load,
    own,
):
    me = lax.axis_index("mp")
    peers = {1: flipped(me, 1), 2: flipped(me, 2), 4: flipped(me, 4)}
    rows = x_ref.shape[0]
    pairs = rows // LEN

    barrier = pltpu.get_barrier_semaphore()
    for peer in peers.values():
        pl.semaphore_signal(barrier, inc=1, device_id={"mp": peer}, device_id_type=MESH)
    pl.semaphore_wait(barrier, 3)

    def source(pack):
        return packs_att.at[pack] if pack < 2 else packs_ffn.at[pack - 2]

    def block(pack, slot, start=0, count=None):
        count = pack_rows(pack) if count is None else count
        return gathered.at[pack, slot, pl.ds(start, count)]

    def remote(pack, kind):
        half = pack_half(pack)
        rest = pack_rows(pack) - half
        if kind == 0:
            src, dst, bits = source(pack), block(pack, 2), 2
        elif kind == 1:
            src, dst, bits = source(pack), block(pack, 4), 4
        elif kind == 2:
            src, dst, bits = block(pack, 4, 0, half), block(pack, 6, 0, half), 2
        elif kind == 3:
            src, dst, bits = block(pack, 2, half, rest), block(pack, 6, half, rest), 4
        elif kind == 4:
            src, dst, bits = source(pack), block(pack, 1), 1
        else:
            slot = 2 * (kind - 4)
            src, dst, bits = block(pack, slot), block(pack, slot + 1), 1
        return pltpu.make_async_remote_copy(
            src_ref=src,
            dst_ref=dst,
            send_sem=send.at[pack, kind],
            recv_sem=recv.at[pack, kind],
            device_id={"mp": peers[bits]},
            device_id_type=MESH,
        )

    def keep_own(pack):
        return pltpu.make_async_copy(source(pack), block(pack, 0), own.at[pack])

    def first_sends(pack):
        for kind in (0, 1, 4):
            remote(pack, kind).start()
        keep_own(pack).start()

    def second_sends(pack):
        remote(pack, 0).wait_recv()
        remote(pack, 3).start()
        remote(pack, 5).start()
        remote(pack, 1).wait_recv()
        remote(pack, 2).start()
        remote(pack, 6).start()

    def load_pair(pack, pair, place):
        return pltpu.make_async_copy(
            gathered.at[pack, pl.ds(2 * pair, 2), pl.ds(0, pack_rows(pack))],
            wide.at[place, :, pl.ds(0, pack_rows(pack))],
            load.at[place],
        )

    def over_pairs(pack, body):
        keep_own(pack).wait()
        remote(pack, 4).wait_recv()
        load_pair(pack, 0, 0).start()
        for pair in range(4):
            place = pair % 2
            load_pair(pack, pair, place).wait()
            if pair < 3:
                if pair == 2:
                    remote(pack, 2).wait_recv()
                    remote(pack, 3).wait_recv()
                    remote(pack, 7).start()
                remote(pack, 5 + pair).wait_recv()
                load_pair(pack, pair + 1, 1 - place).start()
            body(pair, place)

    def attention(pack, qkv_ref, context_ref):
        total[...] = jnp.zeros_like(total)

        def body(pair, place):
            weights = wide[place, :, 0:384].reshape(768, -1)
            projected = dot_nt(x_ref[...], weights)
            for side in range(2):
                slot = 2 * pair + side
                bias = wide[place, side, 512:528]
                bias_rows[pack, slot] = bias
                bias = to_float(bias[0:1])
                part = projected[:, side * 384 : side * 384 + 384]
                query = to_low(part[:, :COLS] + bias[:, :COLS])
                key = to_low(part[:, COLS : 2 * COLS])
                value = to_low(part[:, 2 * COLS :] + bias[:, COLS : 2 * COLS])
                qkv_ref[slot, :, 0:COLS] = query
                qkv_ref[slot, :, COLS : 2 * COLS] = key
                qkv_ref[slot, :, 2 * COLS : 3 * COLS] = value
                for number in range(pairs):
                    here = slice(number * LEN, (number + 1) * LEN)
                    scores = dot_nt(query[here], two_heads(key[here])) * (1.0 / math.sqrt(DH))
                    probs = masked_probs(scores, lengths[me * pairs + number])
                    part_context = dot(to_low(probs), two_heads(value[here]))
                    context_ref[pair, here, side * COLS : (side + 1) * COLS] = to_low(part_context)
            total[...] += dot(context_ref[pair], wide[place, :, 384:512].reshape(256, -1))

        over_pairs(pack, body)

    def first_norm(bias_ref, gain_ref, shift_ref, unit_ref, inverse_ref, index, low_ref):
        @pl.loop(0, rows // 64)
        def _(step):
            here = pl.ds(step * 64, 64)
            values = to_float(x_ref[here]) + total[here] + to_float(bias_ref[0:1])
            unit, inverse = norm_block(values)
            unit_ref[here] = unit
            inverse_ref[here] = inverse
            values = unit * to_float(gain_ref[0:1]) + to_float(shift_ref[0:1])
            normed[index, here] = values
            low_ref[here] = to_low(values)

    def feed_forward(layer, half, low_ref, activation, hidden_ref, slope_ref):
        pack = 2 + 2 * layer + half

        def body(pair, place):
            up = wide[place, :, 0:HALF_UNITS].reshape(2 * HALF_UNITS, -1)
            down = wide[place, :, HALF_UNITS : 2 * HALF_UNITS].reshape(2 * HALF_UNITS, -1)
            start = 2 * COLS + half * HALF_UNITS
            bias = jnp.concatenate(
                [
                    to_float(bias_rows[layer, 2 * pair + side, 0:1, start : start + HALF_UNITS])
                    for side in range(2)
                ],
                axis=1,
            )
            hidden, slope = activation(dot_nt(low_ref[...], up) + bias)
            hidden = to_low(hidden)
            slope_ref[half, pair] = to_low(slope)
            if hidden_ref is not None:
                hidden_ref[half, pair] = hidden
            total[...] += dot(hidden, down)

        if half == 0:
            total[...] = jnp.zeros_like(total)
        over_pairs(pack, body)

    def step_teacher_end():
        @pl.loop(0, rows // 64)
        def _(step):
            here = pl.ds(step * 64, 64)
            unit, inverse = norm_block(normed[0, here] + total[here] + to_float(t_bias[1:2]))
            unit_two[here] = unit
            inverse_two[here] = inverse
            final_t[here] = unit * to_float(t_gain[1:2]) + to_float(t_shift[1:2])

    def step_student_end():
        vectors[...] = jnp.zeros_like(vectors)

        @pl.loop(0, rows // 64)
        def _(step):
            here = pl.ds(step * 64, 64)
            unit, inverse = norm_block(normed[1, here] + total[here] + to_float(s_bias[1:2]))
            gain = to_float(s_gain[1:2])
            final = unit * gain + to_float(s_shift[1:2])
            final_low[here] = to_low(final)
            position = lax.broadcasted_iota(jnp.int32, (64, 1), 0) + lax.rem(step, 2) * 64
            valid = position < lengths[me * pairs + lax.div(step, 2)]
            grad = jnp.where(valid, final - final_t[here], 0.0)
            back = norm_back(grad, unit, inverse, gain)
            grad_s[here] = back
            grad_t[here] = norm_back(
                -grad, unit_two[here], inverse_two[here], to_float(t_gain[1:2])
            )
            vectors[0:1] += jnp.sum(back, axis=0, keepdims=True)
            vectors[1:2] += jnp.sum(grad * unit, axis=0, keepdims=True)
            vectors[2:3] += jnp.sum(grad, axis=0, keepdims=True)

    def use(pack):
        if pack == 0:
            attention(0, qkv_t, context_t)
            first_norm(t_bias, t_gain, t_shift, unit_t, inverse_t, 0, low_t)
        elif pack == 1:
            attention(1, qkv_s, context_s)
            first_norm(s_bias, s_gain, s_shift, unit_s, inverse_s, 1, low_s)
        elif pack < 4:
            feed_forward(0, pack - 2, low_t, plain_act, None, slope_t)
            if pack == 3:
                step_teacher_end()
        else:
            feed_forward(1, pack - 4, low_s, clipped_act, hidden_s, slope_s)
            if pack == 5:
                step_student_end()

    first_sends(0)
    first_sends(1)
    for pack in range(PACKS):
        second_sends(pack)
        if pack + 2 < PACKS:
            first_sends(pack + 2)
        if pack:
            use(pack - 1)
    use(PACKS - 1)
    for pack in range(PACKS):
        for kind in range(8):
            remote(pack, kind).wait_send()


def forward_both(lengths, tokens, packs_att, packs_ffn, teacher_rows, student_rows):
    rows, features = tokens.shape
    low, full = jnp.bfloat16, jnp.float32
    vmem = pl.BlockSpec(memory_space=pltpu.VMEM)
    hbm = pl.BlockSpec(memory_space=pl.ANY)
    shapes = [
        ((PACKS, SLOTS, ATT_ROWS, features), low, hbm),
        ((SLOTS, rows, 3 * COLS), low, vmem),
        ((SLOTS, rows, 3 * COLS), low, vmem),
        ((4, rows, 2 * COLS), low, vmem),
        ((2, 4, rows, 2 * HALF_UNITS), low, vmem),
        ((2, 4, rows, 2 * HALF_UNITS), low, vmem),
        ((2, 4, rows, 2 * HALF_UNITS), low, vmem),
        ((rows, features), full, vmem),
        ((rows, 1), full, vmem),
        ((rows, features), full, vmem),
        ((rows, 1), full, vmem),
        ((rows, features), low, vmem),
        ((rows, features), full, vmem),
        ((rows, features), full, vmem),
        ((rows, features), low, vmem),
        ((8, features), full, vmem),
    ]
    return pl.pallas_call(
        forward_kernel,
        out_shape=[jax.ShapeDtypeStruct(shape, kind) for shape, kind, _ in shapes],
        in_specs=[pl.BlockSpec(memory_space=pltpu.SMEM), vmem, hbm, hbm] + [vmem] * 6,
        out_specs=[spec for _, _, spec in shapes],
        scratch_shapes=[
            pltpu.VMEM((2, 2, ATT_ROWS, features), low),
            pltpu.VMEM((rows, features), full),
            pltpu.VMEM((2, rows, features), full),
            pltpu.VMEM((rows, features), low),
            pltpu.VMEM((4, rows, 2 * COLS), low),
            pltpu.VMEM((2, SLOTS, 16, features), low),
            pltpu.VMEM((rows, features), full),
            pltpu.VMEM((rows, features), full),
            pltpu.VMEM((rows, 1), full),
            pltpu.SemaphoreType.DMA((PACKS, 8)),
            pltpu.SemaphoreType.DMA((PACKS, 8)),
            pltpu.SemaphoreType.DMA((2,)),
            pltpu.SemaphoreType.DMA((PACKS,)),
        ],
        compiler_params=pltpu.CompilerParams(
            collective_id=0, has_side_effects=True, vmem_limit_bytes=60 * 1024 * 1024
        ),
        name="forward_both",
    )(lengths, tokens, packs_att, packs_ffn, *teacher_rows, *student_rows)


def pack_layer(qkv, qv_bias, out, up, up_bias, down):
    features, _, width = qkv.shape
    bias = jnp.concatenate([qv_bias.reshape(-1), up_bias])
    bias = jnp.pad(bias[None], ((0, 15), (0, features - bias.size)))
    att = jnp.concatenate([qkv.transpose(1, 2, 0).reshape(3 * width, features), out, bias], axis=0)
    halves = [
        jnp.concatenate(
            [
                up[:, h * HALF_UNITS : (h + 1) * HALF_UNITS].T,
                down[h * HALF_UNITS : (h + 1) * HALF_UNITS],
            ],
            axis=0,
        )
        for h in range(2)
    ]
    return (att, jnp.stack(halves))


def cut(values, count, axis):
    return jnp.split(values, count, axis=axis)


def per_device(n_dp, n_mp, *args):
    (
        tokens,
        lengths,
        student_qkv,
        student_qv_bias,
        student_out,
        student_up,
        student_up_bias,
        student_down,
        student_out_bias,
        student_gain,
        student_shift,
        teacher_qkv,
        teacher_qv_bias,
        teacher_out,
        teacher_up,
        teacher_up_bias,
        teacher_down,
        teacher_out_bias,
        teacher_gain,
        teacher_shift,
    ) = args
    net = Cube(n_dp) if (n_dp, n_mp) == (4, 8) else Plain(n_mp)
    rows = tokens.shape[0]
    pairs = rows // LEN
    places = jnp.arange(LEN, dtype=jnp.int32)
    me = lax.axis_index("mp")
    own_lengths = lax.dynamic_slice_in_dim(lengths, me * pairs, pairs)
    valid = places[None, :] < own_lengths[:, None]
    token_valid = to_float(valid.reshape(rows, 1))
    pair_valid = valid[:, None, :, None] & valid[:, None, None, :]

    gain = to_float(student_gain)
    shift = to_float(student_shift)
    out_bias = to_float(student_out_bias)
    teach_gain = to_float(teacher_gain)
    if isinstance(net, Cube):
        teach_att, teach_ffn = pack_layer(
            teacher_qkv, teacher_qv_bias, teacher_out, teacher_up, teacher_up_bias, teacher_down
        )
        stud_att, stud_ffn = pack_layer(
            binarize(student_qkv, 0),
            student_qv_bias,
            binarize(student_out, 1),
            binarize(student_up, 0),
            student_up_bias,
            binarize(student_down, 1),
        )
        (gathered, qkv_t, qkv_s, context_s, slope_t, slope_s, hidden_s, unit_t, inverse_t, unit_s,
         inverse_s, low_s, grad_t, grad_s, student_output, vecs) = forward_both(
            lengths, tokens, jnp.stack([teach_att, stud_att]), jnp.concatenate([teach_ffn, stud_ffn]),
            (teacher_out_bias, teacher_gain, teacher_shift),
            (student_out_bias, student_gain, student_shift),
        )
        def unpack(layer):
            att = gathered[layer]
            qkvt = att[:, :384].reshape(8, 3, 128, -1)
            qkv = [qkvt[:, i].reshape(1024, -1).T for i in range(3)]
            out = att[:, 384:512].reshape(1024, -1)
            f = gathered[2 + 2 * layer : 4 + 2 * layer]
            up = f[:, :, 0:256].transpose(1, 0, 2, 3).reshape(4096, -1).T
            down = f[:, :, 256:512].transpose(1, 0, 2, 3).reshape(4096, -1)
            return (qkv, None, None, out, up, None, down)
        def spread(v):
            return v.reshape(2, 4, rows, 2, 256).transpose(2, 1, 3, 0, 4).reshape(rows, 4096)
        def keep(qkv, slope, hidden, unit, inverse, low, context):
            q, k, v = [qkv[:, :, i * 128:(i + 1) * 128].transpose(1, 0, 2).reshape(pairs, LEN, 16, 64) for i in range(3)]
            scores = jnp.einsum("bqhe,bkhe->bhqk", q, k, preferred_element_type=jnp.float32) * (1.0 / math.sqrt(DH))
            masked = jnp.where(valid[:, None, None, :], scores, masked_fill)
            attention = jax.nn.softmax(masked, axis=-1)
            return [q, k, v, scores, attention, context, unit, inverse, low, hidden, spread(slope), None, None]
        teach, stud = unpack(0), unpack(1)
        ctx = context_s.transpose(1, 0, 2).reshape(rows, -1)
        teach_kept = keep(qkv_t, slope_t, None, unit_t, inverse_t, None, None)
        kept = keep(qkv_s, slope_s, spread(hidden_s), unit_s, inverse_s, low_s, ctx)
    else:
        teach = gather_layer(
            net, teacher_qkv, teacher_qv_bias, teacher_out, teacher_up, teacher_up_bias, teacher_down
        )
        stud = gather_layer(
            net,
            binarize(student_qkv, 0),
            student_qv_bias,
            binarize(student_out, 1),
            binarize(student_up, 0),
            student_up_bias,
            binarize(student_down, 1),
        )
        teach_final, teach_kept = forward(
            tokens, teach, to_float(teacher_out_bias), teach_gain, to_float(teacher_shift), plain_act, valid
        )
        final, kept = forward(tokens, stud, out_bias, gain, shift, clipped_act, valid)
        student_output = to_low(final)
        final_grad = token_valid * (final - teach_final)
        grad_s = norm_back(final_grad, kept[11], kept[12], gain[1])
        grad_t = norm_back(-final_grad, teach_kept[11], teach_kept[12], teach_gain[1])
        vecs = jnp.stack([jnp.sum(grad_s, axis=0), jnp.sum(final_grad * kept[11], axis=0), jnp.sum(final_grad, axis=0)])
    extra = score_weight * jnp.where(pair_valid, kept[3] - teach_kept[3], 0.0)

    second_grad, second_low, pre_grad, pre_low, normed_grad, first_grad = backward_ffn(
        kept, stud, grad_s, gain
    )
    hidden, normed_low, context = kept[9], kept[8], kept[5]
    unit_one = kept[6]
    down_grad = net.sum_dp(net.scatter(cut(to_low(dot_tn(hidden, second_low)), n_mp, 0)))
    up_grad = net.sum_dp(net.scatter(cut(to_low(dot_tn(normed_low, pre_low)), n_mp, 1)))
    first_low = to_low(first_grad)
    out_grad = net.sum_dp(net.scatter(cut(to_low(dot_tn(context, first_low)), n_mp, 0)))
    grads = backward_attention(kept, first_low, stud[3], extra)
    lows = [to_low(item) for item in grads]
    wide = jnp.concatenate(
        [to_low(dot_tn(tokens, item)) for item in lows], axis=0
    )
    qkv_grad = net.sum_dp(net.scatter(cut(wide, n_mp, 1)))
    features = tokens.shape[1]
    qkv_grad = qkv_grad.reshape(3, features, -1).transpose(1, 0, 2)

    teach_second, teach_slow, _, _, _, teach_first = backward_ffn(
        teach_kept, teach, grad_t, teach_gain
    )
    teach_grads = backward_attention(teach_kept, to_low(teach_first), teach[3], -extra)
    teach_lows = [to_low(item) for item in teach_grads]
    input_grad = first_grad + teach_first
    for item, matrix in zip(lows, stud[0]):
        input_grad = input_grad + dot_nt(item, matrix)
    for item, matrix in zip(teach_lows, teach[0]):
        input_grad = input_grad + dot_nt(item, matrix)

    vectors = [
        jnp.sum(first_grad, axis=0),
        vecs[0],
        jnp.sum(normed_grad * unit_one, axis=0),
        vecs[1],
        jnp.sum(normed_grad, axis=0),
        vecs[2],
        net.place(jnp.sum(grads[0], axis=0).reshape(n_mp, -1)).reshape(-1),
        net.place(jnp.sum(grads[2], axis=0).reshape(n_mp, -1)).reshape(-1),
    ]
    wide_vector = net.place(jnp.sum(pre_grad, axis=0).reshape(n_mp, -1)).reshape(-1, features)
    total = net.sum_all(jnp.concatenate([jnp.stack(vectors), wide_vector], axis=0))
    width = features // n_mp
    units = wide_vector.size // n_mp
    return (
        student_output,
        input_grad,
        qkv_grad,
        lax.dynamic_slice_in_dim(total[6:8], me * width, width, axis=1),
        out_grad,
        up_grad,
        lax.dynamic_slice_in_dim(total[8:].reshape(-1), me * units, units),
        down_grad,
        total[0:2],
        total[2:4],
        total[4:6],
    )


def solution(mesh):
    n_dp, n_mp = mesh.shape["dp"], mesh.shape["mp"]

    def body(*args):
        return per_device(n_dp, n_mp, *args)

    return jax.shard_map(
        body,
        mesh=mesh,
        in_specs=(
            P(("dp", "mp"), None),
            P("dp"),
            P(None, None, "mp"),
            P(None, "mp"),
            P("mp", None),
            P(None, "mp"),
            P("mp"),
            P("mp", None),
            P(),
            P(),
            P(),
            P(None, None, "mp"),
            P(None, "mp"),
            P("mp", None),
            P(None, "mp"),
            P("mp"),
            P("mp", None),
            P(),
            P(),
            P(),
        ),
        out_specs=(
            P(("dp", "mp"), None),
            P(("dp", "mp"), None),
            P(None, None, "mp"),
            P(None, "mp"),
            P("mp", None),
            P(None, "mp"),
            P("mp"),
            P("mp", None),
            P(),
            P(),
            P(),
        ),
        check_vma=False,
    )
```

```python
import math

import jax
import jax.numpy as jnp
from jax import lax
from jax.experimental import pallas as pl
from jax.experimental.pallas import tpu as pltpu
from jax.sharding import PartitionSpec as P

DH = 64
LEN = 128


norm_epsilon = 1e-06
clip_level = 2.5
score_weight = 0.05
masked_fill = -1000000000.0


def to_float(values):
    return values.astype(jnp.float32)


def to_low(values):
    return values.astype(jnp.bfloat16)


def binarize(matrix, axis_index):
    scaling = jnp.mean(jnp.abs(matrix), axis=axis_index, keepdims=True)
    return (scaling * jnp.sign(matrix)).astype(jnp.bfloat16)


def norm_stats(values):
    centred = values - jnp.mean(values, axis=-1, keepdims=True)
    variance = jnp.mean(centred * centred, axis=-1, keepdims=True)
    inverse = lax.rsqrt(variance + norm_epsilon)
    return (centred * inverse, inverse)


def norm_back(grad, unit, inverse, gain_row):
    scaled = grad * gain_row
    first = jnp.mean(scaled, axis=-1, keepdims=True)
    second = jnp.mean(scaled * unit, axis=-1, keepdims=True)
    return inverse * (scaled - first - unit * second)


def dot(left, right):
    return jnp.dot(left, right, preferred_element_type=jnp.float32)


def dot_nt(left, right):
    return lax.dot_general(left, right, (((1,), (1,)), ((), ())), preferred_element_type=jnp.float32)


def dot_tn(left, right):
    return lax.dot_general(left, right, (((0,), (0,)), ((), ())), preferred_element_type=jnp.float32)


class Cube:
    def __init__(self, n_dp):
        self.n_dp = n_dp
        self.axes = ("dp", "mp")

    def flip(self, values, bits):
        pairs = [
            (z * 8 + m, z * 8 + (m ^ bits)) for z in range(self.n_dp) for m in range(8)
        ]
        return lax.ppermute(values, self.axes, pairs)

    def flip_dp(self, values, bits):
        pairs = [
            (z * 8 + m, (z ^ bits) * 8 + m) for z in range(self.n_dp) for m in range(8)
        ]
        return lax.ppermute(values, self.axes, pairs)

    def gather(self, block):
        half = block.shape[0] // 2
        along_x = self.flip(block, 2)
        along_y = self.flip(block, 4)
        across = jnp.concatenate(
            [self.flip(along_y[:half], 2), self.flip(along_x[half:], 4)], axis=0
        )
        same = [block, along_x, along_y, across]
        other = [self.flip(item, 1) for item in same]
        return [item for pair in zip(same, other) for item in pair]

    def scatter(self, blocks):
        half = blocks[0].shape[0] // 2
        own, to_x, to_y, to_far = [
            to_float(blocks[k]) + to_float(self.flip(blocks[k + 1], 1)) for k in (0, 2, 4, 6)
        ]
        far = to_low(to_far)
        via_x = to_float(self.flip(far[:half], 2))
        via_y = to_float(self.flip(far[half:], 4))
        to_y = to_low(jnp.concatenate([to_y[:half] + via_x, to_y[half:]], axis=0))
        to_x = to_low(jnp.concatenate([to_x[:half], to_x[half:] + via_y], axis=0))
        return own + to_float(self.flip(to_x, 2)) + to_float(self.flip(to_y, 4))

    def sum_dp(self, values):
        half = values.shape[0] // 2
        odd = lax.axis_index("dp") % 2
        low = to_low(values)
        sent = lax.dynamic_slice_in_dim(low, (1 - odd) * half, half)
        kept = lax.dynamic_slice_in_dim(values, odd * half, half)
        kept = kept + to_float(self.flip_dp(sent, 1))
        kept_low = to_low(kept)
        kept = to_low(kept + to_float(self.flip_dp(kept_low, 2)))
        other = self.flip_dp(kept, 1)
        return to_float(
            jnp.concatenate(
                [jnp.where(odd == 0, kept, other), jnp.where(odd == 0, other, kept)], axis=0
            )
        )

    def sum_all(self, values):
        for bits in (1, 2, 4):
            values = values + self.flip(values, bits)
        for bits in (1, 2):
            values = values + self.flip_dp(values, bits)
        return values

    def place(self, values):
        me = lax.axis_index("mp")
        for bit in range(3):
            shape = values.shape
            split = values.reshape((8 >> (bit + 1), 2, 1 << bit) + shape[1:])
            flipped = split[:, ::-1]
            values = jnp.where((me >> bit) % 2 == 1, flipped, split).reshape(shape)
        return values


class Plain:
    def __init__(self, n_mp):
        self.n_mp = n_mp

    def gather(self, block):
        every = lax.all_gather(block, "mp", axis=0)
        return [every[k] for k in range(self.n_mp)]

    def scatter(self, blocks):
        return to_float(
            lax.psum_scatter(jnp.stack(blocks), "mp", scatter_dimension=0, tiled=False)
        )

    def sum_dp(self, values):
        return to_float(lax.psum(to_low(values), "dp"))

    def sum_all(self, values):
        return lax.psum(values, ("dp", "mp"))

    def place(self, values):
        return values


def plain_act(pre):
    gate = 0.5 * (1.0 + lax.erf(pre * math.sqrt(0.5)))
    slope = gate + pre * jnp.exp(-0.5 * pre * pre) * (1.0 / math.sqrt(2.0 * math.pi))
    return (pre * gate, slope)


def clipped_act(pre):
    value, slope = plain_act(pre)
    bent = jnp.tanh(value * (1.0 / clip_level))
    return (clip_level * bent, slope * (1.0 - bent * bent))


def gather_layer(net, qkv, qv_bias, out, up, up_bias, down):
    width = qkv.shape[2]
    units = up.shape[1]
    features = qkv.shape[0]
    extra = jnp.zeros((16, features), jnp.bfloat16)
    extra = extra.at[0, :width].set(qv_bias[0]).at[1, :width].set(qv_bias[1])
    extra = extra.at[2, :units].set(up_bias)
    qkv_parts = net.gather(qkv.transpose(1, 0, 2).reshape(3 * features, width))
    out_parts = net.gather(jnp.concatenate([out, extra], axis=0))
    up_parts = net.gather(up)
    down_parts = net.gather(down)
    count = len(qkv_parts)
    qkv_full = jnp.concatenate(
        [part.reshape(3, features, width) for part in qkv_parts], axis=2
    )
    out_full = jnp.concatenate([part[:width] for part in out_parts], axis=0)
    q_bias = jnp.concatenate([part[width, :width] for part in out_parts])
    v_bias = jnp.concatenate([part[width + 1, :width] for part in out_parts])
    up_b = jnp.concatenate([part[width + 2, :units] for part in out_parts])
    up_full = jnp.concatenate(up_parts, axis=1)
    down_full = jnp.concatenate(down_parts, axis=0)
    return (qkv_full, to_float(q_bias), to_float(v_bias), out_full, up_full, to_float(up_b), down_full)


def forward(tokens, weights, out_bias, gain, shift, activation, key_valid):
    qkv, q_bias, v_bias, out, up, up_bias, down = weights
    rows, features = tokens.shape
    pairs = rows // LEN
    shape = (pairs, LEN, features // DH, DH)
    query = to_low(dot(tokens, qkv[0]) + q_bias).reshape(shape)
    key = to_low(dot(tokens, qkv[1])).reshape(shape)
    value = to_low(dot(tokens, qkv[2]) + v_bias).reshape(shape)
    scores = jnp.einsum("bqhe,bkhe->bhqk", query, key, preferred_element_type=jnp.float32) * (
        1.0 / math.sqrt(DH)
    )
    masked = jnp.where(key_valid[:, None, None, :], scores, masked_fill)
    log_norm = jax.nn.logsumexp(masked, axis=-1, keepdims=True)
    attention = jnp.exp(masked - log_norm)
    context = jnp.einsum(
        "bhqk,bkhe->bqhe", to_low(attention), value, preferred_element_type=jnp.float32
    )
    context = to_low(context).reshape(rows, features)
    first = to_float(tokens) + dot(context, out) + out_bias[0]
    unit_one, inverse_one = norm_stats(first)
    normed = unit_one * gain[0] + shift[0]
    normed_low = to_low(normed)
    hidden, slope = activation(dot(normed_low, up) + up_bias)
    hidden = to_low(hidden)
    second = normed + dot(hidden, down) + out_bias[1]
    unit_two, inverse_two = norm_stats(second)
    final = unit_two * gain[1] + shift[1]
    kept = (query, key, value, scores, attention, context, unit_one, inverse_one, normed_low, hidden,
            to_low(slope), unit_two, inverse_two)
    return (final, kept)


def backward_ffn(kept, weights, second_grad, gain):
    qkv, q_bias, v_bias, out, up, up_bias, down = weights
    (query, key, value, scores, attention, context, unit_one, inverse_one, normed_low, hidden,
     slope, unit_two, inverse_two) = kept
    second_low = to_low(second_grad)
    pre_grad = dot_nt(second_low, down) * slope
    pre_low = to_low(pre_grad)
    normed_grad = second_grad + dot_nt(pre_low, up)
    first_grad = norm_back(normed_grad, unit_one, inverse_one, gain[0])
    return (second_grad, second_low, pre_grad, pre_low, normed_grad, first_grad)


def backward_attention(kept, first_low, out, extra):
    query, key, value, scores, attention = kept[:5]
    rows = first_low.shape[0]
    factor = 1.0 / math.sqrt(DH)
    context_grad = to_low(dot_nt(first_low, out)).reshape(query.shape)
    attention_grad = jnp.einsum(
        "bqhe,bkhe->bhqk", context_grad, value, preferred_element_type=jnp.float32
    )
    value_grad = jnp.einsum(
        "bhqk,bqhe->bkhe", to_low(attention), context_grad, preferred_element_type=jnp.float32
    )
    inner = jnp.sum(attention * attention_grad, axis=-1, keepdims=True)
    score_low = to_low(attention * (attention_grad - inner) + extra)
    query_grad = factor * jnp.einsum(
        "bhqk,bkhe->bqhe", score_low, key, preferred_element_type=jnp.float32
    )
    key_grad = factor * jnp.einsum(
        "bhqk,bqhe->bkhe", score_low, query, preferred_element_type=jnp.float32
    )
    return [item.reshape(rows, -1) for item in (query_grad, key_grad, value_grad)]


MESH = pl.DeviceIdType.MESH
SLOTS = 8
PACKS = 6
ATT_ROWS = 528
FFN_ROWS = 512
HALF_UNITS = 256
COLS = 128


def flipped(me, bits):
    return me + bits - 2 * bits * lax.rem(lax.div(me, bits), 2)


def pack_rows(pack):
    return ATT_ROWS if pack < 2 else FFN_ROWS


def pack_half(pack):
    return 272 if pack < 2 else 256


def masked_probs(scores, length):
    rows = scores.shape[0]
    position = lax.broadcasted_iota(jnp.int32, (rows, LEN), 1)
    parts = []
    for head in range(2):
        part = jnp.where(position < length, scores[:, head * LEN : (head + 1) * LEN], masked_fill)
        part = jnp.exp(part - jnp.max(part, axis=1, keepdims=True))
        parts.append(part / jnp.sum(part, axis=1, keepdims=True))
    return jnp.concatenate(parts, axis=1)


def two_heads(rows):
    first = lax.broadcasted_iota(jnp.int32, rows.shape, 1) < DH
    zero = jnp.zeros_like(rows)
    return jnp.concatenate([jnp.where(first, rows, zero), jnp.where(first, zero, rows)], axis=0)


def norm_block(values):
    centred = values - jnp.mean(values, axis=1, keepdims=True)
    inverse = lax.rsqrt(jnp.mean(centred * centred, axis=1, keepdims=True) + norm_epsilon)
    return (centred * inverse, inverse)


def forward_kernel(
    lengths,
    x_ref,
    packs_att,
    packs_ffn,
    t_bias,
    t_gain,
    t_shift,
    s_bias,
    s_gain,
    s_shift,
    gathered,
    qkv_t,
    qkv_s,
    context_s,
    slope_t,
    slope_s,
    hidden_s,
    unit_t,
    inverse_t,
    unit_s,
    inverse_s,
    low_s,
    grad_t,
    grad_s,
    final_low,
    vectors,
    wide,
    total,
    normed,
    low_t,
    context_t,
    bias_rows,
    final_t,
    unit_two,
    inverse_two,
    send,
    recv,
    load,
    own,
):
    me = lax.axis_index("mp")
    peers = {1: flipped(me, 1), 2: flipped(me, 2), 4: flipped(me, 4)}
    rows = x_ref.shape[0]
    pairs = rows // LEN

    barrier = pltpu.get_barrier_semaphore()
    for peer in peers.values():
        pl.semaphore_signal(barrier, inc=1, device_id={"mp": peer}, device_id_type=MESH)
    pl.semaphore_wait(barrier, 3)

    def source(pack):
        return packs_att.at[pack] if pack < 2 else packs_ffn.at[pack - 2]

    def block(pack, slot, start=0, count=None):
        count = pack_rows(pack) if count is None else count
        return gathered.at[pack, slot, pl.ds(start, count)]

    def remote(pack, kind):
        half = pack_half(pack)
        rest = pack_rows(pack) - half
        if kind == 0:
            src, dst, bits = source(pack), block(pack, 2), 2
        elif kind == 1:
            src, dst, bits = source(pack), block(pack, 4), 4
        elif kind == 2:
            src, dst, bits = block(pack, 4, 0, half), block(pack, 6, 0, half), 2
        elif kind == 3:
            src, dst, bits = block(pack, 2, half, rest), block(pack, 6, half, rest), 4
        elif kind == 4:
            src, dst, bits = source(pack), block(pack, 1), 1
        else:
            slot = 2 * (kind - 4)
            src, dst, bits = block(pack, slot), block(pack, slot + 1), 1
        return pltpu.make_async_remote_copy(
            src_ref=src,
            dst_ref=dst,
            send_sem=send.at[pack, kind],
            recv_sem=recv.at[pack, kind],
            device_id={"mp": peers[bits]},
            device_id_type=MESH,
        )

    def keep_own(pack):
        return pltpu.make_async_copy(source(pack), block(pack, 0), own.at[pack])

    def first_sends(pack):
        for kind in (0, 1, 4):
            remote(pack, kind).start()
        keep_own(pack).start()

    def second_sends(pack):
        remote(pack, 0).wait_recv()
        remote(pack, 3).start()
        remote(pack, 5).start()
        remote(pack, 1).wait_recv()
        remote(pack, 2).start()
        remote(pack, 6).start()

    def load_pair(pack, pair, place):
        return pltpu.make_async_copy(
            gathered.at[pack, pl.ds(2 * pair, 2), pl.ds(0, pack_rows(pack))],
            wide.at[place, :, pl.ds(0, pack_rows(pack))],
            load.at[place],
        )

    def over_pairs(pack, body):
        keep_own(pack).wait()
        remote(pack, 4).wait_recv()
        load_pair(pack, 0, 0).start()
        for pair in range(4):
            place = pair % 2
            load_pair(pack, pair, place).wait()
            if pair < 3:
                if pair == 2:
                    remote(pack, 2).wait_recv()
                    remote(pack, 3).wait_recv()
                    remote(pack, 7).start()
                remote(pack, 5 + pair).wait_recv()
                load_pair(pack, pair + 1, 1 - place).start()
            body(pair, place)

    def attention(pack, qkv_ref, context_ref):
        total[...] = jnp.zeros_like(total)

        def body(pair, place):
            weights = wide[place, :, 0:384].reshape(768, -1)
            projected = dot_nt(x_ref[...], weights)
            for side in range(2):
                slot = 2 * pair + side
                bias = wide[place, side, 512:528]
                bias_rows[pack, slot] = bias
                bias = to_float(bias[0:1])
                part = projected[:, side * 384 : side * 384 + 384]
                query = to_low(part[:, :COLS] + bias[:, :COLS])
                key = to_low(part[:, COLS : 2 * COLS])
                value = to_low(part[:, 2 * COLS :] + bias[:, COLS : 2 * COLS])
                qkv_ref[slot, :, 0:COLS] = query
                qkv_ref[slot, :, COLS : 2 * COLS] = key
                qkv_ref[slot, :, 2 * COLS : 3 * COLS] = value
                for number in range(pairs):
                    here = slice(number * LEN, (number + 1) * LEN)
                    scores = dot_nt(query[here], two_heads(key[here])) * (1.0 / math.sqrt(DH))
                    probs = masked_probs(scores, lengths[me * pairs + number])
                    part_context = dot(to_low(probs), two_heads(value[here]))
                    context_ref[pair, here, side * COLS : (side + 1) * COLS] = to_low(part_context)
            total[...] += dot(context_ref[pair], wide[place, :, 384:512].reshape(256, -1))

        over_pairs(pack, body)

    def first_norm(bias_ref, gain_ref, shift_ref, unit_ref, inverse_ref, index, low_ref):
        @pl.loop(0, rows // 64)
        def _(step):
            here = pl.ds(step * 64, 64)
            values = to_float(x_ref[here]) + total[here] + to_float(bias_ref[0:1])
            unit, inverse = norm_block(values)
            unit_ref[here] = unit
            inverse_ref[here] = inverse
            values = unit * to_float(gain_ref[0:1]) + to_float(shift_ref[0:1])
            normed[index, here] = values
            low_ref[here] = to_low(values)

    def feed_forward(layer, half, low_ref, activation, hidden_ref, slope_ref):
        pack = 2 + 2 * layer + half

        def body(pair, place):
            up = wide[place, :, 0:HALF_UNITS].reshape(2 * HALF_UNITS, -1)
            down = wide[place, :, HALF_UNITS : 2 * HALF_UNITS].reshape(2 * HALF_UNITS, -1)
            start = 2 * COLS + half * HALF_UNITS
            bias = jnp.concatenate(
                [
                    to_float(bias_rows[layer, 2 * pair + side, 0:1, start : start + HALF_UNITS])
                    for side in range(2)
                ],
                axis=1,
            )
            hidden, slope = activation(dot_nt(low_ref[...], up) + bias)
            hidden = to_low(hidden)
            slope_ref[half, pair] = to_low(slope)
            if hidden_ref is not None:
                hidden_ref[half, pair] = hidden
            total[...] += dot(hidden, down)

        if half == 0:
            total[...] = jnp.zeros_like(total)
        over_pairs(pack, body)

    def step_teacher_end():
        @pl.loop(0, rows // 64)
        def _(step):
            here = pl.ds(step * 64, 64)
            unit, inverse = norm_block(normed[0, here] + total[here] + to_float(t_bias[1:2]))
            unit_two[here] = unit
            inverse_two[here] = inverse
            final_t[here] = unit * to_float(t_gain[1:2]) + to_float(t_shift[1:2])

    def step_student_end():
        vectors[...] = jnp.zeros_like(vectors)

        @pl.loop(0, rows // 64)
        def _(step):
            here = pl.ds(step * 64, 64)
            unit, inverse = norm_block(normed[1, here] + total[here] + to_float(s_bias[1:2]))
            gain = to_float(s_gain[1:2])
            final = unit * gain + to_float(s_shift[1:2])
            final_low[here] = to_low(final)
            position = lax.broadcasted_iota(jnp.int32, (64, 1), 0) + lax.rem(step, 2) * 64
            valid = position < lengths[me * pairs + lax.div(step, 2)]
            grad = jnp.where(valid, final - final_t[here], 0.0)
            back = norm_back(grad, unit, inverse, gain)
            grad_s[here] = back
            grad_t[here] = norm_back(
                -grad, unit_two[here], inverse_two[here], to_float(t_gain[1:2])
            )
            vectors[0:1] += jnp.sum(back, axis=0, keepdims=True)
            vectors[1:2] += jnp.sum(grad * unit, axis=0, keepdims=True)
            vectors[2:3] += jnp.sum(grad, axis=0, keepdims=True)

    def use(pack):
        if pack == 0:
            attention(0, qkv_t, context_t)
            first_norm(t_bias, t_gain, t_shift, unit_t, inverse_t, 0, low_t)
        elif pack == 1:
            attention(1, qkv_s, context_s)
            first_norm(s_bias, s_gain, s_shift, unit_s, inverse_s, 1, low_s)
        elif pack < 4:
            feed_forward(0, pack - 2, low_t, plain_act, None, slope_t)
            if pack == 3:
                step_teacher_end()
        else:
            feed_forward(1, pack - 4, low_s, clipped_act, hidden_s, slope_s)
            if pack == 5:
                step_student_end()

    first_sends(0)
    first_sends(1)
    for pack in range(PACKS):
        second_sends(pack)
        if pack + 2 < PACKS:
            first_sends(pack + 2)
        if pack:
            use(pack - 1)
    use(PACKS - 1)
    for pack in range(PACKS):
        for kind in range(8):
            remote(pack, kind).wait_send()


def forward_both(lengths, tokens, packs_att, packs_ffn, teacher_rows, student_rows):
    rows, features = tokens.shape
    low, full = jnp.bfloat16, jnp.float32
    vmem = pl.BlockSpec(memory_space=pltpu.VMEM)
    hbm = pl.BlockSpec(memory_space=pl.ANY)
    shapes = [
        ((PACKS, SLOTS, ATT_ROWS, features), low, hbm),
        ((SLOTS, rows, 3 * COLS), low, vmem),
        ((SLOTS, rows, 3 * COLS), low, vmem),
        ((4, rows, 2 * COLS), low, vmem),
        ((2, 4, rows, 2 * HALF_UNITS), low, vmem),
        ((2, 4, rows, 2 * HALF_UNITS), low, vmem),
        ((2, 4, rows, 2 * HALF_UNITS), low, vmem),
        ((rows, features), full, vmem),
        ((rows, 1), full, vmem),
        ((rows, features), full, vmem),
        ((rows, 1), full, vmem),
        ((rows, features), low, vmem),
        ((rows, features), full, vmem),
        ((rows, features), full, vmem),
        ((rows, features), low, vmem),
        ((8, features), full, vmem),
    ]
    return pl.pallas_call(
        forward_kernel,
        out_shape=[jax.ShapeDtypeStruct(shape, kind) for shape, kind, _ in shapes],
        in_specs=[pl.BlockSpec(memory_space=pltpu.SMEM), vmem, hbm, hbm] + [vmem] * 6,
        out_specs=[spec for _, _, spec in shapes],
        scratch_shapes=[
            pltpu.VMEM((2, 2, ATT_ROWS, features), low),
            pltpu.VMEM((rows, features), full),
            pltpu.VMEM((2, rows, features), full),
            pltpu.VMEM((rows, features), low),
            pltpu.VMEM((4, rows, 2 * COLS), low),
            pltpu.VMEM((2, SLOTS, 16, features), low),
            pltpu.VMEM((rows, features), full),
            pltpu.VMEM((rows, features), full),
            pltpu.VMEM((rows, 1), full),
            pltpu.SemaphoreType.DMA((PACKS, 8)),
            pltpu.SemaphoreType.DMA((PACKS, 8)),
            pltpu.SemaphoreType.DMA((2,)),
            pltpu.SemaphoreType.DMA((PACKS,)),
        ],
        compiler_params=pltpu.CompilerParams(
            collective_id=0, has_side_effects=True, vmem_limit_bytes=60 * 1024 * 1024
        ),
        name="forward_both",
    )(lengths, tokens, packs_att, packs_ffn, *teacher_rows, *student_rows)


def pack_layer(qkv, qv_bias, out, up, up_bias, down):
    features, _, width = qkv.shape
    bias = jnp.concatenate([qv_bias.reshape(-1), up_bias])
    bias = jnp.pad(bias[None], ((0, 15), (0, features - bias.size)))
    att = jnp.concatenate([qkv.transpose(1, 2, 0).reshape(3 * width, features), out, bias], axis=0)
    halves = [
        jnp.concatenate(
            [
                up[:, h * HALF_UNITS : (h + 1) * HALF_UNITS].T,
                down[h * HALF_UNITS : (h + 1) * HALF_UNITS],
            ],
            axis=0,
        )
        for h in range(2)
    ]
    return (att, jnp.stack(halves))


CHUNKS = 3
PARTS = 4
ORDER = (3, 1, 2, 0)


def backward_kernel(
    lengths,
    x_ref,
    gathered,
    qkv_t,
    qkv_s,
    context_s,
    slope_t,
    slope_s,
    hidden_s,
    unit_t,
    inverse_t,
    unit_s,
    inverse_s,
    low_s,
    grad_t,
    grad_s,
    vectors,
    t_gain,
    s_gain,
    grad_in,
    sums_out,
    vec,
    wide,
    hidden_buf,
    slope_buf,
    qkv_s_buf,
    qkv_t_buf,
    context_buf,
    extra_buf,
    unit_buf,
    inverse_buf,
    grad_buf,
    total,
    low_y,
    low_z,
    low_a,
    proj,
    sums,
    even,
    odd,
    from_core,
    from_far,
    from_x,
    from_y,
    from_z,
    from_vec,
    load,
    state_sem,
    odd_send,
    odd_recv,
    free,
    far_send,
    far_recv,
    x_send,
    x_recv,
    y_send,
    y_recv,
    in_send,
    in_recv,
    mid_send,
    mid_recv,
    out_send,
    out_recv,
    vec_send,
    vec_recv,
    done,
):
    me = lax.axis_index("mp")
    z = lax.axis_index("dp")
    rows = x_ref.shape[0]
    pairs = rows // LEN
    core, along_x, along_y = ({"mp": flipped(me, bits)} for bits in (1, 2, 4))
    z_outer, z_inner = {"dp": flipped(z, 1)}, {"dp": 3 - z}
    z_two = {"dp": flipped(z, 2)}
    inner = jnp.logical_or(z == 1, z == 2)
    outer = jnp.logical_or(z == 0, z == 3)

    barrier = pltpu.get_barrier_semaphore()
    greeted = (core, along_x, along_y, z_outer, z_inner, z_two)
    for peer in greeted:
        pl.semaphore_signal(barrier, inc=1, device_id=peer, device_id_type=MESH)
    pl.semaphore_wait(barrier, len(greeted))

    def remote(src, dst, send, recv, peer):
        return pltpu.make_async_remote_copy(
            src_ref=src, dst_ref=dst, send_sem=send, recv_sem=recv, device_id=peer, device_id_type=MESH
        )

    steps = [("fs", 4 + half, pair) for half in range(2) for pair in ORDER]
    steps += [("as", 1, pair) for pair in ORDER]
    steps += [("ft", 2 + half, pair) for half in range(2) for pair in range(4)]
    steps += [("at", 0, pair) for pair in range(4)]

    def loads(number):
        kind, pack, pair = steps[number]
        place = number % 2
        count = pack_rows(pack) if pack > 1 else FFN_ROWS
        two = pl.ds(2 * pair, 2)
        moves = [(gathered.at[pack, two, pl.ds(0, count)], wide.at[place, :, pl.ds(0, count)])]
        if kind == "fs":
            moves.append((hidden_s.at[pack - 4, pair], hidden_buf.at[place]))
            moves.append((slope_s.at[pack - 4, pair], slope_buf.at[place]))
        elif kind == "ft":
            moves.append((slope_t.at[pack - 2, pair], slope_buf.at[place]))
        else:
            moves.append((qkv_t.at[two], qkv_t_buf.at[place]))
            if kind == "as":
                moves.append((qkv_s.at[two], qkv_s_buf.at[place]))
                moves.append((context_s.at[pair], context_buf.at[place]))
        return [
            pltpu.make_async_copy(src, dst, load.at[place, index])
            for index, (src, dst) in enumerate(moves)
        ]

    def state(layer):
        unit, inverse, grad = ((unit_t, inverse_t, grad_t), (unit_s, inverse_s, grad_s))[layer]
        moves = [(grad, grad_buf), (unit, unit_buf), (inverse, inverse_buf)]
        return [
            pltpu.make_async_copy(src, dst, state_sem.at[index])
            for index, (src, dst) in enumerate(moves)
        ]

    def slot_row(slot):
        row = me
        for bits in (1, 2, 4):
            if slot & bits:
                row = flipped(row, bits)
        return row

    def odd_copy(number):
        pair = steps[number][2]
        return remote(
            odd.at[number % 2], from_core.at[pair], odd_send.at[number % 2], odd_recv.at[pair], core
        )

    def keep(chunk, pair):
        return sums.at[chunk] if pair == 0 else even.at[chunk, pair - 1]

    def give(number, pieces):
        pair = steps[number][2]
        chunk = number // 4
        if number >= 2:
            odd_copy(number - 2).wait_send()
        for start, values in pieces:
            count = values.shape[0] // 2
            keep(chunk, pair)[start : start + count] = to_low(values[:count])
            odd[number % 2, start : start + count] = to_low(values[count:])
        if chunk:
            pl.semaphore_wait(free.at[pair], 1)
        odd_copy(number).start()

    def add_rows(target, others, start, count):
        @pl.loop(0, count // 64)
        def _(step):
            here = pl.ds(start + step * 64, 64)
            value = to_float(target[here])
            for other in others:
                value = value + to_float(other[here])
            target[here] = to_low(value)

    def combine(chunk, pair):
        number = chunk * 4 + ORDER.index(pair)
        odd_copy(number).wait_recv()
        add_rows(keep(chunk, pair), [from_core.at[pair]], 0, FFN_ROWS)
        if chunk < CHUNKS - 1:
            pl.semaphore_signal(free.at[pair], inc=1, device_id=core, device_id_type=MESH)
        if pair == 3:
            far_copy(chunk, 0).start()
            far_copy(chunk, 1).start()

    def far_copy(chunk, way):
        part = pl.ds(way * 256, 256)
        return remote(
            even.at[chunk, 2, part],
            from_far.at[chunk, part],
            far_send.at[chunk, way],
            far_recv.at[chunk, way],
            (along_x, along_y)[way],
        )

    part_rows = FFN_ROWS // PARTS

    def plane_copies(chunk, part):
        here = pl.ds(part * part_rows, part_rows)
        return [
            remote(even.at[chunk, 0, here], from_x.at[chunk, here], x_send.at[chunk, part], x_recv.at[chunk, part], along_x),
            remote(even.at[chunk, 1, here], from_y.at[chunk, here], y_send.at[chunk, part], y_recv.at[chunk, part], along_y),
        ]

    def fold(chunk):
        far_copy(chunk, 0).wait_recv()
        add_rows(keep(chunk, 2), [from_far.at[chunk]], 0, 256)
        far_copy(chunk, 1).wait_recv()
        add_rows(keep(chunk, 1), [from_far.at[chunk]], 256, 256)
        for part in range(PARTS):
            for copy in plane_copies(chunk, part):
                copy.start()

    def z_copy(chunk, part, kind):
        here = pl.ds(part * part_rows, part_rows)
        own, first, second = sums.at[chunk, here], from_z.at[chunk, 0, here], from_z.at[chunk, 1, here]
        if kind == 0:
            return remote(own, first, in_send.at[chunk, part], in_recv.at[chunk, part], z_outer)
        if kind == 1:
            return remote(own, second, mid_send.at[chunk, part], mid_recv.at[chunk, part], z_inner)
        return remote(first, first, out_send.at[chunk, part], out_recv.at[chunk, part], z_outer)

    def own_part(chunk, part):
        for copy in plane_copies(chunk, part):
            copy.wait_recv()
        add_rows(sums.at[chunk], [from_x.at[chunk], from_y.at[chunk]], part * part_rows, part_rows)

        @pl.when(outer)
        def _():
            z_copy(chunk, part, 0).start()

    def mid_part(chunk, part):
        @pl.when(inner)
        def _():
            z_copy(chunk, part, 0).wait_recv()
            add_rows(sums.at[chunk], [from_z.at[chunk, 0]], part * part_rows, part_rows)
            z_copy(chunk, part, 1).start()

    def end_part(chunk, part):
        @pl.when(inner)
        def _():
            z_copy(chunk, part, 1).wait_recv()

            @pl.loop(0, part_rows // 64)
            def _(step):
                here = pl.ds(part * part_rows + step * 64, 64)
                value = to_float(sums[chunk, here]) + to_float(from_z[chunk, 1, here])
                from_z[chunk, 0, here] = to_low(value)

            z_copy(chunk, part, 2).start()

    def store_copy(chunk):
        return pltpu.make_async_copy(from_z.at[chunk, 0], sums_out.at[chunk], done.at[chunk])

    def finish(chunk):
        @pl.when(outer)
        def _():
            for part in range(PARTS):
                z_copy(chunk, part, 2).wait_recv()

        store_copy(chunk).start()

    ways = (core, along_x, along_y, z_outer, z_two)

    def vec_copy(way):
        return remote(vec, from_vec.at[way], vec_send.at[way], vec_recv.at[way], ways[way])

    def vec_add(way):
        vec_copy(way).wait_send()
        vec_copy(way).wait_recv()
        vec[...] += from_vec[way]
        if way + 1 < len(ways):
            vec_copy(way + 1).start()

    def put_bias(pair, start, values):
        count = values.shape[1] // 2
        for side in range(2):
            line = lax.broadcasted_iota(jnp.int32, (SLOTS, count), 0)
            part = jnp.broadcast_to(values[:, side * count : (side + 1) * count], (SLOTS, count))
            part = jnp.where(line == slot_row(2 * pair + side), part, 0.0)
            vec[0:SLOTS, start : start + count] += part

    def ffn_step(number):
        kind, pack, pair = steps[number]
        place = number % 2
        up = wide[place, :, 0:HALF_UNITS].reshape(2 * HALF_UNITS, -1)
        down = wide[place, :, HALF_UNITS : 2 * HALF_UNITS].reshape(2 * HALF_UNITS, -1)
        back = dot_nt(low_z[...], down) * to_float(slope_buf[place])
        back_low = to_low(back)
        total[...] += dot(back_low, up)
        if kind == "fs":
            put_bias(pair, 2 * COLS + (pack - 4) * HALF_UNITS, jnp.sum(back, axis=0, keepdims=True))
            up_grad = dot_tn(back_low, low_y[...])
            down_grad = dot_tn(hidden_buf[place], low_z[...])
            give(number, [(0, up_grad), (HALF_UNITS, down_grad)])

    def pick(both):
        first = lax.broadcasted_iota(jnp.int32, (LEN, COLS), 1) < DH
        return jnp.where(first, both[:LEN], both[LEN:])

    def attention_step(number):
        kind, pack, pair = steps[number]
        place = number % 2
        student = kind == "as"
        factor = 1.0 / math.sqrt(DH)
        qkv = qkv_s_buf if student else qkv_t_buf
        out = wide[place, :, 384:512].reshape(2 * COLS, -1)
        context_back = to_low(dot_nt(low_a[...], out))
        query_sums, value_sums = [], []
        for side in range(2):
            query_sum = jnp.zeros((1, COLS), jnp.float32)
            value_sum = jnp.zeros((1, COLS), jnp.float32)
            for number_b in range(pairs):
                here = slice(number_b * LEN, (number_b + 1) * LEN)
                length = lengths[me * pairs + number_b]
                query, key, value = [
                    qkv[place, side, here, i * COLS : (i + 1) * COLS] for i in range(3)
                ]
                keys, values = two_heads(key), two_heads(value)
                scores = dot_nt(query, keys) * factor
                probs = masked_probs(scores, length)
                if student:
                    other = dot_nt(
                        qkv_t_buf[place, side, here, 0:COLS],
                        two_heads(qkv_t_buf[place, side, here, COLS : 2 * COLS]),
                    )
                    spot = lax.broadcasted_iota(jnp.int32, scores.shape, 1)
                    spot = jnp.where(spot < LEN, spot, spot - LEN)
                    line = lax.broadcasted_iota(jnp.int32, scores.shape, 0)
                    gap = score_weight * (scores - other * factor)
                    extra = jnp.where(jnp.maximum(spot, line) < length, gap, 0.0)
                    extra_buf[pair, side, number_b] = to_low(extra)
                else:
                    extra = -to_float(extra_buf[pair, side, number_b])
                part = context_back[here, side * COLS : (side + 1) * COLS]
                probs_back = dot_nt(part, values)
                value_back = pick(dot_tn(to_low(probs), part))
                product = probs * probs_back
                inner_sum = jnp.concatenate(
                    [
                        jnp.broadcast_to(
                            jnp.sum(product[:, i * LEN : (i + 1) * LEN], axis=1, keepdims=True), (LEN, LEN)
                        )
                        for i in range(2)
                    ],
                    axis=1,
                )
                score_back = to_low(product - probs * inner_sum + extra)
                query_back = dot(score_back, keys) * factor
                key_back = pick(dot_tn(score_back, query)) * factor
                start = side * 3 * COLS
                proj[here, start : start + COLS] = to_low(query_back)
                proj[here, start + COLS : start + 2 * COLS] = to_low(key_back)
                proj[here, start + 2 * COLS : start + 3 * COLS] = to_low(value_back)
                if student:
                    query_sum += jnp.sum(query_back, axis=0, keepdims=True)
                    value_sum += jnp.sum(value_back, axis=0, keepdims=True)
            query_sums.append(query_sum)
            value_sums.append(value_sum)
        grad_in[...] += dot(proj[...], wide[place, :, 0:384].reshape(768, -1))
        if student:
            put_bias(pair, 0, jnp.concatenate(query_sums, axis=1))
            put_bias(pair, COLS, jnp.concatenate(value_sums, axis=1))
            qkv_grad = dot_tn(proj[...], x_ref[...])
            out_grad = dot_tn(context_buf[place], low_a[...])
            give(number, [(0, qkv_grad), (3 * COLS, out_grad)])

    def lower_grad():
        @pl.loop(0, rows // 64)
        def _(step):
            here = pl.ds(step * 64, 64)
            low_z[here] = to_low(grad_buf[here])

        total[...] = jnp.zeros_like(total)

    def norm_step(student):
        gain_ref = s_gain if student else t_gain

        @pl.loop(0, rows // 64)
        def _(step):
            here = pl.ds(step * 64, 64)
            grad = grad_buf[here] + total[here]
            unit = unit_buf[here]
            back = norm_back(grad, unit, inverse_buf[here], to_float(gain_ref[0:1]))
            low_a[here] = to_low(back)
            if student:
                grad_in[here] = back
                vec[8:9] += jnp.sum(back, axis=0, keepdims=True)
                vec[9:10] += jnp.sum(grad * unit, axis=0, keepdims=True)
                vec[10:11] += jnp.sum(grad, axis=0, keepdims=True)
            else:
                grad_in[here] += back

    hooks = {
        1: [(combine, 0, 3)],
        2: [(combine, 0, 1)],
        3: [(combine, 0, 2)],
        4: [(combine, 0, 0)],
        5: [(combine, 1, 3)],
        6: [(combine, 1, 1)],
        7: [(combine, 1, 2), (fold, 0)],
        8: [(combine, 1, 0)],
        9: [(combine, 2, 3), (fold, 1)],
        10: [(combine, 2, 1)],
        11: [(combine, 2, 2)],
        12: [(combine, 2, 0)],
        13: [(own_part, 0, 0), (own_part, 0, 1)],
        14: [(own_part, 0, 2), (own_part, 0, 3), (vec_add, 0)],
        16: [(vec_add, 1)],
        18: [(mid_part, 0, 0), (vec_add, 2)],
        19: [(mid_part, 0, 1)],
        20: [(mid_part, 0, 2), (mid_part, 0, 3), (vec_add, 3)],
        21: [(end_part, 0, 0), (end_part, 0, 1), (vec_add, 4)],
        22: [(end_part, 0, 2), (end_part, 0, 3), (own_part, 1, 0), (own_part, 1, 1)],
        23: [(own_part, 1, 2), (own_part, 1, 3), (fold, 2), (mid_part, 1, 0), (mid_part, 1, 1)],
    }

    for copy in state(1):
        copy.start()
    low_copy = pltpu.make_async_copy(low_s, low_y, state_sem.at[3])
    low_copy.start()
    for copy in loads(0):
        copy.start()
    vec[...] = jnp.zeros_like(vec)
    vec[11:14] = vectors[0:3]
    for copy in state(1):
        copy.wait()
    low_copy.wait()
    lower_grad()
    for number, (kind, pack, pair) in enumerate(steps):
        for copy in loads(number):
            copy.wait()
        if number + 1 < len(steps):
            for copy in loads(number + 1):
                copy.start()
        if kind in ("fs", "ft"):
            ffn_step(number)
        else:
            attention_step(number)
        for action, *which in hooks.get(number, ()):
            action(*which)
        if number == 7:
            norm_step(True)
            for copy in state(0):
                copy.start()
        elif number == 11:
            for copy in state(0):
                copy.wait()
            lower_grad()
            vec_copy(0).start()
        elif number == 19:
            norm_step(False)
    mid_part(1, 2)
    mid_part(1, 3)
    for part in range(PARTS):
        end_part(1, part)
    finish(0)
    for part in range(PARTS):
        own_part(2, part)
        mid_part(2, part)
    finish(1)
    for part in range(PARTS):
        end_part(2, part)
    finish(2)

    odd_copy(10).wait_send()
    odd_copy(11).wait_send()
    for chunk in range(CHUNKS):
        far_copy(chunk, 0).wait_send()
        far_copy(chunk, 1).wait_send()
        for part in range(PARTS):
            for copy in plane_copies(chunk, part):
                copy.wait_send()

            @pl.when(outer)
            def _():
                z_copy(chunk, part, 0).wait_send()

            @pl.when(inner)
            def _():
                z_copy(chunk, part, 1).wait_send()
                z_copy(chunk, part, 2).wait_send()

        store_copy(chunk).wait()


def backward_both(lengths, tokens, kept, vectors, t_gain, s_gain):
    rows, features = tokens.shape
    low, full = jnp.bfloat16, jnp.float32
    vmem = pl.BlockSpec(memory_space=pltpu.VMEM)
    hbm = pl.BlockSpec(memory_space=pl.ANY)
    dma = pltpu.SemaphoreType.DMA
    block = (FFN_ROWS, features)
    return pl.pallas_call(
        backward_kernel,
        out_shape=[
            jax.ShapeDtypeStruct((rows, features), full),
            jax.ShapeDtypeStruct((CHUNKS,) + block, low),
            jax.ShapeDtypeStruct((16, features), full),
        ],
        in_specs=[pl.BlockSpec(memory_space=pltpu.SMEM), vmem] + [hbm] * len(kept) + [vmem] * 3,
        out_specs=[vmem, hbm, vmem],
        scratch_shapes=[
            pltpu.VMEM((2, 2) + block, low),
            pltpu.VMEM((2, rows, 2 * HALF_UNITS), low),
            pltpu.VMEM((2, rows, 2 * HALF_UNITS), low),
            pltpu.VMEM((2, 2, rows, 3 * COLS), low),
            pltpu.VMEM((2, 2, rows, 3 * COLS), low),
            pltpu.VMEM((2, rows, 2 * COLS), low),
            pltpu.VMEM((4, 2, rows // LEN, LEN, 2 * LEN), low),
            pltpu.VMEM((rows, features), full),
            pltpu.VMEM((rows, 1), full),
            pltpu.VMEM((rows, features), full),
            pltpu.VMEM((rows, features), full),
            pltpu.VMEM((rows, features), low),
            pltpu.VMEM((rows, features), low),
            pltpu.VMEM((rows, features), low),
            pltpu.VMEM((rows, 6 * COLS), low),
            pltpu.VMEM((CHUNKS,) + block, low),
            pltpu.VMEM((CHUNKS, 3) + block, low),
            pltpu.VMEM((2,) + block, low),
            pltpu.VMEM((4,) + block, low),
            pltpu.VMEM((CHUNKS,) + block, low),
            pltpu.VMEM((CHUNKS,) + block, low),
            pltpu.VMEM((CHUNKS,) + block, low),
            pltpu.VMEM((CHUNKS, 2) + block, low),
            pltpu.VMEM((5, 16, features), full),
            dma((2, 4)),
            dma((4,)),
            dma((2,)),
            dma((4,)),
            pltpu.SemaphoreType.REGULAR((4,)),
            dma((CHUNKS, 2)),
            dma((CHUNKS, 2)),
        ]
        + [dma((CHUNKS, PARTS))] * 10
        + [dma((5,)), dma((5,)), dma((CHUNKS,))],
        compiler_params=pltpu.CompilerParams(
            collective_id=1, has_side_effects=True, vmem_limit_bytes=63 * 1024 * 1024
        ),
        name="backward_both",
    )(lengths, tokens, *kept, vectors, t_gain, s_gain)


def cut(values, count, axis):
    return jnp.split(values, count, axis=axis)


def per_device(n_dp, n_mp, *args):
    (
        tokens,
        lengths,
        student_qkv,
        student_qv_bias,
        student_out,
        student_up,
        student_up_bias,
        student_down,
        student_out_bias,
        student_gain,
        student_shift,
        teacher_qkv,
        teacher_qv_bias,
        teacher_out,
        teacher_up,
        teacher_up_bias,
        teacher_down,
        teacher_out_bias,
        teacher_gain,
        teacher_shift,
    ) = args
    net = Cube(n_dp) if (n_dp, n_mp) == (4, 8) else Plain(n_mp)
    rows = tokens.shape[0]
    pairs = rows // LEN
    places = jnp.arange(LEN, dtype=jnp.int32)
    me = lax.axis_index("mp")
    own_lengths = lax.dynamic_slice_in_dim(lengths, me * pairs, pairs)
    valid = places[None, :] < own_lengths[:, None]
    token_valid = to_float(valid.reshape(rows, 1))
    pair_valid = valid[:, None, :, None] & valid[:, None, None, :]

    gain = to_float(student_gain)
    shift = to_float(student_shift)
    out_bias = to_float(student_out_bias)
    teach_gain = to_float(teacher_gain)
    if isinstance(net, Cube):
        teach_att, teach_ffn = pack_layer(
            teacher_qkv, teacher_qv_bias, teacher_out, teacher_up, teacher_up_bias, teacher_down
        )
        stud_att, stud_ffn = pack_layer(
            binarize(student_qkv, 0),
            student_qv_bias,
            binarize(student_out, 1),
            binarize(student_up, 0),
            student_up_bias,
            binarize(student_down, 1),
        )
        (gathered, qkv_t, qkv_s, context_s, slope_t, slope_s, hidden_s, unit_t, inverse_t, unit_s,
         inverse_s, low_s, grad_t, grad_s, student_output, vecs) = forward_both(
            lengths, tokens, jnp.stack([teach_att, stud_att]), jnp.concatenate([teach_ffn, stud_ffn]),
            (teacher_out_bias, teacher_gain, teacher_shift),
            (student_out_bias, student_gain, student_shift),
        )
        input_grad, sums, vec = backward_both(
            lengths, tokens,
            (gathered, qkv_t, qkv_s, context_s, slope_t, slope_s, hidden_s, unit_t, inverse_t, unit_s,
             inverse_s, low_s, grad_t, grad_s),
            vecs, teacher_gain, student_gain,
        )
        sums = to_float(sums)
        row = lax.dynamic_slice_in_dim(vec, me, 1)[0]
        features = tokens.shape[1]
        return (
            student_output,
            input_grad,
            sums[2, : 3 * COLS].reshape(3, COLS, features).transpose(2, 0, 1),
            row[: 2 * COLS].reshape(2, COLS),
            sums[2, 3 * COLS :],
            sums[:2, :HALF_UNITS].reshape(2 * HALF_UNITS, features).T,
            row[2 * COLS : 2 * COLS + 2 * HALF_UNITS],
            sums[:2, HALF_UNITS:].reshape(2 * HALF_UNITS, features),
            jnp.stack([vec[8], vec[11]]),
            jnp.stack([vec[9], vec[12]]),
            jnp.stack([vec[10], vec[13]]),
        )
    else:
        teach = gather_layer(
            net, teacher_qkv, teacher_qv_bias, teacher_out, teacher_up, teacher_up_bias, teacher_down
        )
        stud = gather_layer(
            net,
            binarize(student_qkv, 0),
            student_qv_bias,
            binarize(student_out, 1),
            binarize(student_up, 0),
            student_up_bias,
            binarize(student_down, 1),
        )
        teach_final, teach_kept = forward(
            tokens, teach, to_float(teacher_out_bias), teach_gain, to_float(teacher_shift), plain_act, valid
        )
        final, kept = forward(tokens, stud, out_bias, gain, shift, clipped_act, valid)
        student_output = to_low(final)
        final_grad = token_valid * (final - teach_final)
        grad_s = norm_back(final_grad, kept[11], kept[12], gain[1])
        grad_t = norm_back(-final_grad, teach_kept[11], teach_kept[12], teach_gain[1])
        vecs = jnp.stack([jnp.sum(grad_s, axis=0), jnp.sum(final_grad * kept[11], axis=0), jnp.sum(final_grad, axis=0)])
    extra = score_weight * jnp.where(pair_valid, kept[3] - teach_kept[3], 0.0)

    second_grad, second_low, pre_grad, pre_low, normed_grad, first_grad = backward_ffn(
        kept, stud, grad_s, gain
    )
    hidden, normed_low, context = kept[9], kept[8], kept[5]
    unit_one = kept[6]
    down_grad = net.sum_dp(net.scatter(cut(to_low(dot_tn(hidden, second_low)), n_mp, 0)))
    up_grad = net.sum_dp(net.scatter(cut(to_low(dot_tn(normed_low, pre_low)), n_mp, 1)))
    first_low = to_low(first_grad)
    out_grad = net.sum_dp(net.scatter(cut(to_low(dot_tn(context, first_low)), n_mp, 0)))
    grads = backward_attention(kept, first_low, stud[3], extra)
    lows = [to_low(item) for item in grads]
    wide = jnp.concatenate(
        [to_low(dot_tn(tokens, item)) for item in lows], axis=0
    )
    qkv_grad = net.sum_dp(net.scatter(cut(wide, n_mp, 1)))
    features = tokens.shape[1]
    qkv_grad = qkv_grad.reshape(3, features, -1).transpose(1, 0, 2)

    teach_second, teach_slow, _, _, _, teach_first = backward_ffn(
        teach_kept, teach, grad_t, teach_gain
    )
    teach_grads = backward_attention(teach_kept, to_low(teach_first), teach[3], -extra)
    teach_lows = [to_low(item) for item in teach_grads]
    input_grad = first_grad + teach_first
    for item, matrix in zip(lows, stud[0]):
        input_grad = input_grad + dot_nt(item, matrix)
    for item, matrix in zip(teach_lows, teach[0]):
        input_grad = input_grad + dot_nt(item, matrix)

    vectors = [
        jnp.sum(first_grad, axis=0),
        vecs[0],
        jnp.sum(normed_grad * unit_one, axis=0),
        vecs[1],
        jnp.sum(normed_grad, axis=0),
        vecs[2],
        net.place(jnp.sum(grads[0], axis=0).reshape(n_mp, -1)).reshape(-1),
        net.place(jnp.sum(grads[2], axis=0).reshape(n_mp, -1)).reshape(-1),
    ]
    wide_vector = net.place(jnp.sum(pre_grad, axis=0).reshape(n_mp, -1)).reshape(-1, features)
    total = net.sum_all(jnp.concatenate([jnp.stack(vectors), wide_vector], axis=0))
    width = features // n_mp
    units = wide_vector.size // n_mp
    return (
        student_output,
        input_grad,
        qkv_grad,
        lax.dynamic_slice_in_dim(total[6:8], me * width, width, axis=1),
        out_grad,
        up_grad,
        lax.dynamic_slice_in_dim(total[8:].reshape(-1), me * units, units),
        down_grad,
        total[0:2],
        total[2:4],
        total[4:6],
    )


def solution(mesh):
    n_dp, n_mp = mesh.shape["dp"], mesh.shape["mp"]

    def body(*args):
        return per_device(n_dp, n_mp, *args)

    return jax.shard_map(
        body,
        mesh=mesh,
        in_specs=(
            P(("dp", "mp"), None),
            P("dp"),
            P(None, None, "mp"),
            P(None, "mp"),
            P("mp", None),
            P(None, "mp"),
            P("mp"),
            P("mp", None),
            P(),
            P(),
            P(),
            P(None, None, "mp"),
            P(None, "mp"),
            P("mp", None),
            P(None, "mp"),
            P("mp"),
            P("mp", None),
            P(),
            P(),
            P(),
        ),
        out_specs=(
            P(("dp", "mp"), None),
            P(("dp", "mp"), None),
            P(None, None, "mp"),
            P(None, "mp"),
            P("mp", None),
            P(None, "mp"),
            P("mp"),
            P("mp", None),
            P(),
            P(),
            P(),
        ),
        check_vma=False,
    )
```

```python
import math

import jax
import jax.numpy as jnp
from jax import lax
from jax.experimental import pallas as pl
from jax.experimental.pallas import tpu as pltpu
from jax.sharding import PartitionSpec as P

DH = 64
LEN = 128


norm_epsilon = 1e-06
clip_level = 2.5
score_weight = 0.05
masked_fill = -1000000000.0


def to_float(values):
    return values.astype(jnp.float32)


def to_low(values):
    return values.astype(jnp.bfloat16)


def binarize(matrix, axis_index):
    scaling = jnp.mean(jnp.abs(matrix), axis=axis_index, keepdims=True)
    return (scaling * jnp.sign(matrix)).astype(jnp.bfloat16)


def norm_stats(values):
    centred = values - jnp.mean(values, axis=-1, keepdims=True)
    variance = jnp.mean(centred * centred, axis=-1, keepdims=True)
    inverse = lax.rsqrt(variance + norm_epsilon)
    return (centred * inverse, inverse)


def norm_back(grad, unit, inverse, gain_row):
    scaled = grad * gain_row
    first = jnp.mean(scaled, axis=-1, keepdims=True)
    second = jnp.mean(scaled * unit, axis=-1, keepdims=True)
    return inverse * (scaled - first - unit * second)


def dot(left, right):
    return jnp.dot(left, right, preferred_element_type=jnp.float32)


def dot_nt(left, right):
    return lax.dot_general(left, right, (((1,), (1,)), ((), ())), preferred_element_type=jnp.float32)


def dot_tn(left, right):
    return lax.dot_general(left, right, (((0,), (0,)), ((), ())), preferred_element_type=jnp.float32)


class Cube:
    def __init__(self, n_dp):
        self.n_dp = n_dp
        self.axes = ("dp", "mp")

    def flip(self, values, bits):
        pairs = [
            (z * 8 + m, z * 8 + (m ^ bits)) for z in range(self.n_dp) for m in range(8)
        ]
        return lax.ppermute(values, self.axes, pairs)

    def flip_dp(self, values, bits):
        pairs = [
            (z * 8 + m, (z ^ bits) * 8 + m) for z in range(self.n_dp) for m in range(8)
        ]
        return lax.ppermute(values, self.axes, pairs)

    def gather(self, block):
        half = block.shape[0] // 2
        along_x = self.flip(block, 2)
        along_y = self.flip(block, 4)
        across = jnp.concatenate(
            [self.flip(along_y[:half], 2), self.flip(along_x[half:], 4)], axis=0
        )
        same = [block, along_x, along_y, across]
        other = [self.flip(item, 1) for item in same]
        return [item for pair in zip(same, other) for item in pair]

    def scatter(self, blocks):
        half = blocks[0].shape[0] // 2
        own, to_x, to_y, to_far = [
            to_float(blocks[k]) + to_float(self.flip(blocks[k + 1], 1)) for k in (0, 2, 4, 6)
        ]
        far = to_low(to_far)
        via_x = to_float(self.flip(far[:half], 2))
        via_y = to_float(self.flip(far[half:], 4))
        to_y = to_low(jnp.concatenate([to_y[:half] + via_x, to_y[half:]], axis=0))
        to_x = to_low(jnp.concatenate([to_x[:half], to_x[half:] + via_y], axis=0))
        return own + to_float(self.flip(to_x, 2)) + to_float(self.flip(to_y, 4))

    def sum_dp(self, values):
        half = values.shape[0] // 2
        odd = lax.axis_index("dp") % 2
        low = to_low(values)
        sent = lax.dynamic_slice_in_dim(low, (1 - odd) * half, half)
        kept = lax.dynamic_slice_in_dim(values, odd * half, half)
        kept = kept + to_float(self.flip_dp(sent, 1))
        kept_low = to_low(kept)
        kept = to_low(kept + to_float(self.flip_dp(kept_low, 2)))
        other = self.flip_dp(kept, 1)
        return to_float(
            jnp.concatenate(
                [jnp.where(odd == 0, kept, other), jnp.where(odd == 0, other, kept)], axis=0
            )
        )

    def sum_all(self, values):
        for bits in (1, 2, 4):
            values = values + self.flip(values, bits)
        for bits in (1, 2):
            values = values + self.flip_dp(values, bits)
        return values

    def place(self, values):
        me = lax.axis_index("mp")
        for bit in range(3):
            shape = values.shape
            split = values.reshape((8 >> (bit + 1), 2, 1 << bit) + shape[1:])
            flipped = split[:, ::-1]
            values = jnp.where((me >> bit) % 2 == 1, flipped, split).reshape(shape)
        return values


class Plain:
    def __init__(self, n_mp):
        self.n_mp = n_mp

    def gather(self, block):
        every = lax.all_gather(block, "mp", axis=0)
        return [every[k] for k in range(self.n_mp)]

    def scatter(self, blocks):
        return to_float(
            lax.psum_scatter(jnp.stack(blocks), "mp", scatter_dimension=0, tiled=False)
        )

    def sum_dp(self, values):
        return to_float(lax.psum(to_low(values), "dp"))

    def sum_all(self, values):
        return lax.psum(values, ("dp", "mp"))

    def place(self, values):
        return values


def plain_act(pre):
    gate = 0.5 * (1.0 + lax.erf(pre * math.sqrt(0.5)))
    slope = gate + pre * jnp.exp(-0.5 * pre * pre) * (1.0 / math.sqrt(2.0 * math.pi))
    return (pre * gate, slope)


def clipped_act(pre):
    value, slope = plain_act(pre)
    bent = jnp.tanh(value * (1.0 / clip_level))
    return (clip_level * bent, slope * (1.0 - bent * bent))


def gather_layer(net, qkv, qv_bias, out, up, up_bias, down):
    width = qkv.shape[2]
    units = up.shape[1]
    features = qkv.shape[0]
    extra = jnp.zeros((16, features), jnp.bfloat16)
    extra = extra.at[0, :width].set(qv_bias[0]).at[1, :width].set(qv_bias[1])
    extra = extra.at[2, :units].set(up_bias)
    qkv_parts = net.gather(qkv.transpose(1, 0, 2).reshape(3 * features, width))
    out_parts = net.gather(jnp.concatenate([out, extra], axis=0))
    up_parts = net.gather(up)
    down_parts = net.gather(down)
    count = len(qkv_parts)
    qkv_full = jnp.concatenate(
        [part.reshape(3, features, width) for part in qkv_parts], axis=2
    )
    out_full = jnp.concatenate([part[:width] for part in out_parts], axis=0)
    q_bias = jnp.concatenate([part[width, :width] for part in out_parts])
    v_bias = jnp.concatenate([part[width + 1, :width] for part in out_parts])
    up_b = jnp.concatenate([part[width + 2, :units] for part in out_parts])
    up_full = jnp.concatenate(up_parts, axis=1)
    down_full = jnp.concatenate(down_parts, axis=0)
    return (qkv_full, to_float(q_bias), to_float(v_bias), out_full, up_full, to_float(up_b), down_full)


def forward(tokens, weights, out_bias, gain, shift, activation, key_valid):
    qkv, q_bias, v_bias, out, up, up_bias, down = weights
    rows, features = tokens.shape
    pairs = rows // LEN
    shape = (pairs, LEN, features // DH, DH)
    query = to_low(dot(tokens, qkv[0]) + q_bias).reshape(shape)
    key = to_low(dot(tokens, qkv[1])).reshape(shape)
    value = to_low(dot(tokens, qkv[2]) + v_bias).reshape(shape)
    scores = jnp.einsum("bqhe,bkhe->bhqk", query, key, preferred_element_type=jnp.float32) * (
        1.0 / math.sqrt(DH)
    )
    masked = jnp.where(key_valid[:, None, None, :], scores, masked_fill)
    log_norm = jax.nn.logsumexp(masked, axis=-1, keepdims=True)
    attention = jnp.exp(masked - log_norm)
    context = jnp.einsum(
        "bhqk,bkhe->bqhe", to_low(attention), value, preferred_element_type=jnp.float32
    )
    context = to_low(context).reshape(rows, features)
    first = to_float(tokens) + dot(context, out) + out_bias[0]
    unit_one, inverse_one = norm_stats(first)
    normed = unit_one * gain[0] + shift[0]
    normed_low = to_low(normed)
    hidden, slope = activation(dot(normed_low, up) + up_bias)
    hidden = to_low(hidden)
    second = normed + dot(hidden, down) + out_bias[1]
    unit_two, inverse_two = norm_stats(second)
    final = unit_two * gain[1] + shift[1]
    kept = (query, key, value, scores, attention, context, unit_one, inverse_one, normed_low, hidden,
            to_low(slope), unit_two, inverse_two)
    return (final, kept)


def backward_ffn(kept, weights, second_grad, gain):
    qkv, q_bias, v_bias, out, up, up_bias, down = weights
    (query, key, value, scores, attention, context, unit_one, inverse_one, normed_low, hidden,
     slope, unit_two, inverse_two) = kept
    second_low = to_low(second_grad)
    pre_grad = dot_nt(second_low, down) * slope
    pre_low = to_low(pre_grad)
    normed_grad = second_grad + dot_nt(pre_low, up)
    first_grad = norm_back(normed_grad, unit_one, inverse_one, gain[0])
    return (second_grad, second_low, pre_grad, pre_low, normed_grad, first_grad)


def backward_attention(kept, first_low, out, extra):
    query, key, value, scores, attention = kept[:5]
    rows = first_low.shape[0]
    factor = 1.0 / math.sqrt(DH)
    context_grad = to_low(dot_nt(first_low, out)).reshape(query.shape)
    attention_grad = jnp.einsum(
        "bqhe,bkhe->bhqk", context_grad, value, preferred_element_type=jnp.float32
    )
    value_grad = jnp.einsum(
        "bhqk,bqhe->bkhe", to_low(attention), context_grad, preferred_element_type=jnp.float32
    )
    inner = jnp.sum(attention * attention_grad, axis=-1, keepdims=True)
    score_low = to_low(attention * (attention_grad - inner) + extra)
    query_grad = factor * jnp.einsum(
        "bhqk,bkhe->bqhe", score_low, key, preferred_element_type=jnp.float32
    )
    key_grad = factor * jnp.einsum(
        "bhqk,bqhe->bkhe", score_low, query, preferred_element_type=jnp.float32
    )
    return [item.reshape(rows, -1) for item in (query_grad, key_grad, value_grad)]


MESH = pl.DeviceIdType.MESH
SLOTS = 8
PACKS = 6
ATT_ROWS = 528
FFN_ROWS = 512
HALF_UNITS = 256
COLS = 128
THIRD = 176


def flipped(me, bits):
    return me + bits - 2 * bits * lax.rem(lax.div(me, bits), 2)


def pack_rows(pack):
    return ATT_ROWS if pack < 2 else FFN_ROWS


def masked_probs(scores, length):
    rows = scores.shape[0]
    position = lax.broadcasted_iota(jnp.int32, (rows, LEN), 1)
    parts = []
    for head in range(2):
        part = jnp.where(position < length, scores[:, head * LEN : (head + 1) * LEN], masked_fill)
        part = jnp.exp(part - jnp.max(part, axis=1, keepdims=True))
        parts.append(part / jnp.sum(part, axis=1, keepdims=True))
    return jnp.concatenate(parts, axis=1)


def two_heads(rows):
    first = lax.broadcasted_iota(jnp.int32, rows.shape, 1) < DH
    zero = jnp.zeros_like(rows)
    return jnp.concatenate([jnp.where(first, rows, zero), jnp.where(first, zero, rows)], axis=0)


def norm_block(values):
    centred = values - jnp.mean(values, axis=1, keepdims=True)
    inverse = lax.rsqrt(jnp.mean(centred * centred, axis=1, keepdims=True) + norm_epsilon)
    return (centred * inverse, inverse)


def forward_kernel(
    lengths,
    x_ref,
    t_weights,
    t_small,
    s_weights,
    s_small,
    gathered,
    kept,
    grad_t,
    grad_s,
    final_low,
    vectors,
    scratch,
    raw_t,
    raw_s,
    mine_att,
    mine_ffn,
    wide,
    total,
    normed,
    low_t,
    context_t,
    bias_rows,
    final_t,
    unit_two,
    inverse_two,
    send,
    recv,
    load,
    fetch,
    save,
):
    t_qv_bias, t_up_bias, t_bias, t_gain, t_shift = t_small
    s_qv_bias, s_up_bias, s_bias, s_gain, s_shift = s_small
    qkv_t, qkv_s, context_s, slope_t, slope_s, hidden_s, unit_t, inverse_t, unit_s, inverse_s, low_s = scratch
    saved = []

    def put(name, index=None):
        src, dst = scratch[name], kept[name]
        if index is not None:
            src, dst = src.at[index], dst.at[index]
        saved.append(pltpu.make_async_copy(src, dst, save.at[len(saved)]))
        saved[-1].start()

    me = lax.axis_index("mp")
    z = lax.axis_index("dp")
    peers = {bits: {"mp": flipped(me, bits)} for bits in (1, 2, 4)}
    peers["z"] = {"dp": flipped(z, 1)}
    upper = lax.rem(z, 2)
    rows = x_ref.shape[0]
    pairs = rows // LEN

    barrier = pltpu.get_barrier_semaphore()
    for peer in peers.values():
        pl.semaphore_signal(barrier, inc=1, device_id=peer, device_id_type=MESH)
    pl.semaphore_wait(barrier, len(peers))

    fetched = []
    for weights, raw, direct in ((t_weights, raw_t, True), (s_weights, raw_s, False)):
        qkv, out, up, down = weights
        moves = [(qkv, raw[0]), (up, raw[1])]
        if direct:
            moves.append((out, mine_att.at[0, pl.ds(3 * COLS, COLS)]))
            moves += [
                (down.at[pl.ds(h * HALF_UNITS, HALF_UNITS)], mine_ffn.at[h, pl.ds(HALF_UNITS, HALF_UNITS)])
                for h in range(2)
            ]
        else:
            moves += [(out, raw[2]), (down, raw[3])]
        for src, dst in moves:
            fetched.append(pltpu.make_async_copy(src, dst, fetch.at[len(fetched)]))
            fetched[-1].start()

    def signed(values, axis):
        scale = jnp.mean(jnp.abs(values), axis=axis, keepdims=True)
        return to_low(jnp.where(values > 0, scale, jnp.where(values < 0, -scale, 0.0)))

    def bias_block(qv_bias, up_bias):
        line = jnp.concatenate(
            [
                to_float(qv_bias[0:1]),
                to_float(qv_bias[1:2]),
                to_float(up_bias[...]),
                jnp.zeros((1, x_ref.shape[1] - 2 * COLS - 2 * HALF_UNITS), jnp.float32),
            ],
            axis=1,
        )
        row = lax.broadcasted_iota(jnp.int32, (16, line.shape[1]), 0)
        return to_low(jnp.where(row == 0, jnp.broadcast_to(line, row.shape), 0.0))

    def own_copy(pack):
        return pltpu.make_async_copy(source(pack), block(pack, 0), fetch.at[9 + pack])

    def prepare(pack):
        if pack == 0:
            fetched[0].wait()
            for i in range(3):
                mine_att[0, i * COLS : (i + 1) * COLS] = raw_t[0][i].T
            mine_att[0, 4 * COLS : 4 * COLS + 16] = bias_block(t_qv_bias, t_up_bias)
            fetched[2].wait()
        elif pack == 1:
            fetched[5].wait()
            for i in range(3):
                mine_att[1, i * COLS : (i + 1) * COLS] = signed(raw_s[0][i], 0).T
            mine_att[1, 4 * COLS : 4 * COLS + 16] = bias_block(s_qv_bias, s_up_bias)
            fetched[7].wait()
            mine_att[1, 3 * COLS : 4 * COLS] = signed(raw_s[2][...], 1)
        else:
            layer, half = divmod(pack - 2, 2)
            here = slice(half * HALF_UNITS, (half + 1) * HALF_UNITS)
            if half == 0:
                fetched[(1, 6)[layer]].wait()
            if layer == 0:
                mine_ffn[half, 0:HALF_UNITS] = raw_t[1][:, here].T
                fetched[3 + half].wait()
            else:
                mine_ffn[2 + half, 0:HALF_UNITS] = signed(raw_s[1][:, here], 0).T
                if half == 0:
                    fetched[8].wait()
                mine_ffn[2 + half, HALF_UNITS : 2 * HALF_UNITS] = signed(raw_s[3][here], 1)
        own_copy(pack).start()

    def source(pack):
        return mine_att.at[pack] if pack < 2 else mine_ffn.at[pack - 2]

    def span(pack, start, count):
        return pl.ds(pl.multiple_of(start, 16), count)

    def block(pack, slot):
        return gathered.at[pack, slot, pl.ds(0, pack_rows(pack))]

    def remote(pack, kind):
        rest = pack_rows(pack) - THIRD
        low = upper * THIRD
        if kind == 0 or kind == 1:
            here = span(pack, low, rest)
            src, dst = source(pack).at[here], gathered.at[pack, 2 + 2 * kind, here]
            peer = peers[2 + 2 * kind]
        elif kind == 2:
            here = span(pack, low, THIRD)
            src, dst, peer = gathered.at[pack, 4, here], gathered.at[pack, 6, here], peers[2]
        elif kind == 3:
            here = span(pack, low + THIRD, rest - THIRD)
            src, dst, peer = gathered.at[pack, 2, here], gathered.at[pack, 6, here], peers[4]
        elif kind == 4:
            src, dst, peer = source(pack), block(pack, 1), peers[1]
        elif kind < 8:
            slot = 2 * (kind - 4)
            src, dst, peer = block(pack, slot), block(pack, slot + 1), peers[1]
        else:
            here = span(pack, upper * rest, THIRD)
            slot = 2 * (kind - 7)
            src, dst, peer = gathered.at[pack, slot, here], gathered.at[pack, slot, here], peers["z"]
        return pltpu.make_async_remote_copy(
            src_ref=src,
            dst_ref=dst,
            send_sem=send.at[pack, kind],
            recv_sem=recv.at[pack, kind],
            device_id=peer,
            device_id_type=MESH,
        )

    def first_sends(pack):
        for kind in (0, 1, 4):
            remote(pack, kind).start()

    def second_sends(pack):
        remote(pack, 0).wait_recv()
        remote(pack, 3).start()
        remote(pack, 8).start()
        remote(pack, 1).wait_recv()
        remote(pack, 2).start()
        remote(pack, 9).start()

    def plane_swap(pack):
        remote(pack, 8).wait_recv()
        remote(pack, 5).start()
        remote(pack, 9).wait_recv()
        remote(pack, 6).start()

    def far_sends(pack):
        remote(pack, 2).wait_recv()
        remote(pack, 3).wait_recv()
        remote(pack, 10).start()

    def far_swap(pack):
        remote(pack, 10).wait_recv()
        remote(pack, 7).start()

    def load_pair(pack, pair, place):
        here = pl.ds(0, pack_rows(pack))
        return pltpu.make_async_copy(
            gathered.at[pack, pl.ds(2 * pair, 2), here], wide.at[place, :, here], load.at[place]
        )

    def over_pairs(pack, chosen, body):
        def begin(pair):
            if pair == 0:
                own_copy(pack).wait()
            remote(pack, 4 + pair).wait_recv()
            load_pair(pack, pair, pair % 2).start()

        begin(chosen[0])
        for pair in chosen:
            load_pair(pack, pair, pair % 2).wait()
            if pair != chosen[-1]:
                begin(pair + 1)
            body(pair, pair % 2)

    def attention(pack, chosen, qkv_ref, context_ref):
        if chosen[0] == 0:
            total[...] = jnp.zeros_like(total)

        def body(pair, place):
            weights = wide[place, :, 0:384].reshape(768, -1)
            projected = dot_nt(x_ref[...], weights)
            for side in range(2):
                slot = 2 * pair + side
                bias = wide[place, side, 512:528]
                bias_rows[pack, slot] = bias
                bias = to_float(bias[0:1])
                part = projected[:, side * 384 : side * 384 + 384]
                query = to_low(part[:, :COLS] + bias[:, :COLS])
                key = to_low(part[:, COLS : 2 * COLS])
                value = to_low(part[:, 2 * COLS :] + bias[:, COLS : 2 * COLS])
                qkv_ref[slot, :, 0:COLS] = query
                qkv_ref[slot, :, COLS : 2 * COLS] = key
                qkv_ref[slot, :, 2 * COLS : 3 * COLS] = value
                for number in range(pairs):
                    here = slice(number * LEN, (number + 1) * LEN)
                    scores = dot_nt(query[here], two_heads(key[here])) * (1.0 / math.sqrt(DH))
                    probs = masked_probs(scores, lengths[me * pairs + number])
                    part_context = dot(to_low(probs), two_heads(value[here]))
                    context_ref[pair, here, side * COLS : (side + 1) * COLS] = to_low(part_context)
            put(pack, pl.ds(2 * pair, 2))
            if pack == 1:
                put(2, pair)
            total[...] += dot(context_ref[pair], wide[place, :, 384:512].reshape(256, -1))

        over_pairs(pack, chosen, body)

    def first_norm(bias_ref, gain_ref, shift_ref, unit_ref, inverse_ref, index, low_ref):
        @pl.loop(0, rows // 64)
        def _(step):
            here = pl.ds(step * 64, 64)
            values = to_float(x_ref[here]) + total[here] + to_float(bias_ref[0:1])
            unit, inverse = norm_block(values)
            unit_ref[here] = unit
            inverse_ref[here] = inverse
            values = unit * to_float(gain_ref[0:1]) + to_float(shift_ref[0:1])
            normed[index, here] = values
            low_ref[here] = to_low(values)

    def feed_forward(pack, chosen, low_ref, activation, hidden_ref, slope_ref):
        layer, half = divmod(pack - 2, 2)

        def body(pair, place):
            up = wide[place, :, 0:HALF_UNITS].reshape(2 * HALF_UNITS, -1)
            down = wide[place, :, HALF_UNITS : 2 * HALF_UNITS].reshape(2 * HALF_UNITS, -1)
            start = 2 * COLS + half * HALF_UNITS
            bias = jnp.concatenate(
                [
                    to_float(bias_rows[layer, 2 * pair + side, 0:1, start : start + HALF_UNITS])
                    for side in range(2)
                ],
                axis=1,
            )
            hidden, slope = activation(dot_nt(low_ref[...], up) + bias)
            hidden = to_low(hidden)
            slope_ref[half, pair] = to_low(slope)
            put(3 + layer, (half, pair))
            if hidden_ref is not None:
                hidden_ref[half, pair] = hidden
                put(5, (half, pair))
            total[...] += dot(hidden, down)

        if half == 0 and chosen[0] == 0:
            total[...] = jnp.zeros_like(total)
        over_pairs(pack, chosen, body)

    def step_teacher_end():
        @pl.loop(0, rows // 64)
        def _(step):
            here = pl.ds(step * 64, 64)
            unit, inverse = norm_block(normed[0, here] + total[here] + to_float(t_bias[1:2]))
            unit_two[here] = unit
            inverse_two[here] = inverse
            final_t[here] = unit * to_float(t_gain[1:2]) + to_float(t_shift[1:2])

    def step_student_end():
        vectors[...] = jnp.zeros_like(vectors)

        @pl.loop(0, rows // 64)
        def _(step):
            here = pl.ds(step * 64, 64)
            unit, inverse = norm_block(normed[1, here] + total[here] + to_float(s_bias[1:2]))
            gain = to_float(s_gain[1:2])
            final = unit * gain + to_float(s_shift[1:2])
            final_low[here] = to_low(final)
            position = lax.broadcasted_iota(jnp.int32, (64, 1), 0) + lax.rem(step, 2) * 64
            valid = position < lengths[me * pairs + lax.div(step, 2)]
            grad = jnp.where(valid, final - final_t[here], 0.0)
            back = norm_back(grad, unit, inverse, gain)
            grad_s[here] = back
            grad_t[here] = norm_back(
                -grad, unit_two[here], inverse_two[here], to_float(t_gain[1:2])
            )
            vectors[0:1] += jnp.sum(back, axis=0, keepdims=True)
            vectors[1:2] += jnp.sum(grad * unit, axis=0, keepdims=True)
            vectors[2:3] += jnp.sum(grad, axis=0, keepdims=True)

    def use(pack, chosen):
        if pack == 0:
            attention(0, chosen, qkv_t, context_t)
        elif pack == 1:
            attention(1, chosen, qkv_s, context_s)
        elif pack < 4:
            feed_forward(pack, chosen, low_t, plain_act, None, slope_t)
        else:
            feed_forward(pack, chosen, low_s, clipped_act, hidden_s, slope_s)

    def end(pack):
        if pack == 0:
            first_norm(t_bias, t_gain, t_shift, unit_t, inverse_t, 0, low_t)
            put(6)
            put(7)
        elif pack == 1:
            first_norm(s_bias, s_gain, s_shift, unit_s, inverse_s, 1, low_s)
            for name in (8, 9, 10):
                put(name)
        elif pack == 3:
            step_teacher_end()

    near, far = (0, 1, 2), (3,)
    prepare(0)
    first_sends(0)
    prepare(1)
    first_sends(1)
    for pack in range(2, PACKS):
        prepare(pack)
    for pack in range(PACKS):
        second_sends(pack)
        if pack + 2 < PACKS:
            first_sends(pack + 2)
        if pack >= 2:
            far_swap(pack - 2)
            use(pack - 2, far)
            end(pack - 2)
        if pack >= 1:
            plane_swap(pack - 1)
            use(pack - 1, near)
            far_sends(pack - 1)
    last = PACKS - 1
    far_sends(last)
    plane_swap(last)
    use(last, near)
    far_swap(last - 1)
    use(last - 1, far)
    far_swap(last)
    use(last, far)
    step_student_end()
    for pack in range(PACKS):
        for kind in range(11):
            remote(pack, kind).wait_send()
    for copy in saved:
        copy.wait()


def forward_both(lengths, tokens, teacher, student):
    rows, features = tokens.shape
    low, full = jnp.bfloat16, jnp.float32
    vmem = pl.BlockSpec(memory_space=pltpu.VMEM)
    hbm = pl.BlockSpec(memory_space=pl.ANY)
    dma = pltpu.SemaphoreType.DMA
    act = (2, 4, rows, 2 * HALF_UNITS)
    kept = [
        ((SLOTS, rows, 3 * COLS), low),
        ((SLOTS, rows, 3 * COLS), low),
        ((4, rows, 2 * COLS), low),
        (act, low),
        (act, low),
        (act, low),
        ((rows, features), full),
        ((rows, 1), full),
        ((rows, features), full),
        ((rows, 1), full),
        ((rows, features), low),
    ]
    shapes = [jax.ShapeDtypeStruct(shape, kind) for shape, kind in kept]
    ends = [((rows, features), full), ((rows, features), full), ((rows, features), low), ((8, features), full)]
    qkv, out, up, down = teacher[0]
    return pl.pallas_call(
        forward_kernel,
        out_shape=[
            jax.ShapeDtypeStruct((PACKS, SLOTS, ATT_ROWS, features), low),
            shapes,
            *[jax.ShapeDtypeStruct(shape, kind) for shape, kind in ends],
        ],
        in_specs=[pl.BlockSpec(memory_space=pltpu.SMEM), vmem] + [[hbm] * 4, [vmem] * 5] * 2,
        out_specs=[hbm, [hbm] * len(kept)] + [vmem] * len(ends),
        scratch_shapes=[
            [pltpu.VMEM(shape, kind) for shape, kind in kept],
            [pltpu.VMEM(qkv.shape, low), pltpu.VMEM(up.shape, low)],
            [pltpu.VMEM(item.shape, full) for item in (qkv, up, out, down)],
            pltpu.VMEM((2, ATT_ROWS, features), low),
            pltpu.VMEM((4, FFN_ROWS, features), low),
            pltpu.VMEM((2, 2, ATT_ROWS, features), low),
            pltpu.VMEM((rows, features), full),
            pltpu.VMEM((2, rows, features), full),
            pltpu.VMEM((rows, features), low),
            pltpu.VMEM((4, rows, 2 * COLS), low),
            pltpu.VMEM((2, SLOTS, 16, features), low),
            pltpu.VMEM((rows, features), full),
            pltpu.VMEM((rows, features), full),
            pltpu.VMEM((rows, 1), full),
            dma((PACKS, 11)),
            dma((PACKS, 11)),
            dma((2,)),
            dma((9 + PACKS,)),
            dma((48,)),
        ],
        compiler_params=pltpu.CompilerParams(
            collective_id=0, has_side_effects=True, vmem_limit_bytes=62 * 1024 * 1024
        ),
        name="forward_both",
    )(lengths, tokens, *teacher, *student)


CHUNKS = 3
PARTS = 4
ORDER = (3, 1, 2, 0)


def backward_kernel(
    lengths,
    x_ref,
    gathered,
    qkv_t,
    qkv_s,
    context_s,
    slope_t,
    slope_s,
    hidden_s,
    unit_t,
    inverse_t,
    unit_s,
    inverse_s,
    low_s,
    grad_t,
    grad_s,
    vectors,
    t_gain,
    s_gain,
    grad_in,
    sums_out,
    vec,
    wide,
    hidden_buf,
    slope_buf,
    qkv_s_buf,
    qkv_t_buf,
    context_buf,
    extra_buf,
    unit_buf,
    inverse_buf,
    grad_buf,
    total,
    low_y,
    low_z,
    low_a,
    proj,
    sums,
    even,
    odd,
    from_core,
    from_far,
    from_x,
    from_y,
    from_z,
    from_vec,
    load,
    state_sem,
    odd_send,
    odd_recv,
    free,
    far_send,
    far_recv,
    x_send,
    x_recv,
    y_send,
    y_recv,
    in_send,
    in_recv,
    mid_send,
    mid_recv,
    out_send,
    out_recv,
    vec_send,
    vec_recv,
    done,
):
    me = lax.axis_index("mp")
    z = lax.axis_index("dp")
    rows = x_ref.shape[0]
    pairs = rows // LEN
    core, along_x, along_y = ({"mp": flipped(me, bits)} for bits in (1, 2, 4))
    z_outer, z_inner = {"dp": flipped(z, 1)}, {"dp": 3 - z}
    z_two = {"dp": flipped(z, 2)}
    inner = jnp.logical_or(z == 1, z == 2)
    outer = jnp.logical_or(z == 0, z == 3)

    barrier = pltpu.get_barrier_semaphore()
    greeted = (core, along_x, along_y, z_outer, z_inner, z_two)
    for peer in greeted:
        pl.semaphore_signal(barrier, inc=1, device_id=peer, device_id_type=MESH)
    pl.semaphore_wait(barrier, len(greeted))

    def remote(src, dst, send, recv, peer):
        return pltpu.make_async_remote_copy(
            src_ref=src, dst_ref=dst, send_sem=send, recv_sem=recv, device_id=peer, device_id_type=MESH
        )

    steps = [("fs", 4 + half, pair) for half in range(2) for pair in ORDER]
    steps += [("as", 1, pair) for pair in ORDER]
    steps += [("ft", 2 + half, pair) for half in range(2) for pair in range(4)]
    steps += [("at", 0, pair) for pair in range(4)]

    def loads(number):
        kind, pack, pair = steps[number]
        place = number % 2
        two = pl.ds(2 * pair, 2)
        here = pl.ds(0, FFN_ROWS)
        moves = [(gathered.at[pack, two, here], wide.at[place])]
        if kind == "fs":
            moves.append((hidden_s.at[pack - 4, pair], hidden_buf.at[place]))
            moves.append((slope_s.at[pack - 4, pair], slope_buf.at[place]))
        elif kind == "ft":
            moves.append((slope_t.at[pack - 2, pair], slope_buf.at[place]))
        else:
            moves.append((qkv_t.at[two], qkv_t_buf.at[place]))
            if kind == "as":
                moves.append((qkv_s.at[two], qkv_s_buf.at[place]))
                moves.append((context_s.at[pair], context_buf.at[place]))
        return [
            pltpu.make_async_copy(src, dst, load.at[place, index])
            for index, (src, dst) in enumerate(moves)
        ]

    def state(layer):
        unit, inverse, grad = ((unit_t, inverse_t, grad_t), (unit_s, inverse_s, grad_s))[layer]
        moves = [(grad, grad_buf), (unit, unit_buf), (inverse, inverse_buf)]
        return [
            pltpu.make_async_copy(src, dst, state_sem.at[index])
            for index, (src, dst) in enumerate(moves)
        ]

    def slot_row(slot):
        row = me
        for bits in (1, 2, 4):
            if slot & bits:
                row = flipped(row, bits)
        return row

    def odd_copy(number):
        pair = steps[number][2]
        return remote(
            odd.at[number % 2], from_core.at[pair], odd_send.at[number % 2], odd_recv.at[pair], core
        )

    def keep(chunk, pair):
        return sums.at[chunk] if pair == 0 else even.at[chunk, pair - 1]

    def give(number, pieces):
        pair = steps[number][2]
        chunk = number // 4
        if number >= 2:
            odd_copy(number - 2).wait_send()
        for start, values in pieces:
            count = values.shape[0] // 2
            keep(chunk, pair)[start : start + count] = to_low(values[:count])
            odd[number % 2, start : start + count] = to_low(values[count:])
        if chunk:
            pl.semaphore_wait(free.at[pair], 1)
        odd_copy(number).start()

    def add_rows(target, others, start, count):
        @pl.loop(0, count // 64)
        def _(step):
            here = pl.ds(start + step * 64, 64)
            value = to_float(target[here])
            for other in others:
                value = value + to_float(other[here])
            target[here] = to_low(value)

    def combine(chunk, pair):
        number = chunk * 4 + ORDER.index(pair)
        odd_copy(number).wait_recv()
        add_rows(keep(chunk, pair), [from_core.at[pair]], 0, FFN_ROWS)
        if chunk < CHUNKS - 1:
            pl.semaphore_signal(free.at[pair], inc=1, device_id=core, device_id_type=MESH)
        if pair == 3:
            far_copy(chunk, 0).start()
            far_copy(chunk, 1).start()

    def far_copy(chunk, way):
        part = pl.ds(way * 256, 256)
        return remote(
            even.at[chunk, 2, part],
            from_far.at[chunk, part],
            far_send.at[chunk, way],
            far_recv.at[chunk, way],
            (along_x, along_y)[way],
        )

    part_rows = FFN_ROWS // PARTS

    def plane_copies(chunk, part):
        here = pl.ds(part * part_rows, part_rows)
        return [
            remote(even.at[chunk, 0, here], from_x.at[chunk, here], x_send.at[chunk, part], x_recv.at[chunk, part], along_x),
            remote(even.at[chunk, 1, here], from_y.at[chunk, here], y_send.at[chunk, part], y_recv.at[chunk, part], along_y),
        ]

    def fold(chunk):
        far_copy(chunk, 0).wait_recv()
        add_rows(keep(chunk, 2), [from_far.at[chunk]], 0, 256)
        far_copy(chunk, 1).wait_recv()
        add_rows(keep(chunk, 1), [from_far.at[chunk]], 256, 256)
        for part in range(PARTS):
            for copy in plane_copies(chunk, part):
                copy.start()

    def z_copy(chunk, part, kind):
        here = pl.ds(part * part_rows, part_rows)
        own, first, second = sums.at[chunk, here], from_z.at[chunk, 0, here], from_z.at[chunk, 1, here]
        if kind == 0:
            return remote(own, first, in_send.at[chunk, part], in_recv.at[chunk, part], z_outer)
        if kind == 1:
            return remote(own, second, mid_send.at[chunk, part], mid_recv.at[chunk, part], z_inner)
        return remote(first, first, out_send.at[chunk, part], out_recv.at[chunk, part], z_outer)

    def own_part(chunk, part):
        for copy in plane_copies(chunk, part):
            copy.wait_recv()
        add_rows(sums.at[chunk], [from_x.at[chunk], from_y.at[chunk]], part * part_rows, part_rows)

        @pl.when(outer)
        def _():
            z_copy(chunk, part, 0).start()

    def mid_part(chunk, part):
        @pl.when(inner)
        def _():
            z_copy(chunk, part, 0).wait_recv()
            add_rows(sums.at[chunk], [from_z.at[chunk, 0]], part * part_rows, part_rows)
            z_copy(chunk, part, 1).start()

    def end_part(chunk, part):
        @pl.when(inner)
        def _():
            z_copy(chunk, part, 1).wait_recv()

            @pl.loop(0, part_rows // 64)
            def _(step):
                here = pl.ds(part * part_rows + step * 64, 64)
                value = to_float(sums[chunk, here]) + to_float(from_z[chunk, 1, here])
                from_z[chunk, 0, here] = to_low(value)

            z_copy(chunk, part, 2).start()

    def store_copy(chunk):
        return pltpu.make_async_copy(from_z.at[chunk, 0], sums_out.at[chunk], done.at[chunk])

    def finish(chunk):
        @pl.when(outer)
        def _():
            for part in range(PARTS):
                z_copy(chunk, part, 2).wait_recv()

        store_copy(chunk).start()

    ways = (core, along_x, along_y, z_outer, z_two)

    def vec_copy(way):
        return remote(vec, from_vec.at[way], vec_send.at[way], vec_recv.at[way], ways[way])

    def vec_add(way):
        vec_copy(way).wait_send()
        vec_copy(way).wait_recv()
        vec[...] += from_vec[way]
        if way + 1 < len(ways):
            vec_copy(way + 1).start()

    def put_bias(pair, start, values):
        count = values.shape[1] // 2
        for side in range(2):
            line = lax.broadcasted_iota(jnp.int32, (SLOTS, count), 0)
            part = jnp.broadcast_to(values[:, side * count : (side + 1) * count], (SLOTS, count))
            part = jnp.where(line == slot_row(2 * pair + side), part, 0.0)
            vec[0:SLOTS, start : start + count] += part

    def ffn_step(number):
        kind, pack, pair = steps[number]
        place = number % 2
        up = wide[place, :, 0:HALF_UNITS].reshape(2 * HALF_UNITS, -1)
        down = wide[place, :, HALF_UNITS : 2 * HALF_UNITS].reshape(2 * HALF_UNITS, -1)
        back = dot_nt(low_z[...], down) * to_float(slope_buf[place])
        back_low = to_low(back)
        total[...] += dot(back_low, up)
        if kind == "fs":
            put_bias(pair, 2 * COLS + (pack - 4) * HALF_UNITS, jnp.sum(back, axis=0, keepdims=True))
            up_grad = dot_tn(back_low, low_y[...])
            down_grad = dot_tn(hidden_buf[place], low_z[...])
            give(number, [(0, up_grad), (HALF_UNITS, down_grad)])

    def pick(both):
        first = lax.broadcasted_iota(jnp.int32, (LEN, COLS), 1) < DH
        return jnp.where(first, both[:LEN], both[LEN:])

    def attention_step(number):
        kind, pack, pair = steps[number]
        place = number % 2
        student = kind == "as"
        factor = 1.0 / math.sqrt(DH)
        qkv = qkv_s_buf if student else qkv_t_buf
        out = wide[place, :, 384:512].reshape(2 * COLS, -1)
        context_back = to_low(dot_nt(low_a[...], out))
        query_sums, value_sums = [], []
        for side in range(2):
            query_sum = jnp.zeros((1, COLS), jnp.float32)
            value_sum = jnp.zeros((1, COLS), jnp.float32)
            for number_b in range(pairs):
                here = slice(number_b * LEN, (number_b + 1) * LEN)
                length = lengths[me * pairs + number_b]
                query, key, value = [
                    qkv[place, side, here, i * COLS : (i + 1) * COLS] for i in range(3)
                ]
                keys, values = two_heads(key), two_heads(value)
                scores = dot_nt(query, keys) * factor
                probs = masked_probs(scores, length)
                if student:
                    other = dot_nt(
                        qkv_t_buf[place, side, here, 0:COLS],
                        two_heads(qkv_t_buf[place, side, here, COLS : 2 * COLS]),
                    )
                    spot = lax.broadcasted_iota(jnp.int32, scores.shape, 1)
                    spot = jnp.where(spot < LEN, spot, spot - LEN)
                    line = lax.broadcasted_iota(jnp.int32, scores.shape, 0)
                    gap = score_weight * (scores - other * factor)
                    extra = jnp.where(jnp.maximum(spot, line) < length, gap, 0.0)
                    extra_buf[pair, side, number_b] = to_low(extra)
                else:
                    extra = -to_float(extra_buf[pair, side, number_b])
                part = context_back[here, side * COLS : (side + 1) * COLS]
                probs_back = dot_nt(part, values)
                value_back = pick(dot_tn(to_low(probs), part))
                product = probs * probs_back
                inner_sum = jnp.concatenate(
                    [
                        jnp.broadcast_to(
                            jnp.sum(product[:, i * LEN : (i + 1) * LEN], axis=1, keepdims=True), (LEN, LEN)
                        )
                        for i in range(2)
                    ],
                    axis=1,
                )
                score_back = to_low(product - probs * inner_sum + extra)
                query_back = dot(score_back, keys) * factor
                key_back = pick(dot_tn(score_back, query)) * factor
                start = side * 3 * COLS
                proj[here, start : start + COLS] = to_low(query_back)
                proj[here, start + COLS : start + 2 * COLS] = to_low(key_back)
                proj[here, start + 2 * COLS : start + 3 * COLS] = to_low(value_back)
                if student:
                    query_sum += jnp.sum(query_back, axis=0, keepdims=True)
                    value_sum += jnp.sum(value_back, axis=0, keepdims=True)
            query_sums.append(query_sum)
            value_sums.append(value_sum)
        grad_in[...] += dot(proj[...], wide[place, :, 0:384].reshape(768, -1))
        if student:
            put_bias(pair, 0, jnp.concatenate(query_sums, axis=1))
            put_bias(pair, COLS, jnp.concatenate(value_sums, axis=1))
            qkv_grad = dot_tn(proj[...], x_ref[...])
            out_grad = dot_tn(context_buf[place], low_a[...])
            give(number, [(0, qkv_grad), (3 * COLS, out_grad)])

    def lower_grad():
        @pl.loop(0, rows // 64)
        def _(step):
            here = pl.ds(step * 64, 64)
            low_z[here] = to_low(grad_buf[here])

        total[...] = jnp.zeros_like(total)

    def norm_step(student):
        gain_ref = s_gain if student else t_gain

        @pl.loop(0, rows // 64)
        def _(step):
            here = pl.ds(step * 64, 64)
            grad = grad_buf[here] + total[here]
            unit = unit_buf[here]
            back = norm_back(grad, unit, inverse_buf[here], to_float(gain_ref[0:1]))
            low_a[here] = to_low(back)
            if student:
                grad_in[here] = back
                vec[8:9] += jnp.sum(back, axis=0, keepdims=True)
                vec[9:10] += jnp.sum(grad * unit, axis=0, keepdims=True)
                vec[10:11] += jnp.sum(grad, axis=0, keepdims=True)
            else:
                grad_in[here] += back

    hooks = {
        1: [(combine, 0, 3)],
        2: [(combine, 0, 1)],
        3: [(combine, 0, 2)],
        4: [(combine, 0, 0)],
        5: [(combine, 1, 3), (fold, 0)],
        6: [(combine, 1, 1)],
        7: [(combine, 1, 2)],
        8: [(combine, 1, 0)],
        9: [(combine, 2, 3), (fold, 1), (own_part, 0, 0)],
        10: [(combine, 2, 1), (own_part, 0, 1), (mid_part, 0, 0), (own_part, 0, 2)],
        11: [(combine, 2, 2), (own_part, 0, 3), (mid_part, 0, 1), (mid_part, 0, 2), (end_part, 0, 0)],
        12: [(combine, 2, 0)],
        13: [(mid_part, 0, 3), (end_part, 0, 1), (vec_add, 0)],
        15: [(end_part, 0, 2), (vec_add, 1)],
        17: [(end_part, 0, 3), (vec_add, 2)],
        19: [(own_part, 1, 0), (vec_add, 3)],
        20: [(fold, 2), (own_part, 1, 1), (mid_part, 1, 0)],
        21: [(own_part, 1, 2), (mid_part, 1, 1), (end_part, 1, 0), (vec_add, 4)],
        22: [(own_part, 1, 3), (mid_part, 1, 2), (end_part, 1, 1)],
    }

    for copy in state(1):
        copy.start()
    low_copy = pltpu.make_async_copy(low_s, low_y, state_sem.at[3])
    low_copy.start()
    for copy in loads(0):
        copy.start()
    vec[...] = jnp.zeros_like(vec)
    vec[11:14] = vectors[0:3]
    for copy in state(1):
        copy.wait()
    low_copy.wait()
    lower_grad()
    for number, (kind, pack, pair) in enumerate(steps):
        for copy in loads(number):
            copy.wait()
        if number + 1 < len(steps):
            for copy in loads(number + 1):
                copy.start()
        if kind in ("fs", "ft"):
            ffn_step(number)
        else:
            attention_step(number)
        for action, *which in hooks.get(number, ()):
            action(*which)
        if number == 7:
            norm_step(True)
            for copy in state(0):
                copy.start()
        elif number == 11:
            for copy in state(0):
                copy.wait()
            lower_grad()
            vec_copy(0).start()
        elif number == 19:
            norm_step(False)
    finish(0)
    own_part(2, 0)
    mid_part(1, 3)
    end_part(1, 2)
    own_part(2, 1)
    mid_part(2, 0)
    end_part(1, 3)
    for step in range(2, PARTS + 2):
        if step < PARTS:
            own_part(2, step)
        if 1 <= step <= PARTS:
            mid_part(2, step - 1)
        if step >= 2:
            end_part(2, step - 2)
    finish(1)
    finish(2)

    odd_copy(10).wait_send()
    odd_copy(11).wait_send()
    for chunk in range(CHUNKS):
        far_copy(chunk, 0).wait_send()
        far_copy(chunk, 1).wait_send()
        for part in range(PARTS):
            for copy in plane_copies(chunk, part):
                copy.wait_send()

            @pl.when(outer)
            def _():
                z_copy(chunk, part, 0).wait_send()

            @pl.when(inner)
            def _():
                z_copy(chunk, part, 1).wait_send()
                z_copy(chunk, part, 2).wait_send()

        store_copy(chunk).wait()


def backward_both(lengths, tokens, kept, vectors, t_gain, s_gain):
    rows, features = tokens.shape
    low, full = jnp.bfloat16, jnp.float32
    vmem = pl.BlockSpec(memory_space=pltpu.VMEM)
    hbm = pl.BlockSpec(memory_space=pl.ANY)
    dma = pltpu.SemaphoreType.DMA
    block = (FFN_ROWS, features)
    return pl.pallas_call(
        backward_kernel,
        out_shape=[
            jax.ShapeDtypeStruct((rows, features), full),
            jax.ShapeDtypeStruct((CHUNKS,) + block, low),
            jax.ShapeDtypeStruct((16, features), full),
        ],
        in_specs=[pl.BlockSpec(memory_space=pltpu.SMEM), vmem] + [hbm] * len(kept) + [vmem] * 3,
        out_specs=[vmem, hbm, vmem],
        scratch_shapes=[
            pltpu.VMEM((2, 2) + block, low),
            pltpu.VMEM((2, rows, 2 * HALF_UNITS), low),
            pltpu.VMEM((2, rows, 2 * HALF_UNITS), low),
            pltpu.VMEM((2, 2, rows, 3 * COLS), low),
            pltpu.VMEM((2, 2, rows, 3 * COLS), low),
            pltpu.VMEM((2, rows, 2 * COLS), low),
            pltpu.VMEM((4, 2, rows // LEN, LEN, 2 * LEN), low),
            pltpu.VMEM((rows, features), full),
            pltpu.VMEM((rows, 1), full),
            pltpu.VMEM((rows, features), full),
            pltpu.VMEM((rows, features), full),
            pltpu.VMEM((rows, features), low),
            pltpu.VMEM((rows, features), low),
            pltpu.VMEM((rows, features), low),
            pltpu.VMEM((rows, 6 * COLS), low),
            pltpu.VMEM((CHUNKS,) + block, low),
            pltpu.VMEM((CHUNKS, 3) + block, low),
            pltpu.VMEM((2,) + block, low),
            pltpu.VMEM((4,) + block, low),
            pltpu.VMEM((CHUNKS,) + block, low),
            pltpu.VMEM((CHUNKS,) + block, low),
            pltpu.VMEM((CHUNKS,) + block, low),
            pltpu.VMEM((CHUNKS, 2) + block, low),
            pltpu.VMEM((5, 16, features), full),
            dma((2, 5)),
            dma((4,)),
            dma((2,)),
            dma((4,)),
            pltpu.SemaphoreType.REGULAR((4,)),
            dma((CHUNKS, 2)),
            dma((CHUNKS, 2)),
        ]
        + [dma((CHUNKS, PARTS))] * 10
        + [dma((5,)), dma((5,)), dma((CHUNKS,))],
        compiler_params=pltpu.CompilerParams(
            collective_id=1, has_side_effects=True, vmem_limit_bytes=63 * 1024 * 1024
        ),
        name="backward_both",
    )(lengths, tokens, *kept, vectors, t_gain, s_gain)


def finish_kernel(sums, vec, qkv_out, qv_out, out_out, up_out, up_bias_out, down_out, bias_out, gain_out, shift_out):
    for i in range(3):
        qkv_out[i] = to_float(sums[2, i * COLS : (i + 1) * COLS]).T
    out_out[...] = to_float(sums[2, 3 * COLS :])
    for half in range(2):
        here = slice(half * HALF_UNITS, (half + 1) * HALF_UNITS)
        up_out[:, here] = to_float(sums[half, :HALF_UNITS]).T
        down_out[here] = to_float(sums[half, HALF_UNITS:])
    line = lax.broadcasted_iota(jnp.int32, (SLOTS, vec.shape[1]), 0)
    row = jnp.sum(jnp.where(line == lax.axis_index("mp"), vec[0:SLOTS], 0.0), axis=0, keepdims=True)
    qv_out[0:1] = row[:, :COLS]
    qv_out[1:2] = row[:, COLS : 2 * COLS]
    up_bias_out[...] = row[:, 2 * COLS : 2 * COLS + 2 * HALF_UNITS]
    for index, ref in enumerate((bias_out, gain_out, shift_out)):
        ref[0:1] = vec[8 + index : 9 + index]
        ref[1:2] = vec[11 + index : 12 + index]


def finish_sums(sums, vec):
    features = vec.shape[1]
    shapes = [
        (3, features, COLS),
        (2, COLS),
        (COLS, features),
        (features, 2 * HALF_UNITS),
        (1, 2 * HALF_UNITS),
        (2 * HALF_UNITS, features),
        (2, features),
        (2, features),
        (2, features),
    ]
    vmem = pl.BlockSpec(memory_space=pltpu.VMEM)
    return pl.pallas_call(
        finish_kernel,
        out_shape=[jax.ShapeDtypeStruct(shape, jnp.float32) for shape in shapes],
        in_specs=[vmem, vmem],
        out_specs=[vmem] * len(shapes),
        compiler_params=pltpu.CompilerParams(vmem_limit_bytes=48 * 1024 * 1024),
        name="finish_sums",
    )(sums, vec)


def cut(values, count, axis):
    return jnp.split(values, count, axis=axis)


def per_device(n_dp, n_mp, *args):
    (
        tokens,
        lengths,
        student_qkv,
        student_qv_bias,
        student_out,
        student_up,
        student_up_bias,
        student_down,
        student_out_bias,
        student_gain,
        student_shift,
        teacher_qkv,
        teacher_qv_bias,
        teacher_out,
        teacher_up,
        teacher_up_bias,
        teacher_down,
        teacher_out_bias,
        teacher_gain,
        teacher_shift,
    ) = args
    net = Cube(n_dp) if (n_dp, n_mp) == (4, 8) else Plain(n_mp)
    rows = tokens.shape[0]
    pairs = rows // LEN
    places = jnp.arange(LEN, dtype=jnp.int32)
    me = lax.axis_index("mp")
    own_lengths = lax.dynamic_slice_in_dim(lengths, me * pairs, pairs)
    valid = places[None, :] < own_lengths[:, None]
    token_valid = to_float(valid.reshape(rows, 1))
    pair_valid = valid[:, None, :, None] & valid[:, None, None, :]

    gain = to_float(student_gain)
    shift = to_float(student_shift)
    out_bias = to_float(student_out_bias)
    teach_gain = to_float(teacher_gain)
    if isinstance(net, Cube):
        gathered, kept, grad_t, grad_s, student_output, vecs = forward_both(
            lengths,
            tokens,
            (
                [teacher_qkv.transpose(1, 0, 2), teacher_out, teacher_up, teacher_down],
                [teacher_qv_bias, teacher_up_bias.reshape(1, -1), teacher_out_bias, teacher_gain, teacher_shift],
            ),
            (
                [student_qkv.transpose(1, 0, 2), student_out, student_up, student_down],
                [student_qv_bias, student_up_bias.reshape(1, -1), student_out_bias, student_gain, student_shift],
            ),
        )
        input_grad, sums, vec = backward_both(
            lengths, tokens, (gathered, *kept, grad_t, grad_s), vecs, teacher_gain, student_gain
        )
        grads = finish_sums(sums, vec)
        return (
            student_output,
            input_grad,
            grads[0].transpose(1, 0, 2),
            grads[1],
            grads[2],
            grads[3],
            grads[4].reshape(-1),
            *grads[5:],
        )
    else:
        teach = gather_layer(
            net, teacher_qkv, teacher_qv_bias, teacher_out, teacher_up, teacher_up_bias, teacher_down
        )
        stud = gather_layer(
            net,
            binarize(student_qkv, 0),
            student_qv_bias,
            binarize(student_out, 1),
            binarize(student_up, 0),
            student_up_bias,
            binarize(student_down, 1),
        )
        teach_final, teach_kept = forward(
            tokens, teach, to_float(teacher_out_bias), teach_gain, to_float(teacher_shift), plain_act, valid
        )
        final, kept = forward(tokens, stud, out_bias, gain, shift, clipped_act, valid)
        student_output = to_low(final)
        final_grad = token_valid * (final - teach_final)
        grad_s = norm_back(final_grad, kept[11], kept[12], gain[1])
        grad_t = norm_back(-final_grad, teach_kept[11], teach_kept[12], teach_gain[1])
        vecs = jnp.stack([jnp.sum(grad_s, axis=0), jnp.sum(final_grad * kept[11], axis=0), jnp.sum(final_grad, axis=0)])
    extra = score_weight * jnp.where(pair_valid, kept[3] - teach_kept[3], 0.0)

    second_grad, second_low, pre_grad, pre_low, normed_grad, first_grad = backward_ffn(
        kept, stud, grad_s, gain
    )
    hidden, normed_low, context = kept[9], kept[8], kept[5]
    unit_one = kept[6]
    down_grad = net.sum_dp(net.scatter(cut(to_low(dot_tn(hidden, second_low)), n_mp, 0)))
    up_grad = net.sum_dp(net.scatter(cut(to_low(dot_tn(normed_low, pre_low)), n_mp, 1)))
    first_low = to_low(first_grad)
    out_grad = net.sum_dp(net.scatter(cut(to_low(dot_tn(context, first_low)), n_mp, 0)))
    grads = backward_attention(kept, first_low, stud[3], extra)
    lows = [to_low(item) for item in grads]
    wide = jnp.concatenate(
        [to_low(dot_tn(tokens, item)) for item in lows], axis=0
    )
    qkv_grad = net.sum_dp(net.scatter(cut(wide, n_mp, 1)))
    features = tokens.shape[1]
    qkv_grad = qkv_grad.reshape(3, features, -1).transpose(1, 0, 2)

    teach_second, teach_slow, _, _, _, teach_first = backward_ffn(
        teach_kept, teach, grad_t, teach_gain
    )
    teach_grads = backward_attention(teach_kept, to_low(teach_first), teach[3], -extra)
    teach_lows = [to_low(item) for item in teach_grads]
    input_grad = first_grad + teach_first
    for item, matrix in zip(lows, stud[0]):
        input_grad = input_grad + dot_nt(item, matrix)
    for item, matrix in zip(teach_lows, teach[0]):
        input_grad = input_grad + dot_nt(item, matrix)

    vectors = [
        jnp.sum(first_grad, axis=0),
        vecs[0],
        jnp.sum(normed_grad * unit_one, axis=0),
        vecs[1],
        jnp.sum(normed_grad, axis=0),
        vecs[2],
        net.place(jnp.sum(grads[0], axis=0).reshape(n_mp, -1)).reshape(-1),
        net.place(jnp.sum(grads[2], axis=0).reshape(n_mp, -1)).reshape(-1),
    ]
    wide_vector = net.place(jnp.sum(pre_grad, axis=0).reshape(n_mp, -1)).reshape(-1, features)
    total = net.sum_all(jnp.concatenate([jnp.stack(vectors), wide_vector], axis=0))
    width = features // n_mp
    units = wide_vector.size // n_mp
    return (
        student_output,
        input_grad,
        qkv_grad,
        lax.dynamic_slice_in_dim(total[6:8], me * width, width, axis=1),
        out_grad,
        up_grad,
        lax.dynamic_slice_in_dim(total[8:].reshape(-1), me * units, units),
        down_grad,
        total[0:2],
        total[2:4],
        total[4:6],
    )


def solution(mesh):
    n_dp, n_mp = mesh.shape["dp"], mesh.shape["mp"]

    def body(*args):
        return per_device(n_dp, n_mp, *args)

    return jax.shard_map(
        body,
        mesh=mesh,
        in_specs=(
            P(("dp", "mp"), None),
            P("dp"),
            P(None, None, "mp"),
            P(None, "mp"),
            P("mp", None),
            P(None, "mp"),
            P("mp"),
            P("mp", None),
            P(),
            P(),
            P(),
            P(None, None, "mp"),
            P(None, "mp"),
            P("mp", None),
            P(None, "mp"),
            P("mp"),
            P("mp", None),
            P(),
            P(),
            P(),
        ),
        out_specs=(
            P(("dp", "mp"), None),
            P(("dp", "mp"), None),
            P(None, None, "mp"),
            P(None, "mp"),
            P("mp", None),
            P(None, "mp"),
            P("mp"),
            P("mp", None),
            P(),
            P(),
            P(),
        ),
        check_vma=False,
    )
```

```python
import math

import jax
import jax.numpy as jnp
from jax import lax
from jax.experimental import pallas as pl
from jax.experimental.pallas import tpu as pltpu
from jax.sharding import PartitionSpec as P

DH = 64
LEN = 128


norm_epsilon = 1e-06
clip_level = 2.5
score_weight = 0.05
masked_fill = -1000000000.0


def to_float(values):
    return values.astype(jnp.float32)


def to_low(values):
    return values.astype(jnp.bfloat16)


def binarize(matrix, axis_index):
    scaling = jnp.mean(jnp.abs(matrix), axis=axis_index, keepdims=True)
    return (scaling * jnp.sign(matrix)).astype(jnp.bfloat16)


def norm_stats(values):
    centred = values - jnp.mean(values, axis=-1, keepdims=True)
    variance = jnp.mean(centred * centred, axis=-1, keepdims=True)
    inverse = lax.rsqrt(variance + norm_epsilon)
    return (centred * inverse, inverse)


def norm_back(grad, unit, inverse, gain_row):
    scaled = grad * gain_row
    first = jnp.mean(scaled, axis=-1, keepdims=True)
    second = jnp.mean(scaled * unit, axis=-1, keepdims=True)
    return inverse * (scaled - first - unit * second)


def dot(left, right):
    return jnp.dot(left, right, preferred_element_type=jnp.float32)


def dot_nt(left, right):
    return lax.dot_general(left, right, (((1,), (1,)), ((), ())), preferred_element_type=jnp.float32)


def dot_tn(left, right):
    return lax.dot_general(left, right, (((0,), (0,)), ((), ())), preferred_element_type=jnp.float32)


class Cube:
    def __init__(self, n_dp):
        self.n_dp = n_dp
        self.axes = ("dp", "mp")

    def flip(self, values, bits):
        pairs = [
            (z * 8 + m, z * 8 + (m ^ bits)) for z in range(self.n_dp) for m in range(8)
        ]
        return lax.ppermute(values, self.axes, pairs)

    def flip_dp(self, values, bits):
        pairs = [
            (z * 8 + m, (z ^ bits) * 8 + m) for z in range(self.n_dp) for m in range(8)
        ]
        return lax.ppermute(values, self.axes, pairs)

    def gather(self, block):
        half = block.shape[0] // 2
        along_x = self.flip(block, 2)
        along_y = self.flip(block, 4)
        across = jnp.concatenate(
            [self.flip(along_y[:half], 2), self.flip(along_x[half:], 4)], axis=0
        )
        same = [block, along_x, along_y, across]
        other = [self.flip(item, 1) for item in same]
        return [item for pair in zip(same, other) for item in pair]

    def scatter(self, blocks):
        half = blocks[0].shape[0] // 2
        own, to_x, to_y, to_far = [
            to_float(blocks[k]) + to_float(self.flip(blocks[k + 1], 1)) for k in (0, 2, 4, 6)
        ]
        far = to_low(to_far)
        via_x = to_float(self.flip(far[:half], 2))
        via_y = to_float(self.flip(far[half:], 4))
        to_y = to_low(jnp.concatenate([to_y[:half] + via_x, to_y[half:]], axis=0))
        to_x = to_low(jnp.concatenate([to_x[:half], to_x[half:] + via_y], axis=0))
        return own + to_float(self.flip(to_x, 2)) + to_float(self.flip(to_y, 4))

    def sum_dp(self, values):
        half = values.shape[0] // 2
        odd = lax.axis_index("dp") % 2
        low = to_low(values)
        sent = lax.dynamic_slice_in_dim(low, (1 - odd) * half, half)
        kept = lax.dynamic_slice_in_dim(values, odd * half, half)
        kept = kept + to_float(self.flip_dp(sent, 1))
        kept_low = to_low(kept)
        kept = to_low(kept + to_float(self.flip_dp(kept_low, 2)))
        other = self.flip_dp(kept, 1)
        return to_float(
            jnp.concatenate(
                [jnp.where(odd == 0, kept, other), jnp.where(odd == 0, other, kept)], axis=0
            )
        )

    def sum_all(self, values):
        for bits in (1, 2, 4):
            values = values + self.flip(values, bits)
        for bits in (1, 2):
            values = values + self.flip_dp(values, bits)
        return values

    def place(self, values):
        me = lax.axis_index("mp")
        for bit in range(3):
            shape = values.shape
            split = values.reshape((8 >> (bit + 1), 2, 1 << bit) + shape[1:])
            flipped = split[:, ::-1]
            values = jnp.where((me >> bit) % 2 == 1, flipped, split).reshape(shape)
        return values


class Plain:
    def __init__(self, n_mp):
        self.n_mp = n_mp

    def gather(self, block):
        every = lax.all_gather(block, "mp", axis=0)
        return [every[k] for k in range(self.n_mp)]

    def scatter(self, blocks):
        return to_float(
            lax.psum_scatter(jnp.stack(blocks), "mp", scatter_dimension=0, tiled=False)
        )

    def sum_dp(self, values):
        return to_float(lax.psum(to_low(values), "dp"))

    def sum_all(self, values):
        return lax.psum(values, ("dp", "mp"))

    def place(self, values):
        return values


def plain_act(pre):
    gate = 0.5 * (1.0 + lax.erf(pre * math.sqrt(0.5)))
    slope = gate + pre * jnp.exp(-0.5 * pre * pre) * (1.0 / math.sqrt(2.0 * math.pi))
    return (pre * gate, slope)


def clipped_act(pre):
    value, slope = plain_act(pre)
    bent = jnp.tanh(value * (1.0 / clip_level))
    return (clip_level * bent, slope * (1.0 - bent * bent))


def gather_layer(net, qkv, qv_bias, out, up, up_bias, down):
    width = qkv.shape[2]
    units = up.shape[1]
    features = qkv.shape[0]
    extra = jnp.zeros((16, features), jnp.bfloat16)
    extra = extra.at[0, :width].set(qv_bias[0]).at[1, :width].set(qv_bias[1])
    extra = extra.at[2, :units].set(up_bias)
    qkv_parts = net.gather(qkv.transpose(1, 0, 2).reshape(3 * features, width))
    out_parts = net.gather(jnp.concatenate([out, extra], axis=0))
    up_parts = net.gather(up)
    down_parts = net.gather(down)
    count = len(qkv_parts)
    qkv_full = jnp.concatenate(
        [part.reshape(3, features, width) for part in qkv_parts], axis=2
    )
    out_full = jnp.concatenate([part[:width] for part in out_parts], axis=0)
    q_bias = jnp.concatenate([part[width, :width] for part in out_parts])
    v_bias = jnp.concatenate([part[width + 1, :width] for part in out_parts])
    up_b = jnp.concatenate([part[width + 2, :units] for part in out_parts])
    up_full = jnp.concatenate(up_parts, axis=1)
    down_full = jnp.concatenate(down_parts, axis=0)
    return (qkv_full, to_float(q_bias), to_float(v_bias), out_full, up_full, to_float(up_b), down_full)


def forward(tokens, weights, out_bias, gain, shift, activation, key_valid):
    qkv, q_bias, v_bias, out, up, up_bias, down = weights
    rows, features = tokens.shape
    pairs = rows // LEN
    shape = (pairs, LEN, features // DH, DH)
    query = to_low(dot(tokens, qkv[0]) + q_bias).reshape(shape)
    key = to_low(dot(tokens, qkv[1])).reshape(shape)
    value = to_low(dot(tokens, qkv[2]) + v_bias).reshape(shape)
    scores = jnp.einsum("bqhe,bkhe->bhqk", query, key, preferred_element_type=jnp.float32) * (
        1.0 / math.sqrt(DH)
    )
    masked = jnp.where(key_valid[:, None, None, :], scores, masked_fill)
    log_norm = jax.nn.logsumexp(masked, axis=-1, keepdims=True)
    attention = jnp.exp(masked - log_norm)
    context = jnp.einsum(
        "bhqk,bkhe->bqhe", to_low(attention), value, preferred_element_type=jnp.float32
    )
    context = to_low(context).reshape(rows, features)
    first = to_float(tokens) + dot(context, out) + out_bias[0]
    unit_one, inverse_one = norm_stats(first)
    normed = unit_one * gain[0] + shift[0]
    normed_low = to_low(normed)
    hidden, slope = activation(dot(normed_low, up) + up_bias)
    hidden = to_low(hidden)
    second = normed + dot(hidden, down) + out_bias[1]
    unit_two, inverse_two = norm_stats(second)
    final = unit_two * gain[1] + shift[1]
    kept = (query, key, value, scores, attention, context, unit_one, inverse_one, normed_low, hidden,
            to_low(slope), unit_two, inverse_two)
    return (final, kept)


def backward_ffn(kept, weights, second_grad, gain):
    qkv, q_bias, v_bias, out, up, up_bias, down = weights
    (query, key, value, scores, attention, context, unit_one, inverse_one, normed_low, hidden,
     slope, unit_two, inverse_two) = kept
    second_low = to_low(second_grad)
    pre_grad = dot_nt(second_low, down) * slope
    pre_low = to_low(pre_grad)
    normed_grad = second_grad + dot_nt(pre_low, up)
    first_grad = norm_back(normed_grad, unit_one, inverse_one, gain[0])
    return (second_grad, second_low, pre_grad, pre_low, normed_grad, first_grad)


def backward_attention(kept, first_low, out, extra):
    query, key, value, scores, attention = kept[:5]
    rows = first_low.shape[0]
    factor = 1.0 / math.sqrt(DH)
    context_grad = to_low(dot_nt(first_low, out)).reshape(query.shape)
    attention_grad = jnp.einsum(
        "bqhe,bkhe->bhqk", context_grad, value, preferred_element_type=jnp.float32
    )
    value_grad = jnp.einsum(
        "bhqk,bqhe->bkhe", to_low(attention), context_grad, preferred_element_type=jnp.float32
    )
    inner = jnp.sum(attention * attention_grad, axis=-1, keepdims=True)
    score_low = to_low(attention * (attention_grad - inner) + extra)
    query_grad = factor * jnp.einsum(
        "bhqk,bkhe->bqhe", score_low, key, preferred_element_type=jnp.float32
    )
    key_grad = factor * jnp.einsum(
        "bhqk,bqhe->bkhe", score_low, query, preferred_element_type=jnp.float32
    )
    return [item.reshape(rows, -1) for item in (query_grad, key_grad, value_grad)]


MESH = pl.DeviceIdType.MESH
SLOTS = 8
PACKS = 6
ATT_ROWS = 528
FFN_ROWS = 512
HALF_UNITS = 256
COLS = 128
SHARED = (160, 160, 160, 160, 160, 96)


def flipped(me, bits):
    return me + bits - 2 * bits * lax.rem(lax.div(me, bits), 2)


def pack_rows(pack):
    return ATT_ROWS if pack < 2 else FFN_ROWS


def masked_probs(scores, length):
    rows = scores.shape[0]
    position = lax.broadcasted_iota(jnp.int32, (rows, LEN), 1)
    parts = []
    for head in range(2):
        part = jnp.where(position < length, scores[:, head * LEN : (head + 1) * LEN], masked_fill)
        part = jnp.exp(part - jnp.max(part, axis=1, keepdims=True))
        parts.append(part / jnp.sum(part, axis=1, keepdims=True))
    return jnp.concatenate(parts, axis=1)


def two_heads(rows):
    first = lax.broadcasted_iota(jnp.int32, rows.shape, 1) < DH
    zero = jnp.zeros_like(rows)
    return jnp.concatenate([jnp.where(first, rows, zero), jnp.where(first, zero, rows)], axis=0)


def norm_block(values):
    centred = values - jnp.mean(values, axis=1, keepdims=True)
    inverse = lax.rsqrt(jnp.mean(centred * centred, axis=1, keepdims=True) + norm_epsilon)
    return (centred * inverse, inverse)


def forward_kernel(
    lengths,
    x_ref,
    t_weights,
    t_small,
    s_weights,
    s_small,
    gathered,
    kept,
    grad_t,
    grad_s,
    final_low,
    vectors,
    scratch,
    raw_t,
    raw_s,
    mine_att,
    mine_ffn,
    wide,
    total,
    normed,
    low_t,
    context_t,
    bias_rows,
    final_t,
    unit_two,
    inverse_two,
    send,
    recv,
    load,
    fetch,
    save,
):
    t_qv_bias, t_up_bias, t_bias, t_gain, t_shift = t_small
    s_qv_bias, s_up_bias, s_bias, s_gain, s_shift = s_small
    qkv_t, qkv_s, context_s, slope_t, slope_s, hidden_s, unit_t, inverse_t, unit_s, inverse_s, low_s = scratch
    saved = []

    def put(name, index=None):
        src, dst = scratch[name], kept[name]
        if index is not None:
            src, dst = src.at[index], dst.at[index]
        saved.append(pltpu.make_async_copy(src, dst, save.at[len(saved)]))
        saved[-1].start()

    me = lax.axis_index("mp")
    z = lax.axis_index("dp")
    peers = {bits: {"mp": flipped(me, bits)} for bits in (1, 2, 4)}
    peers["z"] = {"dp": flipped(z, 1)}
    upper = lax.rem(z, 2)
    rows = x_ref.shape[0]
    pairs = rows // LEN

    barrier = pltpu.get_barrier_semaphore()
    for peer in peers.values():
        pl.semaphore_signal(barrier, inc=1, device_id=peer, device_id_type=MESH)
    pl.semaphore_wait(barrier, len(peers))

    fetched = []
    for weights, raw, direct in ((t_weights, raw_t, True), (s_weights, raw_s, False)):
        qkv, out, up, down = weights
        moves = [(qkv, raw[0]), (up, raw[1])]
        if direct:
            moves.append((out, mine_att.at[0, pl.ds(3 * COLS, COLS)]))
            moves += [
                (down.at[pl.ds(h * HALF_UNITS, HALF_UNITS)], mine_ffn.at[h, pl.ds(HALF_UNITS, HALF_UNITS)])
                for h in range(2)
            ]
        else:
            moves += [(out, raw[2]), (down, raw[3])]
        for src, dst in moves:
            fetched.append(pltpu.make_async_copy(src, dst, fetch.at[len(fetched)]))
            fetched[-1].start()

    def signed(values, axis):
        scale = jnp.mean(jnp.abs(values), axis=axis, keepdims=True)
        return to_low(jnp.where(values > 0, scale, jnp.where(values < 0, -scale, 0.0)))

    def bias_block(qv_bias, up_bias):
        line = jnp.concatenate(
            [
                to_float(qv_bias[0:1]),
                to_float(qv_bias[1:2]),
                to_float(up_bias[...]),
                jnp.zeros((1, x_ref.shape[1] - 2 * COLS - 2 * HALF_UNITS), jnp.float32),
            ],
            axis=1,
        )
        row = lax.broadcasted_iota(jnp.int32, (16, line.shape[1]), 0)
        return to_low(jnp.where(row == 0, jnp.broadcast_to(line, row.shape), 0.0))

    def own_copy(pack):
        return pltpu.make_async_copy(source(pack), block(pack, 0), fetch.at[9 + pack])

    def prepare(pack):
        if pack == 0:
            fetched[0].wait()
            for i in range(3):
                mine_att[0, i * COLS : (i + 1) * COLS] = raw_t[0][i].T
            mine_att[0, 4 * COLS : 4 * COLS + 16] = bias_block(t_qv_bias, t_up_bias)
            fetched[2].wait()
        elif pack == 1:
            fetched[5].wait()
            for i in range(3):
                mine_att[1, i * COLS : (i + 1) * COLS] = signed(raw_s[0][i], 0).T
            mine_att[1, 4 * COLS : 4 * COLS + 16] = bias_block(s_qv_bias, s_up_bias)
            fetched[7].wait()
            mine_att[1, 3 * COLS : 4 * COLS] = signed(raw_s[2][...], 1)
        else:
            layer, half = divmod(pack - 2, 2)
            here = slice(half * HALF_UNITS, (half + 1) * HALF_UNITS)
            if half == 0:
                fetched[(1, 6)[layer]].wait()
            if layer == 0:
                mine_ffn[half, 0:HALF_UNITS] = raw_t[1][:, here].T
                fetched[3 + half].wait()
            else:
                mine_ffn[2 + half, 0:HALF_UNITS] = signed(raw_s[1][:, here], 0).T
                if half == 0:
                    fetched[8].wait()
                mine_ffn[2 + half, HALF_UNITS : 2 * HALF_UNITS] = signed(raw_s[3][here], 1)
        own_copy(pack).start()

    def source(pack):
        return mine_att.at[pack] if pack < 2 else mine_ffn.at[pack - 2]

    def span(pack, start, count):
        return pl.ds(pl.multiple_of(start, 16), count)

    def block(pack, slot):
        return gathered.at[pack, slot, pl.ds(0, pack_rows(pack))]

    def remote(pack, kind):
        shared = SHARED[pack]
        rest = pack_rows(pack) - shared
        first = (rest // 2 + 15) // 16 * 16
        low = upper * shared
        if kind == 0 or kind == 1:
            here = span(pack, low, rest)
            src, dst = source(pack).at[here], gathered.at[pack, 2 + 2 * kind, here]
            peer = peers[2 + 2 * kind]
        elif kind == 2:
            here = span(pack, low, first)
            src, dst, peer = gathered.at[pack, 4, here], gathered.at[pack, 6, here], peers[2]
        elif kind == 3:
            here = span(pack, low + first, rest - first)
            src, dst, peer = gathered.at[pack, 2, here], gathered.at[pack, 6, here], peers[4]
        elif kind == 4:
            src, dst, peer = source(pack), block(pack, 1), peers[1]
        elif kind < 8:
            slot = 2 * (kind - 4)
            src, dst, peer = block(pack, slot), block(pack, slot + 1), peers[1]
        else:
            here = span(pack, upper * rest, shared)
            slot = 2 * (kind - 7)
            src, dst, peer = gathered.at[pack, slot, here], gathered.at[pack, slot, here], peers["z"]
        return pltpu.make_async_remote_copy(
            src_ref=src,
            dst_ref=dst,
            send_sem=send.at[pack, kind],
            recv_sem=recv.at[pack, kind],
            device_id=peer,
            device_id_type=MESH,
        )

    def first_sends(pack):
        for kind in (0, 1, 4):
            remote(pack, kind).start()

    def second_sends(pack):
        remote(pack, 0).wait_recv()
        remote(pack, 3).start()
        remote(pack, 8).start()
        remote(pack, 1).wait_recv()
        remote(pack, 2).start()
        remote(pack, 9).start()

    def plane_swap(pack):
        remote(pack, 8).wait_recv()
        remote(pack, 5).start()
        remote(pack, 9).wait_recv()
        remote(pack, 6).start()

    def far_sends(pack):
        remote(pack, 2).wait_recv()
        remote(pack, 3).wait_recv()
        remote(pack, 10).start()

    def far_swap(pack):
        remote(pack, 10).wait_recv()
        remote(pack, 7).start()

    def load_pair(pack, pair, place):
        here = pl.ds(0, pack_rows(pack))
        return pltpu.make_async_copy(
            gathered.at[pack, pl.ds(2 * pair, 2), here], wide.at[place, :, here], load.at[place]
        )

    def over_pairs(pack, chosen, body, between):
        def begin(pair):
            if pair == 0:
                own_copy(pack).wait()
            remote(pack, 4 + pair).wait_recv()
            load_pair(pack, pair, pair % 2).start()

        begin(chosen[0])
        for pair in chosen:
            load_pair(pack, pair, pair % 2).wait()
            if pair != chosen[-1]:
                begin(pair + 1)
            body(pair, pair % 2)
            if pair in between:
                between[pair]()

    def attention(pack, chosen, between, qkv_ref, context_ref):
        if chosen[0] == 0:
            total[...] = jnp.zeros_like(total)

        def body(pair, place):
            weights = wide[place, :, 0:384].reshape(768, -1)
            projected = dot_nt(x_ref[...], weights)
            for side in range(2):
                slot = 2 * pair + side
                bias = wide[place, side, 512:528]
                bias_rows[pack, slot] = bias
                bias = to_float(bias[0:1])
                part = projected[:, side * 384 : side * 384 + 384]
                query = to_low(part[:, :COLS] + bias[:, :COLS])
                key = to_low(part[:, COLS : 2 * COLS])
                value = to_low(part[:, 2 * COLS :] + bias[:, COLS : 2 * COLS])
                qkv_ref[slot, :, 0:COLS] = query
                qkv_ref[slot, :, COLS : 2 * COLS] = key
                qkv_ref[slot, :, 2 * COLS : 3 * COLS] = value
                for number in range(pairs):
                    here = slice(number * LEN, (number + 1) * LEN)
                    scores = dot_nt(query[here], two_heads(key[here])) * (1.0 / math.sqrt(DH))
                    probs = masked_probs(scores, lengths[me * pairs + number])
                    part_context = dot(to_low(probs), two_heads(value[here]))
                    context_ref[pair, here, side * COLS : (side + 1) * COLS] = to_low(part_context)
            put(pack, pl.ds(2 * pair, 2))
            if pack == 1:
                put(2, pair)
            total[...] += dot(context_ref[pair], wide[place, :, 384:512].reshape(256, -1))

        over_pairs(pack, chosen, body, between)

    def first_norm(bias_ref, gain_ref, shift_ref, unit_ref, inverse_ref, index, low_ref):
        @pl.loop(0, rows // 64)
        def _(step):
            here = pl.ds(step * 64, 64)
            values = to_float(x_ref[here]) + total[here] + to_float(bias_ref[0:1])
            unit, inverse = norm_block(values)
            unit_ref[here] = unit
            inverse_ref[here] = inverse
            values = unit * to_float(gain_ref[0:1]) + to_float(shift_ref[0:1])
            normed[index, here] = values
            low_ref[here] = to_low(values)

    def feed_forward(pack, chosen, between, low_ref, activation, hidden_ref, slope_ref):
        layer, half = divmod(pack - 2, 2)

        def body(pair, place):
            up = wide[place, :, 0:HALF_UNITS].reshape(2 * HALF_UNITS, -1)
            down = wide[place, :, HALF_UNITS : 2 * HALF_UNITS].reshape(2 * HALF_UNITS, -1)
            start = 2 * COLS + half * HALF_UNITS
            bias = jnp.concatenate(
                [
                    to_float(bias_rows[layer, 2 * pair + side, 0:1, start : start + HALF_UNITS])
                    for side in range(2)
                ],
                axis=1,
            )
            hidden, slope = activation(dot_nt(low_ref[...], up) + bias)
            hidden = to_low(hidden)
            slope_ref[half, pair] = to_low(slope)
            put(3 + layer, (half, pair))
            if hidden_ref is not None:
                hidden_ref[half, pair] = hidden
                put(5, (half, pair))
            total[...] += dot(hidden, down)

        if half == 0 and chosen[0] == 0:
            total[...] = jnp.zeros_like(total)
        over_pairs(pack, chosen, body, between)

    def step_teacher_end():
        @pl.loop(0, rows // 64)
        def _(step):
            here = pl.ds(step * 64, 64)
            unit, inverse = norm_block(normed[0, here] + total[here] + to_float(t_bias[1:2]))
            unit_two[here] = unit
            inverse_two[here] = inverse
            final_t[here] = unit * to_float(t_gain[1:2]) + to_float(t_shift[1:2])

    def step_student_end():
        vectors[...] = jnp.zeros_like(vectors)

        @pl.loop(0, rows // 64)
        def _(step):
            here = pl.ds(step * 64, 64)
            unit, inverse = norm_block(normed[1, here] + total[here] + to_float(s_bias[1:2]))
            gain = to_float(s_gain[1:2])
            final = unit * gain + to_float(s_shift[1:2])
            final_low[here] = to_low(final)
            position = lax.broadcasted_iota(jnp.int32, (64, 1), 0) + lax.rem(step, 2) * 64
            valid = position < lengths[me * pairs + lax.div(step, 2)]
            grad = jnp.where(valid, final - final_t[here], 0.0)
            back = norm_back(grad, unit, inverse, gain)
            grad_s[here] = back
            grad_t[here] = norm_back(
                -grad, unit_two[here], inverse_two[here], to_float(t_gain[1:2])
            )
            vectors[0:1] += jnp.sum(back, axis=0, keepdims=True)
            vectors[1:2] += jnp.sum(grad * unit, axis=0, keepdims=True)
            vectors[2:3] += jnp.sum(grad, axis=0, keepdims=True)

    def use(pack, chosen, between={}):
        if pack == 0:
            attention(0, chosen, between, qkv_t, context_t)
        elif pack == 1:
            attention(1, chosen, between, qkv_s, context_s)
        elif pack < 4:
            feed_forward(pack, chosen, between, low_t, plain_act, None, slope_t)
        else:
            feed_forward(pack, chosen, between, low_s, clipped_act, hidden_s, slope_s)

    def end(pack):
        if pack == 0:
            first_norm(t_bias, t_gain, t_shift, unit_t, inverse_t, 0, low_t)
            put(6)
            put(7)
        elif pack == 1:
            first_norm(s_bias, s_gain, s_shift, unit_s, inverse_s, 1, low_s)
            for name in (8, 9, 10):
                put(name)
        elif pack == 3:
            step_teacher_end()

    near, far = (0, 1, 2), (3,)
    prepare(0)
    first_sends(0)
    prepare(1)
    first_sends(1)
    for pack in range(2, PACKS):
        prepare(pack)
    second_sends(0)
    first_sends(2)
    second_sends(1)
    first_sends(3)
    plane_swap(0)
    use(0, near, {1: lambda: far_sends(0)})
    second_sends(2)
    first_sends(4)
    far_swap(0)
    use(0, far)
    end(0)
    far_sends(1)
    plane_swap(1)
    use(1, near)
    second_sends(3)
    first_sends(5)
    far_swap(1)
    use(1, far)
    end(1)
    far_sends(2)
    plane_swap(2)
    use(2, near)
    plane_swap(3)
    use(3, near, {1: lambda: second_sends(4)})
    far_swap(2)
    use(2, far)
    far_sends(3)
    far_swap(3)
    use(3, far)
    second_sends(5)
    end(3)
    plane_swap(4)
    use(4, near, {0: lambda: far_sends(4)})
    plane_swap(5)
    use(5, near, {1: lambda: far_sends(5)})
    far_swap(4)
    use(4, far)
    far_swap(5)
    use(5, far)
    step_student_end()
    for pack in range(PACKS):
        for kind in range(11):
            remote(pack, kind).wait_send()
    for copy in saved:
        copy.wait()


def forward_both(lengths, tokens, teacher, student):
    rows, features = tokens.shape
    low, full = jnp.bfloat16, jnp.float32
    vmem = pl.BlockSpec(memory_space=pltpu.VMEM)
    hbm = pl.BlockSpec(memory_space=pl.ANY)
    dma = pltpu.SemaphoreType.DMA
    act = (2, 4, rows, 2 * HALF_UNITS)
    kept = [
        ((SLOTS, rows, 3 * COLS), low),
        ((SLOTS, rows, 3 * COLS), low),
        ((4, rows, 2 * COLS), low),
        (act, low),
        (act, low),
        (act, low),
        ((rows, features), full),
        ((rows, 1), full),
        ((rows, features), full),
        ((rows, 1), full),
        ((rows, features), low),
    ]
    shapes = [jax.ShapeDtypeStruct(shape, kind) for shape, kind in kept]
    ends = [((rows, features), full), ((rows, features), full), ((rows, features), low), ((8, features), full)]
    qkv, out, up, down = teacher[0]
    return pl.pallas_call(
        forward_kernel,
        out_shape=[
            jax.ShapeDtypeStruct((PACKS, SLOTS, ATT_ROWS, features), low),
            shapes,
            *[jax.ShapeDtypeStruct(shape, kind) for shape, kind in ends],
        ],
        in_specs=[pl.BlockSpec(memory_space=pltpu.SMEM), vmem] + [[hbm] * 4, [vmem] * 5] * 2,
        out_specs=[hbm, [hbm] * len(kept)] + [vmem] * len(ends),
        scratch_shapes=[
            [pltpu.VMEM(shape, kind) for shape, kind in kept],
            [pltpu.VMEM(qkv.shape, low), pltpu.VMEM(up.shape, low)],
            [pltpu.VMEM(item.shape, full) for item in (qkv, up, out, down)],
            pltpu.VMEM((2, ATT_ROWS, features), low),
            pltpu.VMEM((4, FFN_ROWS, features), low),
            pltpu.VMEM((2, 2, ATT_ROWS, features), low),
            pltpu.VMEM((rows, features), full),
            pltpu.VMEM((2, rows, features), full),
            pltpu.VMEM((rows, features), low),
            pltpu.VMEM((4, rows, 2 * COLS), low),
            pltpu.VMEM((2, SLOTS, 16, features), low),
            pltpu.VMEM((rows, features), full),
            pltpu.VMEM((rows, features), full),
            pltpu.VMEM((rows, 1), full),
            dma((PACKS, 11)),
            dma((PACKS, 11)),
            dma((2,)),
            dma((9 + PACKS,)),
            dma((48,)),
        ],
        compiler_params=pltpu.CompilerParams(
            collective_id=0, has_side_effects=True, vmem_limit_bytes=62 * 1024 * 1024
        ),
        name="forward_both",
    )(lengths, tokens, *teacher, *student)


CHUNKS = 3
PARTS = (4, 4, 8)
ORDER = (3, 1, 2, 0)

SCHEDULE = {
    (1, 6): [("combine", 0, 3)],
    (2, 6): [("combine", 0, 1)],
    (3, 6): [("combine", 0, 2)],
    (4, 6): [("combine", 0, 0)],
    (5, 6): [("combine", 1, 3), ("fold", 0, 0)],
    (6, 6): [("combine", 1, 1)],
    (7, 6): [("combine", 1, 2)],
    (7, 7): [("combine", 1, 0)],
    (8, 0): [("fold", 1, 0)],
    (8, 4): [("own", 0, 0)],
    (9, 1): [("combine", 2, 3), ("own", 0, 1)],
    (9, 3): [("mid", 0, 0)],
    (9, 6): [("own", 0, 2)],
    (10, 1): [("combine", 2, 1), ("mid", 0, 1)],
    (10, 2): [("own", 0, 3), ("end", 0, 0)],
    (10, 6): [("mid", 0, 2)],
    (11, 0): [("own", 1, 0), ("end", 0, 1), ("combine", 2, 2)],
    (11, 1): [("mid", 0, 3)],
    (11, 3): [("own", 1, 1), ("end", 0, 2)],
    (11, 6): [("mid", 1, 0)],
    (12, 6): [("combine", 2, 0), ("own", 1, 2), ("end", 0, 3)],
    (13, 6): [("mid", 1, 1), ("vec", 0)],
    (14, 6): [("own", 1, 3), ("end", 1, 0)],
    (15, 6): [("vec", 1)],
    (16, 6): [("mid", 1, 2)],
    (17, 6): [("vec", 2)],
    (18, 6): [("end", 1, 1)],
    (19, 6): [("vec", 3)],
    (19, 7): [("fold", 2, 0), ("mid", 1, 3), ("end", 1, 2)],
    (20, 6): [("own", 2, 0), ("vec", 4)],
    (21, 2): [("own", 2, 1), ("end", 1, 3)],
    (21, 6): [("own", 2, 2), ("mid", 2, 0)],
    (22, 2): [("own", 2, 3), ("mid", 2, 1)],
    (22, 6): [("own", 2, 4), ("mid", 2, 2), ("end", 2, 0)],
    (23, 1): [("end", 2, 1), ("mid", 2, 3), ("own", 2, 5)],
    (23, 4): [("end", 2, 2), ("mid", 2, 4), ("own", 2, 6)],
}
LAST = [
    ("end", 2, 3),
    ("mid", 2, 5),
    ("own", 2, 7),
    ("end", 2, 4),
    ("mid", 2, 6),
    ("end", 2, 5),
    ("mid", 2, 7),
    ("end", 2, 6),
    ("end", 2, 7),
]


def backward_kernel(
    lengths,
    x_ref,
    gathered,
    qkv_t,
    qkv_s,
    context_s,
    slope_t,
    slope_s,
    hidden_s,
    unit_t,
    inverse_t,
    unit_s,
    inverse_s,
    low_s,
    grad_t,
    grad_s,
    vectors,
    t_gain,
    s_gain,
    grad_in,
    sums_out,
    vec,
    wide,
    hidden_buf,
    slope_buf,
    qkv_s_buf,
    qkv_t_buf,
    context_buf,
    extra_buf,
    unit_buf,
    inverse_buf,
    grad_buf,
    total,
    low_y,
    low_z,
    low_a,
    proj,
    sums,
    even,
    odd,
    from_core,
    from_far,
    from_x,
    from_y,
    from_z,
    from_vec,
    load,
    state_sem,
    odd_send,
    odd_recv,
    free,
    far_send,
    far_recv,
    x_send,
    x_recv,
    y_send,
    y_recv,
    in_send,
    in_recv,
    mid_send,
    mid_recv,
    out_send,
    out_recv,
    vec_send,
    vec_recv,
    done,
):
    me = lax.axis_index("mp")
    z = lax.axis_index("dp")
    rows = x_ref.shape[0]
    pairs = rows // LEN
    core, along_x, along_y = ({"mp": flipped(me, bits)} for bits in (1, 2, 4))
    z_outer, z_inner = {"dp": flipped(z, 1)}, {"dp": 3 - z}
    z_two = {"dp": flipped(z, 2)}
    inner = jnp.logical_or(z == 1, z == 2)
    outer = jnp.logical_or(z == 0, z == 3)

    barrier = pltpu.get_barrier_semaphore()
    greeted = (core, along_x, along_y, z_outer, z_inner, z_two)
    for peer in greeted:
        pl.semaphore_signal(barrier, inc=1, device_id=peer, device_id_type=MESH)
    pl.semaphore_wait(barrier, len(greeted))

    def remote(src, dst, send, recv, peer):
        return pltpu.make_async_remote_copy(
            src_ref=src, dst_ref=dst, send_sem=send, recv_sem=recv, device_id=peer, device_id_type=MESH
        )

    steps = [("fs", 4 + half, pair) for half in range(2) for pair in ORDER]
    steps += [("as", 1, pair) for pair in ORDER]
    steps += [("ft", 2 + half, pair) for half in range(2) for pair in range(4)]
    steps += [("at", 0, pair) for pair in range(4)]

    def loads(number):
        kind, pack, pair = steps[number]
        place = number % 2
        two = pl.ds(2 * pair, 2)
        here = pl.ds(0, FFN_ROWS)
        moves = [(gathered.at[pack, two, here], wide.at[place])]
        if kind == "fs":
            moves.append((hidden_s.at[pack - 4, pair], hidden_buf.at[place]))
            moves.append((slope_s.at[pack - 4, pair], slope_buf.at[place]))
        elif kind == "ft":
            moves.append((slope_t.at[pack - 2, pair], slope_buf.at[place]))
        else:
            moves.append((qkv_t.at[two], qkv_t_buf.at[place]))
            if kind == "as":
                moves.append((qkv_s.at[two], qkv_s_buf.at[place]))
                moves.append((context_s.at[pair], context_buf.at[place]))
        return [
            pltpu.make_async_copy(src, dst, load.at[place, index])
            for index, (src, dst) in enumerate(moves)
        ]

    def state(layer):
        unit, inverse, grad = ((unit_t, inverse_t, grad_t), (unit_s, inverse_s, grad_s))[layer]
        moves = [(grad, grad_buf), (unit, unit_buf), (inverse, inverse_buf)]
        return [
            pltpu.make_async_copy(src, dst, state_sem.at[index])
            for index, (src, dst) in enumerate(moves)
        ]

    def slot_row(slot):
        row = me
        for bits in (1, 2, 4):
            if slot & bits:
                row = flipped(row, bits)
        return row

    def odd_copy(number):
        pair = steps[number][2]
        return remote(
            odd.at[number % 2], from_core.at[pair], odd_send.at[number % 2], odd_recv.at[pair], core
        )

    def keep(chunk, pair):
        return sums.at[chunk] if pair == 0 else even.at[chunk, pair - 1]

    def give(number, pieces):
        pair = steps[number][2]
        chunk = number // 4
        if number >= 2:
            odd_copy(number - 2).wait_send()
        for start, values in pieces:
            count = values.shape[0] // 2
            keep(chunk, pair)[start : start + count] = to_low(values[:count])
            odd[number % 2, start : start + count] = to_low(values[count:])
        if chunk:
            pl.semaphore_wait(free.at[pair], 1)
        odd_copy(number).start()

    def add_rows(target, others, start, count):
        @pl.loop(0, count // 64)
        def _(step):
            here = pl.ds(start + step * 64, 64)
            value = to_float(target[here])
            for other in others:
                value = value + to_float(other[here])
            target[here] = to_low(value)

    def combine(chunk, pair):
        number = chunk * 4 + ORDER.index(pair)
        odd_copy(number).wait_recv()
        add_rows(keep(chunk, pair), [from_core.at[pair]], 0, FFN_ROWS)
        if chunk < CHUNKS - 1:
            pl.semaphore_signal(free.at[pair], inc=1, device_id=core, device_id_type=MESH)
        if pair == 3:
            far_copy(chunk, 0).start()
            far_copy(chunk, 1).start()

    def far_copy(chunk, way):
        part = pl.ds(way * 256, 256)
        return remote(
            even.at[chunk, 2, part],
            from_far.at[chunk, part],
            far_send.at[chunk, way],
            far_recv.at[chunk, way],
            (along_x, along_y)[way],
        )

    def part_rows(chunk):
        return FFN_ROWS // PARTS[chunk]

    def part_span(chunk, part):
        return pl.ds(part * part_rows(chunk), part_rows(chunk))

    def plane_copies(chunk, part):
        here = part_span(chunk, part)
        return [
            remote(even.at[chunk, 0, here], from_x.at[chunk, here], x_send.at[chunk, part], x_recv.at[chunk, part], along_x),
            remote(even.at[chunk, 1, here], from_y.at[chunk, here], y_send.at[chunk, part], y_recv.at[chunk, part], along_y),
        ]

    def fold(chunk, _):
        far_copy(chunk, 0).wait_recv()
        add_rows(keep(chunk, 2), [from_far.at[chunk]], 0, 256)
        far_copy(chunk, 1).wait_recv()
        add_rows(keep(chunk, 1), [from_far.at[chunk]], 256, 256)
        for part in range(PARTS[chunk]):
            for copy in plane_copies(chunk, part):
                copy.start()

    def z_copy(chunk, part, kind):
        here = part_span(chunk, part)
        own, first, second = sums.at[chunk, here], from_z.at[chunk, 0, here], from_z.at[chunk, 1, here]
        if kind == 0:
            return remote(own, first, in_send.at[chunk, part], in_recv.at[chunk, part], z_outer)
        if kind == 1:
            return remote(own, second, mid_send.at[chunk, part], mid_recv.at[chunk, part], z_inner)
        return remote(first, first, out_send.at[chunk, part], out_recv.at[chunk, part], z_outer)

    def own_part(chunk, part):
        for copy in plane_copies(chunk, part):
            copy.wait_recv()
        add_rows(sums.at[chunk], [from_x.at[chunk], from_y.at[chunk]], part * part_rows(chunk), part_rows(chunk))

        @pl.when(outer)
        def _():
            z_copy(chunk, part, 0).start()

    def mid_part(chunk, part):
        @pl.when(inner)
        def _():
            z_copy(chunk, part, 0).wait_recv()
            add_rows(sums.at[chunk], [from_z.at[chunk, 0]], part * part_rows(chunk), part_rows(chunk))
            z_copy(chunk, part, 1).start()

    def end_part(chunk, part):
        @pl.when(inner)
        def _():
            z_copy(chunk, part, 1).wait_recv()

            @pl.loop(0, part_rows(chunk) // 64)
            def _(step):
                here = pl.ds(part * part_rows(chunk) + step * 64, 64)
                value = to_float(sums[chunk, here]) + to_float(from_z[chunk, 1, here])
                from_z[chunk, 0, here] = to_low(value)

            z_copy(chunk, part, 2).start()

    def store_copy(chunk):
        return pltpu.make_async_copy(from_z.at[chunk, 0], sums_out.at[chunk], done.at[chunk])

    def finish(chunk):
        @pl.when(outer)
        def _():
            for part in range(PARTS[chunk]):
                z_copy(chunk, part, 2).wait_recv()

        store_copy(chunk).start()

    ways = (core, along_x, along_y, z_outer, z_two)

    def vec_copy(way):
        return remote(vec, from_vec.at[way], vec_send.at[way], vec_recv.at[way], ways[way])

    def vec_add(way):
        vec_copy(way).wait_send()
        vec_copy(way).wait_recv()
        vec[...] += from_vec[way]
        if way + 1 < len(ways):
            vec_copy(way + 1).start()

    def put_bias(pair, start, values):
        count = values.shape[1] // 2
        for side in range(2):
            line = lax.broadcasted_iota(jnp.int32, (SLOTS, count), 0)
            part = jnp.broadcast_to(values[:, side * count : (side + 1) * count], (SLOTS, count))
            part = jnp.where(line == slot_row(2 * pair + side), part, 0.0)
            vec[0:SLOTS, start : start + count] += part

    def ffn_step(number):
        kind, pack, pair = steps[number]
        place = number % 2
        up = wide[place, :, 0:HALF_UNITS].reshape(2 * HALF_UNITS, -1)
        down = wide[place, :, HALF_UNITS : 2 * HALF_UNITS].reshape(2 * HALF_UNITS, -1)
        back = dot_nt(low_z[...], down) * to_float(slope_buf[place])
        back_low = to_low(back)
        total[...] += dot(back_low, up)
        if kind == "fs":
            put_bias(pair, 2 * COLS + (pack - 4) * HALF_UNITS, jnp.sum(back, axis=0, keepdims=True))
            up_grad = dot_tn(back_low, low_y[...])
            down_grad = dot_tn(hidden_buf[place], low_z[...])
            give(number, [(0, up_grad), (HALF_UNITS, down_grad)])

    def pick(both):
        first = lax.broadcasted_iota(jnp.int32, (LEN, COLS), 1) < DH
        return jnp.where(first, both[:LEN], both[LEN:])

    def attention_step(number):
        kind, pack, pair = steps[number]
        place = number % 2
        student = kind == "as"
        factor = 1.0 / math.sqrt(DH)
        qkv = qkv_s_buf if student else qkv_t_buf
        out = wide[place, :, 384:512].reshape(2 * COLS, -1)
        context_back = to_low(dot_nt(low_a[...], out))
        query_sums, value_sums = [], []
        for side in range(2):
            query_sum = jnp.zeros((1, COLS), jnp.float32)
            value_sum = jnp.zeros((1, COLS), jnp.float32)
            for number_b in range(pairs):
                here = slice(number_b * LEN, (number_b + 1) * LEN)
                length = lengths[me * pairs + number_b]
                query, key, value = [
                    qkv[place, side, here, i * COLS : (i + 1) * COLS] for i in range(3)
                ]
                keys, values = two_heads(key), two_heads(value)
                scores = dot_nt(query, keys) * factor
                probs = masked_probs(scores, length)
                if student:
                    other = dot_nt(
                        qkv_t_buf[place, side, here, 0:COLS],
                        two_heads(qkv_t_buf[place, side, here, COLS : 2 * COLS]),
                    )
                    spot = lax.broadcasted_iota(jnp.int32, scores.shape, 1)
                    spot = jnp.where(spot < LEN, spot, spot - LEN)
                    line = lax.broadcasted_iota(jnp.int32, scores.shape, 0)
                    gap = score_weight * (scores - other * factor)
                    extra = jnp.where(jnp.maximum(spot, line) < length, gap, 0.0)
                    extra_buf[pair, side, number_b] = to_low(extra)
                else:
                    extra = -to_float(extra_buf[pair, side, number_b])
                part = context_back[here, side * COLS : (side + 1) * COLS]
                probs_back = dot_nt(part, values)
                value_back = pick(dot_tn(to_low(probs), part))
                product = probs * probs_back
                inner_sum = jnp.concatenate(
                    [
                        jnp.broadcast_to(
                            jnp.sum(product[:, i * LEN : (i + 1) * LEN], axis=1, keepdims=True), (LEN, LEN)
                        )
                        for i in range(2)
                    ],
                    axis=1,
                )
                score_back = to_low(product - probs * inner_sum + extra)
                query_back = dot(score_back, keys) * factor
                key_back = pick(dot_tn(score_back, query)) * factor
                start = side * 3 * COLS
                proj[here, start : start + COLS] = to_low(query_back)
                proj[here, start + COLS : start + 2 * COLS] = to_low(key_back)
                proj[here, start + 2 * COLS : start + 3 * COLS] = to_low(value_back)
                if student:
                    query_sum += jnp.sum(query_back, axis=0, keepdims=True)
                    value_sum += jnp.sum(value_back, axis=0, keepdims=True)
                if side * pairs + number_b < 2 * pairs - 1:
                    after(number, side * pairs + number_b)
            query_sums.append(query_sum)
            value_sums.append(value_sum)
        grad_in[...] += dot(proj[...], wide[place, :, 0:384].reshape(768, -1))
        if student:
            put_bias(pair, 0, jnp.concatenate(query_sums, axis=1))
            put_bias(pair, COLS, jnp.concatenate(value_sums, axis=1))
            qkv_grad = dot_tn(proj[...], x_ref[...])
            out_grad = dot_tn(context_buf[place], low_a[...])
            give(number, [(0, qkv_grad), (3 * COLS, out_grad)])

    def lower_grad():
        @pl.loop(0, rows // 64)
        def _(step):
            here = pl.ds(step * 64, 64)
            low_z[here] = to_low(grad_buf[here])

        total[...] = jnp.zeros_like(total)

    def norm_step(student):
        gain_ref = s_gain if student else t_gain

        @pl.loop(0, rows // 64)
        def _(step):
            here = pl.ds(step * 64, 64)
            grad = grad_buf[here] + total[here]
            unit = unit_buf[here]
            back = norm_back(grad, unit, inverse_buf[here], to_float(gain_ref[0:1]))
            low_a[here] = to_low(back)
            if student:
                grad_in[here] = back
                vec[8:9] += jnp.sum(back, axis=0, keepdims=True)
                vec[9:10] += jnp.sum(grad * unit, axis=0, keepdims=True)
                vec[10:11] += jnp.sum(grad, axis=0, keepdims=True)
            else:
                grad_in[here] += back

    actions = {
        "combine": combine,
        "fold": fold,
        "own": own_part,
        "mid": mid_part,
        "end": end_part,
        "vec": vec_add,
    }

    def after(number, part):
        for name, *which in SCHEDULE.get((number, part), ()):
            actions[name](*which)

    for copy in state(1):
        copy.start()
    low_copy = pltpu.make_async_copy(low_s, low_y, state_sem.at[3])
    low_copy.start()
    for copy in loads(0):
        copy.start()
    vec[...] = jnp.zeros_like(vec)
    vec[11:14] = vectors[0:3]
    for copy in state(1):
        copy.wait()
    low_copy.wait()
    lower_grad()
    for number, (kind, pack, pair) in enumerate(steps):
        for copy in loads(number):
            copy.wait()
        if number + 1 < len(steps):
            for copy in loads(number + 1):
                copy.start()
        if kind in ("fs", "ft"):
            ffn_step(number)
        else:
            attention_step(number)
        after(number, 6)
        if number == 7:
            norm_step(True)
            for copy in state(0):
                copy.start()
        elif number == 11:
            for copy in state(0):
                copy.wait()
            lower_grad()
            vec_copy(0).start()
        elif number == 19:
            norm_step(False)
        after(number, 7)
    for name, *which in LAST:
        actions[name](*which)
    for chunk in range(CHUNKS):
        finish(chunk)

    odd_copy(10).wait_send()
    odd_copy(11).wait_send()
    for chunk in range(CHUNKS):
        far_copy(chunk, 0).wait_send()
        far_copy(chunk, 1).wait_send()
        for part in range(PARTS[chunk]):
            for copy in plane_copies(chunk, part):
                copy.wait_send()

            @pl.when(outer)
            def _():
                z_copy(chunk, part, 0).wait_send()

            @pl.when(inner)
            def _():
                z_copy(chunk, part, 1).wait_send()
                z_copy(chunk, part, 2).wait_send()

        store_copy(chunk).wait()


def backward_both(lengths, tokens, kept, vectors, t_gain, s_gain):
    rows, features = tokens.shape
    low, full = jnp.bfloat16, jnp.float32
    vmem = pl.BlockSpec(memory_space=pltpu.VMEM)
    hbm = pl.BlockSpec(memory_space=pl.ANY)
    dma = pltpu.SemaphoreType.DMA
    block = (FFN_ROWS, features)
    return pl.pallas_call(
        backward_kernel,
        out_shape=[
            jax.ShapeDtypeStruct((rows, features), full),
            jax.ShapeDtypeStruct((CHUNKS,) + block, low),
            jax.ShapeDtypeStruct((16, features), full),
        ],
        in_specs=[pl.BlockSpec(memory_space=pltpu.SMEM), vmem] + [hbm] * len(kept) + [vmem] * 3,
        out_specs=[vmem, hbm, vmem],
        scratch_shapes=[
            pltpu.VMEM((2, 2) + block, low),
            pltpu.VMEM((2, rows, 2 * HALF_UNITS), low),
            pltpu.VMEM((2, rows, 2 * HALF_UNITS), low),
            pltpu.VMEM((2, 2, rows, 3 * COLS), low),
            pltpu.VMEM((2, 2, rows, 3 * COLS), low),
            pltpu.VMEM((2, rows, 2 * COLS), low),
            pltpu.VMEM((4, 2, rows // LEN, LEN, 2 * LEN), low),
            pltpu.VMEM((rows, features), full),
            pltpu.VMEM((rows, 1), full),
            pltpu.VMEM((rows, features), full),
            pltpu.VMEM((rows, features), full),
            pltpu.VMEM((rows, features), low),
            pltpu.VMEM((rows, features), low),
            pltpu.VMEM((rows, features), low),
            pltpu.VMEM((rows, 6 * COLS), low),
            pltpu.VMEM((CHUNKS,) + block, low),
            pltpu.VMEM((CHUNKS, 3) + block, low),
            pltpu.VMEM((2,) + block, low),
            pltpu.VMEM((4,) + block, low),
            pltpu.VMEM((CHUNKS,) + block, low),
            pltpu.VMEM((CHUNKS,) + block, low),
            pltpu.VMEM((CHUNKS,) + block, low),
            pltpu.VMEM((CHUNKS, 2) + block, low),
            pltpu.VMEM((5, 16, features), full),
            dma((2, 5)),
            dma((4,)),
            dma((2,)),
            dma((4,)),
            pltpu.SemaphoreType.REGULAR((4,)),
            dma((CHUNKS, 2)),
            dma((CHUNKS, 2)),
        ]
        + [dma((CHUNKS, max(PARTS)))] * 10
        + [dma((5,)), dma((5,)), dma((CHUNKS,))],
        compiler_params=pltpu.CompilerParams(
            collective_id=1, has_side_effects=True, vmem_limit_bytes=63 * 1024 * 1024
        ),
        name="backward_both",
    )(lengths, tokens, *kept, vectors, t_gain, s_gain)


def finish_kernel(sums, vec, qkv_out, qv_out, out_out, up_out, up_bias_out, down_out, bias_out, gain_out, shift_out):
    for i in range(3):
        qkv_out[i] = to_float(sums[2, i * COLS : (i + 1) * COLS]).T
    out_out[...] = to_float(sums[2, 3 * COLS :])
    for half in range(2):
        here = slice(half * HALF_UNITS, (half + 1) * HALF_UNITS)
        up_out[:, here] = to_float(sums[half, :HALF_UNITS]).T
        down_out[here] = to_float(sums[half, HALF_UNITS:])
    line = lax.broadcasted_iota(jnp.int32, (SLOTS, vec.shape[1]), 0)
    row = jnp.sum(jnp.where(line == lax.axis_index("mp"), vec[0:SLOTS], 0.0), axis=0, keepdims=True)
    qv_out[0:1] = row[:, :COLS]
    qv_out[1:2] = row[:, COLS : 2 * COLS]
    up_bias_out[...] = row[:, 2 * COLS : 2 * COLS + 2 * HALF_UNITS]
    for index, ref in enumerate((bias_out, gain_out, shift_out)):
        ref[0:1] = vec[8 + index : 9 + index]
        ref[1:2] = vec[11 + index : 12 + index]


def finish_sums(sums, vec):
    features = vec.shape[1]
    shapes = [
        (3, features, COLS),
        (2, COLS),
        (COLS, features),
        (features, 2 * HALF_UNITS),
        (1, 2 * HALF_UNITS),
        (2 * HALF_UNITS, features),
        (2, features),
        (2, features),
        (2, features),
    ]
    vmem = pl.BlockSpec(memory_space=pltpu.VMEM)
    return pl.pallas_call(
        finish_kernel,
        out_shape=[jax.ShapeDtypeStruct(shape, jnp.float32) for shape in shapes],
        in_specs=[vmem, vmem],
        out_specs=[vmem] * len(shapes),
        compiler_params=pltpu.CompilerParams(vmem_limit_bytes=48 * 1024 * 1024),
        name="finish_sums",
    )(sums, vec)


def cut(values, count, axis):
    return jnp.split(values, count, axis=axis)


def per_device(n_dp, n_mp, *args):
    (
        tokens,
        lengths,
        student_qkv,
        student_qv_bias,
        student_out,
        student_up,
        student_up_bias,
        student_down,
        student_out_bias,
        student_gain,
        student_shift,
        teacher_qkv,
        teacher_qv_bias,
        teacher_out,
        teacher_up,
        teacher_up_bias,
        teacher_down,
        teacher_out_bias,
        teacher_gain,
        teacher_shift,
    ) = args
    net = Cube(n_dp) if (n_dp, n_mp) == (4, 8) else Plain(n_mp)
    rows = tokens.shape[0]
    pairs = rows // LEN
    places = jnp.arange(LEN, dtype=jnp.int32)
    me = lax.axis_index("mp")
    own_lengths = lax.dynamic_slice_in_dim(lengths, me * pairs, pairs)
    valid = places[None, :] < own_lengths[:, None]
    token_valid = to_float(valid.reshape(rows, 1))
    pair_valid = valid[:, None, :, None] & valid[:, None, None, :]

    gain = to_float(student_gain)
    shift = to_float(student_shift)
    out_bias = to_float(student_out_bias)
    teach_gain = to_float(teacher_gain)
    if isinstance(net, Cube):
        gathered, kept, grad_t, grad_s, student_output, vecs = forward_both(
            lengths,
            tokens,
            (
                [teacher_qkv.transpose(1, 0, 2), teacher_out, teacher_up, teacher_down],
                [teacher_qv_bias, teacher_up_bias.reshape(1, -1), teacher_out_bias, teacher_gain, teacher_shift],
            ),
            (
                [student_qkv.transpose(1, 0, 2), student_out, student_up, student_down],
                [student_qv_bias, student_up_bias.reshape(1, -1), student_out_bias, student_gain, student_shift],
            ),
        )
        input_grad, sums, vec = backward_both(
            lengths, tokens, (gathered, *kept, grad_t, grad_s), vecs, teacher_gain, student_gain
        )
        grads = finish_sums(sums, vec)
        return (
            student_output,
            input_grad,
            grads[0].transpose(1, 0, 2),
            grads[1],
            grads[2],
            grads[3],
            grads[4].reshape(-1),
            *grads[5:],
        )
    else:
        teach = gather_layer(
            net, teacher_qkv, teacher_qv_bias, teacher_out, teacher_up, teacher_up_bias, teacher_down
        )
        stud = gather_layer(
            net,
            binarize(student_qkv, 0),
            student_qv_bias,
            binarize(student_out, 1),
            binarize(student_up, 0),
            student_up_bias,
            binarize(student_down, 1),
        )
        teach_final, teach_kept = forward(
            tokens, teach, to_float(teacher_out_bias), teach_gain, to_float(teacher_shift), plain_act, valid
        )
        final, kept = forward(tokens, stud, out_bias, gain, shift, clipped_act, valid)
        student_output = to_low(final)
        final_grad = token_valid * (final - teach_final)
        grad_s = norm_back(final_grad, kept[11], kept[12], gain[1])
        grad_t = norm_back(-final_grad, teach_kept[11], teach_kept[12], teach_gain[1])
        vecs = jnp.stack([jnp.sum(grad_s, axis=0), jnp.sum(final_grad * kept[11], axis=0), jnp.sum(final_grad, axis=0)])
    extra = score_weight * jnp.where(pair_valid, kept[3] - teach_kept[3], 0.0)

    second_grad, second_low, pre_grad, pre_low, normed_grad, first_grad = backward_ffn(
        kept, stud, grad_s, gain
    )
    hidden, normed_low, context = kept[9], kept[8], kept[5]
    unit_one = kept[6]
    down_grad = net.sum_dp(net.scatter(cut(to_low(dot_tn(hidden, second_low)), n_mp, 0)))
    up_grad = net.sum_dp(net.scatter(cut(to_low(dot_tn(normed_low, pre_low)), n_mp, 1)))
    first_low = to_low(first_grad)
    out_grad = net.sum_dp(net.scatter(cut(to_low(dot_tn(context, first_low)), n_mp, 0)))
    grads = backward_attention(kept, first_low, stud[3], extra)
    lows = [to_low(item) for item in grads]
    wide = jnp.concatenate(
        [to_low(dot_tn(tokens, item)) for item in lows], axis=0
    )
    qkv_grad = net.sum_dp(net.scatter(cut(wide, n_mp, 1)))
    features = tokens.shape[1]
    qkv_grad = qkv_grad.reshape(3, features, -1).transpose(1, 0, 2)

    teach_second, teach_slow, _, _, _, teach_first = backward_ffn(
        teach_kept, teach, grad_t, teach_gain
    )
    teach_grads = backward_attention(teach_kept, to_low(teach_first), teach[3], -extra)
    teach_lows = [to_low(item) for item in teach_grads]
    input_grad = first_grad + teach_first
    for item, matrix in zip(lows, stud[0]):
        input_grad = input_grad + dot_nt(item, matrix)
    for item, matrix in zip(teach_lows, teach[0]):
        input_grad = input_grad + dot_nt(item, matrix)

    vectors = [
        jnp.sum(first_grad, axis=0),
        vecs[0],
        jnp.sum(normed_grad * unit_one, axis=0),
        vecs[1],
        jnp.sum(normed_grad, axis=0),
        vecs[2],
        net.place(jnp.sum(grads[0], axis=0).reshape(n_mp, -1)).reshape(-1),
        net.place(jnp.sum(grads[2], axis=0).reshape(n_mp, -1)).reshape(-1),
    ]
    wide_vector = net.place(jnp.sum(pre_grad, axis=0).reshape(n_mp, -1)).reshape(-1, features)
    total = net.sum_all(jnp.concatenate([jnp.stack(vectors), wide_vector], axis=0))
    width = features // n_mp
    units = wide_vector.size // n_mp
    return (
        student_output,
        input_grad,
        qkv_grad,
        lax.dynamic_slice_in_dim(total[6:8], me * width, width, axis=1),
        out_grad,
        up_grad,
        lax.dynamic_slice_in_dim(total[8:].reshape(-1), me * units, units),
        down_grad,
        total[0:2],
        total[2:4],
        total[4:6],
    )


def solution(mesh):
    n_dp, n_mp = mesh.shape["dp"], mesh.shape["mp"]

    def body(*args):
        return per_device(n_dp, n_mp, *args)

    return jax.shard_map(
        body,
        mesh=mesh,
        in_specs=(
            P(("dp", "mp"), None),
            P("dp"),
            P(None, None, "mp"),
            P(None, "mp"),
            P("mp", None),
            P(None, "mp"),
            P("mp"),
            P("mp", None),
            P(),
            P(),
            P(),
            P(None, None, "mp"),
            P(None, "mp"),
            P("mp", None),
            P(None, "mp"),
            P("mp"),
            P("mp", None),
            P(),
            P(),
            P(),
        ),
        out_specs=(
            P(("dp", "mp"), None),
            P(("dp", "mp"), None),
            P(None, None, "mp"),
            P(None, "mp"),
            P("mp", None),
            P(None, "mp"),
            P("mp"),
            P("mp", None),
            P(),
            P(),
            P(),
        ),
        check_vma=False,
    )
```

```python
import math

import jax
import jax.numpy as jnp
from jax import lax
from jax.experimental import pallas as pl
from jax.experimental.pallas import tpu as pltpu
from jax.sharding import PartitionSpec as P

DH = 64
LEN = 128


norm_epsilon = 1e-06
clip_level = 2.5
score_weight = 0.05
masked_fill = -1000000000.0


def to_float(values):
    return values.astype(jnp.float32)


def to_low(values):
    return values.astype(jnp.bfloat16)


def binarize(matrix, axis_index):
    scaling = jnp.mean(jnp.abs(matrix), axis=axis_index, keepdims=True)
    return (scaling * jnp.sign(matrix)).astype(jnp.bfloat16)


def norm_stats(values):
    centred = values - jnp.mean(values, axis=-1, keepdims=True)
    variance = jnp.mean(centred * centred, axis=-1, keepdims=True)
    inverse = lax.rsqrt(variance + norm_epsilon)
    return (centred * inverse, inverse)


def norm_back(grad, unit, inverse, gain_row):
    scaled = grad * gain_row
    first = jnp.mean(scaled, axis=-1, keepdims=True)
    second = jnp.mean(scaled * unit, axis=-1, keepdims=True)
    return inverse * (scaled - first - unit * second)


def dot(left, right):
    return jnp.dot(left, right, preferred_element_type=jnp.float32)


def dot_nt(left, right):
    return lax.dot_general(left, right, (((1,), (1,)), ((), ())), preferred_element_type=jnp.float32)


def dot_tn(left, right):
    return lax.dot_general(left, right, (((0,), (0,)), ((), ())), preferred_element_type=jnp.float32)


class Cube:
    def __init__(self, n_dp):
        self.n_dp = n_dp
        self.axes = ("dp", "mp")

    def flip(self, values, bits):
        pairs = [
            (z * 8 + m, z * 8 + (m ^ bits)) for z in range(self.n_dp) for m in range(8)
        ]
        return lax.ppermute(values, self.axes, pairs)

    def flip_dp(self, values, bits):
        pairs = [
            (z * 8 + m, (z ^ bits) * 8 + m) for z in range(self.n_dp) for m in range(8)
        ]
        return lax.ppermute(values, self.axes, pairs)

    def gather(self, block):
        half = block.shape[0] // 2
        along_x = self.flip(block, 2)
        along_y = self.flip(block, 4)
        across = jnp.concatenate(
            [self.flip(along_y[:half], 2), self.flip(along_x[half:], 4)], axis=0
        )
        same = [block, along_x, along_y, across]
        other = [self.flip(item, 1) for item in same]
        return [item for pair in zip(same, other) for item in pair]

    def scatter(self, blocks):
        half = blocks[0].shape[0] // 2
        own, to_x, to_y, to_far = [
            to_float(blocks[k]) + to_float(self.flip(blocks[k + 1], 1)) for k in (0, 2, 4, 6)
        ]
        far = to_low(to_far)
        via_x = to_float(self.flip(far[:half], 2))
        via_y = to_float(self.flip(far[half:], 4))
        to_y = to_low(jnp.concatenate([to_y[:half] + via_x, to_y[half:]], axis=0))
        to_x = to_low(jnp.concatenate([to_x[:half], to_x[half:] + via_y], axis=0))
        return own + to_float(self.flip(to_x, 2)) + to_float(self.flip(to_y, 4))

    def sum_dp(self, values):
        half = values.shape[0] // 2
        odd = lax.axis_index("dp") % 2
        low = to_low(values)
        sent = lax.dynamic_slice_in_dim(low, (1 - odd) * half, half)
        kept = lax.dynamic_slice_in_dim(values, odd * half, half)
        kept = kept + to_float(self.flip_dp(sent, 1))
        kept_low = to_low(kept)
        kept = to_low(kept + to_float(self.flip_dp(kept_low, 2)))
        other = self.flip_dp(kept, 1)
        return to_float(
            jnp.concatenate(
                [jnp.where(odd == 0, kept, other), jnp.where(odd == 0, other, kept)], axis=0
            )
        )

    def sum_all(self, values):
        for bits in (1, 2, 4):
            values = values + self.flip(values, bits)
        for bits in (1, 2):
            values = values + self.flip_dp(values, bits)
        return values

    def place(self, values):
        me = lax.axis_index("mp")
        for bit in range(3):
            shape = values.shape
            split = values.reshape((8 >> (bit + 1), 2, 1 << bit) + shape[1:])
            flipped = split[:, ::-1]
            values = jnp.where((me >> bit) % 2 == 1, flipped, split).reshape(shape)
        return values


class Plain:
    def __init__(self, n_mp):
        self.n_mp = n_mp

    def gather(self, block):
        every = lax.all_gather(block, "mp", axis=0)
        return [every[k] for k in range(self.n_mp)]

    def scatter(self, blocks):
        return to_float(
            lax.psum_scatter(jnp.stack(blocks), "mp", scatter_dimension=0, tiled=False)
        )

    def sum_dp(self, values):
        return to_float(lax.psum(to_low(values), "dp"))

    def sum_all(self, values):
        return lax.psum(values, ("dp", "mp"))

    def place(self, values):
        return values


def plain_act(pre):
    gate = 0.5 * (1.0 + lax.erf(pre * math.sqrt(0.5)))
    slope = gate + pre * jnp.exp(-0.5 * pre * pre) * (1.0 / math.sqrt(2.0 * math.pi))
    return (pre * gate, slope)


def clipped_act(pre):
    value, slope = plain_act(pre)
    bent = jnp.tanh(value * (1.0 / clip_level))
    return (clip_level * bent, slope * (1.0 - bent * bent))


def gather_layer(net, qkv, qv_bias, out, up, up_bias, down):
    width = qkv.shape[2]
    units = up.shape[1]
    features = qkv.shape[0]
    extra = jnp.zeros((16, features), jnp.bfloat16)
    extra = extra.at[0, :width].set(qv_bias[0]).at[1, :width].set(qv_bias[1])
    extra = extra.at[2, :units].set(up_bias)
    qkv_parts = net.gather(qkv.transpose(1, 0, 2).reshape(3 * features, width))
    out_parts = net.gather(jnp.concatenate([out, extra], axis=0))
    up_parts = net.gather(up)
    down_parts = net.gather(down)
    count = len(qkv_parts)
    qkv_full = jnp.concatenate(
        [part.reshape(3, features, width) for part in qkv_parts], axis=2
    )
    out_full = jnp.concatenate([part[:width] for part in out_parts], axis=0)
    q_bias = jnp.concatenate([part[width, :width] for part in out_parts])
    v_bias = jnp.concatenate([part[width + 1, :width] for part in out_parts])
    up_b = jnp.concatenate([part[width + 2, :units] for part in out_parts])
    up_full = jnp.concatenate(up_parts, axis=1)
    down_full = jnp.concatenate(down_parts, axis=0)
    return (qkv_full, to_float(q_bias), to_float(v_bias), out_full, up_full, to_float(up_b), down_full)


def forward(tokens, weights, out_bias, gain, shift, activation, key_valid):
    qkv, q_bias, v_bias, out, up, up_bias, down = weights
    rows, features = tokens.shape
    pairs = rows // LEN
    shape = (pairs, LEN, features // DH, DH)
    query = to_low(dot(tokens, qkv[0]) + q_bias).reshape(shape)
    key = to_low(dot(tokens, qkv[1])).reshape(shape)
    value = to_low(dot(tokens, qkv[2]) + v_bias).reshape(shape)
    scores = jnp.einsum("bqhe,bkhe->bhqk", query, key, preferred_element_type=jnp.float32) * (
        1.0 / math.sqrt(DH)
    )
    masked = jnp.where(key_valid[:, None, None, :], scores, masked_fill)
    log_norm = jax.nn.logsumexp(masked, axis=-1, keepdims=True)
    attention = jnp.exp(masked - log_norm)
    context = jnp.einsum(
        "bhqk,bkhe->bqhe", to_low(attention), value, preferred_element_type=jnp.float32
    )
    context = to_low(context).reshape(rows, features)
    first = to_float(tokens) + dot(context, out) + out_bias[0]
    unit_one, inverse_one = norm_stats(first)
    normed = unit_one * gain[0] + shift[0]
    normed_low = to_low(normed)
    hidden, slope = activation(dot(normed_low, up) + up_bias)
    hidden = to_low(hidden)
    second = normed + dot(hidden, down) + out_bias[1]
    unit_two, inverse_two = norm_stats(second)
    final = unit_two * gain[1] + shift[1]
    kept = (query, key, value, scores, attention, context, unit_one, inverse_one, normed_low, hidden,
            to_low(slope), unit_two, inverse_two)
    return (final, kept)


def backward_ffn(kept, weights, second_grad, gain):
    qkv, q_bias, v_bias, out, up, up_bias, down = weights
    (query, key, value, scores, attention, context, unit_one, inverse_one, normed_low, hidden,
     slope, unit_two, inverse_two) = kept
    second_low = to_low(second_grad)
    pre_grad = dot_nt(second_low, down) * slope
    pre_low = to_low(pre_grad)
    normed_grad = second_grad + dot_nt(pre_low, up)
    first_grad = norm_back(normed_grad, unit_one, inverse_one, gain[0])
    return (second_grad, second_low, pre_grad, pre_low, normed_grad, first_grad)


def backward_attention(kept, first_low, out, extra):
    query, key, value, scores, attention = kept[:5]
    rows = first_low.shape[0]
    factor = 1.0 / math.sqrt(DH)
    context_grad = to_low(dot_nt(first_low, out)).reshape(query.shape)
    attention_grad = jnp.einsum(
        "bqhe,bkhe->bhqk", context_grad, value, preferred_element_type=jnp.float32
    )
    value_grad = jnp.einsum(
        "bhqk,bqhe->bkhe", to_low(attention), context_grad, preferred_element_type=jnp.float32
    )
    inner = jnp.sum(attention * attention_grad, axis=-1, keepdims=True)
    score_low = to_low(attention * (attention_grad - inner) + extra)
    query_grad = factor * jnp.einsum(
        "bhqk,bkhe->bqhe", score_low, key, preferred_element_type=jnp.float32
    )
    key_grad = factor * jnp.einsum(
        "bhqk,bqhe->bkhe", score_low, query, preferred_element_type=jnp.float32
    )
    return [item.reshape(rows, -1) for item in (query_grad, key_grad, value_grad)]


MESH = pl.DeviceIdType.MESH
SLOTS = 8
PACKS = 6
ATT_ROWS = 528
FFN_ROWS = 512
HALF_UNITS = 256
COLS = 128

SHARED = (240, 240, 96, 192, 176, 0)
FORWARD = [
    ("prepare", 0), ("meet",), ("first", 0), ("prepare", 1), ("first", 1), ("prepare", 2), ("prepare", 3), ("prepare", 4),
    ("prepare", 5), ("load", 0, 0), ("load", 1, 0), ("pair", 0, 0), ("pair", 1, 0), ("second", 0), ("first", 2),
    ("second", 1), ("first", 3), ("plane_swap", 0), ("far_sends", 0), ("load", 0, 1), ("load", 0, 2),
    ("pair", 0, 1), ("pair", 0, 2), ("second", 2), ("first", 4), ("plane_swap", 1), ("far_sends", 1),
    ("load", 1, 1), ("load", 1, 2), ("pair", 1, 1), ("pair", 1, 2), ("far_swap", 0), ("load", 0, 3), ("pair", 0, 3),
    ("end", 0), ("second", 3), ("first", 5), ("plane_swap", 2), ("load", 2, 0), ("load", 3, 0), ("pair", 2, 0),
    ("far_sends", 2), ("load", 2, 1), ("pair", 3, 0), ("load", 2, 2), ("pair", 2, 1), ("pair", 2, 2),
    ("far_swap", 1), ("load", 1, 3), ("pair", 1, 3), ("end", 1), ("second", 4), ("load", 4, 0), ("load", 5, 0),
    ("pair", 4, 0), ("pair", 5, 0), ("plane_swap", 3), ("far_sends", 3), ("load", 3, 1), ("load", 3, 2),
    ("pair", 3, 1), ("far_swap", 2), ("pair", 3, 2), ("load", 2, 3), ("pair", 2, 3), ("plane_swap", 4),
    ("second", 5), ("plane_swap", 5), ("load", 4, 1), ("load", 4, 2), ("pair", 4, 1), ("load", 5, 1),
    ("pair", 4, 2), ("far_swap", 3), ("far_sends", 4), ("load", 5, 2), ("pair", 5, 1), ("load", 3, 3),
    ("pair", 5, 2), ("pair", 3, 3), ("end", 3), ("far_swap", 4), ("far_sends", 5), ("far_swap", 5), ("load", 4, 3),
    ("load", 5, 3), ("pair", 4, 3), ("pair", 5, 3),
]


def flipped(me, bits):
    return me + bits - 2 * bits * lax.rem(lax.div(me, bits), 2)


def pack_rows(pack):
    return ATT_ROWS if pack < 2 else FFN_ROWS


def masked_probs(scores, length):
    rows = scores.shape[0]
    position = lax.broadcasted_iota(jnp.int32, (rows, LEN), 1)
    parts = []
    for head in range(2):
        part = jnp.where(position < length, scores[:, head * LEN : (head + 1) * LEN], masked_fill)
        part = jnp.exp(part - jnp.max(part, axis=1, keepdims=True))
        parts.append(part / jnp.sum(part, axis=1, keepdims=True))
    return jnp.concatenate(parts, axis=1)


def two_heads(rows):
    first = lax.broadcasted_iota(jnp.int32, rows.shape, 1) < DH
    zero = jnp.zeros_like(rows)
    return jnp.concatenate([jnp.where(first, rows, zero), jnp.where(first, zero, rows)], axis=0)


def norm_block(values):
    centred = values - jnp.mean(values, axis=1, keepdims=True)
    inverse = lax.rsqrt(jnp.mean(centred * centred, axis=1, keepdims=True) + norm_epsilon)
    return (centred * inverse, inverse)


def forward_kernel(
    lengths,
    x_ref,
    t_weights,
    t_small,
    s_weights,
    s_small,
    gathered,
    kept,
    vectors,
    scratch,
    raw_t,
    raw_s,
    mine_att,
    mine_ffn,
    wide,
    total,
    normed,
    low_t,
    context_t,
    bias_rows,
    final_t,
    unit_two,
    inverse_two,
    send,
    recv,
    load,
    fetch,
    save,
):
    t_qv_bias, t_up_bias, t_bias, t_gain, t_shift = t_small
    s_qv_bias, s_up_bias, s_bias, s_gain, s_shift = s_small
    (qkv_t, qkv_s, context_s, slope_t, slope_s, hidden_s, unit_t, inverse_t, unit_s, inverse_s, low_s,
     grad_t, grad_s, final_low) = scratch
    saved = []

    def put(name, index=None):
        src, dst = scratch[name], kept[name]
        if index is not None:
            src, dst = src.at[index], dst.at[index]
        saved.append(pltpu.make_async_copy(src, dst, save.at[len(saved)]))
        saved[-1].start()

    me = lax.axis_index("mp")
    z = lax.axis_index("dp")
    peers = {bits: {"mp": flipped(me, bits)} for bits in (1, 2, 4)}
    peers["z"] = {"dp": flipped(z, 1)}
    upper = lax.rem(z, 2)
    rows = x_ref.shape[0]
    pairs = rows // LEN

    barrier = pltpu.get_barrier_semaphore()
    for peer in peers.values():
        pl.semaphore_signal(barrier, inc=1, device_id=peer, device_id_type=MESH)

    fetched = []
    for weights, raw, direct in ((t_weights, raw_t, True), (s_weights, raw_s, False)):
        qkv, out, up, down = weights
        moves = [(qkv, raw[0]), (up, raw[1])]
        if direct:
            moves.append((out, mine_att.at[0, pl.ds(3 * COLS, COLS)]))
            moves += [
                (down.at[pl.ds(h * HALF_UNITS, HALF_UNITS)], mine_ffn.at[h, pl.ds(HALF_UNITS, HALF_UNITS)])
                for h in range(2)
            ]
        else:
            moves += [(out, raw[2]), (down, raw[3])]
        for src, dst in moves:
            fetched.append(pltpu.make_async_copy(src, dst, fetch.at[len(fetched)]))
            fetched[-1].start()

    def signed(values, axis):
        scale = jnp.mean(jnp.abs(values), axis=axis, keepdims=True)
        return to_low(jnp.where(values > 0, scale, jnp.where(values < 0, -scale, 0.0)))

    def bias_block(qv_bias, up_bias):
        line = jnp.concatenate(
            [
                to_float(qv_bias[0:1]),
                to_float(qv_bias[1:2]),
                to_float(up_bias[...]).reshape(1, -1),
                jnp.zeros((1, x_ref.shape[1] - 2 * COLS - 2 * HALF_UNITS), jnp.float32),
            ],
            axis=1,
        )
        row = lax.broadcasted_iota(jnp.int32, (16, line.shape[1]), 0)
        return to_low(jnp.where(row == 0, jnp.broadcast_to(line, row.shape), 0.0))

    def own_copy(pack):
        return pltpu.make_async_copy(source(pack), block(pack, 0), fetch.at[9 + pack])

    def prepare(pack):
        if pack == 0:
            fetched[0].wait()
            for i in range(3):
                mine_att[0, i * COLS : (i + 1) * COLS] = raw_t[0][i].T
            mine_att[0, 4 * COLS : 4 * COLS + 16] = bias_block(t_qv_bias, t_up_bias)
            fetched[2].wait()
        elif pack == 1:
            fetched[5].wait()
            for i in range(3):
                mine_att[1, i * COLS : (i + 1) * COLS] = signed(raw_s[0][i], 0).T
            mine_att[1, 4 * COLS : 4 * COLS + 16] = bias_block(s_qv_bias, s_up_bias)
            fetched[7].wait()
            mine_att[1, 3 * COLS : 4 * COLS] = signed(raw_s[2][...], 1)
        else:
            layer, half = divmod(pack - 2, 2)
            here = slice(half * HALF_UNITS, (half + 1) * HALF_UNITS)
            if half == 0:
                fetched[(1, 6)[layer]].wait()
            if layer == 0:
                mine_ffn[half, 0:HALF_UNITS] = raw_t[1][:, here].T
                fetched[3 + half].wait()
            else:
                mine_ffn[2 + half, 0:HALF_UNITS] = signed(raw_s[1][:, here], 0).T
                if half == 0:
                    fetched[8].wait()
                mine_ffn[2 + half, HALF_UNITS : 2 * HALF_UNITS] = signed(raw_s[3][here], 1)
        own_copy(pack).start()

    def source(pack):
        return mine_att.at[pack] if pack < 2 else mine_ffn.at[pack - 2]

    def span(pack, start, count):
        return pl.ds(pl.multiple_of(start, 16), count)

    def block(pack, slot):
        return gathered.at[pack, slot, pl.ds(0, pack_rows(pack))]

    def remote(pack, kind):
        shared = SHARED[pack]
        rest = pack_rows(pack) - shared
        first = (rest // 2 + 15) // 16 * 16
        low = upper * shared
        if kind == 0 or kind == 1:
            here = span(pack, low, rest)
            src, dst = source(pack).at[here], gathered.at[pack, 2 + 2 * kind, here]
            peer = peers[2 + 2 * kind]
        elif kind == 2:
            here = span(pack, low, first)
            src, dst, peer = gathered.at[pack, 4, here], gathered.at[pack, 6, here], peers[2]
        elif kind == 3:
            here = span(pack, low + first, rest - first)
            src, dst, peer = gathered.at[pack, 2, here], gathered.at[pack, 6, here], peers[4]
        elif kind == 4:
            src, dst, peer = source(pack), block(pack, 1), peers[1]
        elif kind < 8:
            slot = 2 * (kind - 4)
            src, dst, peer = block(pack, slot), block(pack, slot + 1), peers[1]
        else:
            here = span(pack, upper * rest, shared)
            slot = 2 * (kind - 7)
            src, dst, peer = gathered.at[pack, slot, here], gathered.at[pack, slot, here], peers["z"]
        return pltpu.make_async_remote_copy(
            src_ref=src,
            dst_ref=dst,
            send_sem=send.at[pack, kind],
            recv_sem=recv.at[pack, kind],
            device_id=peer,
            device_id_type=MESH,
        )

    def first_sends(pack):
        for kind in (0, 1, 4):
            remote(pack, kind).start()

    def second_sends(pack):
        remote(pack, 0).wait_recv()
        remote(pack, 3).start()
        if SHARED[pack]:
            remote(pack, 8).start()
        remote(pack, 1).wait_recv()
        remote(pack, 2).start()
        if SHARED[pack]:
            remote(pack, 9).start()

    def plane_swap(pack):
        for kind in (0, 1):
            if SHARED[pack]:
                remote(pack, 8 + kind).wait_recv()
            remote(pack, 5 + kind).start()

    def far_sends(pack):
        remote(pack, 2).wait_recv()
        remote(pack, 3).wait_recv()
        if SHARED[pack]:
            remote(pack, 10).start()

    def far_swap(pack):
        if SHARED[pack]:
            remote(pack, 10).wait_recv()
        remote(pack, 7).start()

    places = {}

    def load_copy(pack, pair):
        here = pl.ds(0, pack_rows(pack))
        place = places[pack, pair]
        return pltpu.make_async_copy(
            gathered.at[pack, pl.ds(2 * pair, 2), here], wide.at[place, :, here], load.at[place]
        )

    def load_pair(pack, pair):
        places[pack, pair] = len(places) % 2
        if pair == 0:
            own_copy(pack).wait()
        remote(pack, 4 + pair).wait_recv()
        load_copy(pack, pair).start()

    started = set()

    def add_total(layer, kind, values):
        if (layer, kind) in started:
            total[layer] += values
        else:
            total[layer] = values
        started.add((layer, kind))

    def attention(pack, pair, place, qkv_ref, context_ref):
        weights = wide[place, :, 0:384].reshape(768, -1)
        projected = dot_nt(x_ref[...], weights)
        for side in range(2):
            slot = 2 * pair + side
            bias = wide[place, side, 512:528]
            bias_rows[pack, slot] = bias
            bias = to_float(bias[0:1])
            part = projected[:, side * 384 : side * 384 + 384]
            query = to_low(part[:, :COLS] + bias[:, :COLS])
            key = to_low(part[:, COLS : 2 * COLS])
            value = to_low(part[:, 2 * COLS :] + bias[:, COLS : 2 * COLS])
            qkv_ref[slot, :, 0:COLS] = query
            qkv_ref[slot, :, COLS : 2 * COLS] = key
            qkv_ref[slot, :, 2 * COLS : 3 * COLS] = value
            for number in range(pairs):
                here = slice(number * LEN, (number + 1) * LEN)
                scores = dot_nt(query[here], two_heads(key[here])) * (1.0 / math.sqrt(DH))
                probs = masked_probs(scores, lengths[me * pairs + number])
                part_context = dot(to_low(probs), two_heads(value[here]))
                context_ref[pair, here, side * COLS : (side + 1) * COLS] = to_low(part_context)
        put(pack, pl.ds(2 * pair, 2))
        if pack == 1:
            put(2, pair)
        add_total(pack, 0, dot(context_ref[pair], wide[place, :, 384:512].reshape(256, -1)))

    def first_norm(bias_ref, gain_ref, shift_ref, unit_ref, inverse_ref, index, low_ref):
        @pl.loop(0, rows // 64)
        def _(step):
            here = pl.ds(step * 64, 64)
            values = to_float(x_ref[here]) + total[index, here] + to_float(bias_ref[0:1])
            unit, inverse = norm_block(values)
            unit_ref[here] = unit
            inverse_ref[here] = inverse
            values = unit * to_float(gain_ref[0:1]) + to_float(shift_ref[0:1])
            normed[index, here] = values
            low_ref[here] = to_low(values)

    def feed_forward(pack, pair, place, low_ref, activation, hidden_ref, slope_ref):
        layer, half = divmod(pack - 2, 2)
        up = wide[place, :, 0:HALF_UNITS].reshape(2 * HALF_UNITS, -1)
        down = wide[place, :, HALF_UNITS : 2 * HALF_UNITS].reshape(2 * HALF_UNITS, -1)
        start = 2 * COLS + half * HALF_UNITS
        bias = jnp.concatenate(
            [
                to_float(bias_rows[layer, 2 * pair + side, 0:1, start : start + HALF_UNITS])
                for side in range(2)
            ],
            axis=1,
        )
        hidden, slope = activation(dot_nt(low_ref[...], up) + bias)
        hidden = to_low(hidden)
        slope_ref[half, pair] = to_low(slope)
        put(3 + layer, (half, pair))
        if hidden_ref is not None:
            hidden_ref[half, pair] = hidden
            put(5, (half, pair))
        add_total(layer, 1, dot(hidden, down))

    def step_teacher_end():
        @pl.loop(0, rows // 64)
        def _(step):
            here = pl.ds(step * 64, 64)
            unit, inverse = norm_block(normed[0, here] + total[0, here] + to_float(t_bias[1:2]))
            unit_two[here] = unit
            inverse_two[here] = inverse
            final_t[here] = unit * to_float(t_gain[1:2]) + to_float(t_shift[1:2])

    def step_student_end():
        vectors[...] = jnp.zeros_like(vectors)
        for step in range(rows // 64):
            here = pl.ds(step * 64, 64)
            unit, inverse = norm_block(normed[1, here] + total[1, here] + to_float(s_bias[1:2]))
            gain = to_float(s_gain[1:2])
            final = unit * gain + to_float(s_shift[1:2])
            final_low[here] = to_low(final)
            position = lax.broadcasted_iota(jnp.int32, (64, 1), 0) + step % 2 * 64
            valid = position < lengths[me * pairs + step // 2]
            grad = jnp.where(valid, final - final_t[here], 0.0)
            back = norm_back(grad, unit, inverse, gain)
            grad_s[here] = back
            grad_t[here] = norm_back(
                -grad, unit_two[here], inverse_two[here], to_float(t_gain[1:2])
            )
            for name in (11, 12, 13):
                put(name, here)
            vectors[0:1] += jnp.sum(back, axis=0, keepdims=True)
            vectors[1:2] += jnp.sum(grad * unit, axis=0, keepdims=True)
            vectors[2:3] += jnp.sum(grad, axis=0, keepdims=True)

    def use(pack, pair):
        place = places[pack, pair]
        load_copy(pack, pair).wait()
        if pack == 0:
            attention(0, pair, place, qkv_t, context_t)
        elif pack == 1:
            attention(1, pair, place, qkv_s, context_s)
        elif pack < 4:
            feed_forward(pack, pair, place, low_t, plain_act, None, slope_t)
        else:
            feed_forward(pack, pair, place, low_s, clipped_act, hidden_s, slope_s)

    def end(pack):
        if pack == 0:
            first_norm(t_bias, t_gain, t_shift, unit_t, inverse_t, 0, low_t)
            put(6)
            put(7)
        elif pack == 1:
            first_norm(s_bias, s_gain, s_shift, unit_s, inverse_s, 1, low_s)
            for name in (8, 9, 10):
                put(name)
        elif pack == 3:
            step_teacher_end()

    def meet():
        pl.semaphore_wait(barrier, len(peers))

    actions = {
        "meet": meet,
        "prepare": prepare,
        "first": first_sends,
        "second": second_sends,
        "plane_swap": plane_swap,
        "far_sends": far_sends,
        "far_swap": far_swap,
        "load": load_pair,
        "pair": use,
        "end": end,
    }
    for name, *which in FORWARD:
        actions[name](*which)
    step_student_end()
    for pack in range(PACKS):
        for kind in range(11 if SHARED[pack] else 8):
            remote(pack, kind).wait_send()
    for copy in saved:
        copy.wait()


def forward_both(lengths, tokens, teacher, student):
    rows, features = tokens.shape
    low, full = jnp.bfloat16, jnp.float32
    vmem = pl.BlockSpec(memory_space=pltpu.VMEM)
    hbm = pl.BlockSpec(memory_space=pl.ANY)
    dma = pltpu.SemaphoreType.DMA
    act = (2, 4, rows, 2 * HALF_UNITS)
    kept = [
        ((SLOTS, rows, 3 * COLS), low),
        ((SLOTS, rows, 3 * COLS), low),
        ((4, rows, 2 * COLS), low),
        (act, low),
        (act, low),
        (act, low),
        ((rows, features), full),
        ((rows, 1), full),
        ((rows, features), full),
        ((rows, 1), full),
        ((rows, features), low),
        ((rows, features), full),
        ((rows, features), full),
        ((rows, features), low),
    ]
    shapes = [jax.ShapeDtypeStruct(shape, kind) for shape, kind in kept]
    qkv, out, up, down = teacher[0]
    return pl.pallas_call(
        forward_kernel,
        out_shape=[
            jax.ShapeDtypeStruct((PACKS, SLOTS, ATT_ROWS, features), low),
            shapes,
            jax.ShapeDtypeStruct((8, features), full),
        ],
        in_specs=[pl.BlockSpec(memory_space=pltpu.SMEM), vmem] + [[hbm] * 4, [vmem] * 5] * 2,
        out_specs=[hbm, [hbm] * len(kept), vmem],
        scratch_shapes=[
            [pltpu.VMEM(shape, kind) for shape, kind in kept],
            [pltpu.VMEM(qkv.shape, low), pltpu.VMEM(up.shape, low)],
            [pltpu.VMEM(item.shape, full) for item in (qkv, up, out, down)],
            pltpu.VMEM((2, ATT_ROWS, features), low),
            pltpu.VMEM((4, FFN_ROWS, features), low),
            pltpu.VMEM((2, 2, ATT_ROWS, features), low),
            pltpu.VMEM((2, rows, features), full),
            pltpu.VMEM((2, rows, features), full),
            pltpu.VMEM((rows, features), low),
            pltpu.VMEM((4, rows, 2 * COLS), low),
            pltpu.VMEM((2, SLOTS, 16, features), low),
            pltpu.VMEM((rows, features), full),
            pltpu.VMEM((rows, features), full),
            pltpu.VMEM((rows, 1), full),
            dma((PACKS, 11)),
            dma((PACKS, 11)),
            dma((2,)),
            dma((9 + PACKS,)),
            dma((64,)),
        ],
        compiler_params=pltpu.CompilerParams(
            collective_id=0, has_side_effects=True, vmem_limit_bytes=62 * 1024 * 1024
        ),
        name="forward_both",
    )(lengths, tokens, *teacher, *student)


CHUNKS = 3
PARTS = (4, 4, 8)
ORDER = (3, 1, 2, 0)

SCHEDULE = {
    (1, 6): [("combine", 0, 3)],
    (2, 6): [("combine", 0, 1)],
    (3, 6): [("combine", 0, 2)],
    (4, 6): [("combine", 0, 0)],
    (5, 6): [("combine", 1, 3), ("fold", 0, 0)],
    (6, 6): [("combine", 1, 1)],
    (7, 6): [("combine", 1, 2)],
    (7, 7): [("combine", 1, 0)],
    (8, 0): [("fold", 1, 0)],
    (8, 4): [("own", 0, 0)],
    (9, 1): [("combine", 2, 3), ("own", 0, 1)],
    (9, 3): [("mid", 0, 0)],
    (9, 6): [("own", 0, 2)],
    (10, 1): [("combine", 2, 1), ("mid", 0, 1)],
    (10, 2): [("own", 0, 3), ("end", 0, 0)],
    (10, 6): [("mid", 0, 2)],
    (11, 0): [("own", 1, 0), ("end", 0, 1), ("combine", 2, 2)],
    (11, 1): [("mid", 0, 3)],
    (11, 3): [("own", 1, 1), ("end", 0, 2)],
    (11, 6): [("mid", 1, 0)],
    (12, 6): [("combine", 2, 0), ("own", 1, 2), ("end", 0, 3)],
    (13, 6): [("mid", 1, 1), ("vec", 0)],
    (14, 6): [("own", 1, 3), ("end", 1, 0)],
    (15, 6): [("vec", 1)],
    (16, 6): [("mid", 1, 2)],
    (17, 6): [("vec", 2)],
    (18, 6): [("end", 1, 1)],
    (19, 6): [("vec", 3)],
    (19, 7): [("fold", 2, 0), ("mid", 1, 3), ("end", 1, 2)],
    (20, 6): [("own", 2, 0), ("vec", 4)],
    (21, 2): [("own", 2, 1), ("end", 1, 3)],
    (21, 6): [("own", 2, 2), ("mid", 2, 0)],
    (22, 2): [("own", 2, 3), ("mid", 2, 1)],
    (22, 6): [("own", 2, 4), ("mid", 2, 2), ("end", 2, 0)],
    (23, 1): [("end", 2, 1), ("mid", 2, 3), ("own", 2, 5)],
    (23, 4): [("end", 2, 2), ("mid", 2, 4), ("own", 2, 6)],
}
LAST = [
    ("end", 2, 3),
    ("mid", 2, 5),
    ("own", 2, 7),
    ("end", 2, 4),
    ("mid", 2, 6),
    ("end", 2, 5),
    ("mid", 2, 7),
    ("end", 2, 6),
    ("end", 2, 7),
]


def backward_kernel(
    lengths,
    x_hbm,
    gathered,
    qkv_t,
    qkv_s,
    context_s,
    slope_t,
    slope_s,
    hidden_s,
    unit_t,
    inverse_t,
    unit_s,
    inverse_s,
    low_s,
    grad_t,
    grad_s,
    vectors,
    t_gain,
    s_gain,
    grad_out,
    sums_out,
    vec,
    x_ref,
    grad_in,
    wide,
    hidden_buf,
    slope_buf,
    qkv_s_buf,
    qkv_t_buf,
    context_buf,
    extra_buf,
    unit_buf,
    inverse_buf,
    grad_buf,
    total,
    low_y,
    low_z,
    low_a,
    proj,
    sums,
    even,
    odd,
    from_core,
    from_far,
    from_x,
    from_y,
    from_z,
    from_vec,
    load,
    state_sem,
    odd_send,
    odd_recv,
    free,
    far_send,
    far_recv,
    x_send,
    x_recv,
    y_send,
    y_recv,
    in_send,
    in_recv,
    mid_send,
    mid_recv,
    out_send,
    out_recv,
    vec_send,
    vec_recv,
    done,
):
    me = lax.axis_index("mp")
    z = lax.axis_index("dp")
    rows = x_ref.shape[0]
    pairs = rows // LEN
    core, along_x, along_y = ({"mp": flipped(me, bits)} for bits in (1, 2, 4))
    z_outer, z_inner = {"dp": flipped(z, 1)}, {"dp": 3 - z}
    z_two = {"dp": flipped(z, 2)}
    inner = jnp.logical_or(z == 1, z == 2)
    outer = jnp.logical_or(z == 0, z == 3)

    barrier = pltpu.get_barrier_semaphore()
    greeted = (core, along_x, along_y, z_outer, z_inner, z_two)
    for peer in greeted:
        pl.semaphore_signal(barrier, inc=1, device_id=peer, device_id_type=MESH)

    def remote(src, dst, send, recv, peer):
        return pltpu.make_async_remote_copy(
            src_ref=src, dst_ref=dst, send_sem=send, recv_sem=recv, device_id=peer, device_id_type=MESH
        )

    steps = [("fs", 4 + half, pair) for half in range(2) for pair in ORDER]
    steps += [("as", 1, pair) for pair in ORDER]
    steps += [("ft", 2 + half, pair) for half in range(2) for pair in range(4)]
    steps += [("at", 0, pair) for pair in range(4)]

    def loads(number):
        kind, pack, pair = steps[number]
        place = number % 2
        two = pl.ds(2 * pair, 2)
        here = pl.ds(0, FFN_ROWS)
        moves = [(gathered.at[pack, two, here], wide.at[place])]
        if kind == "fs":
            moves.append((hidden_s.at[pack - 4, pair], hidden_buf.at[place]))
            moves.append((slope_s.at[pack - 4, pair], slope_buf.at[place]))
        elif kind == "ft":
            moves.append((slope_t.at[pack - 2, pair], slope_buf.at[place]))
        else:
            moves.append((qkv_t.at[two], qkv_t_buf.at[place]))
            if kind == "as":
                moves.append((qkv_s.at[two], qkv_s_buf.at[place]))
                moves.append((context_s.at[pair], context_buf.at[place]))
        return [
            pltpu.make_async_copy(src, dst, load.at[place, index])
            for index, (src, dst) in enumerate(moves)
        ]

    def state(layer):
        unit, inverse, grad = ((unit_t, inverse_t, grad_t), (unit_s, inverse_s, grad_s))[layer]
        moves = [(grad, grad_buf), (inverse, inverse_buf), (unit, unit_buf)]
        return [
            pltpu.make_async_copy(src, dst, state_sem.at[index])
            for index, (src, dst) in enumerate(moves)
        ]

    def slot_row(slot):
        row = me
        for bits in (1, 2, 4):
            if slot & bits:
                row = flipped(row, bits)
        return row

    def odd_copy(number):
        pair = steps[number][2]
        return remote(
            odd.at[number % 2], from_core.at[pair], odd_send.at[number % 2], odd_recv.at[pair], core
        )

    def keep(chunk, pair):
        return sums.at[chunk] if pair == 0 else even.at[chunk, pair - 1]

    def give(number, pieces):
        pair = steps[number][2]
        chunk = number // 4
        if number >= 2:
            odd_copy(number - 2).wait_send()
        for start, values in pieces:
            count = values.shape[0] // 2
            keep(chunk, pair)[start : start + count] = to_low(values[:count])
            odd[number % 2, start : start + count] = to_low(values[count:])
        if chunk:
            pl.semaphore_wait(free.at[pair], 1)
        if number == 0:
            pl.semaphore_wait(barrier, len(greeted))
        odd_copy(number).start()

    def add_rows(target, others, start, count):
        @pl.loop(0, count // 64)
        def _(step):
            here = pl.ds(start + step * 64, 64)
            value = to_float(target[here])
            for other in others:
                value = value + to_float(other[here])
            target[here] = to_low(value)

    def combine(chunk, pair):
        number = chunk * 4 + ORDER.index(pair)
        odd_copy(number).wait_recv()
        add_rows(keep(chunk, pair), [from_core.at[pair]], 0, FFN_ROWS)
        if chunk < CHUNKS - 1:
            pl.semaphore_signal(free.at[pair], inc=1, device_id=core, device_id_type=MESH)
        if pair == 3:
            far_copy(chunk, 0).start()
            far_copy(chunk, 1).start()

    def far_copy(chunk, way):
        part = pl.ds(way * 256, 256)
        return remote(
            even.at[chunk, 2, part],
            from_far.at[chunk, part],
            far_send.at[chunk, way],
            far_recv.at[chunk, way],
            (along_x, along_y)[way],
        )

    def part_rows(chunk):
        return FFN_ROWS // PARTS[chunk]

    def part_span(chunk, part):
        return pl.ds(part * part_rows(chunk), part_rows(chunk))

    def plane_copies(chunk, part):
        here = part_span(chunk, part)
        return [
            remote(even.at[chunk, 0, here], from_x.at[chunk, here], x_send.at[chunk, part], x_recv.at[chunk, part], along_x),
            remote(even.at[chunk, 1, here], from_y.at[chunk, here], y_send.at[chunk, part], y_recv.at[chunk, part], along_y),
        ]

    def fold(chunk, _):
        far_copy(chunk, 0).wait_recv()
        add_rows(keep(chunk, 2), [from_far.at[chunk]], 0, 256)
        far_copy(chunk, 1).wait_recv()
        add_rows(keep(chunk, 1), [from_far.at[chunk]], 256, 256)
        for part in range(PARTS[chunk]):
            for copy in plane_copies(chunk, part):
                copy.start()

    def z_copy(chunk, part, kind):
        here = part_span(chunk, part)
        own, first, second = sums.at[chunk, here], from_z.at[chunk, 0, here], from_z.at[chunk, 1, here]
        if kind == 0:
            return remote(own, first, in_send.at[chunk, part], in_recv.at[chunk, part], z_outer)
        if kind == 1:
            return remote(own, second, mid_send.at[chunk, part], mid_recv.at[chunk, part], z_inner)
        return remote(first, first, out_send.at[chunk, part], out_recv.at[chunk, part], z_outer)

    def own_part(chunk, part):
        for copy in plane_copies(chunk, part):
            copy.wait_recv()
        add_rows(sums.at[chunk], [from_x.at[chunk], from_y.at[chunk]], part * part_rows(chunk), part_rows(chunk))

        @pl.when(outer)
        def _():
            z_copy(chunk, part, 0).start()

    def mid_part(chunk, part):
        @pl.when(inner)
        def _():
            z_copy(chunk, part, 0).wait_recv()
            add_rows(sums.at[chunk], [from_z.at[chunk, 0]], part * part_rows(chunk), part_rows(chunk))
            z_copy(chunk, part, 1).start()

    def end_part(chunk, part):
        @pl.when(inner)
        def _():
            z_copy(chunk, part, 1).wait_recv()

            @pl.loop(0, part_rows(chunk) // 64)
            def _(step):
                here = pl.ds(part * part_rows(chunk) + step * 64, 64)
                value = to_float(sums[chunk, here]) + to_float(from_z[chunk, 1, here])
                from_z[chunk, 0, here] = to_low(value)

            z_copy(chunk, part, 2).start()

    def store_copy(chunk):
        return pltpu.make_async_copy(from_z.at[chunk, 0], sums_out.at[chunk], done.at[chunk])

    def finish(chunk):
        @pl.when(outer)
        def _():
            for part in range(PARTS[chunk]):
                z_copy(chunk, part, 2).wait_recv()

        store_copy(chunk).start()

    ways = (core, along_x, along_y, z_outer, z_two)

    def vec_copy(way):
        return remote(vec, from_vec.at[way], vec_send.at[way], vec_recv.at[way], ways[way])

    def vec_add(way):
        vec_copy(way).wait_send()
        vec_copy(way).wait_recv()
        vec[...] += from_vec[way]
        if way + 1 < len(ways):
            vec_copy(way + 1).start()

    def put_bias(pair, start, values):
        count = values.shape[1] // 2
        for side in range(2):
            line = lax.broadcasted_iota(jnp.int32, (SLOTS, count), 0)
            part = jnp.broadcast_to(values[:, side * count : (side + 1) * count], (SLOTS, count))
            part = jnp.where(line == slot_row(2 * pair + side), part, 0.0)
            vec[0:SLOTS, start : start + count] += part

    def ffn_step(number):
        kind, pack, pair = steps[number]
        place = number % 2
        up = wide[place, :, 0:HALF_UNITS].reshape(2 * HALF_UNITS, -1)
        down = wide[place, :, HALF_UNITS : 2 * HALF_UNITS].reshape(2 * HALF_UNITS, -1)
        back = dot_nt(low_z[...], down) * to_float(slope_buf[place])
        back_low = to_low(back)
        total[...] += dot(back_low, up)
        if kind == "fs":
            put_bias(pair, 2 * COLS + (pack - 4) * HALF_UNITS, jnp.sum(back, axis=0, keepdims=True))
            up_grad = dot_tn(back_low, low_y[...])
            down_grad = dot_tn(hidden_buf[place], low_z[...])
            give(number, [(0, up_grad), (HALF_UNITS, down_grad)])

    def pick(both):
        first = lax.broadcasted_iota(jnp.int32, (LEN, COLS), 1) < DH
        return jnp.where(first, both[:LEN], both[LEN:])

    def attention_step(number):
        kind, pack, pair = steps[number]
        place = number % 2
        student = kind == "as"
        factor = 1.0 / math.sqrt(DH)
        qkv = qkv_s_buf if student else qkv_t_buf
        out = wide[place, :, 384:512].reshape(2 * COLS, -1)
        context_back = to_low(dot_nt(low_a[...], out))
        query_sums, value_sums = [], []
        for side in range(2):
            query_sum = jnp.zeros((1, COLS), jnp.float32)
            value_sum = jnp.zeros((1, COLS), jnp.float32)
            for number_b in range(pairs):
                here = slice(number_b * LEN, (number_b + 1) * LEN)
                length = lengths[me * pairs + number_b]
                query, key, value = [
                    qkv[place, side, here, i * COLS : (i + 1) * COLS] for i in range(3)
                ]
                keys, values = two_heads(key), two_heads(value)
                scores = dot_nt(query, keys) * factor
                probs = masked_probs(scores, length)
                if student:
                    other = dot_nt(
                        qkv_t_buf[place, side, here, 0:COLS],
                        two_heads(qkv_t_buf[place, side, here, COLS : 2 * COLS]),
                    )
                    spot = lax.broadcasted_iota(jnp.int32, scores.shape, 1)
                    spot = jnp.where(spot < LEN, spot, spot - LEN)
                    line = lax.broadcasted_iota(jnp.int32, scores.shape, 0)
                    gap = score_weight * (scores - other * factor)
                    extra = jnp.where(jnp.maximum(spot, line) < length, gap, 0.0)
                    extra_buf[pair, side, number_b] = to_low(extra)
                else:
                    extra = -to_float(extra_buf[pair, side, number_b])
                part = context_back[here, side * COLS : (side + 1) * COLS]
                probs_back = dot_nt(part, values)
                value_back = pick(dot_tn(to_low(probs), part))
                product = probs * probs_back
                inner_sum = jnp.concatenate(
                    [
                        jnp.broadcast_to(
                            jnp.sum(product[:, i * LEN : (i + 1) * LEN], axis=1, keepdims=True), (LEN, LEN)
                        )
                        for i in range(2)
                    ],
                    axis=1,
                )
                score_back = to_low(product - probs * inner_sum + extra)
                query_back = dot(score_back, keys) * factor
                key_back = pick(dot_tn(score_back, query)) * factor
                start = side * 3 * COLS
                proj[here, start : start + COLS] = to_low(query_back)
                proj[here, start + COLS : start + 2 * COLS] = to_low(key_back)
                proj[here, start + 2 * COLS : start + 3 * COLS] = to_low(value_back)
                if student:
                    query_sum += jnp.sum(query_back, axis=0, keepdims=True)
                    value_sum += jnp.sum(value_back, axis=0, keepdims=True)
                if side * pairs + number_b < 2 * pairs - 1:
                    after(number, side * pairs + number_b)
            query_sums.append(query_sum)
            value_sums.append(value_sum)
        grad_in[...] += dot(proj[...], wide[place, :, 0:384].reshape(768, -1))
        if student:
            put_bias(pair, 0, jnp.concatenate(query_sums, axis=1))
            put_bias(pair, COLS, jnp.concatenate(value_sums, axis=1))
            qkv_grad = dot_tn(proj[...], x_ref[...])
            out_grad = dot_tn(context_buf[place], low_a[...])
            give(number, [(0, qkv_grad), (3 * COLS, out_grad)])

    def lower_grad():
        @pl.loop(0, rows // 64)
        def _(step):
            here = pl.ds(step * 64, 64)
            low_z[here] = to_low(grad_buf[here])

        total[...] = jnp.zeros_like(total)

    def norm_step(student):
        gain_ref = s_gain if student else t_gain

        @pl.loop(0, rows // 64)
        def _(step):
            here = pl.ds(step * 64, 64)
            grad = grad_buf[here] + total[here]
            unit = unit_buf[here]
            back = norm_back(grad, unit, inverse_buf[here], to_float(gain_ref[0:1]))
            low_a[here] = to_low(back)
            if student:
                grad_in[here] = back
                vec[8:9] += jnp.sum(back, axis=0, keepdims=True)
                vec[9:10] += jnp.sum(grad * unit, axis=0, keepdims=True)
                vec[10:11] += jnp.sum(grad, axis=0, keepdims=True)
            else:
                grad_in[here] += back

    actions = {
        "combine": combine,
        "fold": fold,
        "own": own_part,
        "mid": mid_part,
        "end": end_part,
        "vec": vec_add,
    }

    def after(number, part):
        for name, *which in SCHEDULE.get((number, part), ()):
            actions[name](*which)

    low_copy = pltpu.make_async_copy(low_s, low_y, state_sem.at[3])
    x_copy = pltpu.make_async_copy(x_hbm, x_ref, done.at[CHUNKS])
    grad_first, *others = state(1)
    grad_first.start()
    for copy in loads(0):
        copy.start()
    for copy in (low_copy, *others, x_copy):
        copy.start()
    vec[...] = jnp.zeros_like(vec)
    vec[11:14] = vectors[0:3]
    grad_first.wait()
    lower_grad()
    low_copy.wait()
    grad_copy = pltpu.make_async_copy(grad_in, grad_out, done.at[CHUNKS + 1])
    for number, (kind, pack, pair) in enumerate(steps):
        for copy in loads(number):
            copy.wait()
        if number + 1 < len(steps):
            for copy in loads(number + 1):
                copy.start()
        if kind in ("fs", "ft"):
            ffn_step(number)
        else:
            attention_step(number)
        if number == len(steps) - 1:
            grad_copy.start()
        after(number, 6)
        if number == 7:
            for copy in others:
                copy.wait()
            x_copy.wait()
            norm_step(True)
            for copy in state(0):
                copy.start()
        elif number == 11:
            for copy in state(0):
                copy.wait()
            lower_grad()
            vec_copy(0).start()
        elif number == 19:
            norm_step(False)
        after(number, 7)
    for name, *which in LAST:
        actions[name](*which)
    for chunk in range(CHUNKS):
        finish(chunk)

    grad_copy.wait()
    odd_copy(10).wait_send()
    odd_copy(11).wait_send()
    for chunk in range(CHUNKS):
        far_copy(chunk, 0).wait_send()
        far_copy(chunk, 1).wait_send()
        for part in range(PARTS[chunk]):
            for copy in plane_copies(chunk, part):
                copy.wait_send()

            @pl.when(outer)
            def _():
                z_copy(chunk, part, 0).wait_send()

            @pl.when(inner)
            def _():
                z_copy(chunk, part, 1).wait_send()
                z_copy(chunk, part, 2).wait_send()

        store_copy(chunk).wait()


def backward_both(lengths, tokens, kept, vectors, t_gain, s_gain):
    rows, features = tokens.shape
    low, full = jnp.bfloat16, jnp.float32
    vmem = pl.BlockSpec(memory_space=pltpu.VMEM)
    hbm = pl.BlockSpec(memory_space=pl.ANY)
    dma = pltpu.SemaphoreType.DMA
    block = (FFN_ROWS, features)
    return pl.pallas_call(
        backward_kernel,
        out_shape=[
            jax.ShapeDtypeStruct((rows, features), full),
            jax.ShapeDtypeStruct((CHUNKS,) + block, low),
            jax.ShapeDtypeStruct((16, features), full),
        ],
        in_specs=[pl.BlockSpec(memory_space=pltpu.SMEM), hbm] + [hbm] * len(kept) + [vmem] * 3,
        out_specs=[hbm, hbm, vmem],
        scratch_shapes=[
            pltpu.VMEM((rows, features), low),
            pltpu.VMEM((rows, features), full),
            pltpu.VMEM((2, 2) + block, low),
            pltpu.VMEM((2, rows, 2 * HALF_UNITS), low),
            pltpu.VMEM((2, rows, 2 * HALF_UNITS), low),
            pltpu.VMEM((2, 2, rows, 3 * COLS), low),
            pltpu.VMEM((2, 2, rows, 3 * COLS), low),
            pltpu.VMEM((2, rows, 2 * COLS), low),
            pltpu.VMEM((4, 2, rows // LEN, LEN, 2 * LEN), low),
            pltpu.VMEM((rows, features), full),
            pltpu.VMEM((rows, 1), full),
            pltpu.VMEM((rows, features), full),
            pltpu.VMEM((rows, features), full),
            pltpu.VMEM((rows, features), low),
            pltpu.VMEM((rows, features), low),
            pltpu.VMEM((rows, features), low),
            pltpu.VMEM((rows, 6 * COLS), low),
            pltpu.VMEM((CHUNKS,) + block, low),
            pltpu.VMEM((CHUNKS, 3) + block, low),
            pltpu.VMEM((2,) + block, low),
            pltpu.VMEM((4,) + block, low),
            pltpu.VMEM((CHUNKS,) + block, low),
            pltpu.VMEM((CHUNKS,) + block, low),
            pltpu.VMEM((CHUNKS,) + block, low),
            pltpu.VMEM((CHUNKS, 2) + block, low),
            pltpu.VMEM((5, 16, features), full),
            dma((2, 5)),
            dma((4,)),
            dma((2,)),
            dma((4,)),
            pltpu.SemaphoreType.REGULAR((4,)),
            dma((CHUNKS, 2)),
            dma((CHUNKS, 2)),
        ]
        + [dma((CHUNKS, max(PARTS)))] * 10
        + [dma((5,)), dma((5,)), dma((CHUNKS + 2,))],
        compiler_params=pltpu.CompilerParams(
            collective_id=1, has_side_effects=True, vmem_limit_bytes=63 * 1024 * 1024
        ),
        name="backward_both",
    )(lengths, tokens, *kept, vectors, t_gain, s_gain)


def finish_kernel(sums, vec, qkv_out, qv_out, out_out, up_out, up_bias_out, down_out, bias_out, gain_out, shift_out):
    for i in range(3):
        qkv_out[i] = to_float(sums[2, i * COLS : (i + 1) * COLS]).T
    out_out[...] = to_float(sums[2, 3 * COLS :])
    for half in range(2):
        here = slice(half * HALF_UNITS, (half + 1) * HALF_UNITS)
        up_out[:, here] = to_float(sums[half, :HALF_UNITS]).T
        down_out[here] = to_float(sums[half, HALF_UNITS:])
    line = lax.broadcasted_iota(jnp.int32, (SLOTS, vec.shape[1]), 0)
    row = jnp.sum(jnp.where(line == lax.axis_index("mp"), vec[0:SLOTS], 0.0), axis=0, keepdims=True)
    qv_out[0:1] = row[:, :COLS]
    qv_out[1:2] = row[:, COLS : 2 * COLS]
    up_bias_out[...] = row[:, 2 * COLS : 2 * COLS + 2 * HALF_UNITS]
    for index, ref in enumerate((bias_out, gain_out, shift_out)):
        ref[0:1] = vec[8 + index : 9 + index]
        ref[1:2] = vec[11 + index : 12 + index]


def finish_sums(sums, vec):
    features = vec.shape[1]
    shapes = [
        (3, features, COLS),
        (2, COLS),
        (COLS, features),
        (features, 2 * HALF_UNITS),
        (1, 2 * HALF_UNITS),
        (2 * HALF_UNITS, features),
        (2, features),
        (2, features),
        (2, features),
    ]
    vmem = pl.BlockSpec(memory_space=pltpu.VMEM)
    return pl.pallas_call(
        finish_kernel,
        out_shape=[jax.ShapeDtypeStruct(shape, jnp.float32) for shape in shapes],
        in_specs=[vmem, vmem],
        out_specs=[vmem] * len(shapes),
        compiler_params=pltpu.CompilerParams(vmem_limit_bytes=48 * 1024 * 1024),
        name="finish_sums",
    )(sums, vec)


def cut(values, count, axis):
    return jnp.split(values, count, axis=axis)


def per_device(n_dp, n_mp, *args):
    (
        tokens,
        lengths,
        student_qkv,
        student_qv_bias,
        student_out,
        student_up,
        student_up_bias,
        student_down,
        student_out_bias,
        student_gain,
        student_shift,
        teacher_qkv,
        teacher_qv_bias,
        teacher_out,
        teacher_up,
        teacher_up_bias,
        teacher_down,
        teacher_out_bias,
        teacher_gain,
        teacher_shift,
    ) = args
    net = Cube(n_dp) if (n_dp, n_mp) == (4, 8) else Plain(n_mp)
    rows = tokens.shape[0]
    pairs = rows // LEN
    places = jnp.arange(LEN, dtype=jnp.int32)
    me = lax.axis_index("mp")
    own_lengths = lax.dynamic_slice_in_dim(lengths, me * pairs, pairs)
    valid = places[None, :] < own_lengths[:, None]
    token_valid = to_float(valid.reshape(rows, 1))
    pair_valid = valid[:, None, :, None] & valid[:, None, None, :]

    gain = to_float(student_gain)
    shift = to_float(student_shift)
    out_bias = to_float(student_out_bias)
    teach_gain = to_float(teacher_gain)
    if isinstance(net, Cube):
        gathered, (*kept, student_output), vecs = forward_both(
            lengths,
            tokens,
            (
                [teacher_qkv.transpose(1, 0, 2), teacher_out, teacher_up, teacher_down],
                [teacher_qv_bias, teacher_up_bias, teacher_out_bias, teacher_gain, teacher_shift],
            ),
            (
                [student_qkv.transpose(1, 0, 2), student_out, student_up, student_down],
                [student_qv_bias, student_up_bias, student_out_bias, student_gain, student_shift],
            ),
        )
        input_grad, sums, vec = backward_both(
            lengths, tokens, (gathered, *kept), vecs, teacher_gain, student_gain
        )
        grads = finish_sums(sums, vec)
        return (
            student_output,
            input_grad,
            grads[0].transpose(1, 0, 2),
            grads[1],
            grads[2],
            grads[3],
            grads[4].reshape(-1),
            *grads[5:],
        )
    else:
        teach = gather_layer(
            net, teacher_qkv, teacher_qv_bias, teacher_out, teacher_up, teacher_up_bias, teacher_down
        )
        stud = gather_layer(
            net,
            binarize(student_qkv, 0),
            student_qv_bias,
            binarize(student_out, 1),
            binarize(student_up, 0),
            student_up_bias,
            binarize(student_down, 1),
        )
        teach_final, teach_kept = forward(
            tokens, teach, to_float(teacher_out_bias), teach_gain, to_float(teacher_shift), plain_act, valid
        )
        final, kept = forward(tokens, stud, out_bias, gain, shift, clipped_act, valid)
        student_output = to_low(final)
        final_grad = token_valid * (final - teach_final)
        grad_s = norm_back(final_grad, kept[11], kept[12], gain[1])
        grad_t = norm_back(-final_grad, teach_kept[11], teach_kept[12], teach_gain[1])
        vecs = jnp.stack([jnp.sum(grad_s, axis=0), jnp.sum(final_grad * kept[11], axis=0), jnp.sum(final_grad, axis=0)])
    extra = score_weight * jnp.where(pair_valid, kept[3] - teach_kept[3], 0.0)

    second_grad, second_low, pre_grad, pre_low, normed_grad, first_grad = backward_ffn(
        kept, stud, grad_s, gain
    )
    hidden, normed_low, context = kept[9], kept[8], kept[5]
    unit_one = kept[6]
    down_grad = net.sum_dp(net.scatter(cut(to_low(dot_tn(hidden, second_low)), n_mp, 0)))
    up_grad = net.sum_dp(net.scatter(cut(to_low(dot_tn(normed_low, pre_low)), n_mp, 1)))
    first_low = to_low(first_grad)
    out_grad = net.sum_dp(net.scatter(cut(to_low(dot_tn(context, first_low)), n_mp, 0)))
    grads = backward_attention(kept, first_low, stud[3], extra)
    lows = [to_low(item) for item in grads]
    wide = jnp.concatenate(
        [to_low(dot_tn(tokens, item)) for item in lows], axis=0
    )
    qkv_grad = net.sum_dp(net.scatter(cut(wide, n_mp, 1)))
    features = tokens.shape[1]
    qkv_grad = qkv_grad.reshape(3, features, -1).transpose(1, 0, 2)

    teach_second, teach_slow, _, _, _, teach_first = backward_ffn(
        teach_kept, teach, grad_t, teach_gain
    )
    teach_grads = backward_attention(teach_kept, to_low(teach_first), teach[3], -extra)
    teach_lows = [to_low(item) for item in teach_grads]
    input_grad = first_grad + teach_first
    for item, matrix in zip(lows, stud[0]):
        input_grad = input_grad + dot_nt(item, matrix)
    for item, matrix in zip(teach_lows, teach[0]):
        input_grad = input_grad + dot_nt(item, matrix)

    vectors = [
        jnp.sum(first_grad, axis=0),
        vecs[0],
        jnp.sum(normed_grad * unit_one, axis=0),
        vecs[1],
        jnp.sum(normed_grad, axis=0),
        vecs[2],
        net.place(jnp.sum(grads[0], axis=0).reshape(n_mp, -1)).reshape(-1),
        net.place(jnp.sum(grads[2], axis=0).reshape(n_mp, -1)).reshape(-1),
    ]
    wide_vector = net.place(jnp.sum(pre_grad, axis=0).reshape(n_mp, -1)).reshape(-1, features)
    total = net.sum_all(jnp.concatenate([jnp.stack(vectors), wide_vector], axis=0))
    width = features // n_mp
    units = wide_vector.size // n_mp
    return (
        student_output,
        input_grad,
        qkv_grad,
        lax.dynamic_slice_in_dim(total[6:8], me * width, width, axis=1),
        out_grad,
        up_grad,
        lax.dynamic_slice_in_dim(total[8:].reshape(-1), me * units, units),
        down_grad,
        total[0:2],
        total[2:4],
        total[4:6],
    )


def solution(mesh):
    n_dp, n_mp = mesh.shape["dp"], mesh.shape["mp"]

    def body(*args):
        return per_device(n_dp, n_mp, *args)

    return jax.shard_map(
        body,
        mesh=mesh,
        in_specs=(
            P(("dp", "mp"), None),
            P("dp"),
            P(None, None, "mp"),
            P(None, "mp"),
            P("mp", None),
            P(None, "mp"),
            P("mp"),
            P("mp", None),
            P(),
            P(),
            P(),
            P(None, None, "mp"),
            P(None, "mp"),
            P("mp", None),
            P(None, "mp"),
            P("mp"),
            P("mp", None),
            P(),
            P(),
            P(),
        ),
        out_specs=(
            P(("dp", "mp"), None),
            P(("dp", "mp"), None),
            P(None, None, "mp"),
            P(None, "mp"),
            P("mp", None),
            P(None, "mp"),
            P("mp"),
            P("mp", None),
            P(),
            P(),
            P(),
        ),
        check_vma=False,
    )
```

```python
import math

import jax
import jax.numpy as jnp
from jax import lax
from jax.experimental import pallas as pl
from jax.experimental.pallas import tpu as pltpu
from jax.sharding import PartitionSpec as P

DH = 64
LEN = 128


norm_epsilon = 1e-06
clip_level = 2.5
score_weight = 0.05
masked_fill = -1000000000.0


def to_float(values):
    return values.astype(jnp.float32)


def to_low(values):
    return values.astype(jnp.bfloat16)


def binarize(matrix, axis_index):
    scaling = jnp.mean(jnp.abs(matrix), axis=axis_index, keepdims=True)
    return (scaling * jnp.sign(matrix)).astype(jnp.bfloat16)


def norm_stats(values):
    centred = values - jnp.mean(values, axis=-1, keepdims=True)
    variance = jnp.mean(centred * centred, axis=-1, keepdims=True)
    inverse = lax.rsqrt(variance + norm_epsilon)
    return (centred * inverse, inverse)


def norm_back(grad, unit, inverse, gain_row):
    scaled = grad * gain_row
    first = jnp.mean(scaled, axis=-1, keepdims=True)
    second = jnp.mean(scaled * unit, axis=-1, keepdims=True)
    return inverse * (scaled - first - unit * second)


def dot(left, right):
    return jnp.dot(left, right, preferred_element_type=jnp.float32)


def dot_nt(left, right):
    return lax.dot_general(left, right, (((1,), (1,)), ((), ())), preferred_element_type=jnp.float32)


def dot_tn(left, right):
    return lax.dot_general(left, right, (((0,), (0,)), ((), ())), preferred_element_type=jnp.float32)


class Cube:
    def __init__(self, n_dp):
        self.n_dp = n_dp
        self.axes = ("dp", "mp")

    def flip(self, values, bits):
        pairs = [
            (z * 8 + m, z * 8 + (m ^ bits)) for z in range(self.n_dp) for m in range(8)
        ]
        return lax.ppermute(values, self.axes, pairs)

    def flip_dp(self, values, bits):
        pairs = [
            (z * 8 + m, (z ^ bits) * 8 + m) for z in range(self.n_dp) for m in range(8)
        ]
        return lax.ppermute(values, self.axes, pairs)

    def gather(self, block):
        half = block.shape[0] // 2
        along_x = self.flip(block, 2)
        along_y = self.flip(block, 4)
        across = jnp.concatenate(
            [self.flip(along_y[:half], 2), self.flip(along_x[half:], 4)], axis=0
        )
        same = [block, along_x, along_y, across]
        other = [self.flip(item, 1) for item in same]
        return [item for pair in zip(same, other) for item in pair]

    def scatter(self, blocks):
        half = blocks[0].shape[0] // 2
        own, to_x, to_y, to_far = [
            to_float(blocks[k]) + to_float(self.flip(blocks[k + 1], 1)) for k in (0, 2, 4, 6)
        ]
        far = to_low(to_far)
        via_x = to_float(self.flip(far[:half], 2))
        via_y = to_float(self.flip(far[half:], 4))
        to_y = to_low(jnp.concatenate([to_y[:half] + via_x, to_y[half:]], axis=0))
        to_x = to_low(jnp.concatenate([to_x[:half], to_x[half:] + via_y], axis=0))
        return own + to_float(self.flip(to_x, 2)) + to_float(self.flip(to_y, 4))

    def sum_dp(self, values):
        half = values.shape[0] // 2
        odd = lax.axis_index("dp") % 2
        low = to_low(values)
        sent = lax.dynamic_slice_in_dim(low, (1 - odd) * half, half)
        kept = lax.dynamic_slice_in_dim(values, odd * half, half)
        kept = kept + to_float(self.flip_dp(sent, 1))
        kept_low = to_low(kept)
        kept = to_low(kept + to_float(self.flip_dp(kept_low, 2)))
        other = self.flip_dp(kept, 1)
        return to_float(
            jnp.concatenate(
                [jnp.where(odd == 0, kept, other), jnp.where(odd == 0, other, kept)], axis=0
            )
        )

    def sum_all(self, values):
        for bits in (1, 2, 4):
            values = values + self.flip(values, bits)
        for bits in (1, 2):
            values = values + self.flip_dp(values, bits)
        return values

    def place(self, values):
        me = lax.axis_index("mp")
        for bit in range(3):
            shape = values.shape
            split = values.reshape((8 >> (bit + 1), 2, 1 << bit) + shape[1:])
            flipped = split[:, ::-1]
            values = jnp.where((me >> bit) % 2 == 1, flipped, split).reshape(shape)
        return values


class Plain:
    def __init__(self, n_mp):
        self.n_mp = n_mp

    def gather(self, block):
        every = lax.all_gather(block, "mp", axis=0)
        return [every[k] for k in range(self.n_mp)]

    def scatter(self, blocks):
        return to_float(
            lax.psum_scatter(jnp.stack(blocks), "mp", scatter_dimension=0, tiled=False)
        )

    def sum_dp(self, values):
        return to_float(lax.psum(to_low(values), "dp"))

    def sum_all(self, values):
        return lax.psum(values, ("dp", "mp"))

    def place(self, values):
        return values


def plain_act(pre):
    gate = 0.5 * (1.0 + lax.erf(pre * math.sqrt(0.5)))
    slope = gate + pre * jnp.exp(-0.5 * pre * pre) * (1.0 / math.sqrt(2.0 * math.pi))
    return (pre * gate, slope)


def clipped_act(pre):
    value, slope = plain_act(pre)
    bent = jnp.tanh(value * (1.0 / clip_level))
    return (clip_level * bent, slope * (1.0 - bent * bent))


def gather_layer(net, qkv, qv_bias, out, up, up_bias, down):
    width = qkv.shape[2]
    units = up.shape[1]
    features = qkv.shape[0]
    extra = jnp.zeros((16, features), jnp.bfloat16)
    extra = extra.at[0, :width].set(qv_bias[0]).at[1, :width].set(qv_bias[1])
    extra = extra.at[2, :units].set(up_bias)
    qkv_parts = net.gather(qkv.transpose(1, 0, 2).reshape(3 * features, width))
    out_parts = net.gather(jnp.concatenate([out, extra], axis=0))
    up_parts = net.gather(up)
    down_parts = net.gather(down)
    count = len(qkv_parts)
    qkv_full = jnp.concatenate(
        [part.reshape(3, features, width) for part in qkv_parts], axis=2
    )
    out_full = jnp.concatenate([part[:width] for part in out_parts], axis=0)
    q_bias = jnp.concatenate([part[width, :width] for part in out_parts])
    v_bias = jnp.concatenate([part[width + 1, :width] for part in out_parts])
    up_b = jnp.concatenate([part[width + 2, :units] for part in out_parts])
    up_full = jnp.concatenate(up_parts, axis=1)
    down_full = jnp.concatenate(down_parts, axis=0)
    return (qkv_full, to_float(q_bias), to_float(v_bias), out_full, up_full, to_float(up_b), down_full)


def forward(tokens, weights, out_bias, gain, shift, activation, key_valid):
    qkv, q_bias, v_bias, out, up, up_bias, down = weights
    rows, features = tokens.shape
    pairs = rows // LEN
    shape = (pairs, LEN, features // DH, DH)
    query = to_low(dot(tokens, qkv[0]) + q_bias).reshape(shape)
    key = to_low(dot(tokens, qkv[1])).reshape(shape)
    value = to_low(dot(tokens, qkv[2]) + v_bias).reshape(shape)
    scores = jnp.einsum("bqhe,bkhe->bhqk", query, key, preferred_element_type=jnp.float32) * (
        1.0 / math.sqrt(DH)
    )
    masked = jnp.where(key_valid[:, None, None, :], scores, masked_fill)
    log_norm = jax.nn.logsumexp(masked, axis=-1, keepdims=True)
    attention = jnp.exp(masked - log_norm)
    context = jnp.einsum(
        "bhqk,bkhe->bqhe", to_low(attention), value, preferred_element_type=jnp.float32
    )
    context = to_low(context).reshape(rows, features)
    first = to_float(tokens) + dot(context, out) + out_bias[0]
    unit_one, inverse_one = norm_stats(first)
    normed = unit_one * gain[0] + shift[0]
    normed_low = to_low(normed)
    hidden, slope = activation(dot(normed_low, up) + up_bias)
    hidden = to_low(hidden)
    second = normed + dot(hidden, down) + out_bias[1]
    unit_two, inverse_two = norm_stats(second)
    final = unit_two * gain[1] + shift[1]
    kept = (query, key, value, scores, attention, context, unit_one, inverse_one, normed_low, hidden,
            to_low(slope), unit_two, inverse_two)
    return (final, kept)


def backward_ffn(kept, weights, second_grad, gain):
    qkv, q_bias, v_bias, out, up, up_bias, down = weights
    (query, key, value, scores, attention, context, unit_one, inverse_one, normed_low, hidden,
     slope, unit_two, inverse_two) = kept
    second_low = to_low(second_grad)
    pre_grad = dot_nt(second_low, down) * slope
    pre_low = to_low(pre_grad)
    normed_grad = second_grad + dot_nt(pre_low, up)
    first_grad = norm_back(normed_grad, unit_one, inverse_one, gain[0])
    return (second_grad, second_low, pre_grad, pre_low, normed_grad, first_grad)


def backward_attention(kept, first_low, out, extra):
    query, key, value, scores, attention = kept[:5]
    rows = first_low.shape[0]
    factor = 1.0 / math.sqrt(DH)
    context_grad = to_low(dot_nt(first_low, out)).reshape(query.shape)
    attention_grad = jnp.einsum(
        "bqhe,bkhe->bhqk", context_grad, value, preferred_element_type=jnp.float32
    )
    value_grad = jnp.einsum(
        "bhqk,bqhe->bkhe", to_low(attention), context_grad, preferred_element_type=jnp.float32
    )
    inner = jnp.sum(attention * attention_grad, axis=-1, keepdims=True)
    score_low = to_low(attention * (attention_grad - inner) + extra)
    query_grad = factor * jnp.einsum(
        "bhqk,bkhe->bqhe", score_low, key, preferred_element_type=jnp.float32
    )
    key_grad = factor * jnp.einsum(
        "bhqk,bqhe->bkhe", score_low, query, preferred_element_type=jnp.float32
    )
    return [item.reshape(rows, -1) for item in (query_grad, key_grad, value_grad)]


MESH = pl.DeviceIdType.MESH
SLOTS = 8
PACKS = 6
ATT_ROWS = 528
FFN_ROWS = 512
HALF_UNITS = 256
COLS = 128

SHARED = (240, 240, 96, 192, 176, 0)
MEET, PREPARE, FIRST, SECOND, PLANE_SWAP, FAR_SENDS, FAR_SWAP, LOAD, USE, END = range(10)
FORWARD = [
    (PREPARE, 0), (MEET,), (FIRST, 0), (PREPARE, 1), (FIRST, 1), (PREPARE, 2), (PREPARE, 3), (PREPARE, 4),
    (PREPARE, 5), (LOAD, 0, 0), (LOAD, 1, 0), (USE, 0, 0), (USE, 1, 0), (SECOND, 0), (FIRST, 2),
    (SECOND, 1), (FIRST, 3), (PLANE_SWAP, 0), (FAR_SENDS, 0), (LOAD, 0, 1), (LOAD, 0, 2),
    (USE, 0, 1), (USE, 0, 2), (SECOND, 2), (FIRST, 4), (PLANE_SWAP, 1), (FAR_SENDS, 1),
    (LOAD, 1, 1), (LOAD, 1, 2), (USE, 1, 1), (USE, 1, 2), (FAR_SWAP, 0), (LOAD, 0, 3), (USE, 0, 3),
    (END, 0), (SECOND, 3), (FIRST, 5), (PLANE_SWAP, 2), (LOAD, 2, 0), (LOAD, 3, 0), (USE, 2, 0),
    (FAR_SENDS, 2), (LOAD, 2, 1), (USE, 3, 0), (LOAD, 2, 2), (USE, 2, 1), (USE, 2, 2),
    (FAR_SWAP, 1), (LOAD, 1, 3), (USE, 1, 3), (END, 1), (SECOND, 4), (LOAD, 4, 0), (LOAD, 5, 0),
    (USE, 4, 0), (USE, 5, 0), (PLANE_SWAP, 3), (FAR_SENDS, 3), (LOAD, 3, 1), (LOAD, 3, 2),
    (USE, 3, 1), (FAR_SWAP, 2), (USE, 3, 2), (LOAD, 2, 3), (USE, 2, 3), (PLANE_SWAP, 4),
    (SECOND, 5), (PLANE_SWAP, 5), (LOAD, 4, 1), (LOAD, 4, 2), (USE, 4, 1), (LOAD, 5, 1),
    (USE, 4, 2), (FAR_SWAP, 3), (FAR_SENDS, 4), (LOAD, 5, 2), (USE, 5, 1), (LOAD, 3, 3),
    (USE, 5, 2), (USE, 3, 3), (END, 3), (FAR_SWAP, 4), (FAR_SENDS, 5), (FAR_SWAP, 5), (LOAD, 4, 3),
    (LOAD, 5, 3), (USE, 4, 3), (USE, 5, 3),
]


def flipped(me, bits):
    return me + bits - 2 * bits * lax.rem(lax.div(me, bits), 2)


def pack_rows(pack):
    return ATT_ROWS if pack < 2 else FFN_ROWS


def masked_probs(scores, length):
    rows = scores.shape[0]
    position = lax.broadcasted_iota(jnp.int32, (rows, LEN), 1)
    parts = []
    for head in range(2):
        part = jnp.where(position < length, scores[:, head * LEN : (head + 1) * LEN], masked_fill)
        part = jnp.exp(part - jnp.max(part, axis=1, keepdims=True))
        parts.append(part / jnp.sum(part, axis=1, keepdims=True))
    return jnp.concatenate(parts, axis=1)


def two_heads(rows):
    first = lax.broadcasted_iota(jnp.int32, rows.shape, 1) < DH
    zero = jnp.zeros_like(rows)
    return jnp.concatenate([jnp.where(first, rows, zero), jnp.where(first, zero, rows)], axis=0)


def norm_block(values):
    centred = values - jnp.mean(values, axis=1, keepdims=True)
    inverse = lax.rsqrt(jnp.mean(centred * centred, axis=1, keepdims=True) + norm_epsilon)
    return (centred * inverse, inverse)


def forward_kernel(
    lengths,
    x_ref,
    t_weights,
    t_small,
    s_weights,
    s_small,
    gathered,
    kept,
    vectors,
    scratch,
    raw_t,
    raw_s,
    mine_att,
    mine_ffn,
    wide,
    total,
    normed,
    low_t,
    context_t,
    bias_rows,
    final_t,
    unit_two,
    inverse_two,
    send,
    recv,
    load,
    fetch,
    save,
):
    t_qv_bias, t_up_bias, t_bias, t_gain, t_shift = t_small
    s_qv_bias, s_up_bias, s_bias, s_gain, s_shift = s_small
    (qkv_t, qkv_s, context_s, slope_t, slope_s, hidden_s, unit_t, inverse_t, unit_s, inverse_s, low_s,
     grad_t, grad_s, final_low) = scratch
    saved = []

    def put(name, index=None):
        src, dst = scratch[name], kept[name]
        if index is not None:
            src, dst = src.at[index], dst.at[index]
        saved.append(pltpu.make_async_copy(src, dst, save.at[len(saved)]))
        saved[-1].start()

    me = lax.axis_index("mp")
    z = lax.axis_index("dp")
    peers = {bits: {"mp": flipped(me, bits)} for bits in (1, 2, 4)}
    peers["z"] = {"dp": flipped(z, 1)}
    upper = lax.rem(z, 2)
    rows = x_ref.shape[0]
    pairs = rows // LEN

    barrier = pltpu.get_barrier_semaphore()
    for peer in peers.values():
        pl.semaphore_signal(barrier, inc=1, device_id=peer, device_id_type=MESH)

    fetched = []
    for weights, raw, direct in ((t_weights, raw_t, True), (s_weights, raw_s, False)):
        qkv, out, up, down = weights
        moves = [(qkv, raw[0]), (up, raw[1])]
        if direct:
            moves.append((out, mine_att.at[0, pl.ds(3 * COLS, COLS)]))
            moves += [
                (down.at[pl.ds(h * HALF_UNITS, HALF_UNITS)], mine_ffn.at[h, pl.ds(HALF_UNITS, HALF_UNITS)])
                for h in range(2)
            ]
        else:
            moves += [(out, raw[2]), (down, raw[3])]
        for src, dst in moves:
            fetched.append(pltpu.make_async_copy(src, dst, fetch.at[len(fetched)]))
            fetched[-1].start()

    def signed(values, axis):
        scale = jnp.mean(jnp.abs(values), axis=axis, keepdims=True)
        return to_low(jnp.where(values > 0, scale, jnp.where(values < 0, -scale, 0.0)))

    def bias_block(qv_bias, up_bias):
        line = jnp.concatenate(
            [
                to_float(qv_bias[0:1]),
                to_float(qv_bias[1:2]),
                to_float(up_bias[...]).reshape(1, -1),
                jnp.zeros((1, x_ref.shape[1] - 2 * COLS - 2 * HALF_UNITS), jnp.float32),
            ],
            axis=1,
        )
        row = lax.broadcasted_iota(jnp.int32, (16, line.shape[1]), 0)
        return to_low(jnp.where(row == 0, jnp.broadcast_to(line, row.shape), 0.0))

    def own_copy(pack):
        return pltpu.make_async_copy(source(pack), block(pack, 0), fetch.at[9 + pack])

    def prepare(pack):
        if pack == 0:
            fetched[0].wait()
            for i in range(3):
                mine_att[0, i * COLS : (i + 1) * COLS] = raw_t[0][i].T
            mine_att[0, 4 * COLS : 4 * COLS + 16] = bias_block(t_qv_bias, t_up_bias)
            fetched[2].wait()
        elif pack == 1:
            fetched[5].wait()
            for i in range(3):
                mine_att[1, i * COLS : (i + 1) * COLS] = signed(raw_s[0][i], 0).T
            mine_att[1, 4 * COLS : 4 * COLS + 16] = bias_block(s_qv_bias, s_up_bias)
            fetched[7].wait()
            mine_att[1, 3 * COLS : 4 * COLS] = signed(raw_s[2][...], 1)
        else:
            layer, half = divmod(pack - 2, 2)
            here = slice(half * HALF_UNITS, (half + 1) * HALF_UNITS)
            if half == 0:
                fetched[(1, 6)[layer]].wait()
            if layer == 0:
                mine_ffn[half, 0:HALF_UNITS] = raw_t[1][:, here].T
                fetched[3 + half].wait()
            else:
                mine_ffn[2 + half, 0:HALF_UNITS] = signed(raw_s[1][:, here], 0).T
                if half == 0:
                    fetched[8].wait()
                mine_ffn[2 + half, HALF_UNITS : 2 * HALF_UNITS] = signed(raw_s[3][here], 1)
        own_copy(pack).start()

    def source(pack):
        return mine_att.at[pack] if pack < 2 else mine_ffn.at[pack - 2]

    def span(pack, start, count):
        return pl.ds(pl.multiple_of(start, 16), count)

    def block(pack, slot):
        return gathered.at[pack, slot, pl.ds(0, pack_rows(pack))]

    def remote(pack, kind):
        shared = SHARED[pack]
        rest = pack_rows(pack) - shared
        first = (rest // 2 + 15) // 16 * 16
        low = upper * shared
        if kind == 0 or kind == 1:
            here = span(pack, low, rest)
            src, dst = source(pack).at[here], gathered.at[pack, 2 + 2 * kind, here]
            peer = peers[2 + 2 * kind]
        elif kind == 2:
            here = span(pack, low, first)
            src, dst, peer = gathered.at[pack, 4, here], gathered.at[pack, 6, here], peers[2]
        elif kind == 3:
            here = span(pack, low + first, rest - first)
            src, dst, peer = gathered.at[pack, 2, here], gathered.at[pack, 6, here], peers[4]
        elif kind == 4:
            src, dst, peer = source(pack), block(pack, 1), peers[1]
        elif kind < 8:
            slot = 2 * (kind - 4)
            src, dst, peer = block(pack, slot), block(pack, slot + 1), peers[1]
        else:
            here = span(pack, upper * rest, shared)
            slot = 2 * (kind - 7)
            src, dst, peer = gathered.at[pack, slot, here], gathered.at[pack, slot, here], peers["z"]
        return pltpu.make_async_remote_copy(
            src_ref=src,
            dst_ref=dst,
            send_sem=send.at[pack, kind],
            recv_sem=recv.at[pack, kind],
            device_id=peer,
            device_id_type=MESH,
        )

    def first_sends(pack):
        for kind in (0, 1, 4):
            remote(pack, kind).start()

    def second_sends(pack):
        remote(pack, 0).wait_recv()
        remote(pack, 3).start()
        if SHARED[pack]:
            remote(pack, 8).start()
        remote(pack, 1).wait_recv()
        remote(pack, 2).start()
        if SHARED[pack]:
            remote(pack, 9).start()

    def plane_swap(pack):
        for kind in (0, 1):
            if SHARED[pack]:
                remote(pack, 8 + kind).wait_recv()
            remote(pack, 5 + kind).start()

    def far_sends(pack):
        remote(pack, 2).wait_recv()
        remote(pack, 3).wait_recv()
        if SHARED[pack]:
            remote(pack, 10).start()

    def far_swap(pack):
        if SHARED[pack]:
            remote(pack, 10).wait_recv()
        remote(pack, 7).start()

    places = {}

    def load_copy(pack, pair):
        here = pl.ds(0, pack_rows(pack))
        place = places[pack, pair]
        return pltpu.make_async_copy(
            gathered.at[pack, pl.ds(2 * pair, 2), here], wide.at[place, :, here], load.at[place]
        )

    def load_pair(pack, pair):
        places[pack, pair] = len(places) % 2
        if pair == 0:
            own_copy(pack).wait()
        remote(pack, 4 + pair).wait_recv()
        load_copy(pack, pair).start()

    started = set()

    def add_total(layer, kind, values):
        if (layer, kind) in started:
            total[layer] += values
        else:
            total[layer] = values
        started.add((layer, kind))

    def attention(pack, pair, place, qkv_ref, context_ref):
        weights = wide[place, :, 0:384].reshape(768, -1)
        projected = dot_nt(x_ref[...], weights)
        for side in range(2):
            slot = 2 * pair + side
            bias = wide[place, side, 512:528]
            bias_rows[pack, slot] = bias
            bias = to_float(bias[0:1])
            part = projected[:, side * 384 : side * 384 + 384]
            query = to_low(part[:, :COLS] + bias[:, :COLS])
            key = to_low(part[:, COLS : 2 * COLS])
            value = to_low(part[:, 2 * COLS :] + bias[:, COLS : 2 * COLS])
            qkv_ref[slot, :, 0:COLS] = query
            qkv_ref[slot, :, COLS : 2 * COLS] = key
            qkv_ref[slot, :, 2 * COLS : 3 * COLS] = value
            for number in range(pairs):
                here = slice(number * LEN, (number + 1) * LEN)
                scores = dot_nt(query[here], two_heads(key[here])) * (1.0 / math.sqrt(DH))
                probs = masked_probs(scores, lengths[me * pairs + number])
                part_context = dot(to_low(probs), two_heads(value[here]))
                context_ref[pair, here, side * COLS : (side + 1) * COLS] = to_low(part_context)
        put(pack, pl.ds(2 * pair, 2))
        if pack == 1:
            put(2, pair)
        add_total(pack, 0, dot(context_ref[pair], wide[place, :, 384:512].reshape(256, -1)))

    def first_norm(bias_ref, gain_ref, shift_ref, unit_ref, inverse_ref, index, low_ref):
        @pl.loop(0, rows // 64)
        def _(step):
            here = pl.ds(step * 64, 64)
            values = to_float(x_ref[here]) + total[index, here] + to_float(bias_ref[0:1])
            unit, inverse = norm_block(values)
            unit_ref[here] = unit
            inverse_ref[here] = inverse
            values = unit * to_float(gain_ref[0:1]) + to_float(shift_ref[0:1])
            normed[index, here] = values
            low_ref[here] = to_low(values)

    def feed_forward(pack, pair, place, low_ref, activation, hidden_ref, slope_ref):
        layer, half = divmod(pack - 2, 2)
        up = wide[place, :, 0:HALF_UNITS].reshape(2 * HALF_UNITS, -1)
        down = wide[place, :, HALF_UNITS : 2 * HALF_UNITS].reshape(2 * HALF_UNITS, -1)
        start = 2 * COLS + half * HALF_UNITS
        bias = jnp.concatenate(
            [
                to_float(bias_rows[layer, 2 * pair + side, 0:1, start : start + HALF_UNITS])
                for side in range(2)
            ],
            axis=1,
        )
        hidden, slope = activation(dot_nt(low_ref[...], up) + bias)
        hidden = to_low(hidden)
        slope_ref[half, pair] = to_low(slope)
        put(3 + layer, (half, pair))
        if hidden_ref is not None:
            hidden_ref[half, pair] = hidden
            put(5, (half, pair))
        add_total(layer, 1, dot(hidden, down))

    def step_teacher_end():
        @pl.loop(0, rows // 64)
        def _(step):
            here = pl.ds(step * 64, 64)
            unit, inverse = norm_block(normed[0, here] + total[0, here] + to_float(t_bias[1:2]))
            unit_two[here] = unit
            inverse_two[here] = inverse
            final_t[here] = unit * to_float(t_gain[1:2]) + to_float(t_shift[1:2])

    def step_student_end():
        vectors[...] = jnp.zeros_like(vectors)
        for step in range(rows // 64):
            here = pl.ds(step * 64, 64)
            unit, inverse = norm_block(normed[1, here] + total[1, here] + to_float(s_bias[1:2]))
            gain = to_float(s_gain[1:2])
            final = unit * gain + to_float(s_shift[1:2])
            final_low[here] = to_low(final)
            position = lax.broadcasted_iota(jnp.int32, (64, 1), 0) + step % 2 * 64
            valid = position < lengths[me * pairs + step // 2]
            grad = jnp.where(valid, final - final_t[here], 0.0)
            back = norm_back(grad, unit, inverse, gain)
            grad_s[here] = back
            grad_t[here] = norm_back(
                -grad, unit_two[here], inverse_two[here], to_float(t_gain[1:2])
            )
            for name in (11, 12, 13):
                put(name, here)
            vectors[0:1] += jnp.sum(back, axis=0, keepdims=True)
            vectors[1:2] += jnp.sum(grad * unit, axis=0, keepdims=True)
            vectors[2:3] += jnp.sum(grad, axis=0, keepdims=True)

    def use(pack, pair):
        place = places[pack, pair]
        load_copy(pack, pair).wait()
        if pack == 0:
            attention(0, pair, place, qkv_t, context_t)
        elif pack == 1:
            attention(1, pair, place, qkv_s, context_s)
        elif pack < 4:
            feed_forward(pack, pair, place, low_t, plain_act, None, slope_t)
        else:
            feed_forward(pack, pair, place, low_s, clipped_act, hidden_s, slope_s)

    def end(pack):
        if pack == 0:
            first_norm(t_bias, t_gain, t_shift, unit_t, inverse_t, 0, low_t)
            put(6)
            put(7)
        elif pack == 1:
            first_norm(s_bias, s_gain, s_shift, unit_s, inverse_s, 1, low_s)
            for name in (8, 9, 10):
                put(name)
        elif pack == 3:
            step_teacher_end()

    def meet():
        pl.semaphore_wait(barrier, len(peers))

    actions = (meet, prepare, first_sends, second_sends, plane_swap, far_sends, far_swap, load_pair, use, end)
    for action, *which in FORWARD:
        actions[action](*which)
    step_student_end()
    for pack in range(PACKS):
        for kind in range(11 if SHARED[pack] else 8):
            remote(pack, kind).wait_send()
    for copy in saved:
        copy.wait()


def forward_both(lengths, tokens, teacher, student):
    rows, features = tokens.shape
    low, full = jnp.bfloat16, jnp.float32
    vmem = pl.BlockSpec(memory_space=pltpu.VMEM)
    hbm = pl.BlockSpec(memory_space=pl.ANY)
    dma = pltpu.SemaphoreType.DMA
    act = (2, 4, rows, 2 * HALF_UNITS)
    kept = [
        ((SLOTS, rows, 3 * COLS), low),
        ((SLOTS, rows, 3 * COLS), low),
        ((4, rows, 2 * COLS), low),
        (act, low),
        (act, low),
        (act, low),
        ((rows, features), full),
        ((rows, 1), full),
        ((rows, features), full),
        ((rows, 1), full),
        ((rows, features), low),
        ((rows, features), full),
        ((rows, features), full),
        ((rows, features), low),
    ]
    shapes = [jax.ShapeDtypeStruct(shape, kind) for shape, kind in kept]
    qkv, out, up, down = teacher[0]
    return pl.pallas_call(
        forward_kernel,
        out_shape=[
            jax.ShapeDtypeStruct((PACKS, SLOTS, ATT_ROWS, features), low),
            shapes,
            jax.ShapeDtypeStruct((8, features), full),
        ],
        in_specs=[pl.BlockSpec(memory_space=pltpu.SMEM), vmem] + [[hbm] * 4, [vmem] * 5] * 2,
        out_specs=[hbm, [hbm] * len(kept), vmem],
        scratch_shapes=[
            [pltpu.VMEM(shape, kind) for shape, kind in kept],
            [pltpu.VMEM(qkv.shape, low), pltpu.VMEM(up.shape, low)],
            [pltpu.VMEM(item.shape, full) for item in (qkv, up, out, down)],
            pltpu.VMEM((2, ATT_ROWS, features), low),
            pltpu.VMEM((4, FFN_ROWS, features), low),
            pltpu.VMEM((2, 2, ATT_ROWS, features), low),
            pltpu.VMEM((2, rows, features), full),
            pltpu.VMEM((2, rows, features), full),
            pltpu.VMEM((rows, features), low),
            pltpu.VMEM((4, rows, 2 * COLS), low),
            pltpu.VMEM((2, SLOTS, 16, features), low),
            pltpu.VMEM((rows, features), full),
            pltpu.VMEM((rows, features), full),
            pltpu.VMEM((rows, 1), full),
            dma((PACKS, 11)),
            dma((PACKS, 11)),
            dma((2,)),
            dma((9 + PACKS,)),
            dma((64,)),
        ],
        compiler_params=pltpu.CompilerParams(
            collective_id=0, has_side_effects=True, vmem_limit_bytes=62 * 1024 * 1024
        ),
        name="forward_both",
    )(lengths, tokens, *teacher, *student)


CHUNKS = 3
PARTS = (4, 4, 8)
ORDER = (3, 1, 2, 0)
STUDENT_FFN, STUDENT_ATT, TEACHER_FFN, TEACHER_ATT = range(4)

COMBINE, FOLD, OWN, MID, OUT, VEC = range(6)
SCHEDULE = {
    (1, 6): [(COMBINE, 0, 3)],
    (2, 6): [(COMBINE, 0, 1)],
    (3, 6): [(COMBINE, 0, 2)],
    (4, 6): [(COMBINE, 0, 0)],
    (5, 6): [(COMBINE, 1, 3), (FOLD, 0, 0)],
    (6, 6): [(COMBINE, 1, 1)],
    (7, 6): [(COMBINE, 1, 2)],
    (7, 7): [(COMBINE, 1, 0)],
    (8, 0): [(FOLD, 1, 0)],
    (8, 4): [(OWN, 0, 0)],
    (9, 1): [(COMBINE, 2, 3), (OWN, 0, 1)],
    (9, 3): [(MID, 0, 0)],
    (9, 6): [(OWN, 0, 2)],
    (10, 1): [(COMBINE, 2, 1), (MID, 0, 1)],
    (10, 2): [(OWN, 0, 3), (OUT, 0, 0)],
    (10, 6): [(MID, 0, 2)],
    (11, 0): [(OWN, 1, 0), (OUT, 0, 1), (COMBINE, 2, 2)],
    (11, 1): [(MID, 0, 3)],
    (11, 3): [(OWN, 1, 1), (OUT, 0, 2)],
    (11, 6): [(MID, 1, 0)],
    (12, 6): [(COMBINE, 2, 0), (OWN, 1, 2), (OUT, 0, 3)],
    (13, 6): [(MID, 1, 1), (VEC, 0)],
    (14, 6): [(OWN, 1, 3), (OUT, 1, 0)],
    (15, 6): [(VEC, 1)],
    (16, 6): [(MID, 1, 2)],
    (17, 6): [(VEC, 2)],
    (18, 6): [(OUT, 1, 1)],
    (19, 6): [(VEC, 3)],
    (19, 7): [(FOLD, 2, 0), (MID, 1, 3), (OUT, 1, 2)],
    (20, 6): [(OWN, 2, 0), (VEC, 4)],
    (21, 2): [(OWN, 2, 1), (OUT, 1, 3)],
    (21, 6): [(OWN, 2, 2), (MID, 2, 0)],
    (22, 2): [(OWN, 2, 3), (MID, 2, 1)],
    (22, 6): [(OWN, 2, 4), (MID, 2, 2), (OUT, 2, 0)],
    (23, 1): [(OUT, 2, 1), (MID, 2, 3), (OWN, 2, 5)],
    (23, 4): [(OUT, 2, 2), (MID, 2, 4), (OWN, 2, 6)],
}
LAST = [
    (OUT, 2, 3),
    (MID, 2, 5),
    (OWN, 2, 7),
    (OUT, 2, 4),
    (MID, 2, 6),
    (OUT, 2, 5),
    (MID, 2, 7),
    (OUT, 2, 6),
    (OUT, 2, 7),
]


def backward_kernel(
    lengths,
    x_hbm,
    gathered,
    qkv_t,
    qkv_s,
    context_s,
    slope_t,
    slope_s,
    hidden_s,
    unit_t,
    inverse_t,
    unit_s,
    inverse_s,
    low_s,
    grad_t,
    grad_s,
    vectors,
    t_gain,
    s_gain,
    grad_out,
    sums_out,
    vec,
    x_ref,
    grad_in,
    wide,
    hidden_buf,
    slope_buf,
    qkv_s_buf,
    qkv_t_buf,
    context_buf,
    extra_buf,
    unit_buf,
    inverse_buf,
    grad_buf,
    total,
    low_y,
    low_z,
    low_a,
    proj,
    sums,
    even,
    odd,
    from_core,
    from_far,
    from_x,
    from_y,
    from_z,
    from_vec,
    load,
    state_sem,
    odd_send,
    odd_recv,
    free,
    far_send,
    far_recv,
    x_send,
    x_recv,
    y_send,
    y_recv,
    in_send,
    in_recv,
    mid_send,
    mid_recv,
    out_send,
    out_recv,
    vec_send,
    vec_recv,
    done,
):
    me = lax.axis_index("mp")
    z = lax.axis_index("dp")
    rows = x_ref.shape[0]
    pairs = rows // LEN
    core, along_x, along_y = ({"mp": flipped(me, bits)} for bits in (1, 2, 4))
    z_outer, z_inner = {"dp": flipped(z, 1)}, {"dp": 3 - z}
    z_two = {"dp": flipped(z, 2)}
    inner = jnp.logical_or(z == 1, z == 2)
    outer = jnp.logical_or(z == 0, z == 3)

    barrier = pltpu.get_barrier_semaphore()
    greeted = (core, along_x, along_y, z_outer, z_inner, z_two)
    for peer in greeted:
        pl.semaphore_signal(barrier, inc=1, device_id=peer, device_id_type=MESH)

    def remote(src, dst, send, recv, peer):
        return pltpu.make_async_remote_copy(
            src_ref=src, dst_ref=dst, send_sem=send, recv_sem=recv, device_id=peer, device_id_type=MESH
        )

    steps = [(STUDENT_FFN, 4 + half, pair) for half in range(2) for pair in ORDER]
    steps += [(STUDENT_ATT, 1, pair) for pair in ORDER]
    steps += [(TEACHER_FFN, 2 + half, pair) for half in range(2) for pair in range(4)]
    steps += [(TEACHER_ATT, 0, pair) for pair in range(4)]

    def loads(number):
        kind, pack, pair = steps[number]
        place = number % 2
        two = pl.ds(2 * pair, 2)
        here = pl.ds(0, FFN_ROWS)
        moves = [(gathered.at[pack, two, here], wide.at[place])]
        if kind == STUDENT_FFN:
            moves.append((hidden_s.at[pack - 4, pair], hidden_buf.at[place]))
            moves.append((slope_s.at[pack - 4, pair], slope_buf.at[place]))
        elif kind == TEACHER_FFN:
            moves.append((slope_t.at[pack - 2, pair], slope_buf.at[place]))
        else:
            moves.append((qkv_t.at[two], qkv_t_buf.at[place]))
            if kind == STUDENT_ATT:
                moves.append((qkv_s.at[two], qkv_s_buf.at[place]))
                moves.append((context_s.at[pair], context_buf.at[place]))
        return [
            pltpu.make_async_copy(src, dst, load.at[place, index])
            for index, (src, dst) in enumerate(moves)
        ]

    def state(layer):
        unit, inverse, grad = ((unit_t, inverse_t, grad_t), (unit_s, inverse_s, grad_s))[layer]
        moves = [(grad, grad_buf), (inverse, inverse_buf), (unit, unit_buf)]
        return [
            pltpu.make_async_copy(src, dst, state_sem.at[index])
            for index, (src, dst) in enumerate(moves)
        ]

    def slot_row(slot):
        row = me
        for bits in (1, 2, 4):
            if slot & bits:
                row = flipped(row, bits)
        return row

    def odd_copy(number):
        pair = steps[number][2]
        return remote(
            odd.at[number % 2], from_core.at[pair], odd_send.at[number % 2], odd_recv.at[pair], core
        )

    def keep(chunk, pair):
        return sums.at[chunk] if pair == 0 else even.at[chunk, pair - 1]

    def give(number, pieces):
        pair = steps[number][2]
        chunk = number // 4
        if number >= 2:
            odd_copy(number - 2).wait_send()
        for start, values in pieces:
            count = values.shape[0] // 2
            keep(chunk, pair)[start : start + count] = to_low(values[:count])
            odd[number % 2, start : start + count] = to_low(values[count:])
        if chunk:
            pl.semaphore_wait(free.at[pair], 1)
        if number == 0:
            pl.semaphore_wait(barrier, len(greeted))
        odd_copy(number).start()

    def add_rows(target, others, start, count):
        @pl.loop(0, count // 64)
        def _(step):
            here = pl.ds(start + step * 64, 64)
            value = to_float(target[here])
            for other in others:
                value = value + to_float(other[here])
            target[here] = to_low(value)

    def combine(chunk, pair):
        number = chunk * 4 + ORDER.index(pair)
        odd_copy(number).wait_recv()
        add_rows(keep(chunk, pair), [from_core.at[pair]], 0, FFN_ROWS)
        if chunk < CHUNKS - 1:
            pl.semaphore_signal(free.at[pair], inc=1, device_id=core, device_id_type=MESH)
        if pair == 3:
            far_copy(chunk, 0).start()
            far_copy(chunk, 1).start()

    def far_copy(chunk, way):
        part = pl.ds(way * 256, 256)
        return remote(
            even.at[chunk, 2, part],
            from_far.at[chunk, part],
            far_send.at[chunk, way],
            far_recv.at[chunk, way],
            (along_x, along_y)[way],
        )

    def part_rows(chunk):
        return FFN_ROWS // PARTS[chunk]

    def part_span(chunk, part):
        return pl.ds(part * part_rows(chunk), part_rows(chunk))

    def plane_copies(chunk, part):
        here = part_span(chunk, part)
        return [
            remote(even.at[chunk, 0, here], from_x.at[chunk, here], x_send.at[chunk, part], x_recv.at[chunk, part], along_x),
            remote(even.at[chunk, 1, here], from_y.at[chunk, here], y_send.at[chunk, part], y_recv.at[chunk, part], along_y),
        ]

    def fold(chunk, _):
        far_copy(chunk, 0).wait_recv()
        add_rows(keep(chunk, 2), [from_far.at[chunk]], 0, 256)
        far_copy(chunk, 1).wait_recv()
        add_rows(keep(chunk, 1), [from_far.at[chunk]], 256, 256)
        for part in range(PARTS[chunk]):
            for copy in plane_copies(chunk, part):
                copy.start()

    def z_copy(chunk, part, kind):
        here = part_span(chunk, part)
        own, first, second = sums.at[chunk, here], from_z.at[chunk, 0, here], from_z.at[chunk, 1, here]
        if kind == 0:
            return remote(own, first, in_send.at[chunk, part], in_recv.at[chunk, part], z_outer)
        if kind == 1:
            return remote(own, second, mid_send.at[chunk, part], mid_recv.at[chunk, part], z_inner)
        return remote(first, first, out_send.at[chunk, part], out_recv.at[chunk, part], z_outer)

    def own_part(chunk, part):
        for copy in plane_copies(chunk, part):
            copy.wait_recv()
        add_rows(sums.at[chunk], [from_x.at[chunk], from_y.at[chunk]], part * part_rows(chunk), part_rows(chunk))

        @pl.when(outer)
        def _():
            z_copy(chunk, part, 0).start()

    def mid_part(chunk, part):
        @pl.when(inner)
        def _():
            z_copy(chunk, part, 0).wait_recv()
            add_rows(sums.at[chunk], [from_z.at[chunk, 0]], part * part_rows(chunk), part_rows(chunk))
            z_copy(chunk, part, 1).start()

    def end_part(chunk, part):
        @pl.when(inner)
        def _():
            z_copy(chunk, part, 1).wait_recv()

            @pl.loop(0, part_rows(chunk) // 64)
            def _(step):
                here = pl.ds(part * part_rows(chunk) + step * 64, 64)
                value = to_float(sums[chunk, here]) + to_float(from_z[chunk, 1, here])
                from_z[chunk, 0, here] = to_low(value)

            z_copy(chunk, part, 2).start()

    def store_copy(chunk):
        return pltpu.make_async_copy(from_z.at[chunk, 0], sums_out.at[chunk], done.at[chunk])

    def finish(chunk):
        @pl.when(outer)
        def _():
            for part in range(PARTS[chunk]):
                z_copy(chunk, part, 2).wait_recv()

        store_copy(chunk).start()

    ways = (core, along_x, along_y, z_outer, z_two)

    def vec_copy(way):
        return remote(vec, from_vec.at[way], vec_send.at[way], vec_recv.at[way], ways[way])

    def vec_add(way):
        vec_copy(way).wait_send()
        vec_copy(way).wait_recv()
        vec[...] += from_vec[way]
        if way + 1 < len(ways):
            vec_copy(way + 1).start()

    def put_bias(pair, start, values):
        count = values.shape[1] // 2
        for side in range(2):
            line = lax.broadcasted_iota(jnp.int32, (SLOTS, count), 0)
            part = jnp.broadcast_to(values[:, side * count : (side + 1) * count], (SLOTS, count))
            part = jnp.where(line == slot_row(2 * pair + side), part, 0.0)
            vec[0:SLOTS, start : start + count] += part

    def ffn_step(number):
        kind, pack, pair = steps[number]
        place = number % 2
        up = wide[place, :, 0:HALF_UNITS].reshape(2 * HALF_UNITS, -1)
        down = wide[place, :, HALF_UNITS : 2 * HALF_UNITS].reshape(2 * HALF_UNITS, -1)
        back = dot_nt(low_z[...], down) * to_float(slope_buf[place])
        back_low = to_low(back)
        total[...] += dot(back_low, up)
        if kind == STUDENT_FFN:
            put_bias(pair, 2 * COLS + (pack - 4) * HALF_UNITS, jnp.sum(back, axis=0, keepdims=True))
            up_grad = dot_tn(back_low, low_y[...])
            down_grad = dot_tn(hidden_buf[place], low_z[...])
            give(number, [(0, up_grad), (HALF_UNITS, down_grad)])

    def pick(both):
        first = lax.broadcasted_iota(jnp.int32, (LEN, COLS), 1) < DH
        return jnp.where(first, both[:LEN], both[LEN:])

    def attention_step(number):
        kind, pack, pair = steps[number]
        place = number % 2
        student = kind == STUDENT_ATT
        factor = 1.0 / math.sqrt(DH)
        qkv = qkv_s_buf if student else qkv_t_buf
        out = wide[place, :, 384:512].reshape(2 * COLS, -1)
        context_back = to_low(dot_nt(low_a[...], out))
        query_sums, value_sums = [], []
        for side in range(2):
            query_sum = jnp.zeros((1, COLS), jnp.float32)
            value_sum = jnp.zeros((1, COLS), jnp.float32)
            for number_b in range(pairs):
                here = slice(number_b * LEN, (number_b + 1) * LEN)
                length = lengths[me * pairs + number_b]
                query, key, value = [
                    qkv[place, side, here, i * COLS : (i + 1) * COLS] for i in range(3)
                ]
                keys, values = two_heads(key), two_heads(value)
                scores = dot_nt(query, keys) * factor
                probs = masked_probs(scores, length)
                if student:
                    other = dot_nt(
                        qkv_t_buf[place, side, here, 0:COLS],
                        two_heads(qkv_t_buf[place, side, here, COLS : 2 * COLS]),
                    )
                    spot = lax.broadcasted_iota(jnp.int32, scores.shape, 1)
                    spot = jnp.where(spot < LEN, spot, spot - LEN)
                    line = lax.broadcasted_iota(jnp.int32, scores.shape, 0)
                    gap = score_weight * (scores - other * factor)
                    extra = jnp.where(jnp.maximum(spot, line) < length, gap, 0.0)
                    extra_buf[pair, side, number_b] = to_low(extra)
                else:
                    extra = -to_float(extra_buf[pair, side, number_b])
                part = context_back[here, side * COLS : (side + 1) * COLS]
                probs_back = dot_nt(part, values)
                value_back = pick(dot_tn(to_low(probs), part))
                product = probs * probs_back
                inner_sum = jnp.concatenate(
                    [
                        jnp.broadcast_to(
                            jnp.sum(product[:, i * LEN : (i + 1) * LEN], axis=1, keepdims=True), (LEN, LEN)
                        )
                        for i in range(2)
                    ],
                    axis=1,
                )
                score_back = to_low(product - probs * inner_sum + extra)
                query_back = dot(score_back, keys) * factor
                key_back = pick(dot_tn(score_back, query)) * factor
                start = side * 3 * COLS
                proj[here, start : start + COLS] = to_low(query_back)
                proj[here, start + COLS : start + 2 * COLS] = to_low(key_back)
                proj[here, start + 2 * COLS : start + 3 * COLS] = to_low(value_back)
                if student:
                    query_sum += jnp.sum(query_back, axis=0, keepdims=True)
                    value_sum += jnp.sum(value_back, axis=0, keepdims=True)
                if side * pairs + number_b < 2 * pairs - 1:
                    after(number, side * pairs + number_b)
            query_sums.append(query_sum)
            value_sums.append(value_sum)
        grad_in[...] += dot(proj[...], wide[place, :, 0:384].reshape(768, -1))
        if student:
            put_bias(pair, 0, jnp.concatenate(query_sums, axis=1))
            put_bias(pair, COLS, jnp.concatenate(value_sums, axis=1))
            qkv_grad = dot_tn(proj[...], x_ref[...])
            out_grad = dot_tn(context_buf[place], low_a[...])
            give(number, [(0, qkv_grad), (3 * COLS, out_grad)])

    def lower_grad():
        @pl.loop(0, rows // 64)
        def _(step):
            here = pl.ds(step * 64, 64)
            low_z[here] = to_low(grad_buf[here])

        total[...] = jnp.zeros_like(total)

    def norm_step(student):
        gain_ref = s_gain if student else t_gain

        @pl.loop(0, rows // 64)
        def _(step):
            here = pl.ds(step * 64, 64)
            grad = grad_buf[here] + total[here]
            unit = unit_buf[here]
            back = norm_back(grad, unit, inverse_buf[here], to_float(gain_ref[0:1]))
            low_a[here] = to_low(back)
            if student:
                grad_in[here] = back
                vec[8:9] += jnp.sum(back, axis=0, keepdims=True)
                vec[9:10] += jnp.sum(grad * unit, axis=0, keepdims=True)
                vec[10:11] += jnp.sum(grad, axis=0, keepdims=True)
            else:
                grad_in[here] += back

    actions = (combine, fold, own_part, mid_part, end_part, vec_add)

    def after(number, part):
        for action, *which in SCHEDULE.get((number, part), ()):
            actions[action](*which)

    low_copy = pltpu.make_async_copy(low_s, low_y, state_sem.at[3])
    x_copy = pltpu.make_async_copy(x_hbm, x_ref, done.at[CHUNKS])
    grad_first, *others = state(1)
    grad_first.start()
    for copy in loads(0):
        copy.start()
    for copy in (low_copy, *others, x_copy):
        copy.start()
    vec[...] = jnp.zeros_like(vec)
    vec[11:14] = vectors[0:3]
    grad_first.wait()
    lower_grad()
    low_copy.wait()
    grad_copy = pltpu.make_async_copy(grad_in, grad_out, done.at[CHUNKS + 1])
    for number, (kind, pack, pair) in enumerate(steps):
        for copy in loads(number):
            copy.wait()
        if number + 1 < len(steps):
            for copy in loads(number + 1):
                copy.start()
        if kind in (STUDENT_FFN, TEACHER_FFN):
            ffn_step(number)
        else:
            attention_step(number)
        if number == len(steps) - 1:
            grad_copy.start()
        after(number, 6)
        if number == 7:
            for copy in others:
                copy.wait()
            x_copy.wait()
            norm_step(True)
            for copy in state(0):
                copy.start()
        elif number == 11:
            for copy in state(0):
                copy.wait()
            lower_grad()
            vec_copy(0).start()
        elif number == 19:
            norm_step(False)
        after(number, 7)
    for action, *which in LAST:
        actions[action](*which)
    for chunk in range(CHUNKS):
        finish(chunk)

    grad_copy.wait()
    odd_copy(10).wait_send()
    odd_copy(11).wait_send()
    for chunk in range(CHUNKS):
        far_copy(chunk, 0).wait_send()
        far_copy(chunk, 1).wait_send()
        for part in range(PARTS[chunk]):
            for copy in plane_copies(chunk, part):
                copy.wait_send()

            @pl.when(outer)
            def _():
                z_copy(chunk, part, 0).wait_send()

            @pl.when(inner)
            def _():
                z_copy(chunk, part, 1).wait_send()
                z_copy(chunk, part, 2).wait_send()

        store_copy(chunk).wait()


def backward_both(lengths, tokens, kept, vectors, t_gain, s_gain):
    rows, features = tokens.shape
    low, full = jnp.bfloat16, jnp.float32
    vmem = pl.BlockSpec(memory_space=pltpu.VMEM)
    hbm = pl.BlockSpec(memory_space=pl.ANY)
    dma = pltpu.SemaphoreType.DMA
    block = (FFN_ROWS, features)
    return pl.pallas_call(
        backward_kernel,
        out_shape=[
            jax.ShapeDtypeStruct((rows, features), full),
            jax.ShapeDtypeStruct((CHUNKS,) + block, low),
            jax.ShapeDtypeStruct((16, features), full),
        ],
        in_specs=[pl.BlockSpec(memory_space=pltpu.SMEM), hbm] + [hbm] * len(kept) + [vmem] * 3,
        out_specs=[hbm, hbm, vmem],
        scratch_shapes=[
            pltpu.VMEM((rows, features), low),
            pltpu.VMEM((rows, features), full),
            pltpu.VMEM((2, 2) + block, low),
            pltpu.VMEM((2, rows, 2 * HALF_UNITS), low),
            pltpu.VMEM((2, rows, 2 * HALF_UNITS), low),
            pltpu.VMEM((2, 2, rows, 3 * COLS), low),
            pltpu.VMEM((2, 2, rows, 3 * COLS), low),
            pltpu.VMEM((2, rows, 2 * COLS), low),
            pltpu.VMEM((4, 2, rows // LEN, LEN, 2 * LEN), low),
            pltpu.VMEM((rows, features), full),
            pltpu.VMEM((rows, 1), full),
            pltpu.VMEM((rows, features), full),
            pltpu.VMEM((rows, features), full),
            pltpu.VMEM((rows, features), low),
            pltpu.VMEM((rows, features), low),
            pltpu.VMEM((rows, features), low),
            pltpu.VMEM((rows, 6 * COLS), low),
            pltpu.VMEM((CHUNKS,) + block, low),
            pltpu.VMEM((CHUNKS, 3) + block, low),
            pltpu.VMEM((2,) + block, low),
            pltpu.VMEM((4,) + block, low),
            pltpu.VMEM((CHUNKS,) + block, low),
            pltpu.VMEM((CHUNKS,) + block, low),
            pltpu.VMEM((CHUNKS,) + block, low),
            pltpu.VMEM((CHUNKS, 2) + block, low),
            pltpu.VMEM((5, 16, features), full),
            dma((2, 5)),
            dma((4,)),
            dma((2,)),
            dma((4,)),
            pltpu.SemaphoreType.REGULAR((4,)),
            dma((CHUNKS, 2)),
            dma((CHUNKS, 2)),
        ]
        + [dma((CHUNKS, max(PARTS)))] * 10
        + [dma((5,)), dma((5,)), dma((CHUNKS + 2,))],
        compiler_params=pltpu.CompilerParams(
            collective_id=1, has_side_effects=True, vmem_limit_bytes=63 * 1024 * 1024
        ),
        name="backward_both",
    )(lengths, tokens, *kept, vectors, t_gain, s_gain)


def finish_kernel(sums, vec, qkv_out, qv_out, out_out, up_out, up_bias_out, down_out, bias_out, gain_out, shift_out):
    for i in range(3):
        qkv_out[i] = to_float(sums[2, i * COLS : (i + 1) * COLS]).T
    out_out[...] = to_float(sums[2, 3 * COLS :])
    for half in range(2):
        here = slice(half * HALF_UNITS, (half + 1) * HALF_UNITS)
        up_out[:, here] = to_float(sums[half, :HALF_UNITS]).T
        down_out[here] = to_float(sums[half, HALF_UNITS:])
    line = lax.broadcasted_iota(jnp.int32, (SLOTS, vec.shape[1]), 0)
    row = jnp.sum(jnp.where(line == lax.axis_index("mp"), vec[0:SLOTS], 0.0), axis=0, keepdims=True)
    qv_out[0:1] = row[:, :COLS]
    qv_out[1:2] = row[:, COLS : 2 * COLS]
    up_bias_out[...] = row[:, 2 * COLS : 2 * COLS + 2 * HALF_UNITS]
    for index, ref in enumerate((bias_out, gain_out, shift_out)):
        ref[0:1] = vec[8 + index : 9 + index]
        ref[1:2] = vec[11 + index : 12 + index]


def finish_sums(sums, vec):
    features = vec.shape[1]
    shapes = [
        (3, features, COLS),
        (2, COLS),
        (COLS, features),
        (features, 2 * HALF_UNITS),
        (1, 2 * HALF_UNITS),
        (2 * HALF_UNITS, features),
        (2, features),
        (2, features),
        (2, features),
    ]
    vmem = pl.BlockSpec(memory_space=pltpu.VMEM)
    return pl.pallas_call(
        finish_kernel,
        out_shape=[jax.ShapeDtypeStruct(shape, jnp.float32) for shape in shapes],
        in_specs=[vmem, vmem],
        out_specs=[vmem] * len(shapes),
        compiler_params=pltpu.CompilerParams(vmem_limit_bytes=48 * 1024 * 1024),
        name="finish_sums",
    )(sums, vec)


def cut(values, count, axis):
    return jnp.split(values, count, axis=axis)


def per_device(n_dp, n_mp, *args):
    (
        tokens,
        lengths,
        student_qkv,
        student_qv_bias,
        student_out,
        student_up,
        student_up_bias,
        student_down,
        student_out_bias,
        student_gain,
        student_shift,
        teacher_qkv,
        teacher_qv_bias,
        teacher_out,
        teacher_up,
        teacher_up_bias,
        teacher_down,
        teacher_out_bias,
        teacher_gain,
        teacher_shift,
    ) = args
    net = Cube(n_dp) if (n_dp, n_mp) == (4, 8) else Plain(n_mp)
    rows = tokens.shape[0]
    pairs = rows // LEN
    places = jnp.arange(LEN, dtype=jnp.int32)
    me = lax.axis_index("mp")
    own_lengths = lax.dynamic_slice_in_dim(lengths, me * pairs, pairs)
    valid = places[None, :] < own_lengths[:, None]
    token_valid = to_float(valid.reshape(rows, 1))
    pair_valid = valid[:, None, :, None] & valid[:, None, None, :]

    gain = to_float(student_gain)
    shift = to_float(student_shift)
    out_bias = to_float(student_out_bias)
    teach_gain = to_float(teacher_gain)
    if isinstance(net, Cube):
        gathered, (*kept, student_output), vecs = forward_both(
            lengths,
            tokens,
            (
                [teacher_qkv.transpose(1, 0, 2), teacher_out, teacher_up, teacher_down],
                [teacher_qv_bias, teacher_up_bias, teacher_out_bias, teacher_gain, teacher_shift],
            ),
            (
                [student_qkv.transpose(1, 0, 2), student_out, student_up, student_down],
                [student_qv_bias, student_up_bias, student_out_bias, student_gain, student_shift],
            ),
        )
        input_grad, sums, vec = backward_both(
            lengths, tokens, (gathered, *kept), vecs, teacher_gain, student_gain
        )
        grads = finish_sums(sums, vec)
        return (
            student_output,
            input_grad,
            grads[0].transpose(1, 0, 2),
            grads[1],
            grads[2],
            grads[3],
            grads[4].reshape(-1),
            *grads[5:],
        )
    else:
        teach = gather_layer(
            net, teacher_qkv, teacher_qv_bias, teacher_out, teacher_up, teacher_up_bias, teacher_down
        )
        stud = gather_layer(
            net,
            binarize(student_qkv, 0),
            student_qv_bias,
            binarize(student_out, 1),
            binarize(student_up, 0),
            student_up_bias,
            binarize(student_down, 1),
        )
        teach_final, teach_kept = forward(
            tokens, teach, to_float(teacher_out_bias), teach_gain, to_float(teacher_shift), plain_act, valid
        )
        final, kept = forward(tokens, stud, out_bias, gain, shift, clipped_act, valid)
        student_output = to_low(final)
        final_grad = token_valid * (final - teach_final)
        grad_s = norm_back(final_grad, kept[11], kept[12], gain[1])
        grad_t = norm_back(-final_grad, teach_kept[11], teach_kept[12], teach_gain[1])
        vecs = jnp.stack([jnp.sum(grad_s, axis=0), jnp.sum(final_grad * kept[11], axis=0), jnp.sum(final_grad, axis=0)])
    extra = score_weight * jnp.where(pair_valid, kept[3] - teach_kept[3], 0.0)

    second_grad, second_low, pre_grad, pre_low, normed_grad, first_grad = backward_ffn(
        kept, stud, grad_s, gain
    )
    hidden, normed_low, context = kept[9], kept[8], kept[5]
    unit_one = kept[6]
    down_grad = net.sum_dp(net.scatter(cut(to_low(dot_tn(hidden, second_low)), n_mp, 0)))
    up_grad = net.sum_dp(net.scatter(cut(to_low(dot_tn(normed_low, pre_low)), n_mp, 1)))
    first_low = to_low(first_grad)
    out_grad = net.sum_dp(net.scatter(cut(to_low(dot_tn(context, first_low)), n_mp, 0)))
    grads = backward_attention(kept, first_low, stud[3], extra)
    lows = [to_low(item) for item in grads]
    wide = jnp.concatenate(
        [to_low(dot_tn(tokens, item)) for item in lows], axis=0
    )
    qkv_grad = net.sum_dp(net.scatter(cut(wide, n_mp, 1)))
    features = tokens.shape[1]
    qkv_grad = qkv_grad.reshape(3, features, -1).transpose(1, 0, 2)

    teach_second, teach_slow, _, _, _, teach_first = backward_ffn(
        teach_kept, teach, grad_t, teach_gain
    )
    teach_grads = backward_attention(teach_kept, to_low(teach_first), teach[3], -extra)
    teach_lows = [to_low(item) for item in teach_grads]
    input_grad = first_grad + teach_first
    for item, matrix in zip(lows, stud[0]):
        input_grad = input_grad + dot_nt(item, matrix)
    for item, matrix in zip(teach_lows, teach[0]):
        input_grad = input_grad + dot_nt(item, matrix)

    vectors = [
        jnp.sum(first_grad, axis=0),
        vecs[0],
        jnp.sum(normed_grad * unit_one, axis=0),
        vecs[1],
        jnp.sum(normed_grad, axis=0),
        vecs[2],
        net.place(jnp.sum(grads[0], axis=0).reshape(n_mp, -1)).reshape(-1),
        net.place(jnp.sum(grads[2], axis=0).reshape(n_mp, -1)).reshape(-1),
    ]
    wide_vector = net.place(jnp.sum(pre_grad, axis=0).reshape(n_mp, -1)).reshape(-1, features)
    total = net.sum_all(jnp.concatenate([jnp.stack(vectors), wide_vector], axis=0))
    width = features // n_mp
    units = wide_vector.size // n_mp
    return (
        student_output,
        input_grad,
        qkv_grad,
        lax.dynamic_slice_in_dim(total[6:8], me * width, width, axis=1),
        out_grad,
        up_grad,
        lax.dynamic_slice_in_dim(total[8:].reshape(-1), me * units, units),
        down_grad,
        total[0:2],
        total[2:4],
        total[4:6],
    )


def solution(mesh):
    n_dp, n_mp = mesh.shape["dp"], mesh.shape["mp"]

    def body(*args):
        return per_device(n_dp, n_mp, *args)

    return jax.shard_map(
        body,
        mesh=mesh,
        in_specs=(
            P(("dp", "mp"), None),
            P("dp"),
            P(None, None, "mp"),
            P(None, "mp"),
            P("mp", None),
            P(None, "mp"),
            P("mp"),
            P("mp", None),
            P(),
            P(),
            P(),
            P(None, None, "mp"),
            P(None, "mp"),
            P("mp", None),
            P(None, "mp"),
            P("mp"),
            P("mp", None),
            P(),
            P(),
            P(),
        ),
        out_specs=(
            P(("dp", "mp"), None),
            P(("dp", "mp"), None),
            P(None, None, "mp"),
            P(None, "mp"),
            P("mp", None),
            P(None, "mp"),
            P("mp"),
            P("mp", None),
            P(),
            P(),
            P(),
        ),
        check_vma=False,
    )
```

```python
import math

import jax
import jax.numpy as jnp
from jax import lax
from jax.experimental import pallas as pl
from jax.experimental.pallas import tpu as pltpu
from jax.sharding import PartitionSpec as P

DH = 64
LEN = 128


norm_epsilon = 1e-06
clip_level = 2.5
score_weight = 0.05
masked_fill = -1000000000.0


def to_float(values):
    return values.astype(jnp.float32)


def to_low(values):
    return values.astype(jnp.bfloat16)


def binarize(matrix, axis_index):
    scaling = jnp.mean(jnp.abs(matrix), axis=axis_index, keepdims=True)
    return (scaling * jnp.sign(matrix)).astype(jnp.bfloat16)


def norm_stats(values):
    centred = values - jnp.mean(values, axis=-1, keepdims=True)
    variance = jnp.mean(centred * centred, axis=-1, keepdims=True)
    inverse = lax.rsqrt(variance + norm_epsilon)
    return (centred * inverse, inverse)


def norm_back(grad, unit, inverse, gain_row):
    scaled = grad * gain_row
    first = jnp.mean(scaled, axis=-1, keepdims=True)
    second = jnp.mean(scaled * unit, axis=-1, keepdims=True)
    return inverse * (scaled - first - unit * second)


def dot(left, right):
    return jnp.dot(left, right, preferred_element_type=jnp.float32)


def dot_nt(left, right):
    return lax.dot_general(left, right, (((1,), (1,)), ((), ())), preferred_element_type=jnp.float32)


def dot_tn(left, right):
    return lax.dot_general(left, right, (((0,), (0,)), ((), ())), preferred_element_type=jnp.float32)


class Cube:
    def __init__(self, n_dp):
        self.n_dp = n_dp
        self.axes = ("dp", "mp")

    def flip(self, values, bits):
        pairs = [
            (z * 8 + m, z * 8 + (m ^ bits)) for z in range(self.n_dp) for m in range(8)
        ]
        return lax.ppermute(values, self.axes, pairs)

    def flip_dp(self, values, bits):
        pairs = [
            (z * 8 + m, (z ^ bits) * 8 + m) for z in range(self.n_dp) for m in range(8)
        ]
        return lax.ppermute(values, self.axes, pairs)

    def gather(self, block):
        half = block.shape[0] // 2
        along_x = self.flip(block, 2)
        along_y = self.flip(block, 4)
        across = jnp.concatenate(
            [self.flip(along_y[:half], 2), self.flip(along_x[half:], 4)], axis=0
        )
        same = [block, along_x, along_y, across]
        other = [self.flip(item, 1) for item in same]
        return [item for pair in zip(same, other) for item in pair]

    def scatter(self, blocks):
        half = blocks[0].shape[0] // 2
        own, to_x, to_y, to_far = [
            to_float(blocks[k]) + to_float(self.flip(blocks[k + 1], 1)) for k in (0, 2, 4, 6)
        ]
        far = to_low(to_far)
        via_x = to_float(self.flip(far[:half], 2))
        via_y = to_float(self.flip(far[half:], 4))
        to_y = to_low(jnp.concatenate([to_y[:half] + via_x, to_y[half:]], axis=0))
        to_x = to_low(jnp.concatenate([to_x[:half], to_x[half:] + via_y], axis=0))
        return own + to_float(self.flip(to_x, 2)) + to_float(self.flip(to_y, 4))

    def sum_dp(self, values):
        half = values.shape[0] // 2
        odd = lax.axis_index("dp") % 2
        low = to_low(values)
        sent = lax.dynamic_slice_in_dim(low, (1 - odd) * half, half)
        kept = lax.dynamic_slice_in_dim(values, odd * half, half)
        kept = kept + to_float(self.flip_dp(sent, 1))
        kept_low = to_low(kept)
        kept = to_low(kept + to_float(self.flip_dp(kept_low, 2)))
        other = self.flip_dp(kept, 1)
        return to_float(
            jnp.concatenate(
                [jnp.where(odd == 0, kept, other), jnp.where(odd == 0, other, kept)], axis=0
            )
        )

    def sum_all(self, values):
        for bits in (1, 2, 4):
            values = values + self.flip(values, bits)
        for bits in (1, 2):
            values = values + self.flip_dp(values, bits)
        return values

    def place(self, values):
        me = lax.axis_index("mp")
        for bit in range(3):
            shape = values.shape
            split = values.reshape((8 >> (bit + 1), 2, 1 << bit) + shape[1:])
            flipped = split[:, ::-1]
            values = jnp.where((me >> bit) % 2 == 1, flipped, split).reshape(shape)
        return values


class Plain:
    def __init__(self, n_mp):
        self.n_mp = n_mp

    def gather(self, block):
        every = lax.all_gather(block, "mp", axis=0)
        return [every[k] for k in range(self.n_mp)]

    def scatter(self, blocks):
        return to_float(
            lax.psum_scatter(jnp.stack(blocks), "mp", scatter_dimension=0, tiled=False)
        )

    def sum_dp(self, values):
        return to_float(lax.psum(to_low(values), "dp"))

    def sum_all(self, values):
        return lax.psum(values, ("dp", "mp"))

    def place(self, values):
        return values


def plain_act(pre):
    gate = 0.5 * (1.0 + lax.erf(pre * math.sqrt(0.5)))
    slope = gate + pre * jnp.exp(-0.5 * pre * pre) * (1.0 / math.sqrt(2.0 * math.pi))
    return (pre * gate, slope)


def clipped_act(pre):
    value, slope = plain_act(pre)
    bent = jnp.tanh(value * (1.0 / clip_level))
    return (clip_level * bent, slope * (1.0 - bent * bent))


def gather_layer(net, qkv, qv_bias, out, up, up_bias, down):
    width = qkv.shape[2]
    units = up.shape[1]
    features = qkv.shape[0]
    extra = jnp.zeros((16, features), jnp.bfloat16)
    extra = extra.at[0, :width].set(qv_bias[0]).at[1, :width].set(qv_bias[1])
    extra = extra.at[2, :units].set(up_bias)
    qkv_parts = net.gather(qkv.transpose(1, 0, 2).reshape(3 * features, width))
    out_parts = net.gather(jnp.concatenate([out, extra], axis=0))
    up_parts = net.gather(up)
    down_parts = net.gather(down)
    count = len(qkv_parts)
    qkv_full = jnp.concatenate(
        [part.reshape(3, features, width) for part in qkv_parts], axis=2
    )
    out_full = jnp.concatenate([part[:width] for part in out_parts], axis=0)
    q_bias = jnp.concatenate([part[width, :width] for part in out_parts])
    v_bias = jnp.concatenate([part[width + 1, :width] for part in out_parts])
    up_b = jnp.concatenate([part[width + 2, :units] for part in out_parts])
    up_full = jnp.concatenate(up_parts, axis=1)
    down_full = jnp.concatenate(down_parts, axis=0)
    return (qkv_full, to_float(q_bias), to_float(v_bias), out_full, up_full, to_float(up_b), down_full)


def forward(tokens, weights, out_bias, gain, shift, activation, key_valid):
    qkv, q_bias, v_bias, out, up, up_bias, down = weights
    rows, features = tokens.shape
    pairs = rows // LEN
    shape = (pairs, LEN, features // DH, DH)
    query = to_low(dot(tokens, qkv[0]) + q_bias).reshape(shape)
    key = to_low(dot(tokens, qkv[1])).reshape(shape)
    value = to_low(dot(tokens, qkv[2]) + v_bias).reshape(shape)
    scores = jnp.einsum("bqhe,bkhe->bhqk", query, key, preferred_element_type=jnp.float32) * (
        1.0 / math.sqrt(DH)
    )
    masked = jnp.where(key_valid[:, None, None, :], scores, masked_fill)
    log_norm = jax.nn.logsumexp(masked, axis=-1, keepdims=True)
    attention = jnp.exp(masked - log_norm)
    context = jnp.einsum(
        "bhqk,bkhe->bqhe", to_low(attention), value, preferred_element_type=jnp.float32
    )
    context = to_low(context).reshape(rows, features)
    first = to_float(tokens) + dot(context, out) + out_bias[0]
    unit_one, inverse_one = norm_stats(first)
    normed = unit_one * gain[0] + shift[0]
    normed_low = to_low(normed)
    hidden, slope = activation(dot(normed_low, up) + up_bias)
    hidden = to_low(hidden)
    second = normed + dot(hidden, down) + out_bias[1]
    unit_two, inverse_two = norm_stats(second)
    final = unit_two * gain[1] + shift[1]
    kept = (query, key, value, scores, attention, context, unit_one, inverse_one, normed_low, hidden,
            to_low(slope), unit_two, inverse_two)
    return (final, kept)


def backward_ffn(kept, weights, second_grad, gain):
    qkv, q_bias, v_bias, out, up, up_bias, down = weights
    (query, key, value, scores, attention, context, unit_one, inverse_one, normed_low, hidden,
     slope, unit_two, inverse_two) = kept
    second_low = to_low(second_grad)
    pre_grad = dot_nt(second_low, down) * slope
    pre_low = to_low(pre_grad)
    normed_grad = second_grad + dot_nt(pre_low, up)
    first_grad = norm_back(normed_grad, unit_one, inverse_one, gain[0])
    return (second_grad, second_low, pre_grad, pre_low, normed_grad, first_grad)


def backward_attention(kept, first_low, out, extra):
    query, key, value, scores, attention = kept[:5]
    rows = first_low.shape[0]
    factor = 1.0 / math.sqrt(DH)
    context_grad = to_low(dot_nt(first_low, out)).reshape(query.shape)
    attention_grad = jnp.einsum(
        "bqhe,bkhe->bhqk", context_grad, value, preferred_element_type=jnp.float32
    )
    value_grad = jnp.einsum(
        "bhqk,bqhe->bkhe", to_low(attention), context_grad, preferred_element_type=jnp.float32
    )
    inner = jnp.sum(attention * attention_grad, axis=-1, keepdims=True)
    score_low = to_low(attention * (attention_grad - inner) + extra)
    query_grad = factor * jnp.einsum(
        "bhqk,bkhe->bqhe", score_low, key, preferred_element_type=jnp.float32
    )
    key_grad = factor * jnp.einsum(
        "bhqk,bqhe->bkhe", score_low, query, preferred_element_type=jnp.float32
    )
    return [item.reshape(rows, -1) for item in (query_grad, key_grad, value_grad)]


MESH = pl.DeviceIdType.MESH
SLOTS = 8
PACKS = 5
SHARED_FFN = 2
ATT_ROWS = 528
FFN_ROWS = 512
HALF_UNITS = 256
COLS = 128

SHARED = (240, 192, 0, 160, 0)
MEET, PREPARE, FIRST, SECOND, PLANE_SWAP, FAR_SENDS, FAR_SWAP, LOW, PART, LOAD, USE, END = range(12)
FORWARD = [
    (PREPARE, 0), (MEET,), (FIRST, 0), (PREPARE, 1), (FIRST, 1), (PREPARE, 2), (PREPARE, 3), (PREPARE, 4),
    (LOAD, 0, 0), (LOAD, 1, 0), (USE, 0, 0), (USE, 1, 0), (SECOND, 0), (FIRST, 2), (SECOND, 1), (FIRST, 3),
    (PLANE_SWAP, 0), (FAR_SENDS, 0), (LOAD, 0, 1), (LOAD, 0, 2), (USE, 0, 1), (USE, 0, 2), (PLANE_SWAP, 1),
    (LOAD, 1, 1), (LOAD, 1, 2), (USE, 1, 1), (SECOND, 2), (FIRST, 4), (PLANE_SWAP, 2), (USE, 1, 2), (FAR_SWAP, 0),
    (FAR_SENDS, 1), (LOAD, 0, 3), (USE, 0, 3), (END, 0), (FAR_SWAP, 1), (LOAD, 1, 3), (USE, 1, 3), (END, 1),
    (SECOND, 3), (LOAD, 3, 0), (LOAD, 4, 0), (USE, 3, 0), (USE, 4, 0), (FAR_SENDS, 2), (FAR_SWAP, 2), (LOW,),
    (LOAD, 2, 0), (LOAD, 2, 1), (USE, 2, 0), (LOAD, 2, 2), (USE, 2, 1), (LOAD, 2, 3), (USE, 2, 2), (USE, 2, 3),
    (PART,), (PLANE_SWAP, 3), (LOAD, 3, 1), (LOAD, 3, 2), (USE, 3, 1), (SECOND, 4), (PLANE_SWAP, 4), (USE, 3, 2),
    (LOAD, 4, 1), (LOAD, 4, 2), (USE, 4, 1), (FAR_SENDS, 3), (USE, 4, 2), (END, 2), (FAR_SENDS, 4), (FAR_SWAP, 4),
    (FAR_SWAP, 3), (LOAD, 4, 3), (LOAD, 3, 3), (USE, 4, 3), (USE, 3, 3), (END, 4),
]


def flipped(me, bits):
    return me + bits - 2 * bits * lax.rem(lax.div(me, bits), 2)


def pack_rows(pack):
    return ATT_ROWS if pack < 2 else FFN_ROWS


def masked_probs(scores, length):
    rows = scores.shape[0]
    position = lax.broadcasted_iota(jnp.int32, (rows, LEN), 1)
    parts = []
    for head in range(2):
        part = jnp.where(position < length, scores[:, head * LEN : (head + 1) * LEN], masked_fill)
        part = jnp.exp(part - jnp.max(part, axis=1, keepdims=True))
        parts.append(part / jnp.sum(part, axis=1, keepdims=True))
    return jnp.concatenate(parts, axis=1)


def two_heads(rows):
    first = lax.broadcasted_iota(jnp.int32, rows.shape, 1) < DH
    zero = jnp.zeros_like(rows)
    return jnp.concatenate([jnp.where(first, rows, zero), jnp.where(first, zero, rows)], axis=0)


def norm_block(values):
    centred = values - jnp.mean(values, axis=1, keepdims=True)
    inverse = lax.rsqrt(jnp.mean(centred * centred, axis=1, keepdims=True) + norm_epsilon)
    return (centred * inverse, inverse)


def forward_kernel(
    lengths,
    x_ref,
    t_weights,
    t_small,
    s_weights,
    s_small,
    gathered,
    kept,
    vectors,
    scratch,
    raw_t,
    raw_s,
    mine_att,
    mine_ffn,
    wide,
    total,
    normed,
    low_t,
    context_t,
    bias_rows,
    final_t,
    unit_two,
    inverse_two,
    part_out,
    part_in,
    send,
    recv,
    swap_send,
    swap_recv,
    load,
    fetch,
    save,
):
    t_qv_bias, t_up_bias, t_bias, t_gain, t_shift = t_small
    s_qv_bias, s_up_bias, s_bias, s_gain, s_shift = s_small
    (qkv_t, qkv_s, context_s, slope_t, slope_s, hidden_s, unit_t, inverse_t, unit_s, inverse_s, low_s,
     grad_t, grad_s, final_low) = scratch
    saved = []

    def put(name, index=None):
        src, dst = scratch[name], kept[name]
        if index is not None:
            src, dst = src.at[index], dst.at[index]
        saved.append(pltpu.make_async_copy(src, dst, save.at[len(saved)]))
        saved[-1].start()

    me = lax.axis_index("mp")
    z = lax.axis_index("dp")
    peers = {bits: {"mp": flipped(me, bits)} for bits in (1, 2, 4)}
    peers["z"] = {"dp": flipped(z, 1)}
    upper = lax.rem(z, 2)
    rows = x_ref.shape[0]
    pairs = rows // LEN

    barrier = pltpu.get_barrier_semaphore()
    for peer in peers.values():
        pl.semaphore_signal(barrier, inc=1, device_id=peer, device_id_type=MESH)

    fetched = []
    for weights, raw, direct in ((t_weights, raw_t, True), (s_weights, raw_s, False)):
        qkv, out, up, down = weights
        if direct:
            half = pl.ds(pl.multiple_of(upper * HALF_UNITS, HALF_UNITS), HALF_UNITS)
            moves = [
                (qkv, raw[0]),
                (up.at[:, half], raw[1]),
                (out, mine_att.at[0, pl.ds(3 * COLS, COLS)]),
                (down.at[half], mine_ffn.at[0, pl.ds(HALF_UNITS, HALF_UNITS)]),
            ]
        else:
            moves = [(qkv, raw[0]), (up, raw[1]), (out, raw[2]), (down, raw[3])]
        for src, dst in moves:
            fetched.append(pltpu.make_async_copy(src, dst, fetch.at[len(fetched)]))
            fetched[-1].start()

    def signed(values, axis):
        scale = jnp.mean(jnp.abs(values), axis=axis, keepdims=True)
        return to_low(jnp.where(values > 0, scale, jnp.where(values < 0, -scale, 0.0)))

    def bias_block(qv_bias, up_bias):
        line = jnp.concatenate(
            [
                to_float(qv_bias[0:1]),
                to_float(qv_bias[1:2]),
                to_float(up_bias[...]).reshape(1, -1),
                jnp.zeros((1, x_ref.shape[1] - 2 * COLS - 2 * HALF_UNITS), jnp.float32),
            ],
            axis=1,
        )
        row = lax.broadcasted_iota(jnp.int32, (16, line.shape[1]), 0)
        return to_low(jnp.where(row == 0, jnp.broadcast_to(line, row.shape), 0.0))

    def own_copy(pack):
        return pltpu.make_async_copy(source(pack), block(pack, 0), fetch.at[8 + pack])

    def prepare(pack):
        if pack == 0:
            fetched[0].wait()
            for i in range(3):
                mine_att[0, i * COLS : (i + 1) * COLS] = raw_t[0][i].T
            mine_att[0, 4 * COLS : 4 * COLS + 16] = bias_block(t_qv_bias, t_up_bias)
            fetched[2].wait()
        elif pack == 1:
            fetched[4].wait()
            for i in range(3):
                mine_att[1, i * COLS : (i + 1) * COLS] = signed(raw_s[0][i], 0).T
            mine_att[1, 4 * COLS : 4 * COLS + 16] = bias_block(s_qv_bias, s_up_bias)
            fetched[6].wait()
            mine_att[1, 3 * COLS : 4 * COLS] = signed(raw_s[2][...], 1)
        elif pack == SHARED_FFN:
            fetched[1].wait()
            mine_ffn[0, 0:HALF_UNITS] = raw_t[1][...].T
            fetched[3].wait()
        else:
            half = pack - 3
            here = slice(half * HALF_UNITS, (half + 1) * HALF_UNITS)
            if half == 0:
                fetched[5].wait()
                fetched[7].wait()
            mine_ffn[1 + half, 0:HALF_UNITS] = signed(raw_s[1][:, here], 0).T
            mine_ffn[1 + half, HALF_UNITS : 2 * HALF_UNITS] = signed(raw_s[3][here], 1)
        own_copy(pack).start()

    def source(pack):
        return mine_att.at[pack] if pack < 2 else mine_ffn.at[pack - 2]

    def span(pack, start, count):
        return pl.ds(pl.multiple_of(start, 16), count)

    def block(pack, slot):
        return gathered.at[pack, slot, pl.ds(0, pack_rows(pack))]

    def remote(pack, kind):
        shared = SHARED[pack]
        rest = pack_rows(pack) - shared
        first = (rest // 2 + 15) // 16 * 16
        low = upper * shared
        if kind == 0 or kind == 1:
            here = span(pack, low, rest)
            src, dst = source(pack).at[here], gathered.at[pack, 2 + 2 * kind, here]
            peer = peers[2 + 2 * kind]
        elif kind == 2:
            here = span(pack, low, first)
            src, dst, peer = gathered.at[pack, 4, here], gathered.at[pack, 6, here], peers[2]
        elif kind == 3:
            here = span(pack, low + first, rest - first)
            src, dst, peer = gathered.at[pack, 2, here], gathered.at[pack, 6, here], peers[4]
        elif kind == 4:
            src, dst, peer = source(pack), block(pack, 1), peers[1]
        elif kind < 8:
            slot = 2 * (kind - 4)
            src, dst, peer = block(pack, slot), block(pack, slot + 1), peers[1]
        else:
            here = span(pack, upper * rest, shared)
            slot = 2 * (kind - 7)
            src, dst, peer = gathered.at[pack, slot, here], gathered.at[pack, slot, here], peers["z"]
        return pltpu.make_async_remote_copy(
            src_ref=src,
            dst_ref=dst,
            send_sem=send.at[pack, kind],
            recv_sem=recv.at[pack, kind],
            device_id=peer,
            device_id_type=MESH,
        )

    def first_sends(pack):
        for kind in (0, 1, 4):
            remote(pack, kind).start()

    def second_sends(pack):
        remote(pack, 0).wait_recv()
        remote(pack, 3).start()
        if SHARED[pack]:
            remote(pack, 8).start()
        remote(pack, 1).wait_recv()
        remote(pack, 2).start()
        if SHARED[pack]:
            remote(pack, 9).start()

    def plane_swap(pack):
        for kind in (0, 1):
            if SHARED[pack]:
                remote(pack, 8 + kind).wait_recv()
            remote(pack, 5 + kind).start()

    def far_sends(pack):
        remote(pack, 2).wait_recv()
        remote(pack, 3).wait_recv()
        if SHARED[pack]:
            remote(pack, 10).start()

    def far_swap(pack):
        if SHARED[pack]:
            remote(pack, 10).wait_recv()
        remote(pack, 7).start()

    places = {}

    def load_copy(pack, pair):
        here = pl.ds(0, pack_rows(pack))
        place = places[pack, pair]
        return pltpu.make_async_copy(
            gathered.at[pack, pl.ds(2 * pair, 2), here], wide.at[place, :, here], load.at[place]
        )

    def load_pair(pack, pair):
        places[pack, pair] = len(places) % 2
        if pair == 0:
            own_copy(pack).wait()
        remote(pack, 4 + pair).wait_recv()
        load_copy(pack, pair).start()

    started = set()
    student, own, both = slice(0, rows), slice(rows, 2 * rows), slice(rows, 3 * rows)

    def add_total(here, kind, values):
        if kind in started:
            total[here] += values
        else:
            total[here] = values
        started.add(kind)

    def attention(pack, pair, place, qkv_ref, context_ref):
        weights = wide[place, :, 0:384].reshape(768, -1)
        projected = dot_nt(x_ref[...], weights)
        for side in range(2):
            slot = 2 * pair + side
            bias = wide[place, side, 512:528]
            bias_rows[pack, slot] = bias
            bias = to_float(bias[0:1])
            part = projected[:, side * 384 : side * 384 + 384]
            query = to_low(part[:, :COLS] + bias[:, :COLS])
            key = to_low(part[:, COLS : 2 * COLS])
            value = to_low(part[:, 2 * COLS :] + bias[:, COLS : 2 * COLS])
            qkv_ref[slot, :, 0:COLS] = query
            qkv_ref[slot, :, COLS : 2 * COLS] = key
            qkv_ref[slot, :, 2 * COLS : 3 * COLS] = value
            for number in range(pairs):
                here = slice(number * LEN, (number + 1) * LEN)
                scores = dot_nt(query[here], two_heads(key[here])) * (1.0 / math.sqrt(DH))
                probs = masked_probs(scores, lengths[me * pairs + number])
                part_context = dot(to_low(probs), two_heads(value[here]))
                context_ref[pair, here, side * COLS : (side + 1) * COLS] = to_low(part_context)
        put(pack, pl.ds(2 * pair, 2))
        if pack == 1:
            put(2, pair)
        add_total((own, student)[pack], pack, dot(context_ref[pair], wide[place, :, 384:512].reshape(256, -1)))

    def first_norm(bias_ref, gain_ref, shift_ref, unit_ref, inverse_ref, index, low_ref, start):
        @pl.loop(0, rows // 64)
        def _(step):
            here = pl.ds(step * 64, 64)
            values = to_float(x_ref[here]) + total[pl.ds(start + step * 64, 64)] + to_float(bias_ref[0:1])
            unit, inverse = norm_block(values)
            unit_ref[here] = unit
            inverse_ref[here] = inverse
            values = unit * to_float(gain_ref[0:1]) + to_float(shift_ref[0:1])
            normed[index, here] = values
            low_ref[here] = to_low(values)

    def feed_forward(pack, pair, place, low_ref, activation, hidden_ref, slope_ref):
        up = wide[place, :, 0:HALF_UNITS].reshape(2 * HALF_UNITS, -1)
        down = wide[place, :, HALF_UNITS : 2 * HALF_UNITS].reshape(2 * HALF_UNITS, -1)
        layer, half = (0, upper) if pack == SHARED_FFN else (1, pack - 3)
        start = pl.multiple_of(2 * COLS + half * HALF_UNITS, HALF_UNITS)
        bias = jnp.concatenate(
            [to_float(bias_rows[layer, 2 * pair + side, 0:1, pl.ds(start, HALF_UNITS)]) for side in range(2)],
            axis=1,
        )
        hidden, slope = activation(dot_nt(low_ref[...], up) + bias)
        hidden = to_low(hidden)
        if pack == SHARED_FFN:
            slope_ref[pair] = to_low(slope)
            put(3, pair)
        else:
            slope_ref[half, pair] = to_low(slope)
            put(4, (half, pair))
            hidden_ref[half, pair] = hidden
            put(5, (half, pair))
        add_total((both, student)[layer], 2 + layer, dot(hidden, down))

    def swap(number, src, dst):
        return pltpu.make_async_remote_copy(
            src_ref=src,
            dst_ref=dst,
            send_sem=swap_send.at[number],
            recv_sem=swap_recv.at[number],
            device_id=peers["z"],
            device_id_type=MESH,
        )

    low_swap = swap(0, low_t.at[pl.ds(0, rows)], low_t.at[pl.ds(rows, rows)])
    part_swap = swap(1, part_out, part_in)

    def send_part():
        part_out[...] = to_low(total[2 * rows : 3 * rows])
        part_swap.start()

    def step_teacher_end():
        part_swap.wait_recv()

        @pl.loop(0, rows // 64)
        def _(step):
            here = pl.ds(step * 64, 64)
            unit, inverse = norm_block(
                normed[0, here]
                + total[pl.ds(rows + step * 64, 64)]
                + to_float(part_in[here])
                + to_float(t_bias[1:2])
            )
            unit_two[here] = unit
            inverse_two[here] = inverse
            final_t[here] = unit * to_float(t_gain[1:2]) + to_float(t_shift[1:2])

    def step_student_end():
        vectors[...] = jnp.zeros_like(vectors)
        for step in range(rows // 64):
            here = pl.ds(step * 64, 64)
            unit, inverse = norm_block(normed[1, here] + total[here] + to_float(s_bias[1:2]))
            gain = to_float(s_gain[1:2])
            final = unit * gain + to_float(s_shift[1:2])
            final_low[here] = to_low(final)
            position = lax.broadcasted_iota(jnp.int32, (64, 1), 0) + step % 2 * 64
            valid = position < lengths[me * pairs + step // 2]
            grad = jnp.where(valid, final - final_t[here], 0.0)
            back = norm_back(grad, unit, inverse, gain)
            grad_s[here] = back
            grad_t[here] = norm_back(
                -grad, unit_two[here], inverse_two[here], to_float(t_gain[1:2])
            )
            for name in (11, 12, 13):
                put(name, here)
            vectors[0:1] += jnp.sum(back, axis=0, keepdims=True)
            vectors[1:2] += jnp.sum(grad * unit, axis=0, keepdims=True)
            vectors[2:3] += jnp.sum(grad, axis=0, keepdims=True)

    def use(pack, pair):
        place = places[pack, pair]
        load_copy(pack, pair).wait()
        if pack == 0:
            attention(0, pair, place, qkv_t, context_t)
        elif pack == 1:
            attention(1, pair, place, qkv_s, context_s)
        elif pack == SHARED_FFN:
            feed_forward(pack, pair, place, low_t, plain_act, None, slope_t)
        else:
            feed_forward(pack, pair, place, low_s, clipped_act, hidden_s, slope_s)

    def end(pack):
        if pack == 0:
            first_norm(t_bias, t_gain, t_shift, unit_t, inverse_t, 0, low_t, rows)
            low_swap.start()
            put(6)
            put(7)
        elif pack == 1:
            first_norm(s_bias, s_gain, s_shift, unit_s, inverse_s, 1, low_s, 0)
            for name in (8, 9, 10):
                put(name)
        elif pack == SHARED_FFN:
            step_teacher_end()
        else:
            step_student_end()

    def meet():
        pl.semaphore_wait(barrier, len(peers))

    actions = (
        meet, prepare, first_sends, second_sends, plane_swap, far_sends, far_swap, low_swap.wait_recv, send_part,
        load_pair, use, end,
    )
    for action, *which in FORWARD:
        actions[action](*which)
    low_swap.wait_send()
    part_swap.wait_send()
    for pack in range(PACKS):
        for kind in range(11 if SHARED[pack] else 8):
            remote(pack, kind).wait_send()
    for copy in saved:
        copy.wait()


def forward_both(lengths, tokens, teacher, student):
    rows, features = tokens.shape
    low, full = jnp.bfloat16, jnp.float32
    vmem = pl.BlockSpec(memory_space=pltpu.VMEM)
    hbm = pl.BlockSpec(memory_space=pl.ANY)
    dma = pltpu.SemaphoreType.DMA
    act = (2, 4, rows, 2 * HALF_UNITS)
    kept = [
        ((SLOTS, rows, 3 * COLS), low),
        ((SLOTS, rows, 3 * COLS), low),
        ((4, rows, 2 * COLS), low),
        ((4, 2 * rows, 2 * HALF_UNITS), low),
        (act, low),
        (act, low),
        ((rows, features), full),
        ((rows, 1), full),
        ((rows, features), full),
        ((rows, 1), full),
        ((rows, features), low),
        ((rows, features), full),
        ((rows, features), full),
        ((rows, features), low),
    ]
    shapes = [jax.ShapeDtypeStruct(shape, kind) for shape, kind in kept]
    qkv, out, up, down = teacher[0]
    return pl.pallas_call(
        forward_kernel,
        out_shape=[
            jax.ShapeDtypeStruct((PACKS, SLOTS, ATT_ROWS, features), low),
            shapes,
            jax.ShapeDtypeStruct((8, features), full),
        ],
        in_specs=[pl.BlockSpec(memory_space=pltpu.SMEM), vmem] + [[hbm] * 4, [vmem] * 5] * 2,
        out_specs=[hbm, [hbm] * len(kept), vmem],
        scratch_shapes=[
            [pltpu.VMEM(shape, kind) for shape, kind in kept],
            [pltpu.VMEM(qkv.shape, low), pltpu.VMEM((features, HALF_UNITS), low)],
            [pltpu.VMEM(item.shape, full) for item in (qkv, up, out, down)],
            pltpu.VMEM((2, ATT_ROWS, features), low),
            pltpu.VMEM((3, FFN_ROWS, features), low),
            pltpu.VMEM((2, 2, ATT_ROWS, features), low),
            pltpu.VMEM((3 * rows, features), full),
            pltpu.VMEM((2, rows, features), full),
            pltpu.VMEM((2 * rows, features), low),
            pltpu.VMEM((4, rows, 2 * COLS), low),
            pltpu.VMEM((2, SLOTS, 16, features), low),
            pltpu.VMEM((rows, features), full),
            pltpu.VMEM((rows, features), full),
            pltpu.VMEM((rows, 1), full),
            pltpu.VMEM((rows, features), low),
            pltpu.VMEM((rows, features), low),
            dma((PACKS, 11)),
            dma((PACKS, 11)),
            dma((2,)),
            dma((2,)),
            dma((2,)),
            dma((8 + PACKS,)),
            dma((64,)),
        ],
        compiler_params=pltpu.CompilerParams(
            collective_id=0, has_side_effects=True, vmem_limit_bytes=62 * 1024 * 1024
        ),
        name="forward_both",
    )(lengths, tokens, *teacher, *student)


CHUNKS = 3
PARTS = (4, 4, 8)
ORDER = (3, 1, 2, 0)
STUDENT_FFN, STUDENT_ATT, TEACHER_FFN, TEACHER_ATT = range(4)

COMBINE, FOLD, OWN, MID, OUT, VEC = range(6)
SCHEDULE = {
    (1, 6): [(COMBINE, 0, 3)],
    (2, 6): [(COMBINE, 0, 1)],
    (3, 6): [(COMBINE, 0, 2)],
    (4, 6): [(COMBINE, 0, 0)],
    (5, 6): [(FOLD, 0, 0), (COMBINE, 1, 3)],
    (6, 6): [(COMBINE, 1, 1)],
    (7, 6): [(OWN, 0, 0), (COMBINE, 1, 2)],
    (7, 7): [(COMBINE, 1, 0)],
    (8, 6): [(OWN, 0, 1)],
    (9, 6): [(MID, 0, 0), (OWN, 0, 2)],
    (11, 6): [(MID, 0, 1), (OWN, 0, 3), (OUT, 0, 0)],
    (12, 1): [(MID, 0, 2)],
    (12, 6): [(OUT, 0, 1)],
    (13, 0): [(FOLD, 1, 0)],
    (13, 1): [(COMBINE, 2, 3)],
    (13, 2): [(OUT, 0, 2)],
    (14, 0): [(OWN, 1, 0)],
    (14, 1): [(COMBINE, 2, 1)],
    (14, 6): [(OWN, 1, 1), (MID, 0, 3)],
    (15, 1): [(COMBINE, 2, 2), (OWN, 1, 2)],
    (15, 3): [(MID, 1, 0)],
    (15, 6): [(OUT, 0, 3)],
    (15, 7): [(MID, 1, 1), (OWN, 1, 3), (COMBINE, 2, 0)],
    (16, 0): [(OUT, 1, 0)],
    (16, 3): [(VEC, 0)],
    (16, 4): [(MID, 1, 2)],
    (17, 0): [(OUT, 1, 1), (VEC, 1)],
    (17, 1): [(FOLD, 2, 0)],
    (17, 3): [(MID, 1, 3)],
    (17, 6): [(VEC, 2)],
    (18, 0): [(OUT, 1, 2), (OWN, 2, 0)],
    (18, 4): [(OWN, 2, 1)],
    (18, 6): [(VEC, 3)],
    (19, 0): [(MID, 2, 0), (OWN, 2, 2), (OUT, 1, 3)],
    (19, 3): [(MID, 2, 1), (OWN, 2, 3), (VEC, 4)],
    (19, 6): [(OUT, 2, 0), (MID, 2, 2)],
}
LAST = [
    (OWN, 2, 4), (OUT, 2, 1), (MID, 2, 3), (OWN, 2, 5), (OUT, 2, 2), (MID, 2, 4), (OWN, 2, 6), (OUT, 2, 3),
    (MID, 2, 5), (OWN, 2, 7), (OUT, 2, 4), (MID, 2, 6), (OUT, 2, 5), (MID, 2, 7), (OUT, 2, 6), (OUT, 2, 7),
]


def backward_kernel(
    lengths,
    x_hbm,
    gathered,
    qkv_t,
    qkv_s,
    context_s,
    slope_t,
    slope_s,
    hidden_s,
    unit_t,
    inverse_t,
    unit_s,
    inverse_s,
    low_s,
    grad_t,
    grad_s,
    vectors,
    t_gain,
    s_gain,
    grad_out,
    sums_out,
    vec,
    x_ref,
    grad_in,
    wide,
    hidden_buf,
    slope_buf,
    qkv_s_buf,
    qkv_t_buf,
    context_buf,
    extra_buf,
    unit_buf,
    inverse_buf,
    grad_buf,
    total,
    low_y,
    low_z,
    low_zt,
    back_out,
    back_in,
    low_a,
    proj,
    sums,
    even,
    odd,
    from_core,
    from_far,
    from_x,
    from_y,
    from_z,
    from_vec,
    load,
    state_sem,
    odd_send,
    odd_recv,
    free,
    far_send,
    far_recv,
    x_send,
    x_recv,
    y_send,
    y_recv,
    in_send,
    in_recv,
    mid_send,
    mid_recv,
    out_send,
    out_recv,
    vec_send,
    vec_recv,
    swap_send,
    swap_recv,
    done,
):
    me = lax.axis_index("mp")
    z = lax.axis_index("dp")
    rows = x_ref.shape[0]
    pairs = rows // LEN
    core, along_x, along_y = ({"mp": flipped(me, bits)} for bits in (1, 2, 4))
    z_outer, z_inner = {"dp": flipped(z, 1)}, {"dp": 3 - z}
    z_two = {"dp": flipped(z, 2)}
    inner = jnp.logical_or(z == 1, z == 2)
    outer = jnp.logical_or(z == 0, z == 3)

    barrier = pltpu.get_barrier_semaphore()
    greeted = (core, along_x, along_y, z_outer, z_inner, z_two)
    for peer in greeted:
        pl.semaphore_signal(barrier, inc=1, device_id=peer, device_id_type=MESH)

    def remote(src, dst, send, recv, peer):
        return pltpu.make_async_remote_copy(
            src_ref=src, dst_ref=dst, send_sem=send, recv_sem=recv, device_id=peer, device_id_type=MESH
        )

    steps = [(STUDENT_FFN, 3 + half, pair) for half in range(2) for pair in ORDER]
    steps += [(TEACHER_FFN, SHARED_FFN, pair) for pair in range(4)]
    steps += [(STUDENT_ATT, 1, pair) for pair in ORDER]
    steps += [(TEACHER_ATT, 0, pair) for pair in range(4)]
    norm_at = (7, 15)

    def given(number):
        return number if number < 8 else number - 4

    def loads(number):
        kind, pack, pair = steps[number]
        place = number % 2
        two = pl.ds(2 * pair, 2)
        here = pl.ds(0, FFN_ROWS)
        moves = [(gathered.at[pack, two, here], wide.at[place])]
        if kind == STUDENT_FFN:
            moves.append((hidden_s.at[pack - 3, pair], hidden_buf.at[place]))
            moves.append((slope_s.at[pack - 3, pair], slope_buf.at[place, pl.ds(0, rows)]))
        elif kind == TEACHER_FFN:
            moves.append((slope_t.at[pair], slope_buf.at[place]))
        else:
            moves.append((qkv_t.at[two], qkv_t_buf.at[place]))
            if kind == STUDENT_ATT:
                moves.append((qkv_s.at[two], qkv_s_buf.at[place]))
                moves.append((context_s.at[pair], context_buf.at[place]))
        return [
            pltpu.make_async_copy(src, dst, load.at[place, index])
            for index, (src, dst) in enumerate(moves)
        ]

    def state(layer):
        unit, inverse = ((unit_t, inverse_t), (unit_s, inverse_s))[layer]
        return [
            pltpu.make_async_copy(src, dst, state_sem.at[index])
            for index, (src, dst) in enumerate([(inverse, inverse_buf), (unit, unit_buf)])
        ]

    def slot_row(slot):
        row = me
        for bits in (1, 2, 4):
            if slot & bits:
                row = flipped(row, bits)
        return row

    def odd_copy(index):
        pair = ORDER[index % 4]
        return remote(
            odd.at[index % 2], from_core.at[pair], odd_send.at[index % 2], odd_recv.at[pair], core
        )

    def keep(chunk, pair):
        return sums.at[chunk] if pair == 0 else even.at[chunk, pair - 1]

    def give(number, pieces):
        pair = steps[number][2]
        index = given(number)
        chunk = index // 4
        if index >= 2:
            odd_copy(index - 2).wait_send()
        for start, values in pieces:
            count = values.shape[0] // 2
            keep(chunk, pair)[start : start + count] = to_low(values[:count])
            odd[index % 2, start : start + count] = to_low(values[count:])
        if chunk:
            pl.semaphore_wait(free.at[pair], 1)
        if number == 0:
            pl.semaphore_wait(barrier, len(greeted))
        odd_copy(index).start()

    def add_rows(target, others, start, count):
        @pl.loop(0, count // 64)
        def _(step):
            here = pl.ds(start + step * 64, 64)
            value = to_float(target[here])
            for other in others:
                value = value + to_float(other[here])
            target[here] = to_low(value)

    def combine(chunk, pair):
        number = chunk * 4 + ORDER.index(pair)
        odd_copy(number).wait_recv()
        add_rows(keep(chunk, pair), [from_core.at[pair]], 0, FFN_ROWS)
        if chunk < CHUNKS - 1:
            pl.semaphore_signal(free.at[pair], inc=1, device_id=core, device_id_type=MESH)
        if pair == 3:
            far_copy(chunk, 0).start()
            far_copy(chunk, 1).start()

    def far_copy(chunk, way):
        part = pl.ds(way * 256, 256)
        return remote(
            even.at[chunk, 2, part],
            from_far.at[chunk, part],
            far_send.at[chunk, way],
            far_recv.at[chunk, way],
            (along_x, along_y)[way],
        )

    def part_rows(chunk):
        return FFN_ROWS // PARTS[chunk]

    def part_span(chunk, part):
        return pl.ds(part * part_rows(chunk), part_rows(chunk))

    def plane_copies(chunk, part):
        here = part_span(chunk, part)
        return [
            remote(even.at[chunk, 0, here], from_x.at[chunk, here], x_send.at[chunk, part], x_recv.at[chunk, part], along_x),
            remote(even.at[chunk, 1, here], from_y.at[chunk, here], y_send.at[chunk, part], y_recv.at[chunk, part], along_y),
        ]

    def fold(chunk, _):
        far_copy(chunk, 0).wait_recv()
        add_rows(keep(chunk, 2), [from_far.at[chunk]], 0, 256)
        far_copy(chunk, 1).wait_recv()
        add_rows(keep(chunk, 1), [from_far.at[chunk]], 256, 256)
        for part in range(PARTS[chunk]):
            for copy in plane_copies(chunk, part):
                copy.start()

    def z_copy(chunk, part, kind):
        here = part_span(chunk, part)
        own, first, second = sums.at[chunk, here], from_z.at[chunk, 0, here], from_z.at[chunk, 1, here]
        if kind == 0:
            return remote(own, first, in_send.at[chunk, part], in_recv.at[chunk, part], z_outer)
        if kind == 1:
            return remote(own, second, mid_send.at[chunk, part], mid_recv.at[chunk, part], z_inner)
        return remote(first, first, out_send.at[chunk, part], out_recv.at[chunk, part], z_outer)

    def own_part(chunk, part):
        for copy in plane_copies(chunk, part):
            copy.wait_recv()
        add_rows(sums.at[chunk], [from_x.at[chunk], from_y.at[chunk]], part * part_rows(chunk), part_rows(chunk))

        @pl.when(outer)
        def _():
            z_copy(chunk, part, 0).start()

    def mid_part(chunk, part):
        @pl.when(inner)
        def _():
            z_copy(chunk, part, 0).wait_recv()
            add_rows(sums.at[chunk], [from_z.at[chunk, 0]], part * part_rows(chunk), part_rows(chunk))
            z_copy(chunk, part, 1).start()

    def end_part(chunk, part):
        @pl.when(inner)
        def _():
            z_copy(chunk, part, 1).wait_recv()

            @pl.loop(0, part_rows(chunk) // 64)
            def _(step):
                here = pl.ds(part * part_rows(chunk) + step * 64, 64)
                value = to_float(sums[chunk, here]) + to_float(from_z[chunk, 1, here])
                from_z[chunk, 0, here] = to_low(value)

            z_copy(chunk, part, 2).start()

    def store_copy(chunk):
        return pltpu.make_async_copy(from_z.at[chunk, 0], sums_out.at[chunk], done.at[chunk])

    def finish(chunk):
        @pl.when(outer)
        def _():
            for part in range(PARTS[chunk]):
                z_copy(chunk, part, 2).wait_recv()

        store_copy(chunk).start()

    ways = (core, along_x, along_y, z_outer, z_two)

    def vec_copy(way):
        return remote(vec, from_vec.at[way], vec_send.at[way], vec_recv.at[way], ways[way])

    def vec_add(way):
        vec_copy(way).wait_send()
        vec_copy(way).wait_recv()
        vec[...] += from_vec[way]
        if way + 1 < len(ways):
            vec_copy(way + 1).start()

    def put_bias(pair, start, values):
        count = values.shape[1] // 2
        for side in range(2):
            line = lax.broadcasted_iota(jnp.int32, (SLOTS, count), 0)
            part = jnp.broadcast_to(values[:, side * count : (side + 1) * count], (SLOTS, count))
            part = jnp.where(line == slot_row(2 * pair + side), part, 0.0)
            vec[0:SLOTS, start : start + count] += part

    def ffn_step(number):
        kind, pack, pair = steps[number]
        place = number % 2
        up = wide[place, :, 0:HALF_UNITS].reshape(2 * HALF_UNITS, -1)
        down = wide[place, :, HALF_UNITS : 2 * HALF_UNITS].reshape(2 * HALF_UNITS, -1)
        student = kind == STUDENT_FFN
        grad, here = (low_z, slice(0, rows)) if student else (low_zt, slice(0, 2 * rows))
        back = dot_nt(grad[...], down) * to_float(slope_buf[place, here])
        back_low = to_low(back)
        if number in (0, 8):
            total[here] = dot(back_low, up)
        else:
            total[here] += dot(back_low, up)
        if student:
            put_bias(pair, 2 * COLS + (pack - 3) * HALF_UNITS, jnp.sum(back, axis=0, keepdims=True))
            up_grad = dot_tn(back_low, low_y[...])
            down_grad = dot_tn(hidden_buf[place], low_z[...])
            give(number, [(0, up_grad), (HALF_UNITS, down_grad)])

    def pick(both):
        first = lax.broadcasted_iota(jnp.int32, (LEN, COLS), 1) < DH
        return jnp.where(first, both[:LEN], both[LEN:])

    def attention_step(number):
        kind, pack, pair = steps[number]
        place = number % 2
        student = kind == STUDENT_ATT
        factor = 1.0 / math.sqrt(DH)
        qkv = qkv_s_buf if student else qkv_t_buf
        out = wide[place, :, 384:512].reshape(2 * COLS, -1)
        context_back = to_low(dot_nt(low_a[...], out))
        query_sums, value_sums = [], []
        for side in range(2):
            query_sum = jnp.zeros((1, COLS), jnp.float32)
            value_sum = jnp.zeros((1, COLS), jnp.float32)
            for number_b in range(pairs):
                here = slice(number_b * LEN, (number_b + 1) * LEN)
                length = lengths[me * pairs + number_b]
                query, key, value = [
                    qkv[place, side, here, i * COLS : (i + 1) * COLS] for i in range(3)
                ]
                keys, values = two_heads(key), two_heads(value)
                scores = dot_nt(query, keys) * factor
                probs = masked_probs(scores, length)
                if student:
                    other = dot_nt(
                        qkv_t_buf[place, side, here, 0:COLS],
                        two_heads(qkv_t_buf[place, side, here, COLS : 2 * COLS]),
                    )
                    spot = lax.broadcasted_iota(jnp.int32, scores.shape, 1)
                    spot = jnp.where(spot < LEN, spot, spot - LEN)
                    line = lax.broadcasted_iota(jnp.int32, scores.shape, 0)
                    gap = score_weight * (scores - other * factor)
                    extra = jnp.where(jnp.maximum(spot, line) < length, gap, 0.0)
                    extra_buf[pair, side, number_b] = to_low(extra)
                else:
                    extra = -to_float(extra_buf[pair, side, number_b])
                part = context_back[here, side * COLS : (side + 1) * COLS]
                probs_back = dot_nt(part, values)
                value_back = pick(dot_tn(to_low(probs), part))
                product = probs * probs_back
                inner_sum = jnp.concatenate(
                    [
                        jnp.broadcast_to(
                            jnp.sum(product[:, i * LEN : (i + 1) * LEN], axis=1, keepdims=True), (LEN, LEN)
                        )
                        for i in range(2)
                    ],
                    axis=1,
                )
                score_back = to_low(product - probs * inner_sum + extra)
                query_back = dot(score_back, keys) * factor
                key_back = pick(dot_tn(score_back, query)) * factor
                start = side * 3 * COLS
                proj[here, start : start + COLS] = to_low(query_back)
                proj[here, start + COLS : start + 2 * COLS] = to_low(key_back)
                proj[here, start + 2 * COLS : start + 3 * COLS] = to_low(value_back)
                if student:
                    query_sum += jnp.sum(query_back, axis=0, keepdims=True)
                    value_sum += jnp.sum(value_back, axis=0, keepdims=True)
                if side * pairs + number_b < 2 * pairs - 1:
                    after(number, side * pairs + number_b)
            query_sums.append(query_sum)
            value_sums.append(value_sum)
        grad_in[...] += dot(proj[...], wide[place, :, 0:384].reshape(768, -1))
        if student:
            put_bias(pair, 0, jnp.concatenate(query_sums, axis=1))
            put_bias(pair, COLS, jnp.concatenate(value_sums, axis=1))
            qkv_grad = dot_tn(proj[...], x_ref[...])
            out_grad = dot_tn(context_buf[place], low_a[...])
            give(number, [(0, qkv_grad), (3 * COLS, out_grad)])

    def lower_grad(src, start, dst):
        @pl.loop(0, rows // 64)
        def _(step):
            dst[pl.ds(step * 64, 64)] = to_low(src[pl.ds(start + step * 64, 64)])

    grad_swap = remote(
        low_zt.at[pl.ds(0, rows)], low_zt.at[pl.ds(rows, rows)], swap_send.at[0], swap_recv.at[0], z_outer
    )
    back_swap = remote(back_out, back_in, swap_send.at[1], swap_recv.at[1], z_outer)

    def norm_step(student):
        gain_ref = s_gain if student else t_gain

        @pl.loop(0, rows // 64)
        def _(step):
            here = pl.ds(step * 64, 64)
            grad = grad_buf[here] + total[here]
            if not student:
                grad = grad + to_float(back_in[here])
            unit = unit_buf[here]
            back = norm_back(grad, unit, inverse_buf[here], to_float(gain_ref[0:1]))
            low_a[here] = to_low(back)
            if student:
                grad_in[here] = back
                vec[8:9] += jnp.sum(back, axis=0, keepdims=True)
                vec[9:10] += jnp.sum(grad * unit, axis=0, keepdims=True)
                vec[10:11] += jnp.sum(grad, axis=0, keepdims=True)
            else:
                grad_in[here] += back

    actions = (combine, fold, own_part, mid_part, end_part, vec_add)

    def after(number, part):
        for action, *which in SCHEDULE.get((number, part), ()):
            actions[action](*which)

    low_copy = pltpu.make_async_copy(low_s, low_y, state_sem.at[2])
    x_copy = pltpu.make_async_copy(x_hbm, x_ref, done.at[CHUNKS])
    grad_copies = [
        pltpu.make_async_copy(src, dst, state_sem.at[3 + index])
        for index, (src, dst) in enumerate(
            [(grad_s, grad_buf), (grad_t, total.at[pl.ds(rows, rows)]), (grad_t, grad_buf)]
        )
    ]
    grad_copies[0].start()
    for copy in loads(0):
        copy.start()
    for copy in (low_copy, grad_copies[1], *state(1), x_copy):
        copy.start()
    vec[...] = jnp.zeros_like(vec)
    vec[11:14] = vectors[0:3]
    grad_copies[0].wait()
    lower_grad(grad_buf, 0, low_z)
    low_copy.wait()
    grad_copy = pltpu.make_async_copy(grad_in, grad_out, done.at[CHUNKS + 1])
    for number, (kind, pack, pair) in enumerate(steps):
        for copy in loads(number):
            copy.wait()
        if number + 1 < len(steps):
            for copy in loads(number + 1):
                copy.start()
        if kind in (STUDENT_FFN, TEACHER_FFN):
            ffn_step(number)
        else:
            attention_step(number)
        if number == len(steps) - 1:
            grad_copy.start()
        after(number, 6)
        if number == 0:
            grad_copies[1].wait()
            lower_grad(total, rows, low_zt)
            grad_swap.start()
        elif number == 7:
            for copy in state(1):
                copy.wait()
            x_copy.wait()
            norm_step(True)
            for copy in (*state(0), grad_copies[2]):
                copy.start()
            grad_swap.wait_recv()
        elif number == 11:
            back_out[...] = to_low(total[rows : 2 * rows])
            back_swap.start()
        elif number == 15:
            vec_copy(0).start()
            for copy in (*state(0), grad_copies[2]):
                copy.wait()
            back_swap.wait_recv()
            norm_step(False)
        after(number, 7)
    for action, *which in LAST:
        actions[action](*which)
    for chunk in range(CHUNKS):
        finish(chunk)

    grad_copy.wait()
    grad_swap.wait_send()
    back_swap.wait_send()
    odd_copy(10).wait_send()
    odd_copy(11).wait_send()
    for chunk in range(CHUNKS):
        far_copy(chunk, 0).wait_send()
        far_copy(chunk, 1).wait_send()
        for part in range(PARTS[chunk]):
            for copy in plane_copies(chunk, part):
                copy.wait_send()

            @pl.when(outer)
            def _():
                z_copy(chunk, part, 0).wait_send()

            @pl.when(inner)
            def _():
                z_copy(chunk, part, 1).wait_send()
                z_copy(chunk, part, 2).wait_send()

        store_copy(chunk).wait()


def backward_both(lengths, tokens, kept, vectors, t_gain, s_gain):
    rows, features = tokens.shape
    low, full = jnp.bfloat16, jnp.float32
    vmem = pl.BlockSpec(memory_space=pltpu.VMEM)
    hbm = pl.BlockSpec(memory_space=pl.ANY)
    dma = pltpu.SemaphoreType.DMA
    block = (FFN_ROWS, features)
    return pl.pallas_call(
        backward_kernel,
        out_shape=[
            jax.ShapeDtypeStruct((rows, features), full),
            jax.ShapeDtypeStruct((CHUNKS,) + block, low),
            jax.ShapeDtypeStruct((16, features), full),
        ],
        in_specs=[pl.BlockSpec(memory_space=pltpu.SMEM), hbm] + [hbm] * len(kept) + [vmem] * 3,
        out_specs=[hbm, hbm, vmem],
        scratch_shapes=[
            pltpu.VMEM((rows, features), low),
            pltpu.VMEM((rows, features), full),
            pltpu.VMEM((2, 2) + block, low),
            pltpu.VMEM((2, rows, 2 * HALF_UNITS), low),
            pltpu.VMEM((2, 2 * rows, 2 * HALF_UNITS), low),
            pltpu.VMEM((2, 2, rows, 3 * COLS), low),
            pltpu.VMEM((2, 2, rows, 3 * COLS), low),
            pltpu.VMEM((2, rows, 2 * COLS), low),
            pltpu.VMEM((4, 2, rows // LEN, LEN, 2 * LEN), low),
            pltpu.VMEM((rows, features), full),
            pltpu.VMEM((rows, 1), full),
            pltpu.VMEM((rows, features), full),
            pltpu.VMEM((2 * rows, features), full),
            pltpu.VMEM((rows, features), low),
            pltpu.VMEM((rows, features), low),
            pltpu.VMEM((2 * rows, features), low),
            pltpu.VMEM((rows, features), low),
            pltpu.VMEM((rows, features), low),
            pltpu.VMEM((rows, features), low),
            pltpu.VMEM((rows, 6 * COLS), low),
            pltpu.VMEM((CHUNKS,) + block, low),
            pltpu.VMEM((CHUNKS, 3) + block, low),
            pltpu.VMEM((2,) + block, low),
            pltpu.VMEM((4,) + block, low),
            pltpu.VMEM((CHUNKS,) + block, low),
            pltpu.VMEM((CHUNKS,) + block, low),
            pltpu.VMEM((CHUNKS,) + block, low),
            pltpu.VMEM((CHUNKS, 2) + block, low),
            pltpu.VMEM((5, 16, features), full),
            dma((2, 5)),
            dma((6,)),
            dma((2,)),
            dma((4,)),
            pltpu.SemaphoreType.REGULAR((4,)),
            dma((CHUNKS, 2)),
            dma((CHUNKS, 2)),
        ]
        + [dma((CHUNKS, max(PARTS)))] * 10
        + [dma((5,)), dma((5,)), dma((2,)), dma((2,)), dma((CHUNKS + 2,))],
        compiler_params=pltpu.CompilerParams(
            collective_id=1, has_side_effects=True, vmem_limit_bytes=63 * 1024 * 1024
        ),
        name="backward_both",
    )(lengths, tokens, *kept, vectors, t_gain, s_gain)


def finish_kernel(sums, vec, qkv_out, qv_out, out_out, up_out, up_bias_out, down_out, bias_out, gain_out, shift_out):
    for i in range(3):
        qkv_out[i] = to_float(sums[2, i * COLS : (i + 1) * COLS]).T
    out_out[...] = to_float(sums[2, 3 * COLS :])
    for half in range(2):
        here = slice(half * HALF_UNITS, (half + 1) * HALF_UNITS)
        up_out[:, here] = to_float(sums[half, :HALF_UNITS]).T
        down_out[here] = to_float(sums[half, HALF_UNITS:])
    line = lax.broadcasted_iota(jnp.int32, (SLOTS, vec.shape[1]), 0)
    row = jnp.sum(jnp.where(line == lax.axis_index("mp"), vec[0:SLOTS], 0.0), axis=0, keepdims=True)
    qv_out[0:1] = row[:, :COLS]
    qv_out[1:2] = row[:, COLS : 2 * COLS]
    up_bias_out[...] = row[:, 2 * COLS : 2 * COLS + 2 * HALF_UNITS]
    for index, ref in enumerate((bias_out, gain_out, shift_out)):
        ref[0:1] = vec[8 + index : 9 + index]
        ref[1:2] = vec[11 + index : 12 + index]


def finish_sums(sums, vec):
    features = vec.shape[1]
    shapes = [
        (3, features, COLS),
        (2, COLS),
        (COLS, features),
        (features, 2 * HALF_UNITS),
        (1, 2 * HALF_UNITS),
        (2 * HALF_UNITS, features),
        (2, features),
        (2, features),
        (2, features),
    ]
    vmem = pl.BlockSpec(memory_space=pltpu.VMEM)
    return pl.pallas_call(
        finish_kernel,
        out_shape=[jax.ShapeDtypeStruct(shape, jnp.float32) for shape in shapes],
        in_specs=[vmem, vmem],
        out_specs=[vmem] * len(shapes),
        compiler_params=pltpu.CompilerParams(vmem_limit_bytes=48 * 1024 * 1024),
        name="finish_sums",
    )(sums, vec)


def cut(values, count, axis):
    return jnp.split(values, count, axis=axis)


def per_device(n_dp, n_mp, *args):
    (
        tokens,
        lengths,
        student_qkv,
        student_qv_bias,
        student_out,
        student_up,
        student_up_bias,
        student_down,
        student_out_bias,
        student_gain,
        student_shift,
        teacher_qkv,
        teacher_qv_bias,
        teacher_out,
        teacher_up,
        teacher_up_bias,
        teacher_down,
        teacher_out_bias,
        teacher_gain,
        teacher_shift,
    ) = args
    net = Cube(n_dp) if (n_dp, n_mp) == (4, 8) else Plain(n_mp)
    rows = tokens.shape[0]
    pairs = rows // LEN
    places = jnp.arange(LEN, dtype=jnp.int32)
    me = lax.axis_index("mp")
    own_lengths = lax.dynamic_slice_in_dim(lengths, me * pairs, pairs)
    valid = places[None, :] < own_lengths[:, None]
    token_valid = to_float(valid.reshape(rows, 1))
    pair_valid = valid[:, None, :, None] & valid[:, None, None, :]

    gain = to_float(student_gain)
    shift = to_float(student_shift)
    out_bias = to_float(student_out_bias)
    teach_gain = to_float(teacher_gain)
    if isinstance(net, Cube):
        gathered, (*kept, student_output), vecs = forward_both(
            lengths,
            tokens,
            (
                [teacher_qkv.transpose(1, 0, 2), teacher_out, teacher_up, teacher_down],
                [teacher_qv_bias, teacher_up_bias, teacher_out_bias, teacher_gain, teacher_shift],
            ),
            (
                [student_qkv.transpose(1, 0, 2), student_out, student_up, student_down],
                [student_qv_bias, student_up_bias, student_out_bias, student_gain, student_shift],
            ),
        )
        input_grad, sums, vec = backward_both(
            lengths, tokens, (gathered, *kept), vecs, teacher_gain, student_gain
        )
        grads = finish_sums(sums, vec)
        return (
            student_output,
            input_grad,
            grads[0].transpose(1, 0, 2),
            grads[1],
            grads[2],
            grads[3],
            grads[4].reshape(-1),
            *grads[5:],
        )
    else:
        teach = gather_layer(
            net, teacher_qkv, teacher_qv_bias, teacher_out, teacher_up, teacher_up_bias, teacher_down
        )
        stud = gather_layer(
            net,
            binarize(student_qkv, 0),
            student_qv_bias,
            binarize(student_out, 1),
            binarize(student_up, 0),
            student_up_bias,
            binarize(student_down, 1),
        )
        teach_final, teach_kept = forward(
            tokens, teach, to_float(teacher_out_bias), teach_gain, to_float(teacher_shift), plain_act, valid
        )
        final, kept = forward(tokens, stud, out_bias, gain, shift, clipped_act, valid)
        student_output = to_low(final)
        final_grad = token_valid * (final - teach_final)
        grad_s = norm_back(final_grad, kept[11], kept[12], gain[1])
        grad_t = norm_back(-final_grad, teach_kept[11], teach_kept[12], teach_gain[1])
        vecs = jnp.stack([jnp.sum(grad_s, axis=0), jnp.sum(final_grad * kept[11], axis=0), jnp.sum(final_grad, axis=0)])
    extra = score_weight * jnp.where(pair_valid, kept[3] - teach_kept[3], 0.0)

    second_grad, second_low, pre_grad, pre_low, normed_grad, first_grad = backward_ffn(
        kept, stud, grad_s, gain
    )
    hidden, normed_low, context = kept[9], kept[8], kept[5]
    unit_one = kept[6]
    down_grad = net.sum_dp(net.scatter(cut(to_low(dot_tn(hidden, second_low)), n_mp, 0)))
    up_grad = net.sum_dp(net.scatter(cut(to_low(dot_tn(normed_low, pre_low)), n_mp, 1)))
    first_low = to_low(first_grad)
    out_grad = net.sum_dp(net.scatter(cut(to_low(dot_tn(context, first_low)), n_mp, 0)))
    grads = backward_attention(kept, first_low, stud[3], extra)
    lows = [to_low(item) for item in grads]
    wide = jnp.concatenate(
        [to_low(dot_tn(tokens, item)) for item in lows], axis=0
    )
    qkv_grad = net.sum_dp(net.scatter(cut(wide, n_mp, 1)))
    features = tokens.shape[1]
    qkv_grad = qkv_grad.reshape(3, features, -1).transpose(1, 0, 2)

    teach_second, teach_slow, _, _, _, teach_first = backward_ffn(
        teach_kept, teach, grad_t, teach_gain
    )
    teach_grads = backward_attention(teach_kept, to_low(teach_first), teach[3], -extra)
    teach_lows = [to_low(item) for item in teach_grads]
    input_grad = first_grad + teach_first
    for item, matrix in zip(lows, stud[0]):
        input_grad = input_grad + dot_nt(item, matrix)
    for item, matrix in zip(teach_lows, teach[0]):
        input_grad = input_grad + dot_nt(item, matrix)

    vectors = [
        jnp.sum(first_grad, axis=0),
        vecs[0],
        jnp.sum(normed_grad * unit_one, axis=0),
        vecs[1],
        jnp.sum(normed_grad, axis=0),
        vecs[2],
        net.place(jnp.sum(grads[0], axis=0).reshape(n_mp, -1)).reshape(-1),
        net.place(jnp.sum(grads[2], axis=0).reshape(n_mp, -1)).reshape(-1),
    ]
    wide_vector = net.place(jnp.sum(pre_grad, axis=0).reshape(n_mp, -1)).reshape(-1, features)
    total = net.sum_all(jnp.concatenate([jnp.stack(vectors), wide_vector], axis=0))
    width = features // n_mp
    units = wide_vector.size // n_mp
    return (
        student_output,
        input_grad,
        qkv_grad,
        lax.dynamic_slice_in_dim(total[6:8], me * width, width, axis=1),
        out_grad,
        up_grad,
        lax.dynamic_slice_in_dim(total[8:].reshape(-1), me * units, units),
        down_grad,
        total[0:2],
        total[2:4],
        total[4:6],
    )


def solution(mesh):
    n_dp, n_mp = mesh.shape["dp"], mesh.shape["mp"]

    def body(*args):
        return per_device(n_dp, n_mp, *args)

    return jax.shard_map(
        body,
        mesh=mesh,
        in_specs=(
            P(("dp", "mp"), None),
            P("dp"),
            P(None, None, "mp"),
            P(None, "mp"),
            P("mp", None),
            P(None, "mp"),
            P("mp"),
            P("mp", None),
            P(),
            P(),
            P(),
            P(None, None, "mp"),
            P(None, "mp"),
            P("mp", None),
            P(None, "mp"),
            P("mp"),
            P("mp", None),
            P(),
            P(),
            P(),
        ),
        out_specs=(
            P(("dp", "mp"), None),
            P(("dp", "mp"), None),
            P(None, None, "mp"),
            P(None, "mp"),
            P("mp", None),
            P(None, "mp"),
            P("mp"),
            P("mp", None),
            P(),
            P(),
            P(),
        ),
        check_vma=False,
    )
```

```python
import math

import jax
import jax.numpy as jnp
from jax import lax
from jax.experimental import pallas as pl
from jax.experimental.pallas import tpu as pltpu
from jax.sharding import PartitionSpec as P

DH = 64
LEN = 128


norm_epsilon = 1e-06
clip_level = 2.5
score_weight = 0.05
masked_fill = -1000000000.0


def to_float(values):
    return values.astype(jnp.float32)


def to_low(values):
    return values.astype(jnp.bfloat16)


def binarize(matrix, axis_index):
    scaling = jnp.mean(jnp.abs(matrix), axis=axis_index, keepdims=True)
    return (scaling * jnp.sign(matrix)).astype(jnp.bfloat16)


def norm_stats(values):
    centred = values - jnp.mean(values, axis=-1, keepdims=True)
    variance = jnp.mean(centred * centred, axis=-1, keepdims=True)
    inverse = lax.rsqrt(variance + norm_epsilon)
    return (centred * inverse, inverse)


def norm_back(grad, unit, inverse, gain_row):
    scaled = grad * gain_row
    first = jnp.mean(scaled, axis=-1, keepdims=True)
    second = jnp.mean(scaled * unit, axis=-1, keepdims=True)
    return inverse * (scaled - first - unit * second)


def dot(left, right):
    return jnp.dot(left, right, preferred_element_type=jnp.float32)


def dot_nt(left, right):
    return lax.dot_general(left, right, (((1,), (1,)), ((), ())), preferred_element_type=jnp.float32)


def dot_tn(left, right):
    return lax.dot_general(left, right, (((0,), (0,)), ((), ())), preferred_element_type=jnp.float32)


class Cube:
    def __init__(self, n_dp):
        self.n_dp = n_dp
        self.axes = ("dp", "mp")

    def flip(self, values, bits):
        pairs = [
            (z * 8 + m, z * 8 + (m ^ bits)) for z in range(self.n_dp) for m in range(8)
        ]
        return lax.ppermute(values, self.axes, pairs)

    def flip_dp(self, values, bits):
        pairs = [
            (z * 8 + m, (z ^ bits) * 8 + m) for z in range(self.n_dp) for m in range(8)
        ]
        return lax.ppermute(values, self.axes, pairs)

    def gather(self, block):
        half = block.shape[0] // 2
        along_x = self.flip(block, 2)
        along_y = self.flip(block, 4)
        across = jnp.concatenate(
            [self.flip(along_y[:half], 2), self.flip(along_x[half:], 4)], axis=0
        )
        same = [block, along_x, along_y, across]
        other = [self.flip(item, 1) for item in same]
        return [item for pair in zip(same, other) for item in pair]

    def scatter(self, blocks):
        half = blocks[0].shape[0] // 2
        own, to_x, to_y, to_far = [
            to_float(blocks[k]) + to_float(self.flip(blocks[k + 1], 1)) for k in (0, 2, 4, 6)
        ]
        far = to_low(to_far)
        via_x = to_float(self.flip(far[:half], 2))
        via_y = to_float(self.flip(far[half:], 4))
        to_y = to_low(jnp.concatenate([to_y[:half] + via_x, to_y[half:]], axis=0))
        to_x = to_low(jnp.concatenate([to_x[:half], to_x[half:] + via_y], axis=0))
        return own + to_float(self.flip(to_x, 2)) + to_float(self.flip(to_y, 4))

    def sum_dp(self, values):
        half = values.shape[0] // 2
        odd = lax.axis_index("dp") % 2
        low = to_low(values)
        sent = lax.dynamic_slice_in_dim(low, (1 - odd) * half, half)
        kept = lax.dynamic_slice_in_dim(values, odd * half, half)
        kept = kept + to_float(self.flip_dp(sent, 1))
        kept_low = to_low(kept)
        kept = to_low(kept + to_float(self.flip_dp(kept_low, 2)))
        other = self.flip_dp(kept, 1)
        return to_float(
            jnp.concatenate(
                [jnp.where(odd == 0, kept, other), jnp.where(odd == 0, other, kept)], axis=0
            )
        )

    def sum_all(self, values):
        for bits in (1, 2, 4):
            values = values + self.flip(values, bits)
        for bits in (1, 2):
            values = values + self.flip_dp(values, bits)
        return values

    def place(self, values):
        me = lax.axis_index("mp")
        for bit in range(3):
            shape = values.shape
            split = values.reshape((8 >> (bit + 1), 2, 1 << bit) + shape[1:])
            flipped = split[:, ::-1]
            values = jnp.where((me >> bit) % 2 == 1, flipped, split).reshape(shape)
        return values


class Plain:
    def __init__(self, n_mp):
        self.n_mp = n_mp

    def gather(self, block):
        every = lax.all_gather(block, "mp", axis=0)
        return [every[k] for k in range(self.n_mp)]

    def scatter(self, blocks):
        return to_float(
            lax.psum_scatter(jnp.stack(blocks), "mp", scatter_dimension=0, tiled=False)
        )

    def sum_dp(self, values):
        return to_float(lax.psum(to_low(values), "dp"))

    def sum_all(self, values):
        return lax.psum(values, ("dp", "mp"))

    def place(self, values):
        return values


def plain_act(pre):
    gate = 0.5 * (1.0 + lax.erf(pre * math.sqrt(0.5)))
    slope = gate + pre * jnp.exp(-0.5 * pre * pre) * (1.0 / math.sqrt(2.0 * math.pi))
    return (pre * gate, slope)


def clipped_act(pre):
    value, slope = plain_act(pre)
    bent = jnp.tanh(value * (1.0 / clip_level))
    return (clip_level * bent, slope * (1.0 - bent * bent))


def gather_layer(net, qkv, qv_bias, out, up, up_bias, down):
    width = qkv.shape[2]
    units = up.shape[1]
    features = qkv.shape[0]
    extra = jnp.zeros((16, features), jnp.bfloat16)
    extra = extra.at[0, :width].set(qv_bias[0]).at[1, :width].set(qv_bias[1])
    extra = extra.at[2, :units].set(up_bias)
    qkv_parts = net.gather(qkv.transpose(1, 0, 2).reshape(3 * features, width))
    out_parts = net.gather(jnp.concatenate([out, extra], axis=0))
    up_parts = net.gather(up)
    down_parts = net.gather(down)
    count = len(qkv_parts)
    qkv_full = jnp.concatenate(
        [part.reshape(3, features, width) for part in qkv_parts], axis=2
    )
    out_full = jnp.concatenate([part[:width] for part in out_parts], axis=0)
    q_bias = jnp.concatenate([part[width, :width] for part in out_parts])
    v_bias = jnp.concatenate([part[width + 1, :width] for part in out_parts])
    up_b = jnp.concatenate([part[width + 2, :units] for part in out_parts])
    up_full = jnp.concatenate(up_parts, axis=1)
    down_full = jnp.concatenate(down_parts, axis=0)
    return (qkv_full, to_float(q_bias), to_float(v_bias), out_full, up_full, to_float(up_b), down_full)


def forward(tokens, weights, out_bias, gain, shift, activation, key_valid):
    qkv, q_bias, v_bias, out, up, up_bias, down = weights
    rows, features = tokens.shape
    pairs = rows // LEN
    shape = (pairs, LEN, features // DH, DH)
    query = to_low(dot(tokens, qkv[0]) + q_bias).reshape(shape)
    key = to_low(dot(tokens, qkv[1])).reshape(shape)
    value = to_low(dot(tokens, qkv[2]) + v_bias).reshape(shape)
    scores = jnp.einsum("bqhe,bkhe->bhqk", query, key, preferred_element_type=jnp.float32) * (
        1.0 / math.sqrt(DH)
    )
    masked = jnp.where(key_valid[:, None, None, :], scores, masked_fill)
    log_norm = jax.nn.logsumexp(masked, axis=-1, keepdims=True)
    attention = jnp.exp(masked - log_norm)
    context = jnp.einsum(
        "bhqk,bkhe->bqhe", to_low(attention), value, preferred_element_type=jnp.float32
    )
    context = to_low(context).reshape(rows, features)
    first = to_float(tokens) + dot(context, out) + out_bias[0]
    unit_one, inverse_one = norm_stats(first)
    normed = unit_one * gain[0] + shift[0]
    normed_low = to_low(normed)
    hidden, slope = activation(dot(normed_low, up) + up_bias)
    hidden = to_low(hidden)
    second = normed + dot(hidden, down) + out_bias[1]
    unit_two, inverse_two = norm_stats(second)
    final = unit_two * gain[1] + shift[1]
    kept = (query, key, value, scores, attention, context, unit_one, inverse_one, normed_low, hidden,
            to_low(slope), unit_two, inverse_two)
    return (final, kept)


def backward_ffn(kept, weights, second_grad, gain):
    qkv, q_bias, v_bias, out, up, up_bias, down = weights
    (query, key, value, scores, attention, context, unit_one, inverse_one, normed_low, hidden,
     slope, unit_two, inverse_two) = kept
    second_low = to_low(second_grad)
    pre_grad = dot_nt(second_low, down) * slope
    pre_low = to_low(pre_grad)
    normed_grad = second_grad + dot_nt(pre_low, up)
    first_grad = norm_back(normed_grad, unit_one, inverse_one, gain[0])
    return (second_grad, second_low, pre_grad, pre_low, normed_grad, first_grad)


def backward_attention(kept, first_low, out, extra):
    query, key, value, scores, attention = kept[:5]
    rows = first_low.shape[0]
    factor = 1.0 / math.sqrt(DH)
    context_grad = to_low(dot_nt(first_low, out)).reshape(query.shape)
    attention_grad = jnp.einsum(
        "bqhe,bkhe->bhqk", context_grad, value, preferred_element_type=jnp.float32
    )
    value_grad = jnp.einsum(
        "bhqk,bqhe->bkhe", to_low(attention), context_grad, preferred_element_type=jnp.float32
    )
    inner = jnp.sum(attention * attention_grad, axis=-1, keepdims=True)
    score_low = to_low(attention * (attention_grad - inner) + extra)
    query_grad = factor * jnp.einsum(
        "bhqk,bkhe->bqhe", score_low, key, preferred_element_type=jnp.float32
    )
    key_grad = factor * jnp.einsum(
        "bhqk,bqhe->bkhe", score_low, query, preferred_element_type=jnp.float32
    )
    return [item.reshape(rows, -1) for item in (query_grad, key_grad, value_grad)]


MESH = pl.DeviceIdType.MESH
SLOTS = 8
PACKS = 5
SHARED_FFN = 2
ATT_ROWS = 528
FFN_ROWS = 512
HALF_UNITS = 256
COLS = 128

SHARED = (240, 192, 0, 160, 0)
MEET, PREPARE, FIRST, SECOND, PLANE_SWAP, FAR_SENDS, FAR_SWAP, LOW, PART, LOAD, USE, END = range(12)
FORWARD = [
    (PREPARE, 0), (MEET,), (FIRST, 0), (PREPARE, 1), (FIRST, 1), (PREPARE, 2), (PREPARE, 3), (PREPARE, 4),
    (LOAD, 0, 0), (LOAD, 1, 0), (USE, 0, 0), (USE, 1, 0), (SECOND, 0), (FIRST, 2), (SECOND, 1), (FIRST, 3),
    (PLANE_SWAP, 0), (FAR_SENDS, 0), (LOAD, 0, 1), (LOAD, 0, 2), (USE, 0, 1), (USE, 0, 2), (PLANE_SWAP, 1),
    (LOAD, 1, 1), (LOAD, 1, 2), (USE, 1, 1), (SECOND, 2), (FIRST, 4), (PLANE_SWAP, 2), (USE, 1, 2), (FAR_SWAP, 0),
    (FAR_SENDS, 1), (LOAD, 0, 3), (USE, 0, 3), (END, 0), (FAR_SWAP, 1), (LOAD, 1, 3), (USE, 1, 3), (END, 1),
    (SECOND, 3), (LOAD, 3, 0), (LOAD, 4, 0), (USE, 3, 0), (USE, 4, 0), (FAR_SENDS, 2), (FAR_SWAP, 2), (LOW,),
    (LOAD, 2, 0), (LOAD, 2, 1), (USE, 2, 0), (LOAD, 2, 2), (USE, 2, 1), (LOAD, 2, 3), (USE, 2, 2), (USE, 2, 3),
    (PART,), (PLANE_SWAP, 3), (LOAD, 3, 1), (LOAD, 3, 2), (USE, 3, 1), (SECOND, 4), (PLANE_SWAP, 4), (USE, 3, 2),
    (LOAD, 4, 1), (LOAD, 4, 2), (USE, 4, 1), (FAR_SENDS, 3), (USE, 4, 2), (END, 2), (FAR_SENDS, 4), (FAR_SWAP, 4),
    (FAR_SWAP, 3), (LOAD, 4, 3), (LOAD, 3, 3), (USE, 4, 3), (USE, 3, 3), (END, 4),
]


def flipped(me, bits):
    return me + bits - 2 * bits * lax.rem(lax.div(me, bits), 2)


def pack_rows(pack):
    return ATT_ROWS if pack < 2 else FFN_ROWS


def masked_probs(scores, length):
    rows = scores.shape[0]
    position = lax.broadcasted_iota(jnp.int32, (rows, LEN), 1)
    parts = []
    for head in range(2):
        part = jnp.where(position < length, scores[:, head * LEN : (head + 1) * LEN], masked_fill)
        part = jnp.exp(part - jnp.max(part, axis=1, keepdims=True))
        parts.append(part / jnp.sum(part, axis=1, keepdims=True))
    return jnp.concatenate(parts, axis=1)


def two_heads(rows):
    first = lax.broadcasted_iota(jnp.int32, rows.shape, 1) < DH
    zero = jnp.zeros_like(rows)
    return jnp.concatenate([jnp.where(first, rows, zero), jnp.where(first, zero, rows)], axis=0)


def norm_block(values):
    centred = values - jnp.mean(values, axis=1, keepdims=True)
    inverse = lax.rsqrt(jnp.mean(centred * centred, axis=1, keepdims=True) + norm_epsilon)
    return (centred * inverse, inverse)


def forward_kernel(
    lengths,
    x_hbm,
    t_weights,
    t_small,
    s_weights,
    s_small,
    gathered,
    kept,
    vectors,
    x_ref,
    scratch,
    raw_t,
    raw_s,
    mine_att,
    mine_ffn,
    wide,
    total,
    normed,
    low_t,
    context_t,
    bias_rows,
    final_t,
    unit_two,
    inverse_two,
    part_out,
    part_in,
    send,
    recv,
    swap_send,
    swap_recv,
    load,
    fetch,
    save,
):
    t_qv_bias, t_up_bias, t_bias, t_gain, t_shift = t_small
    s_qv_bias, s_up_bias, s_bias, s_gain, s_shift = s_small
    (qkv_t, qkv_s, context_s, slope_t, slope_s, hidden_s, unit_t, inverse_t, unit_s, inverse_s, low_s,
     grad_t, grad_s, final_low) = scratch
    saved = []

    def put(name, index=None):
        src, dst = scratch[name], kept[name]
        if index is not None:
            src, dst = src.at[index], dst.at[index]
        saved.append(pltpu.make_async_copy(src, dst, save.at[len(saved)]))
        saved[-1].start()

    me = lax.axis_index("mp")
    z = lax.axis_index("dp")
    peers = {bits: {"mp": flipped(me, bits)} for bits in (1, 2, 4)}
    peers["z"] = {"dp": flipped(z, 1)}
    upper = lax.rem(z, 2)
    rows = x_ref.shape[0]
    pairs = rows // LEN

    barrier = pltpu.get_barrier_semaphore()
    for peer in peers.values():
        pl.semaphore_signal(barrier, inc=1, device_id=peer, device_id_type=MESH)

    fetched = []
    for weights, raw, direct in ((t_weights, raw_t, True), (s_weights, raw_s, False)):
        qkv, out, up, down = weights
        if direct:
            half = pl.ds(pl.multiple_of(upper * HALF_UNITS, HALF_UNITS), HALF_UNITS)
            moves = [
                (qkv, raw[0]),
                (up.at[:, half], raw[1]),
                (out, mine_att.at[0, pl.ds(3 * COLS, COLS)]),
                (down.at[half], mine_ffn.at[0, pl.ds(HALF_UNITS, HALF_UNITS)]),
            ]
        else:
            moves = [(qkv, raw[0]), (up, raw[1]), (out, raw[2]), (down, raw[3])]
        for src, dst in moves:
            fetched.append(pltpu.make_async_copy(src, dst, fetch.at[len(fetched)]))
            fetched[-1].start()

    x_copy = pltpu.make_async_copy(x_hbm, x_ref, fetch.at[8 + PACKS])
    x_copy.start()

    def signed(values, axis):
        scale = jnp.mean(jnp.abs(values), axis=axis, keepdims=True)
        return to_low(jnp.where(values > 0, scale, jnp.where(values < 0, -scale, 0.0)))

    def bias_block(qv_bias, up_bias):
        line = jnp.concatenate(
            [
                to_float(qv_bias[0:1]),
                to_float(qv_bias[1:2]),
                to_float(up_bias[...]).reshape(1, -1),
                jnp.zeros((1, x_ref.shape[1] - 2 * COLS - 2 * HALF_UNITS), jnp.float32),
            ],
            axis=1,
        )
        row = lax.broadcasted_iota(jnp.int32, (16, line.shape[1]), 0)
        return to_low(jnp.where(row == 0, jnp.broadcast_to(line, row.shape), 0.0))

    def own_copy(pack):
        return pltpu.make_async_copy(source(pack), block(pack, 0), fetch.at[8 + pack])

    def prepare(pack):
        if pack == 0:
            fetched[0].wait()
            for i in range(3):
                mine_att[0, i * COLS : (i + 1) * COLS] = raw_t[0][i].T
            mine_att[0, 4 * COLS : 4 * COLS + 16] = bias_block(t_qv_bias, t_up_bias)
            fetched[2].wait()
        elif pack == 1:
            fetched[4].wait()
            for i in range(3):
                mine_att[1, i * COLS : (i + 1) * COLS] = signed(raw_s[0][i], 0).T
            mine_att[1, 4 * COLS : 4 * COLS + 16] = bias_block(s_qv_bias, s_up_bias)
            fetched[6].wait()
            mine_att[1, 3 * COLS : 4 * COLS] = signed(raw_s[2][...], 1)
        elif pack == SHARED_FFN:
            fetched[1].wait()
            mine_ffn[0, 0:HALF_UNITS] = raw_t[1][...].T
            fetched[3].wait()
        else:
            half = pack - 3
            here = slice(half * HALF_UNITS, (half + 1) * HALF_UNITS)
            if half == 0:
                fetched[5].wait()
                fetched[7].wait()
            mine_ffn[1 + half, 0:HALF_UNITS] = signed(raw_s[1][:, here], 0).T
            mine_ffn[1 + half, HALF_UNITS : 2 * HALF_UNITS] = signed(raw_s[3][here], 1)
        own_copy(pack).start()

    def source(pack):
        return mine_att.at[pack] if pack < 2 else mine_ffn.at[pack - 2]

    def span(pack, start, count):
        return pl.ds(pl.multiple_of(start, 16), count)

    def block(pack, slot):
        return gathered.at[pack, slot, pl.ds(0, pack_rows(pack))]

    def remote(pack, kind):
        shared = SHARED[pack]
        rest = pack_rows(pack) - shared
        first = (rest // 2 + 15) // 16 * 16
        low = upper * shared
        if kind == 0 or kind == 1:
            here = span(pack, low, rest)
            src, dst = source(pack).at[here], gathered.at[pack, 2 + 2 * kind, here]
            peer = peers[2 + 2 * kind]
        elif kind == 2:
            here = span(pack, low, first)
            src, dst, peer = gathered.at[pack, 4, here], gathered.at[pack, 6, here], peers[2]
        elif kind == 3:
            here = span(pack, low + first, rest - first)
            src, dst, peer = gathered.at[pack, 2, here], gathered.at[pack, 6, here], peers[4]
        elif kind == 4:
            src, dst, peer = source(pack), block(pack, 1), peers[1]
        elif kind < 8:
            slot = 2 * (kind - 4)
            src, dst, peer = block(pack, slot), block(pack, slot + 1), peers[1]
        else:
            here = span(pack, upper * rest, shared)
            slot = 2 * (kind - 7)
            src, dst, peer = gathered.at[pack, slot, here], gathered.at[pack, slot, here], peers["z"]
        return pltpu.make_async_remote_copy(
            src_ref=src,
            dst_ref=dst,
            send_sem=send.at[pack, kind],
            recv_sem=recv.at[pack, kind],
            device_id=peer,
            device_id_type=MESH,
        )

    def first_sends(pack):
        for kind in (0, 1, 4):
            remote(pack, kind).start()

    def second_sends(pack):
        remote(pack, 0).wait_recv()
        remote(pack, 3).start()
        if SHARED[pack]:
            remote(pack, 8).start()
        remote(pack, 1).wait_recv()
        remote(pack, 2).start()
        if SHARED[pack]:
            remote(pack, 9).start()

    def plane_swap(pack):
        for kind in (0, 1):
            if SHARED[pack]:
                remote(pack, 8 + kind).wait_recv()
            remote(pack, 5 + kind).start()

    def far_sends(pack):
        remote(pack, 2).wait_recv()
        remote(pack, 3).wait_recv()
        if SHARED[pack]:
            remote(pack, 10).start()

    def far_swap(pack):
        if SHARED[pack]:
            remote(pack, 10).wait_recv()
        remote(pack, 7).start()

    places = {}

    def load_copy(pack, pair):
        here = pl.ds(0, pack_rows(pack))
        place = places[pack, pair]
        return pltpu.make_async_copy(
            gathered.at[pack, pl.ds(2 * pair, 2), here], wide.at[place, :, here], load.at[place]
        )

    def load_pair(pack, pair):
        places[pack, pair] = len(places) % 2
        if pair == 0:
            own_copy(pack).wait()
        remote(pack, 4 + pair).wait_recv()
        load_copy(pack, pair).start()

    started = set()
    student, own, both = slice(0, rows), slice(rows, 2 * rows), slice(rows, 3 * rows)

    def add_total(here, kind, values):
        if kind in started:
            total[here] += values
        else:
            total[here] = values
        started.add(kind)

    def attention(pack, pair, place, qkv_ref, context_ref):
        weights = wide[place, :, 0:384].reshape(768, -1)
        projected = dot_nt(x_ref[...], weights)
        for side in range(2):
            slot = 2 * pair + side
            bias = wide[place, side, 512:528]
            bias_rows[pack, slot] = bias
            bias = to_float(bias[0:1])
            part = projected[:, side * 384 : side * 384 + 384]
            query = to_low(part[:, :COLS] + bias[:, :COLS])
            key = to_low(part[:, COLS : 2 * COLS])
            value = to_low(part[:, 2 * COLS :] + bias[:, COLS : 2 * COLS])
            qkv_ref[slot, :, 0:COLS] = query
            qkv_ref[slot, :, COLS : 2 * COLS] = key
            qkv_ref[slot, :, 2 * COLS : 3 * COLS] = value
            for number in range(pairs):
                here = slice(number * LEN, (number + 1) * LEN)
                scores = dot_nt(query[here], two_heads(key[here])) * (1.0 / math.sqrt(DH))
                probs = masked_probs(scores, lengths[me * pairs + number])
                part_context = dot(to_low(probs), two_heads(value[here]))
                context_ref[pair, here, side * COLS : (side + 1) * COLS] = to_low(part_context)
        put(pack, pl.ds(2 * pair, 2))
        if pack == 1:
            put(2, pair)
        add_total((own, student)[pack], pack, dot(context_ref[pair], wide[place, :, 384:512].reshape(256, -1)))

    def first_norm(bias_ref, gain_ref, shift_ref, unit_ref, inverse_ref, index, low_ref, start):
        @pl.loop(0, rows // 64)
        def _(step):
            here = pl.ds(step * 64, 64)
            values = to_float(x_ref[here]) + total[pl.ds(start + step * 64, 64)] + to_float(bias_ref[0:1])
            unit, inverse = norm_block(values)
            unit_ref[here] = unit
            inverse_ref[here] = inverse
            values = unit * to_float(gain_ref[0:1]) + to_float(shift_ref[0:1])
            normed[index, here] = values
            low_ref[here] = to_low(values)

    def feed_forward(pack, pair, place, low_ref, activation, hidden_ref, slope_ref):
        up = wide[place, :, 0:HALF_UNITS].reshape(2 * HALF_UNITS, -1)
        down = wide[place, :, HALF_UNITS : 2 * HALF_UNITS].reshape(2 * HALF_UNITS, -1)
        layer, half = (0, upper) if pack == SHARED_FFN else (1, pack - 3)
        start = pl.multiple_of(2 * COLS + half * HALF_UNITS, HALF_UNITS)
        bias = jnp.concatenate(
            [to_float(bias_rows[layer, 2 * pair + side, 0:1, pl.ds(start, HALF_UNITS)]) for side in range(2)],
            axis=1,
        )
        hidden, slope = activation(dot_nt(low_ref[...], up) + bias)
        hidden = to_low(hidden)
        if pack == SHARED_FFN:
            slope_ref[pair] = to_low(slope)
            put(3, pair)
        else:
            slope_ref[half, pair] = to_low(slope)
            put(4, (half, pair))
            hidden_ref[half, pair] = hidden
            put(5, (half, pair))
        add_total((both, student)[layer], 2 + layer, dot(hidden, down))

    def swap(number, src, dst):
        return pltpu.make_async_remote_copy(
            src_ref=src,
            dst_ref=dst,
            send_sem=swap_send.at[number],
            recv_sem=swap_recv.at[number],
            device_id=peers["z"],
            device_id_type=MESH,
        )

    low_swap = swap(0, low_t.at[pl.ds(0, rows)], low_t.at[pl.ds(rows, rows)])
    part_swap = swap(1, part_out, part_in)

    def send_part():
        part_out[...] = to_low(total[2 * rows : 3 * rows])
        part_swap.start()

    def step_teacher_end():
        part_swap.wait_recv()

        @pl.loop(0, rows // 64)
        def _(step):
            here = pl.ds(step * 64, 64)
            unit, inverse = norm_block(
                normed[0, here]
                + total[pl.ds(rows + step * 64, 64)]
                + to_float(part_in[here])
                + to_float(t_bias[1:2])
            )
            unit_two[here] = unit
            inverse_two[here] = inverse
            final_t[here] = unit * to_float(t_gain[1:2]) + to_float(t_shift[1:2])

    def step_student_end():
        vectors[...] = jnp.zeros_like(vectors)
        for step in range(rows // 64):
            here = pl.ds(step * 64, 64)
            unit, inverse = norm_block(normed[1, here] + total[here] + to_float(s_bias[1:2]))
            gain = to_float(s_gain[1:2])
            final = unit * gain + to_float(s_shift[1:2])
            final_low[here] = to_low(final)
            position = lax.broadcasted_iota(jnp.int32, (64, 1), 0) + step % 2 * 64
            valid = position < lengths[me * pairs + step // 2]
            grad = jnp.where(valid, final - final_t[here], 0.0)
            back = norm_back(grad, unit, inverse, gain)
            grad_s[here] = back
            grad_t[here] = norm_back(
                -grad, unit_two[here], inverse_two[here], to_float(t_gain[1:2])
            )
            for name in (11, 12, 13):
                put(name, here)
            vectors[0:1] += jnp.sum(back, axis=0, keepdims=True)
            vectors[1:2] += jnp.sum(grad * unit, axis=0, keepdims=True)
            vectors[2:3] += jnp.sum(grad, axis=0, keepdims=True)

    def use(pack, pair):
        place = places[pack, pair]
        load_copy(pack, pair).wait()
        if pack == 0:
            attention(0, pair, place, qkv_t, context_t)
        elif pack == 1:
            attention(1, pair, place, qkv_s, context_s)
        elif pack == SHARED_FFN:
            feed_forward(pack, pair, place, low_t, plain_act, None, slope_t)
        else:
            feed_forward(pack, pair, place, low_s, clipped_act, hidden_s, slope_s)

    def end(pack):
        if pack == 0:
            first_norm(t_bias, t_gain, t_shift, unit_t, inverse_t, 0, low_t, rows)
            low_swap.start()
            put(6)
            put(7)
        elif pack == 1:
            first_norm(s_bias, s_gain, s_shift, unit_s, inverse_s, 1, low_s, 0)
            for name in (8, 9, 10):
                put(name)
        elif pack == SHARED_FFN:
            step_teacher_end()
        else:
            step_student_end()

    def meet():
        pl.semaphore_wait(barrier, len(peers))
        x_copy.wait()

    actions = (
        meet, prepare, first_sends, second_sends, plane_swap, far_sends, far_swap, low_swap.wait_recv, send_part,
        load_pair, use, end,
    )
    for action, *which in FORWARD:
        actions[action](*which)
    low_swap.wait_send()
    part_swap.wait_send()
    for pack in range(PACKS):
        for kind in range(11 if SHARED[pack] else 8):
            remote(pack, kind).wait_send()
    for copy in saved:
        copy.wait()


def forward_both(lengths, tokens, teacher, student):
    rows, features = tokens.shape
    low, full = jnp.bfloat16, jnp.float32
    vmem = pl.BlockSpec(memory_space=pltpu.VMEM)
    hbm = pl.BlockSpec(memory_space=pl.ANY)
    dma = pltpu.SemaphoreType.DMA
    act = (2, 4, rows, 2 * HALF_UNITS)
    kept = [
        ((SLOTS, rows, 3 * COLS), low),
        ((SLOTS, rows, 3 * COLS), low),
        ((4, rows, 2 * COLS), low),
        ((4, 2 * rows, 2 * HALF_UNITS), low),
        (act, low),
        (act, low),
        ((rows, features), full),
        ((rows, 1), full),
        ((rows, features), full),
        ((rows, 1), full),
        ((rows, features), low),
        ((rows, features), full),
        ((rows, features), full),
        ((rows, features), low),
    ]
    shapes = [jax.ShapeDtypeStruct(shape, kind) for shape, kind in kept]
    qkv, out, up, down = teacher[0]
    return pl.pallas_call(
        forward_kernel,
        out_shape=[
            jax.ShapeDtypeStruct((PACKS, SLOTS, ATT_ROWS, features), low),
            shapes,
            jax.ShapeDtypeStruct((8, features), full),
        ],
        in_specs=[pl.BlockSpec(memory_space=pltpu.SMEM), hbm] + [[hbm] * 4, [vmem] * 5] * 2,
        out_specs=[hbm, [hbm] * len(kept), vmem],
        scratch_shapes=[
            pltpu.VMEM((rows, features), low),
            [pltpu.VMEM(shape, kind) for shape, kind in kept],
            [pltpu.VMEM(qkv.shape, low), pltpu.VMEM((features, HALF_UNITS), low)],
            [pltpu.VMEM(item.shape, full) for item in (qkv, up, out, down)],
            pltpu.VMEM((2, ATT_ROWS, features), low),
            pltpu.VMEM((3, FFN_ROWS, features), low),
            pltpu.VMEM((2, 2, ATT_ROWS, features), low),
            pltpu.VMEM((3 * rows, features), full),
            pltpu.VMEM((2, rows, features), full),
            pltpu.VMEM((2 * rows, features), low),
            pltpu.VMEM((4, rows, 2 * COLS), low),
            pltpu.VMEM((2, SLOTS, 16, features), low),
            pltpu.VMEM((rows, features), full),
            pltpu.VMEM((rows, features), full),
            pltpu.VMEM((rows, 1), full),
            pltpu.VMEM((rows, features), low),
            pltpu.VMEM((rows, features), low),
            dma((PACKS, 11)),
            dma((PACKS, 11)),
            dma((2,)),
            dma((2,)),
            dma((2,)),
            dma((9 + PACKS,)),
            dma((64,)),
        ],
        compiler_params=pltpu.CompilerParams(
            collective_id=0, has_side_effects=True, vmem_limit_bytes=62 * 1024 * 1024
        ),
        name="forward_both",
    )(lengths, tokens, *teacher, *student)


CHUNKS = 3
PARTS = (4, 4, 8)
ORDER = (3, 1, 2, 0)
STUDENT_FFN, STUDENT_ATT, TEACHER_FFN, TEACHER_ATT = range(4)

COMBINE, FOLD, OWN, MID, OUT, VEC = range(6)
SCHEDULE = {
    (1, 6): [(COMBINE, 0, 3)],
    (2, 6): [(COMBINE, 0, 1)],
    (3, 6): [(COMBINE, 0, 2)],
    (4, 6): [(COMBINE, 0, 0)],
    (5, 6): [(FOLD, 0, 0), (COMBINE, 1, 3)],
    (6, 6): [(COMBINE, 1, 1)],
    (7, 6): [(OWN, 0, 0), (COMBINE, 1, 2)],
    (7, 7): [(COMBINE, 1, 0)],
    (8, 6): [(OWN, 0, 1)],
    (9, 6): [(MID, 0, 0), (OWN, 0, 2)],
    (11, 6): [(MID, 0, 1), (OWN, 0, 3), (OUT, 0, 0)],
    (12, 1): [(MID, 0, 2)],
    (12, 6): [(OUT, 0, 1)],
    (13, 0): [(FOLD, 1, 0)],
    (13, 1): [(COMBINE, 2, 3)],
    (13, 2): [(OUT, 0, 2)],
    (14, 0): [(OWN, 1, 0)],
    (14, 1): [(COMBINE, 2, 1)],
    (14, 6): [(OWN, 1, 1), (MID, 0, 3)],
    (15, 1): [(COMBINE, 2, 2), (OWN, 1, 2)],
    (15, 3): [(MID, 1, 0)],
    (15, 6): [(OUT, 0, 3)],
    (15, 7): [(MID, 1, 1), (OWN, 1, 3), (COMBINE, 2, 0)],
    (16, 0): [(OUT, 1, 0)],
    (16, 3): [(VEC, 0)],
    (16, 4): [(MID, 1, 2)],
    (17, 0): [(OUT, 1, 1), (VEC, 1)],
    (17, 1): [(FOLD, 2, 0)],
    (17, 3): [(MID, 1, 3)],
    (17, 6): [(VEC, 2)],
    (18, 0): [(OUT, 1, 2), (OWN, 2, 0)],
    (18, 4): [(OWN, 2, 1)],
    (18, 6): [(VEC, 3)],
    (19, 0): [(MID, 2, 0), (OWN, 2, 2), (OUT, 1, 3)],
    (19, 3): [(MID, 2, 1), (OWN, 2, 3), (VEC, 4)],
    (19, 6): [(OUT, 2, 0), (MID, 2, 2)],
}
LAST = [
    (OWN, 2, 4), (OUT, 2, 1), (MID, 2, 3), (OWN, 2, 5), (OUT, 2, 2), (MID, 2, 4), (OWN, 2, 6), (OUT, 2, 3),
    (MID, 2, 5), (OWN, 2, 7), (OUT, 2, 4), (MID, 2, 6), (OUT, 2, 5), (MID, 2, 7), (OUT, 2, 6), (OUT, 2, 7),
]


def backward_kernel(
    lengths,
    x_hbm,
    gathered,
    qkv_t,
    qkv_s,
    context_s,
    slope_t,
    slope_s,
    hidden_s,
    unit_t,
    inverse_t,
    unit_s,
    inverse_s,
    low_s,
    grad_t,
    grad_s,
    vectors,
    t_gain,
    s_gain,
    grad_out,
    sums_out,
    vec,
    x_ref,
    grad_in,
    wide,
    hidden_buf,
    slope_buf,
    qkv_s_buf,
    qkv_t_buf,
    context_buf,
    extra_buf,
    unit_buf,
    inverse_buf,
    grad_buf,
    total,
    low_y,
    low_z,
    low_zt,
    back_out,
    back_in,
    low_a,
    proj,
    sums,
    even,
    odd,
    from_core,
    from_far,
    from_x,
    from_y,
    from_z,
    from_vec,
    load,
    state_sem,
    odd_send,
    odd_recv,
    free,
    far_send,
    far_recv,
    x_send,
    x_recv,
    y_send,
    y_recv,
    in_send,
    in_recv,
    mid_send,
    mid_recv,
    out_send,
    out_recv,
    vec_send,
    vec_recv,
    swap_send,
    swap_recv,
    done,
):
    me = lax.axis_index("mp")
    z = lax.axis_index("dp")
    rows = x_ref.shape[0]
    pairs = rows // LEN
    core, along_x, along_y = ({"mp": flipped(me, bits)} for bits in (1, 2, 4))
    z_outer, z_inner = {"dp": flipped(z, 1)}, {"dp": 3 - z}
    z_two = {"dp": flipped(z, 2)}
    inner = jnp.logical_or(z == 1, z == 2)
    outer = jnp.logical_or(z == 0, z == 3)

    barrier = pltpu.get_barrier_semaphore()
    greeted = (core, along_x, along_y, z_outer, z_inner, z_two)
    for peer in greeted:
        pl.semaphore_signal(barrier, inc=1, device_id=peer, device_id_type=MESH)

    def remote(src, dst, send, recv, peer):
        return pltpu.make_async_remote_copy(
            src_ref=src, dst_ref=dst, send_sem=send, recv_sem=recv, device_id=peer, device_id_type=MESH
        )

    steps = [(STUDENT_FFN, 3 + half, pair) for half in range(2) for pair in ORDER]
    steps += [(TEACHER_FFN, SHARED_FFN, pair) for pair in range(4)]
    steps += [(STUDENT_ATT, 1, pair) for pair in ORDER]
    steps += [(TEACHER_ATT, 0, pair) for pair in range(4)]
    norm_at = (7, 15)

    def given(number):
        return number if number < 8 else number - 4

    def loads(number):
        kind, pack, pair = steps[number]
        place = number % 2
        two = pl.ds(2 * pair, 2)
        here = pl.ds(0, FFN_ROWS)
        moves = [(gathered.at[pack, two, here], wide.at[place])]
        if kind == STUDENT_FFN:
            moves.append((hidden_s.at[pack - 3, pair], hidden_buf.at[place]))
            moves.append((slope_s.at[pack - 3, pair], slope_buf.at[place, pl.ds(0, rows)]))
        elif kind == TEACHER_FFN:
            moves.append((slope_t.at[pair], slope_buf.at[place]))
        else:
            moves.append((qkv_t.at[two], qkv_t_buf.at[place]))
            if kind == STUDENT_ATT:
                moves.append((qkv_s.at[two], qkv_s_buf.at[place]))
                moves.append((context_s.at[pair], context_buf.at[place]))
        return [
            pltpu.make_async_copy(src, dst, load.at[place, index])
            for index, (src, dst) in enumerate(moves)
        ]

    def state(layer):
        unit, inverse = ((unit_t, inverse_t), (unit_s, inverse_s))[layer]
        return [
            pltpu.make_async_copy(src, dst, state_sem.at[index])
            for index, (src, dst) in enumerate([(inverse, inverse_buf), (unit, unit_buf)])
        ]

    def slot_row(slot):
        row = me
        for bits in (1, 2, 4):
            if slot & bits:
                row = flipped(row, bits)
        return row

    def odd_copy(index):
        pair = ORDER[index % 4]
        return remote(
            odd.at[index % 2], from_core.at[pair], odd_send.at[index % 2], odd_recv.at[pair], core
        )

    def keep(chunk, pair):
        return sums.at[chunk] if pair == 0 else even.at[chunk, pair - 1]

    def give(number, pieces):
        pair = steps[number][2]
        index = given(number)
        chunk = index // 4
        if index >= 2:
            odd_copy(index - 2).wait_send()
        for start, values in pieces:
            count = values.shape[0] // 2
            keep(chunk, pair)[start : start + count] = to_low(values[:count])
            odd[index % 2, start : start + count] = to_low(values[count:])
        if chunk:
            pl.semaphore_wait(free.at[pair], 1)
        if number == 0:
            pl.semaphore_wait(barrier, len(greeted))
        odd_copy(index).start()

    def add_rows(target, others, start, count):
        @pl.loop(0, count // 64)
        def _(step):
            here = pl.ds(start + step * 64, 64)
            value = to_float(target[here])
            for other in others:
                value = value + to_float(other[here])
            target[here] = to_low(value)

    def combine(chunk, pair):
        number = chunk * 4 + ORDER.index(pair)
        odd_copy(number).wait_recv()
        add_rows(keep(chunk, pair), [from_core.at[pair]], 0, FFN_ROWS)
        if chunk < CHUNKS - 1:
            pl.semaphore_signal(free.at[pair], inc=1, device_id=core, device_id_type=MESH)
        if pair == 3:
            far_copy(chunk, 0).start()
            far_copy(chunk, 1).start()

    def far_copy(chunk, way):
        part = pl.ds(way * 256, 256)
        return remote(
            even.at[chunk, 2, part],
            from_far.at[chunk, part],
            far_send.at[chunk, way],
            far_recv.at[chunk, way],
            (along_x, along_y)[way],
        )

    def part_rows(chunk):
        return FFN_ROWS // PARTS[chunk]

    def part_span(chunk, part):
        return pl.ds(part * part_rows(chunk), part_rows(chunk))

    def plane_copies(chunk, part):
        here = part_span(chunk, part)
        return [
            remote(even.at[chunk, 0, here], from_x.at[chunk, here], x_send.at[chunk, part], x_recv.at[chunk, part], along_x),
            remote(even.at[chunk, 1, here], from_y.at[chunk, here], y_send.at[chunk, part], y_recv.at[chunk, part], along_y),
        ]

    def fold(chunk, _):
        far_copy(chunk, 0).wait_recv()
        add_rows(keep(chunk, 2), [from_far.at[chunk]], 0, 256)
        far_copy(chunk, 1).wait_recv()
        add_rows(keep(chunk, 1), [from_far.at[chunk]], 256, 256)
        for part in range(PARTS[chunk]):
            for copy in plane_copies(chunk, part):
                copy.start()

    def z_copy(chunk, part, kind):
        here = part_span(chunk, part)
        own, first, second = sums.at[chunk, here], from_z.at[chunk, 0, here], from_z.at[chunk, 1, here]
        if kind == 0:
            return remote(own, first, in_send.at[chunk, part], in_recv.at[chunk, part], z_outer)
        if kind == 1:
            return remote(own, second, mid_send.at[chunk, part], mid_recv.at[chunk, part], z_inner)
        return remote(first, first, out_send.at[chunk, part], out_recv.at[chunk, part], z_outer)

    def own_part(chunk, part):
        for copy in plane_copies(chunk, part):
            copy.wait_recv()
        add_rows(sums.at[chunk], [from_x.at[chunk], from_y.at[chunk]], part * part_rows(chunk), part_rows(chunk))

        @pl.when(outer)
        def _():
            z_copy(chunk, part, 0).start()

    def mid_part(chunk, part):
        @pl.when(inner)
        def _():
            z_copy(chunk, part, 0).wait_recv()
            add_rows(sums.at[chunk], [from_z.at[chunk, 0]], part * part_rows(chunk), part_rows(chunk))
            z_copy(chunk, part, 1).start()

    def end_part(chunk, part):
        @pl.when(inner)
        def _():
            z_copy(chunk, part, 1).wait_recv()

            @pl.loop(0, part_rows(chunk) // 64)
            def _(step):
                here = pl.ds(part * part_rows(chunk) + step * 64, 64)
                value = to_float(sums[chunk, here]) + to_float(from_z[chunk, 1, here])
                from_z[chunk, 0, here] = to_low(value)

            z_copy(chunk, part, 2).start()

    def store_copy(chunk):
        return pltpu.make_async_copy(from_z.at[chunk, 0], sums_out.at[chunk], done.at[chunk])

    def finish(chunk):
        @pl.when(outer)
        def _():
            for part in range(PARTS[chunk]):
                z_copy(chunk, part, 2).wait_recv()

        store_copy(chunk).start()

    ways = (core, along_x, along_y, z_outer, z_two)

    def vec_copy(way):
        return remote(vec, from_vec.at[way], vec_send.at[way], vec_recv.at[way], ways[way])

    def vec_add(way):
        vec_copy(way).wait_send()
        vec_copy(way).wait_recv()
        vec[...] += from_vec[way]
        if way + 1 < len(ways):
            vec_copy(way + 1).start()

    def put_bias(pair, start, values):
        count = values.shape[1] // 2
        for side in range(2):
            line = lax.broadcasted_iota(jnp.int32, (SLOTS, count), 0)
            part = jnp.broadcast_to(values[:, side * count : (side + 1) * count], (SLOTS, count))
            part = jnp.where(line == slot_row(2 * pair + side), part, 0.0)
            vec[0:SLOTS, start : start + count] += part

    def ffn_step(number):
        kind, pack, pair = steps[number]
        place = number % 2
        up = wide[place, :, 0:HALF_UNITS].reshape(2 * HALF_UNITS, -1)
        down = wide[place, :, HALF_UNITS : 2 * HALF_UNITS].reshape(2 * HALF_UNITS, -1)
        student = kind == STUDENT_FFN
        grad, here = (low_z, slice(0, rows)) if student else (low_zt, slice(0, 2 * rows))
        back = dot_nt(grad[...], down) * to_float(slope_buf[place, here])
        back_low = to_low(back)
        if number in (0, 8):
            total[here] = dot(back_low, up)
        else:
            total[here] += dot(back_low, up)
        if student:
            put_bias(pair, 2 * COLS + (pack - 3) * HALF_UNITS, jnp.sum(back, axis=0, keepdims=True))
            up_grad = dot_tn(back_low, low_y[...])
            down_grad = dot_tn(hidden_buf[place], low_z[...])
            give(number, [(0, up_grad), (HALF_UNITS, down_grad)])

    def pick(both):
        first = lax.broadcasted_iota(jnp.int32, (LEN, COLS), 1) < DH
        return jnp.where(first, both[:LEN], both[LEN:])

    def attention_step(number):
        kind, pack, pair = steps[number]
        place = number % 2
        student = kind == STUDENT_ATT
        factor = 1.0 / math.sqrt(DH)
        qkv = qkv_s_buf if student else qkv_t_buf
        out = wide[place, :, 384:512].reshape(2 * COLS, -1)
        context_back = to_low(dot_nt(low_a[...], out))
        query_sums, value_sums = [], []
        for side in range(2):
            query_sum = jnp.zeros((1, COLS), jnp.float32)
            value_sum = jnp.zeros((1, COLS), jnp.float32)
            for number_b in range(pairs):
                here = slice(number_b * LEN, (number_b + 1) * LEN)
                length = lengths[me * pairs + number_b]
                query, key, value = [
                    qkv[place, side, here, i * COLS : (i + 1) * COLS] for i in range(3)
                ]
                keys, values = two_heads(key), two_heads(value)
                scores = dot_nt(query, keys) * factor
                probs = masked_probs(scores, length)
                if student:
                    other = dot_nt(
                        qkv_t_buf[place, side, here, 0:COLS],
                        two_heads(qkv_t_buf[place, side, here, COLS : 2 * COLS]),
                    )
                    spot = lax.broadcasted_iota(jnp.int32, scores.shape, 1)
                    spot = jnp.where(spot < LEN, spot, spot - LEN)
                    line = lax.broadcasted_iota(jnp.int32, scores.shape, 0)
                    gap = score_weight * (scores - other * factor)
                    extra = jnp.where(jnp.maximum(spot, line) < length, gap, 0.0)
                    extra_buf[pair, side, number_b] = to_low(extra)
                else:
                    extra = -to_float(extra_buf[pair, side, number_b])
                part = context_back[here, side * COLS : (side + 1) * COLS]
                probs_back = dot_nt(part, values)
                value_back = pick(dot_tn(to_low(probs), part))
                product = probs * probs_back
                inner_sum = jnp.concatenate(
                    [
                        jnp.broadcast_to(
                            jnp.sum(product[:, i * LEN : (i + 1) * LEN], axis=1, keepdims=True), (LEN, LEN)
                        )
                        for i in range(2)
                    ],
                    axis=1,
                )
                score_back = to_low(product - probs * inner_sum + extra)
                query_back = dot(score_back, keys) * factor
                key_back = pick(dot_tn(score_back, query)) * factor
                start = side * 3 * COLS
                proj[here, start : start + COLS] = to_low(query_back)
                proj[here, start + COLS : start + 2 * COLS] = to_low(key_back)
                proj[here, start + 2 * COLS : start + 3 * COLS] = to_low(value_back)
                if student:
                    query_sum += jnp.sum(query_back, axis=0, keepdims=True)
                    value_sum += jnp.sum(value_back, axis=0, keepdims=True)
                if side * pairs + number_b < 2 * pairs - 1:
                    after(number, side * pairs + number_b)
            query_sums.append(query_sum)
            value_sums.append(value_sum)
        grad_in[...] += dot(proj[...], wide[place, :, 0:384].reshape(768, -1))
        if student:
            put_bias(pair, 0, jnp.concatenate(query_sums, axis=1))
            put_bias(pair, COLS, jnp.concatenate(value_sums, axis=1))
            qkv_grad = dot_tn(proj[...], x_ref[...])
            out_grad = dot_tn(context_buf[place], low_a[...])
            give(number, [(0, qkv_grad), (3 * COLS, out_grad)])

    def lower_grad(src, start, dst):
        @pl.loop(0, rows // 64)
        def _(step):
            dst[pl.ds(step * 64, 64)] = to_low(src[pl.ds(start + step * 64, 64)])

    grad_swap = remote(
        low_zt.at[pl.ds(0, rows)], low_zt.at[pl.ds(rows, rows)], swap_send.at[0], swap_recv.at[0], z_outer
    )
    back_swap = remote(back_out, back_in, swap_send.at[1], swap_recv.at[1], z_outer)

    def norm_step(student):
        gain_ref = s_gain if student else t_gain

        @pl.loop(0, rows // 64)
        def _(step):
            here = pl.ds(step * 64, 64)
            grad = grad_buf[here] + total[here]
            if not student:
                grad = grad + to_float(back_in[here])
            unit = unit_buf[here]
            back = norm_back(grad, unit, inverse_buf[here], to_float(gain_ref[0:1]))
            low_a[here] = to_low(back)
            if student:
                grad_in[here] = back
                vec[8:9] += jnp.sum(back, axis=0, keepdims=True)
                vec[9:10] += jnp.sum(grad * unit, axis=0, keepdims=True)
                vec[10:11] += jnp.sum(grad, axis=0, keepdims=True)
            else:
                grad_in[here] += back

    actions = (combine, fold, own_part, mid_part, end_part, vec_add)

    def after(number, part):
        for action, *which in SCHEDULE.get((number, part), ()):
            actions[action](*which)

    low_copy = pltpu.make_async_copy(low_s, low_y, state_sem.at[2])
    x_copy = pltpu.make_async_copy(x_hbm, x_ref, done.at[CHUNKS])
    grad_copies = [
        pltpu.make_async_copy(src, dst, state_sem.at[3 + index])
        for index, (src, dst) in enumerate(
            [(grad_s, grad_buf), (grad_t, total.at[pl.ds(rows, rows)]), (grad_t, grad_buf)]
        )
    ]
    grad_copies[0].start()
    for copy in loads(0):
        copy.start()
    for copy in (low_copy, grad_copies[1], *state(1), x_copy):
        copy.start()
    vec[...] = jnp.zeros_like(vec)
    vec[11:14] = vectors[0:3]
    grad_copies[0].wait()
    lower_grad(grad_buf, 0, low_z)
    low_copy.wait()
    grad_copy = pltpu.make_async_copy(grad_in, grad_out, done.at[CHUNKS + 1])
    for number, (kind, pack, pair) in enumerate(steps):
        for copy in loads(number):
            copy.wait()
        if number + 1 < len(steps):
            for copy in loads(number + 1):
                copy.start()
        if kind in (STUDENT_FFN, TEACHER_FFN):
            ffn_step(number)
        else:
            attention_step(number)
        if number == len(steps) - 1:
            grad_copy.start()
        after(number, 6)
        if number == 0:
            grad_copies[1].wait()
            lower_grad(total, rows, low_zt)
            grad_swap.start()
        elif number == 7:
            for copy in state(1):
                copy.wait()
            x_copy.wait()
            norm_step(True)
            for copy in (*state(0), grad_copies[2]):
                copy.start()
            grad_swap.wait_recv()
        elif number == 11:
            back_out[...] = to_low(total[rows : 2 * rows])
            back_swap.start()
        elif number == 15:
            vec_copy(0).start()
            for copy in (*state(0), grad_copies[2]):
                copy.wait()
            back_swap.wait_recv()
            norm_step(False)
        after(number, 7)
    for action, *which in LAST:
        actions[action](*which)
    for chunk in range(CHUNKS):
        finish(chunk)

    grad_copy.wait()
    grad_swap.wait_send()
    back_swap.wait_send()
    odd_copy(10).wait_send()
    odd_copy(11).wait_send()
    for chunk in range(CHUNKS):
        far_copy(chunk, 0).wait_send()
        far_copy(chunk, 1).wait_send()
        for part in range(PARTS[chunk]):
            for copy in plane_copies(chunk, part):
                copy.wait_send()

            @pl.when(outer)
            def _():
                z_copy(chunk, part, 0).wait_send()

            @pl.when(inner)
            def _():
                z_copy(chunk, part, 1).wait_send()
                z_copy(chunk, part, 2).wait_send()

        store_copy(chunk).wait()


def backward_both(lengths, tokens, kept, vectors, t_gain, s_gain):
    rows, features = tokens.shape
    low, full = jnp.bfloat16, jnp.float32
    vmem = pl.BlockSpec(memory_space=pltpu.VMEM)
    hbm = pl.BlockSpec(memory_space=pl.ANY)
    dma = pltpu.SemaphoreType.DMA
    block = (FFN_ROWS, features)
    return pl.pallas_call(
        backward_kernel,
        out_shape=[
            jax.ShapeDtypeStruct((rows, features), full),
            jax.ShapeDtypeStruct((CHUNKS,) + block, low),
            jax.ShapeDtypeStruct((16, features), full),
        ],
        in_specs=[pl.BlockSpec(memory_space=pltpu.SMEM), hbm] + [hbm] * len(kept) + [vmem] * 3,
        out_specs=[hbm, hbm, vmem],
        scratch_shapes=[
            pltpu.VMEM((rows, features), low),
            pltpu.VMEM((rows, features), full),
            pltpu.VMEM((2, 2) + block, low),
            pltpu.VMEM((2, rows, 2 * HALF_UNITS), low),
            pltpu.VMEM((2, 2 * rows, 2 * HALF_UNITS), low),
            pltpu.VMEM((2, 2, rows, 3 * COLS), low),
            pltpu.VMEM((2, 2, rows, 3 * COLS), low),
            pltpu.VMEM((2, rows, 2 * COLS), low),
            pltpu.VMEM((4, 2, rows // LEN, LEN, 2 * LEN), low),
            pltpu.VMEM((rows, features), full),
            pltpu.VMEM((rows, 1), full),
            pltpu.VMEM((rows, features), full),
            pltpu.VMEM((2 * rows, features), full),
            pltpu.VMEM((rows, features), low),
            pltpu.VMEM((rows, features), low),
            pltpu.VMEM((2 * rows, features), low),
            pltpu.VMEM((rows, features), low),
            pltpu.VMEM((rows, features), low),
            pltpu.VMEM((rows, features), low),
            pltpu.VMEM((rows, 6 * COLS), low),
            pltpu.VMEM((CHUNKS,) + block, low),
            pltpu.VMEM((CHUNKS, 3) + block, low),
            pltpu.VMEM((2,) + block, low),
            pltpu.VMEM((4,) + block, low),
            pltpu.VMEM((CHUNKS,) + block, low),
            pltpu.VMEM((CHUNKS,) + block, low),
            pltpu.VMEM((CHUNKS,) + block, low),
            pltpu.VMEM((CHUNKS, 2) + block, low),
            pltpu.VMEM((5, 16, features), full),
            dma((2, 5)),
            dma((6,)),
            dma((2,)),
            dma((4,)),
            pltpu.SemaphoreType.REGULAR((4,)),
            dma((CHUNKS, 2)),
            dma((CHUNKS, 2)),
        ]
        + [dma((CHUNKS, max(PARTS)))] * 10
        + [dma((5,)), dma((5,)), dma((2,)), dma((2,)), dma((CHUNKS + 2,))],
        compiler_params=pltpu.CompilerParams(
            collective_id=1, has_side_effects=True, vmem_limit_bytes=63 * 1024 * 1024
        ),
        name="backward_both",
    )(lengths, tokens, *kept, vectors, t_gain, s_gain)


def finish_kernel(sums, vec, qkv_out, qv_out, out_out, up_out, up_bias_out, down_out, bias_out, gain_out, shift_out):
    for i in range(3):
        qkv_out[i] = to_float(sums[2, i * COLS : (i + 1) * COLS]).T
    out_out[...] = to_float(sums[2, 3 * COLS :])
    for half in range(2):
        here = slice(half * HALF_UNITS, (half + 1) * HALF_UNITS)
        up_out[:, here] = to_float(sums[half, :HALF_UNITS]).T
        down_out[here] = to_float(sums[half, HALF_UNITS:])
    line = lax.broadcasted_iota(jnp.int32, (SLOTS, vec.shape[1]), 0)
    row = jnp.sum(jnp.where(line == lax.axis_index("mp"), vec[0:SLOTS], 0.0), axis=0, keepdims=True)
    qv_out[0:1] = row[:, :COLS]
    qv_out[1:2] = row[:, COLS : 2 * COLS]
    up_bias_out[...] = row[:, 2 * COLS : 2 * COLS + 2 * HALF_UNITS]
    for index, ref in enumerate((bias_out, gain_out, shift_out)):
        ref[0:1] = vec[8 + index : 9 + index]
        ref[1:2] = vec[11 + index : 12 + index]


def finish_sums(sums, vec):
    features = vec.shape[1]
    shapes = [
        (3, features, COLS),
        (2, COLS),
        (COLS, features),
        (features, 2 * HALF_UNITS),
        (1, 2 * HALF_UNITS),
        (2 * HALF_UNITS, features),
        (2, features),
        (2, features),
        (2, features),
    ]
    vmem = pl.BlockSpec(memory_space=pltpu.VMEM)
    return pl.pallas_call(
        finish_kernel,
        out_shape=[jax.ShapeDtypeStruct(shape, jnp.float32) for shape in shapes],
        in_specs=[vmem, vmem],
        out_specs=[vmem] * len(shapes),
        compiler_params=pltpu.CompilerParams(vmem_limit_bytes=48 * 1024 * 1024),
        name="finish_sums",
    )(sums, vec)


def cut(values, count, axis):
    return jnp.split(values, count, axis=axis)


def per_device(n_dp, n_mp, *args):
    (
        tokens,
        lengths,
        student_qkv,
        student_qv_bias,
        student_out,
        student_up,
        student_up_bias,
        student_down,
        student_out_bias,
        student_gain,
        student_shift,
        teacher_qkv,
        teacher_qv_bias,
        teacher_out,
        teacher_up,
        teacher_up_bias,
        teacher_down,
        teacher_out_bias,
        teacher_gain,
        teacher_shift,
    ) = args
    net = Cube(n_dp) if (n_dp, n_mp) == (4, 8) else Plain(n_mp)
    rows = tokens.shape[0]
    pairs = rows // LEN
    places = jnp.arange(LEN, dtype=jnp.int32)
    me = lax.axis_index("mp")
    own_lengths = lax.dynamic_slice_in_dim(lengths, me * pairs, pairs)
    valid = places[None, :] < own_lengths[:, None]
    token_valid = to_float(valid.reshape(rows, 1))
    pair_valid = valid[:, None, :, None] & valid[:, None, None, :]

    gain = to_float(student_gain)
    shift = to_float(student_shift)
    out_bias = to_float(student_out_bias)
    teach_gain = to_float(teacher_gain)
    if isinstance(net, Cube):
        gathered, (*kept, student_output), vecs = forward_both(
            lengths,
            tokens,
            (
                [teacher_qkv.transpose(1, 0, 2), teacher_out, teacher_up, teacher_down],
                [teacher_qv_bias, teacher_up_bias, teacher_out_bias, teacher_gain, teacher_shift],
            ),
            (
                [student_qkv.transpose(1, 0, 2), student_out, student_up, student_down],
                [student_qv_bias, student_up_bias, student_out_bias, student_gain, student_shift],
            ),
        )
        input_grad, sums, vec = backward_both(
            lengths, tokens, (gathered, *kept), vecs, teacher_gain, student_gain
        )
        grads = finish_sums(sums, vec)
        return (
            student_output,
            input_grad,
            grads[0].transpose(1, 0, 2),
            grads[1],
            grads[2],
            grads[3],
            grads[4].reshape(-1),
            *grads[5:],
        )
    else:
        teach = gather_layer(
            net, teacher_qkv, teacher_qv_bias, teacher_out, teacher_up, teacher_up_bias, teacher_down
        )
        stud = gather_layer(
            net,
            binarize(student_qkv, 0),
            student_qv_bias,
            binarize(student_out, 1),
            binarize(student_up, 0),
            student_up_bias,
            binarize(student_down, 1),
        )
        teach_final, teach_kept = forward(
            tokens, teach, to_float(teacher_out_bias), teach_gain, to_float(teacher_shift), plain_act, valid
        )
        final, kept = forward(tokens, stud, out_bias, gain, shift, clipped_act, valid)
        student_output = to_low(final)
        final_grad = token_valid * (final - teach_final)
        grad_s = norm_back(final_grad, kept[11], kept[12], gain[1])
        grad_t = norm_back(-final_grad, teach_kept[11], teach_kept[12], teach_gain[1])
        vecs = jnp.stack([jnp.sum(grad_s, axis=0), jnp.sum(final_grad * kept[11], axis=0), jnp.sum(final_grad, axis=0)])
    extra = score_weight * jnp.where(pair_valid, kept[3] - teach_kept[3], 0.0)

    second_grad, second_low, pre_grad, pre_low, normed_grad, first_grad = backward_ffn(
        kept, stud, grad_s, gain
    )
    hidden, normed_low, context = kept[9], kept[8], kept[5]
    unit_one = kept[6]
    down_grad = net.sum_dp(net.scatter(cut(to_low(dot_tn(hidden, second_low)), n_mp, 0)))
    up_grad = net.sum_dp(net.scatter(cut(to_low(dot_tn(normed_low, pre_low)), n_mp, 1)))
    first_low = to_low(first_grad)
    out_grad = net.sum_dp(net.scatter(cut(to_low(dot_tn(context, first_low)), n_mp, 0)))
    grads = backward_attention(kept, first_low, stud[3], extra)
    lows = [to_low(item) for item in grads]
    wide = jnp.concatenate(
        [to_low(dot_tn(tokens, item)) for item in lows], axis=0
    )
    qkv_grad = net.sum_dp(net.scatter(cut(wide, n_mp, 1)))
    features = tokens.shape[1]
    qkv_grad = qkv_grad.reshape(3, features, -1).transpose(1, 0, 2)

    teach_second, teach_slow, _, _, _, teach_first = backward_ffn(
        teach_kept, teach, grad_t, teach_gain
    )
    teach_grads = backward_attention(teach_kept, to_low(teach_first), teach[3], -extra)
    teach_lows = [to_low(item) for item in teach_grads]
    input_grad = first_grad + teach_first
    for item, matrix in zip(lows, stud[0]):
        input_grad = input_grad + dot_nt(item, matrix)
    for item, matrix in zip(teach_lows, teach[0]):
        input_grad = input_grad + dot_nt(item, matrix)

    vectors = [
        jnp.sum(first_grad, axis=0),
        vecs[0],
        jnp.sum(normed_grad * unit_one, axis=0),
        vecs[1],
        jnp.sum(normed_grad, axis=0),
        vecs[2],
        net.place(jnp.sum(grads[0], axis=0).reshape(n_mp, -1)).reshape(-1),
        net.place(jnp.sum(grads[2], axis=0).reshape(n_mp, -1)).reshape(-1),
    ]
    wide_vector = net.place(jnp.sum(pre_grad, axis=0).reshape(n_mp, -1)).reshape(-1, features)
    total = net.sum_all(jnp.concatenate([jnp.stack(vectors), wide_vector], axis=0))
    width = features // n_mp
    units = wide_vector.size // n_mp
    return (
        student_output,
        input_grad,
        qkv_grad,
        lax.dynamic_slice_in_dim(total[6:8], me * width, width, axis=1),
        out_grad,
        up_grad,
        lax.dynamic_slice_in_dim(total[8:].reshape(-1), me * units, units),
        down_grad,
        total[0:2],
        total[2:4],
        total[4:6],
    )


def solution(mesh):
    n_dp, n_mp = mesh.shape["dp"], mesh.shape["mp"]

    def body(*args):
        return per_device(n_dp, n_mp, *args)

    return jax.shard_map(
        body,
        mesh=mesh,
        in_specs=(
            P(("dp", "mp"), None),
            P("dp"),
            P(None, None, "mp"),
            P(None, "mp"),
            P("mp", None),
            P(None, "mp"),
            P("mp"),
            P("mp", None),
            P(),
            P(),
            P(),
            P(None, None, "mp"),
            P(None, "mp"),
            P("mp", None),
            P(None, "mp"),
            P("mp"),
            P("mp", None),
            P(),
            P(),
            P(),
        ),
        out_specs=(
            P(("dp", "mp"), None),
            P(("dp", "mp"), None),
            P(None, None, "mp"),
            P(None, "mp"),
            P("mp", None),
            P(None, "mp"),
            P("mp"),
            P("mp", None),
            P(),
            P(),
            P(),
        ),
        check_vma=False,
    )
```
